32 devices in a mesh: ctx: 16 (over z, x, core), tp: 2 (over y).
Axes of the slice: x: 2, y: 2, z: 4, core: 2. Of those that a mesh axis runs over, the one named last changes fastest.
Arguments:
- tokens: bfloat16 [2048, 2048], P('ctx'), may hold values from -6 to 6
- block_order: int32 [32], replicated, may hold values from 0 to 31, each once
- ln_gain: float32 [2048], replicated, may hold values from 0.1 to 1.9
- ln_bias: float32 [2048], replicated, may hold values from -1.8 to 1.8
- qkv_weight: bfloat16 [2048, 3, 2048], P('ctx', None, 'tp'), may hold values from -0.125 to 0.125
- qkv_bias: float32 [3, 2048], P(None, 'tp'), may hold values from -3 to 3
- out_weight: bfloat16 [2048, 2048], P('ctx', 'tp'), may hold values from -0.5 to 0.5
- fc1_weight: bfloat16 [2048, 8192], P('ctx', 'tp'), may hold values from -0.125 to 0.125
- fc1_bias: float32 [8192], P('tp'), may hold values from -3 to 3
- fc2_weight: bfloat16 [2048, 8192], P('ctx', 'tp'), may hold values from -0.09375 to 0.09375
- out_bias: float32 [2048], replicated, may hold values from -3 to 3
- cotangent: bfloat16 [2048, 2048], P('ctx'), may hold values from -6 to 6
Outputs:
- output: float32 [2048, 2048], P('ctx')
- input_grad: float32 [2048, 2048], P('ctx')
- ln_gain_grad: float32 [2048], replicated
- ln_bias_grad: float32 [2048], replicated
- qkv_weight_grad: float32 [2048, 3, 2048], P('ctx', None, 'tp')
- qkv_bias_grad: float32 [3, 2048], P(None, 'tp')
- out_weight_grad: float32 [2048, 2048], P('ctx', 'tp')
- fc1_weight_grad: float32 [2048, 8192], P('ctx', 'tp')
- fc1_bias_grad: float32 [8192], P('tp')
- fc2_weight_grad: float32 [2048, 8192], P('ctx', 'tp')
- out_bias_grad: float32 [2048], replicated
The draws below stay inside these ranges and needn't reach their ends.
Inputs may be any that keep to these rules, and one draw needn't show every extreme that they name: block_order is a permutation: each of the 32 half-blocks of 64 positions is held by exactly one pair of rows.
All inputs are finite; a program needn't handle non-finite values.
Results may differ from the reference program's by a relative error of at most 0.015.
Values may be sent and summed in bfloat16 or wider, within the bound.
A program may use at most 256 MiB of HBM per device.

```python
import math
import jax
import jax.numpy as jnp
from jax import lax

D = 2048
HEADS = 32
HEAD = 64
ROT = 32
FF = 8192
TOK_DEV = 128
SEQ = 2048
HALVES = 32


def raised(array, own_key, source, target, shards_of, factor):
    owner, partner = [(jnp.arange(array.shape[dim]) // (array.shape[dim] // shards_of)).reshape([-1 if axis == dim else 1 for axis in range(array.ndim)]) for dim in (source, target)]
    chosen = jax.random.permutation(own_key, shards_of)[partner]
    strong = (owner == chosen) | (owner == (partner + shards_of // 2) % shards_of)
    return jnp.where(strong, factor * array, array)


def level_of(rng, shape, shards, low, largest):
    loudness, own = 1.0, jax.random.fold_in(rng, 6)
    for axis_at, shards_of in shards:
        steps = jnp.exp(jax.random.uniform(jax.random.fold_in(own, axis_at), (shards_of,), jnp.float32, low / len(shards), largest / len(shards)))
        loudness = loudness * jnp.repeat(steps, shape[axis_at] // shards_of).reshape([-1 if axis == axis_at else 1 for axis in range(len(shape))])
    return loudness


def bell_draw(own_key, extent, scale, bound, pieces=(), held_as=jnp.bfloat16):
    entries = scale * jax.random.normal(own_key, extent, jnp.float32)
    if pieces:
        entries = entries * level_of(own_key, extent, pieces, -0.22, 0.18)
    return jnp.clip(entries, -bound, bound).astype(held_as)


def bell_draw_with(stream_key, dims, deviation, limit, split, heavy, kind=jnp.bfloat16):
    values = deviation * jax.random.normal(stream_key, dims, jnp.float32)
    if split:
        values = values * level_of(stream_key, dims, split, -0.22, 0.18)
    return jnp.clip(raised(values, jax.random.fold_in(stream_key, 3), *heavy), -limit, limit).astype(kind)


def setup_inputs(seed: int = 0) -> dict:
    splits = jax.random.split(jax.random.key(seed), 13)
    tokens = bell_draw(splits[0], (SEQ, D), 1.0, 6.0, ((0, 16),))
    block_order = jax.random.permutation(splits[1], HALVES).astype(jnp.int32)
    ln_gain = jnp.clip(1.0 + 0.18 * jax.random.normal(splits[2], (D,), jnp.float32), 0.1, 1.9)
    ln_bias = bell_draw(splits[3], (D,), 0.3, 1.8, (), jnp.float32)
    qkv_weight = bell_draw(splits[4], (D, 3, D), D ** -0.5, 0.125, ((0, 16), (2, 2)))
    qkv_bias = bell_draw(splits[5], (3, D), 0.5, 3.0, ((1, 2),), jnp.float32)
    out_weight = bell_draw(splits[6], (D, D), (D // 16) ** -0.5, 0.5, ((0, 16), (1, 2)))
    fc1_weight = bell_draw(splits[7], (D, FF), D ** -0.5, 0.125, ((0, 16), (1, 2)))
    fc1_bias = bell_draw(splits[8], (FF,), 0.5, 3.0, ((0, 2),), jnp.float32)
    fc2_weight = bell_draw(splits[9], (D, FF), (FF // 2) ** -0.5, 0.09375, ((0, 16), (1, 2)))
    out_bias = bell_draw(splits[10], (D,), 0.5, 3.0, (), jnp.float32)
    cotangent = bell_draw_with(splits[11], (SEQ, D), 1.0, 6.0, ((0, 16),), (0, 1, 16, 2.0))
    return {"tokens": tokens, "block_order": block_order, "ln_gain": ln_gain, "ln_bias": ln_bias, "qkv_weight": qkv_weight, "qkv_bias": qkv_bias, "out_weight": out_weight, "fc1_weight": fc1_weight, "fc1_bias": fc1_bias, "fc2_weight": fc2_weight, "out_bias": out_bias, "cotangent": cotangent}


EPS = 1e-05
NEG = -1e+30
HIGH = lax.Precision.HIGHEST

@jax.custom_vjp
def low(v):
    return lax.optimization_barrier(v.astype(jnp.bfloat16)).astype(jnp.float32)

@jax.custom_vjp
def low_back(v):
    return v

def low_keep(v):
    return (low(v), None)

def low_pass(kept, grad):
    return (grad,)

def back_keep(v):
    return (v, None)

def back_low(kept, grad):
    return (low(grad),)
low.defvjp(low_keep, low_pass)
low_back.defvjp(back_keep, back_low)

def tables(positions, width):
    freqs = 10000.0 ** (-(jnp.arange(width // 2, dtype=jnp.float32) * 2.0) / width)
    angles = positions.astype(jnp.float32)[:, None] * freqs[None, :]
    angles = jnp.concatenate([angles, angles], axis=-1)
    return (jnp.cos(angles), jnp.sin(angles))

def rotate(value, cosine, sine):
    width = cosine.shape[-1]
    part = value[..., :width]
    turned = jnp.concatenate([-part[..., width // 2:], part[..., :width // 2]], axis=-1)
    moved = part * cosine[:, None, :] + turned * sine[:, None, :]
    return jnp.concatenate([moved, value[..., width:]], axis=-1)

def gelu_tanh(value):
    return jax.nn.gelu(value, approximate=True)

def attend(queries, keys, values, positions):
    count = queries.shape[0]
    block = math.gcd(256, count)
    scale = 1.0 / math.sqrt(HEAD)
    query_blocks = queries.reshape(count // block, block, HEADS, HEAD)
    place_blocks = positions.reshape(count // block, block)

    def one_block(pair):
        query_part, place_part = pair
        scores = jnp.einsum('qhe,khe->hqk', query_part, keys, precision=HIGH) * scale
        scores = low_back(scores)
        visible = (place_part[:, None] >= positions[None, :])[None]
        scores = jnp.where(visible, scores, NEG)
        top = lax.optimization_barrier(jnp.max(scores, axis=-1, keepdims=True))
        expo = jnp.where(visible, jnp.exp(scores - top), 0.0)
        total = lax.optimization_barrier(jnp.sum(expo, axis=-1))
        summed = jnp.einsum('hqk,khe->qhe', low(expo), values, precision=HIGH)
        return summed / jnp.transpose(total)[..., None]
    result = lax.map(jax.checkpoint(one_block), (query_blocks, place_blocks))
    return result.reshape(count, HEADS, HEAD)

def reference(tokens, block_order, ln_gain, ln_bias, qkv_weight, qkv_bias, out_weight, fc1_weight, fc1_bias, fc2_weight, out_bias, cotangent):
    half = TOK_DEV // 2
    positions = (block_order[:, None] * half + jnp.arange(half, dtype=jnp.int32)[None, :]).reshape(-1).astype(jnp.int32)
    cosine, sine = tables(positions, ROT)

    def layer(inputs, gain, shift, w_qkv, b_qkv, w_out, w_up, b_up, w_down, b_out):
        count = inputs.shape[0]
        center = inputs - lax.optimization_barrier(jnp.mean(inputs, axis=-1, keepdims=True))
        unit = center * lax.rsqrt(lax.optimization_barrier(jnp.mean(center * center, axis=-1, keepdims=True)) + EPS)
        normed = low(unit * gain + shift)
        mixed = jnp.einsum('td,dcf->tcf', normed, w_qkv, precision=HIGH) + b_qkv
        queries = low(rotate(low_back(mixed[:, 0].reshape(count, HEADS, HEAD)), cosine, sine))
        keys = low(rotate(low_back(mixed[:, 1].reshape(count, HEADS, HEAD)), cosine, sine))
        values = low(low_back(mixed[:, 2].reshape(count, HEADS, HEAD)))
        attended = attend(queries, keys, values, positions)
        attended = low(low_back(attended.reshape(count, D)))
        attn_part = jnp.einsum('tf,of->to', attended, w_out, precision=HIGH)
        upward = low_back(jnp.dot(normed, w_up, precision=HIGH) + b_up)
        activated = low(gelu_tanh(upward))
        mlp_part = jnp.einsum('tf,of->to', activated, w_down, precision=HIGH)
        return inputs + attn_part + mlp_part + b_out
    primals = (tokens.astype(jnp.float32), ln_gain.astype(jnp.float32), ln_bias.astype(jnp.float32), qkv_weight.astype(jnp.float32), qkv_bias.astype(jnp.float32), out_weight.astype(jnp.float32), fc1_weight.astype(jnp.float32), fc1_bias.astype(jnp.float32), fc2_weight.astype(jnp.float32), out_bias.astype(jnp.float32))
    output, pullback = jax.vjp(layer, *primals)
    grads = pullback(cotangent.astype(jnp.float32))
    return (output, grads[0], grads[1], grads[2], grads[3], grads[4], grads[5], grads[6], grads[7], grads[8], grads[9])
```

```python
import functools
import math

import jax
import jax.numpy as jnp
from jax import lax
from jax.experimental import pallas as pl
from jax.experimental.pallas import tpu as pltpu
from jax.sharding import PartitionSpec as P

HEAD = 64
ROT = 32
EPS = 1e-05
NEG = -1e30
BF = jnp.bfloat16
F32 = jnp.float32
NN = (((1,), (0,)), ((), ()))
NT = (((1,), (1,)), ((), ()))
TN = (((0,), (0,)), ((), ()))


def mm(left, right, dims=NN):
    return lax.dot_general(left, right, dims, preferred_element_type=F32)


def tables(positions, width):
    freqs = 10000.0 ** (-(jnp.arange(width // 2, dtype=F32) * 2.0) / width)
    angles = positions.astype(F32)[:, None] * freqs[None, :]
    return (jnp.cos(angles), jnp.sin(angles))


def turned(value, cosine, sine):
    half = cosine.shape[-1]
    first, second = value[..., :half], value[..., half : 2 * half]
    return jnp.concatenate(
        [first * cosine - second * sine, second * cosine + first * sine, value[..., 2 * half :]],
        axis=-1,
    )


def attention_kernel(
    block, order_ref, mixed_ref, gatt_ref, cos_ref, sin_ref, att_ref, gmix_ref,
    placed, gplaced, q_s, k_s, v_s, kt_s, vt_s, ga_s, gat_s, st, dk_s, dv_s, att_s, gm_s,
):
    count, width = gatt_ref.shape
    heads = width // HEAD
    halves = order_ref.shape[0]
    half = count // halves
    blocks = count // block
    scale = 1.0 / math.sqrt(HEAD)

    def place(at, carry):
        source = pl.ds(pl.multiple_of(at * half, half), half)
        target = pl.ds(pl.multiple_of(order_ref[at] * half, half), half)
        placed[target, :] = mixed_ref[source, :]
        gplaced[target, :] = gatt_ref[source, :].astype(F32)
        return carry

    lax.fori_loop(0, halves, place, 0)
    below = lax.broadcasted_iota(jnp.int32, (block, block), 0) <= lax.broadcasted_iota(
        jnp.int32, (block, block), 1
    )

    def rows_of(at):
        return pl.ds(pl.multiple_of(at * block, block), block)

    for head in range(heads):
        def column(kind, head=head):
            return pl.ds(kind * width + head * HEAD, HEAD)

        def prepare(at, carry):
            rows = rows_of(at)
            cosine, sine = cos_ref[rows, :], sin_ref[rows, :]
            query = turned(placed[rows, column(0)], cosine, sine).astype(BF)
            key = turned(placed[rows, column(1)], cosine, sine)
            value = placed[rows, column(2)]
            grad = gplaced[rows, pl.ds(head * HEAD, HEAD)]
            q_s[rows, :] = query * jnp.asarray(scale, BF)
            k_s[rows, :] = key.astype(BF)
            v_s[rows, :] = value.astype(BF)
            ga_s[rows, :] = grad.astype(BF)
            keyvalue = jnp.concatenate([key, value], axis=1).T
            kt_s[:, rows] = keyvalue[:HEAD].astype(BF)
            vt_s[:, rows] = keyvalue[HEAD:].astype(BF)
            gat_s[:, rows] = jnp.concatenate([grad, grad], axis=1).T[:HEAD]
            dk_s[rows, :] = jnp.zeros((block, HEAD), F32)
            dv_s[rows, :] = jnp.zeros((block, HEAD), F32)
            return carry

        lax.fori_loop(0, blocks, prepare, 0)

        def query_block(at, carry):
            rows = rows_of(at)
            query, grad = q_s[rows, :], ga_s[rows, :]

            def folded(value):
                return value.reshape(block // 8, 8, block)

            def scored(place, top):
                scores = mm(k_s[rows_of(place), :], query, NT)
                st[rows_of(place), :] = scores
                return jnp.maximum(top, jnp.max(folded(scores), axis=0))

            top = lax.fori_loop(0, at, scored, jnp.full((8, block), NEG, F32))
            scores = jnp.where(below, mm(k_s[rows, :], query, NT), NEG)
            st[rows, :] = scores
            top = jnp.maximum(top, jnp.max(folded(scores), axis=0))
            top = jnp.max(top, axis=0, keepdims=True)

            def weighed(place, state):
                total, summed = state
                expo = jnp.exp(st[rows_of(place), :] - top)
                st[rows_of(place), :] = expo
                total = total + jnp.sum(folded(expo), axis=0)
                return (total, summed + mm(vt_s[:, rows_of(place)], expo.astype(BF)))

            total, summed = lax.fori_loop(
                0, at + 1, weighed, (jnp.zeros((8, block), F32), jnp.zeros((HEAD, block), F32))
            )
            inverse = 1.0 / jnp.sum(total, axis=0, keepdims=True)
            attended = summed * inverse
            delta = jnp.sum(gat_s[:, rows] * attended, axis=0, keepdims=True)

            def back(place, query_grad):
                here = rows_of(place)
                prob = st[here, :] * inverse
                dprob = mm(v_s[here, :], grad, NT)
                dscore = (prob * (dprob - delta)).astype(BF)
                dk_s[here, :] += mm(dscore, query)
                dv_s[here, :] += mm(prob.astype(BF), grad)
                return query_grad + mm(kt_s[:, here], dscore)

            query_grad = lax.fori_loop(0, at + 1, back, jnp.zeros((HEAD, block), F32))
            both = jnp.concatenate([attended, query_grad], axis=0).T
            att_s[rows, pl.ds(head * HEAD, HEAD)] = both[:, :HEAD].astype(BF)
            gm_s[rows, column(0)] = turned(
                both[:, HEAD:] * scale, cos_ref[rows, :], -sin_ref[rows, :]
            ).astype(BF)
            return carry

        lax.fori_loop(0, blocks, query_block, 0)

        def finish(at, carry):
            rows = rows_of(at)
            gm_s[rows, column(1)] = turned(dk_s[rows, :], cos_ref[rows, :], -sin_ref[rows, :]).astype(BF)
            gm_s[rows, column(2)] = dv_s[rows, :].astype(BF)
            return carry

        lax.fori_loop(0, blocks, finish, 0)

    def unplace(at, carry):
        target = pl.ds(pl.multiple_of(at * half, half), half)
        source = pl.ds(pl.multiple_of(order_ref[at] * half, half), half)
        att_ref[target, :] = att_s[source, :]
        gmix_ref[target, :] = gm_s[source, :]
        return carry

    lax.fori_loop(0, halves, unplace, 0)


def attention_sorted(order, mixed, grad_att):
    count, width = grad_att.shape
    block = math.gcd(256, count)
    cosine, sine = tables(jnp.arange(count, dtype=jnp.int32), ROT)
    vmem = pl.BlockSpec(memory_space=pltpu.VMEM)
    pairs = count * count // 2 * (width // HEAD)
    return pl.pallas_call(
        functools.partial(attention_kernel, block),
        out_shape=(
            jax.ShapeDtypeStruct((count, width), BF),
            jax.ShapeDtypeStruct((count, 3 * width), BF),
        ),
        in_specs=[pl.BlockSpec(memory_space=pltpu.SMEM)] + [vmem] * 4,
        out_specs=(vmem, vmem),
        scratch_shapes=[
            pltpu.VMEM((count, 3 * width), F32),
            pltpu.VMEM((count, width), F32),
            pltpu.VMEM((count, HEAD), BF),
            pltpu.VMEM((count, HEAD), BF),
            pltpu.VMEM((count, HEAD), BF),
            pltpu.VMEM((HEAD, count), BF),
            pltpu.VMEM((HEAD, count), BF),
            pltpu.VMEM((count, HEAD), BF),
            pltpu.VMEM((HEAD, count), F32),
            pltpu.VMEM((count, block), F32),
            pltpu.VMEM((count, HEAD), F32),
            pltpu.VMEM((count, HEAD), F32),
            pltpu.VMEM((count, width), BF),
            pltpu.VMEM((count, 3 * width), BF),
        ],
        compiler_params=pltpu.CompilerParams(vmem_limit_bytes=40 * 1024 * 1024),
        cost_estimate=pl.CostEstimate(
            flops=12 * pairs * HEAD, bytes_accessed=count * width * 30, transcendentals=pairs
        ),
    )(order, mixed, grad_att, cosine, sine)


def attention_blocks(own_place, places, mixed, grad_att, gather, scatter):
    count, width = grad_att.shape
    heads = width // HEAD
    scale = 1.0 / math.sqrt(HEAD)
    cosine, sine = tables(own_place, ROT)
    cosine, sine = cosine[:, None, :], sine[:, None, :]
    kinds = [mixed[:, kind * width : (kind + 1) * width].reshape(count, heads, HEAD) for kind in range(3)]
    queries = turned(kinds[0], cosine, sine).astype(BF)
    keys = gather(turned(kinds[1], cosine, sine).astype(BF))
    values = gather(kinds[2].astype(BF))
    grad_att = grad_att.reshape(count, heads, HEAD)
    block = math.gcd(128, count)

    def one(at, carry):
        key_grad, value_grad, attended, query_grad = carry
        query = lax.dynamic_slice_in_dim(queries, at * block, block)
        grad = lax.dynamic_slice_in_dim(grad_att, at * block, block)
        place = lax.dynamic_slice_in_dim(own_place, at * block, block)
        visible = (place[:, None] >= places[None, :])[None]
        scores = jnp.einsum("qhe,khe->hqk", query, keys, preferred_element_type=F32) * scale
        scores = jnp.where(visible, scores, NEG)
        top = jnp.max(scores, axis=-1, keepdims=True)
        expo = jnp.where(visible, jnp.exp(scores - top), 0.0)
        total = jnp.sum(expo, axis=-1)
        summed = jnp.einsum("hqk,khe->qhe", expo.astype(BF), values, preferred_element_type=F32)
        attend = summed / jnp.transpose(total)[..., None]
        delta = jnp.transpose(jnp.sum(grad.astype(F32) * attend, axis=-1))
        prob = expo / total[..., None]
        dprob = jnp.einsum("qhe,khe->hqk", grad, values, preferred_element_type=F32)
        dscore = (prob * (dprob - delta[..., None])).astype(BF)
        part_q = jnp.einsum("hqk,khe->qhe", dscore, keys, preferred_element_type=F32) * scale
        key_grad += jnp.einsum("hqk,qhe->khe", dscore, query, preferred_element_type=F32) * scale
        value_grad += jnp.einsum("hqk,qhe->khe", prob.astype(BF), grad, preferred_element_type=F32)
        attended = lax.dynamic_update_slice_in_dim(attended, attend.astype(BF), at * block, 0)
        query_grad = lax.dynamic_update_slice_in_dim(query_grad, part_q, at * block, 0)
        return (key_grad, value_grad, attended, query_grad)

    zeros = jnp.zeros(keys.shape, F32)
    own = jnp.zeros((count, heads, HEAD), F32)
    key_grad, value_grad, attended, query_grad = lax.fori_loop(
        0, count // block, one, (zeros, zeros, own.astype(BF), own)
    )
    key_grad, value_grad = scatter(key_grad), scatter(value_grad)
    grad_mixed = jnp.concatenate(
        [
            turned(query_grad, cosine, -sine).astype(BF).reshape(count, width),
            turned(key_grad, cosine, -sine).astype(BF).reshape(count, width),
            value_grad.astype(BF).reshape(count, width),
        ],
        axis=1,
    )
    return attended.reshape(count, width), grad_mixed


def gelu_tanh(value):
    return jax.nn.gelu(value, approximate=True)


def local(
    tokens, block_order, ln_gain, ln_bias, qkv_weight, qkv_bias, out_weight, fc1_weight, fc1_bias,
    fc2_weight, out_bias, cotangent,
):
    devices = lax.axis_size("ctx")
    myself = lax.axis_index("ctx")
    rows_here, features = tokens.shape
    weight_rows = qkv_weight.shape[0]
    half = devices * rows_here // block_order.shape[0]
    heads_here = qkv_weight.shape[2] // HEAD
    columns = math.gcd(devices, heads_here)
    groups = devices // columns
    mine = myself % columns
    width = qkv_weight.shape[2] // columns
    hidden = fc1_weight.shape[1] // columns
    count = columns * rows_here
    side = [[r * columns + c for c in range(columns)] for r in range(groups)]
    across = [[r * columns + c for r in range(groups)] for c in range(columns)]

    def group_gather(value):
        return lax.all_gather(value, "ctx", axis=0, tiled=True, axis_index_groups=side)

    def group_scatter(value):
        return lax.psum_scatter(
            value, "ctx", scatter_dimension=0, tiled=True, axis_index_groups=side
        )

    packed = jnp.concatenate(
        [
            qkv_weight.reshape(weight_rows, 3, columns, width).transpose(2, 0, 1, 3).reshape(
                columns, weight_rows, 3 * width
            ),
            fc1_weight.reshape(weight_rows, columns, hidden).transpose(1, 0, 2),
            out_weight.reshape(weight_rows, columns, width).transpose(1, 0, 2),
            fc2_weight.reshape(weight_rows, columns, hidden).transpose(1, 0, 2),
        ],
        axis=2,
    )
    if groups > 1:
        packed = jnp.tile(packed, (groups, 1, 1))
    packed = lax.all_to_all(packed, "ctx", split_axis=0, concat_axis=0, tiled=True)
    packed = packed.reshape(devices * weight_rows, packed.shape[2])
    inner_width = 3 * width + hidden
    w_in, w_out = packed[:, :inner_width], packed[:, inner_width:]
    bias_in = jnp.concatenate(
        [
            lax.dynamic_slice_in_dim(qkv_bias, mine * width, width, 1).reshape(-1),
            lax.dynamic_slice_in_dim(fc1_bias, mine * hidden, hidden, 0),
        ]
    )

    x_all = group_gather(tokens)
    g_all = group_gather(cotangent)
    inputs = x_all.astype(F32)
    center = inputs - jnp.mean(inputs, axis=-1, keepdims=True)
    inv_std = lax.rsqrt(jnp.mean(center * center, axis=-1, keepdims=True) + EPS)
    unit = center * inv_std
    normed = (unit * ln_gain + ln_bias).astype(BF)

    mixed = mm(normed, w_in[:, : 3 * width]) + bias_in[: 3 * width]
    upward = mm(normed, w_in[:, 3 * width :]) + bias_in[3 * width :]
    activated, gelu_back = jax.vjp(gelu_tanh, upward)
    activated = activated.astype(BF)
    grad_att = mm(g_all, w_out[:, :width]).astype(BF)
    grad_up = gelu_back(mm(g_all, w_out[:, width:]))[0].astype(BF)
    if groups == 1:
        attended, grad_mixed = attention_sorted(block_order, mixed, grad_att)
    else:
        places = (block_order[:, None] * half + jnp.arange(half, dtype=jnp.int32)[None, :]).reshape(-1)
        attended, grad_mixed = attention_blocks(
            lax.dynamic_slice_in_dim(places, (myself // columns) * count, count),
            places,
            mixed,
            grad_att,
            lambda value: lax.all_gather(
                value, "ctx", axis=0, tiled=True, axis_index_groups=across
            ),
            lambda value: lax.psum_scatter(
                value, "ctx", scatter_dimension=0, tiled=True, axis_index_groups=across
            ),
        )
    hiddens = jnp.concatenate([attended, activated], axis=1)
    grads = jnp.concatenate([grad_mixed, grad_up], axis=1)

    branches = group_scatter(mm(hiddens, w_out, NT).astype(BF))
    normed_part = mm(grads, w_in, NT)
    branches, own_normed = lax.psum(
        (branches, group_scatter(normed_part.astype(BF))), "tp"
    )
    outer = mm(g_all, hiddens, TN).astype(BF)
    inner = mm(normed, grads, TN).astype(BF)
    back = jnp.concatenate([inner, outer], axis=1).reshape(devices, weight_rows, -1)
    back = lax.all_to_all(back, "ctx", split_axis=0, concat_axis=0, tiled=True)
    back = back.reshape(groups, columns, weight_rows, -1)
    back = back[0].astype(F32) if groups == 1 else jnp.sum(back.astype(F32), axis=0)

    def spread(piece, kinds):
        piece = piece.reshape(columns, weight_rows, kinds, -1).transpose(1, 2, 0, 3)
        return piece.reshape(weight_rows, kinds, -1)

    qkv_grad = spread(back[:, :, : 3 * width], 3)
    fc1_grad = spread(back[:, :, 3 * width : inner_width], 1)[:, 0]
    out_grad = spread(back[:, :, inner_width : inner_width + width], 1)[:, 0]
    fc2_grad = spread(back[:, :, inner_width + width :], 1)[:, 0]

    column_sums = jnp.sum(grads.astype(F32), axis=0)
    qkv_sums = lax.dynamic_update_slice(
        jnp.zeros(qkv_bias.shape, F32), column_sums[: 3 * width].reshape(3, width), (0, mine * width)
    )
    fc1_sums = lax.dynamic_update_slice(
        jnp.zeros(fc1_bias.shape, F32), column_sums[3 * width :], (mine * hidden,)
    )
    g_sum = jnp.sum(g_all.astype(F32), axis=0) / columns
    qkv_sums, fc1_sums, g_sum = lax.psum((qkv_sums, fc1_sums, g_sum), "ctx")
    gain_sum, shift_sum = lax.psum(
        (jnp.sum(unit * normed_part, axis=0), jnp.sum(normed_part, axis=0)), ("ctx", "tp")
    )

    own = tokens.astype(F32)
    center = own - jnp.mean(own, axis=-1, keepdims=True)
    inv_std = lax.rsqrt(jnp.mean(center * center, axis=-1, keepdims=True) + EPS)
    unit = center * inv_std
    output = own + branches.astype(F32) + out_bias
    grad_unit = own_normed.astype(F32) * ln_gain
    input_grad = cotangent.astype(F32) + inv_std * (
        grad_unit
        - jnp.mean(grad_unit, axis=-1, keepdims=True)
        - unit * jnp.mean(grad_unit * unit, axis=-1, keepdims=True)
    )
    return (
        output, input_grad, gain_sum, shift_sum, qkv_grad, qkv_sums, out_grad, fc1_grad, fc1_sums,
        fc2_grad, g_sum,
    )


def solution(mesh):
    rows, tall = P("ctx", None), P("ctx", "tp")
    kinds, bias = P("ctx", None, "tp"), P(None, "tp")
    return jax.shard_map(
        local,
        mesh=mesh,
        in_specs=(rows, P(), P(), P(), kinds, bias, tall, tall, P("tp"), tall, P(), rows),
        out_specs=(rows, rows, P(), P(), kinds, bias, tall, tall, P("tp"), tall, P()),
        check_vma=False,
    )
```

```python
import functools
import math

import jax
import jax.numpy as jnp
from jax import lax
from jax.experimental import pallas as pl
from jax.experimental.pallas import tpu as pltpu
from jax.sharding import PartitionSpec as P

HEAD = 64
ROT = 32
EPS = 1e-05
NEG = -1e30
BF = jnp.bfloat16
F32 = jnp.float32
NN = (((1,), (0,)), ((), ()))
NT = (((1,), (1,)), ((), ()))
TN = (((0,), (0,)), ((), ()))


def mm(left, right, dims=NN):
    return lax.dot_general(left, right, dims, preferred_element_type=F32)


def tables(positions, width):
    freqs = 10000.0 ** (-(jnp.arange(width // 2, dtype=F32) * 2.0) / width)
    angles = positions.astype(F32)[:, None] * freqs[None, :]
    return (jnp.cos(angles), jnp.sin(angles))


def turned(value, cosine, sine):
    half = cosine.shape[-1]
    first, second = value[..., :half], value[..., half : 2 * half]
    return jnp.concatenate(
        [first * cosine - second * sine, second * cosine + first * sine, value[..., 2 * half :]],
        axis=-1,
    )


def attention_kernel(
    block, order_ref, mixed_ref, gatt_ref, cos_ref, sin_ref, att_ref, gmix_ref,
    placed, gplaced, q_s, k_s, v_s, kt_s, vt_s, ga_s, gat_s, st, dk_s, dv_s, att_s, gm_s,
):
    count = gatt_ref.shape[0]
    width = gatt_ref.shape[1] // 4
    heads = width // HEAD
    halves = order_ref.shape[0]
    half = count // halves
    blocks = count // block
    scale = 1.0 / math.sqrt(HEAD)

    def place(at, carry):
        source = pl.ds(pl.multiple_of(at * half, half), half)
        target = pl.ds(pl.multiple_of(order_ref[at] * half, half), half)
        placed[target, :] = mixed_ref[source, :]
        gplaced[target, :] = gatt_ref[source, pl.ds(3 * width, width)]
        return carry

    lax.fori_loop(0, halves, place, 0)
    below = lax.broadcasted_iota(jnp.int32, (block, block), 0) <= lax.broadcasted_iota(
        jnp.int32, (block, block), 1
    )

    def rows_of(at):
        return pl.ds(pl.multiple_of(at * block, block), block)

    for head in range(heads):
        def column(kind, head=head):
            return pl.ds(kind * width + head * HEAD, HEAD)

        def prepare(at, carry):
            rows = rows_of(at)
            cosine, sine = cos_ref[rows, :], sin_ref[rows, :]
            query = turned(placed[rows, column(0)], cosine, sine).astype(BF)
            key = turned(placed[rows, column(1)], cosine, sine)
            value = placed[rows, column(2)]
            grad = gplaced[rows, pl.ds(head * HEAD, HEAD)].astype(BF).astype(F32)
            q_s[rows, :] = query * jnp.asarray(scale, BF)
            k_s[rows, :] = key.astype(BF)
            v_s[rows, :] = value.astype(BF)
            ga_s[rows, :] = grad.astype(BF)
            keyvalue = jnp.concatenate([key, value], axis=1).T
            kt_s[:, rows] = keyvalue[:HEAD].astype(BF)
            vt_s[:, rows] = keyvalue[HEAD:].astype(BF)
            gat_s[:, rows] = jnp.concatenate([grad, grad], axis=1).T[:HEAD]
            dk_s[rows, :] = jnp.zeros((block, HEAD), F32)
            dv_s[rows, :] = jnp.zeros((block, HEAD), F32)
            return carry

        lax.fori_loop(0, blocks, prepare, 0)

        def query_block(at, carry):
            rows = rows_of(at)
            query, grad = q_s[rows, :], ga_s[rows, :]

            def folded(value):
                return value.reshape(block // 8, 8, block)

            def scored(place, top):
                scores = mm(k_s[rows_of(place), :], query, NT)
                st[rows_of(place), :] = scores
                return jnp.maximum(top, jnp.max(folded(scores), axis=0))

            top = lax.fori_loop(0, at, scored, jnp.full((8, block), NEG, F32))
            scores = jnp.where(below, mm(k_s[rows, :], query, NT), NEG)
            st[rows, :] = scores
            top = jnp.maximum(top, jnp.max(folded(scores), axis=0))
            top = jnp.max(top, axis=0, keepdims=True)

            def weighed(place, state):
                total, summed = state
                expo = jnp.exp(st[rows_of(place), :] - top)
                st[rows_of(place), :] = expo
                total = total + jnp.sum(folded(expo), axis=0)
                return (total, summed + mm(vt_s[:, rows_of(place)], expo.astype(BF)))

            total, summed = lax.fori_loop(
                0, at + 1, weighed, (jnp.zeros((8, block), F32), jnp.zeros((HEAD, block), F32))
            )
            inverse = 1.0 / jnp.sum(total, axis=0, keepdims=True)
            attended = summed * inverse
            delta = jnp.sum(gat_s[:, rows] * attended, axis=0, keepdims=True)

            def back(place, query_grad):
                here = rows_of(place)
                prob = st[here, :] * inverse
                dprob = mm(v_s[here, :], grad, NT)
                dscore = (prob * (dprob - delta)).astype(BF)
                dk_s[here, :] += mm(dscore, query)
                dv_s[here, :] += mm(prob.astype(BF), grad)
                return query_grad + mm(kt_s[:, here], dscore)

            query_grad = lax.fori_loop(0, at + 1, back, jnp.zeros((HEAD, block), F32))
            both = jnp.concatenate([attended, query_grad], axis=0).T
            att_s[rows, pl.ds(head * HEAD, HEAD)] = both[:, :HEAD].astype(BF)
            gm_s[rows, column(0)] = turned(
                both[:, HEAD:] * scale, cos_ref[rows, :], -sin_ref[rows, :]
            ).astype(BF)
            return carry

        lax.fori_loop(0, blocks, query_block, 0)

        def finish(at, carry):
            rows = rows_of(at)
            gm_s[rows, column(1)] = turned(dk_s[rows, :], cos_ref[rows, :], -sin_ref[rows, :]).astype(BF)
            gm_s[rows, column(2)] = dv_s[rows, :].astype(BF)
            return carry

        lax.fori_loop(0, blocks, finish, 0)

    def unplace(at, carry):
        target = pl.ds(pl.multiple_of(at * half, half), half)
        source = pl.ds(pl.multiple_of(order_ref[at] * half, half), half)
        attended, grads = att_s[source, :], gm_s[source, :]
        att_ref[target, :] = jnp.concatenate([jnp.zeros_like(grads), attended], axis=1)
        gmix_ref[target, :] = jnp.concatenate([grads, jnp.zeros_like(attended)], axis=1)
        return carry

    lax.fori_loop(0, halves, unplace, 0)


def attention_sorted(order, mixed, grad_att):
    count, width = grad_att.shape[0], grad_att.shape[1] // 4
    block = math.gcd(256, count)
    cosine, sine = tables(jnp.arange(count, dtype=jnp.int32), ROT)
    vmem = pl.BlockSpec(memory_space=pltpu.VMEM)
    pairs = count * count // 2 * (width // HEAD)
    return pl.pallas_call(
        functools.partial(attention_kernel, block),
        out_shape=(
            jax.ShapeDtypeStruct((count, 4 * width), BF),
            jax.ShapeDtypeStruct((count, 4 * width), BF),
        ),
        in_specs=[pl.BlockSpec(memory_space=pltpu.SMEM)] + [vmem] * 4,
        out_specs=(vmem, vmem),
        scratch_shapes=[
            pltpu.VMEM((count, 4 * width), F32),
            pltpu.VMEM((count, width), F32),
            pltpu.VMEM((count, HEAD), BF),
            pltpu.VMEM((count, HEAD), BF),
            pltpu.VMEM((count, HEAD), BF),
            pltpu.VMEM((HEAD, count), BF),
            pltpu.VMEM((HEAD, count), BF),
            pltpu.VMEM((count, HEAD), BF),
            pltpu.VMEM((HEAD, count), F32),
            pltpu.VMEM((count, block), F32),
            pltpu.VMEM((count, HEAD), F32),
            pltpu.VMEM((count, HEAD), F32),
            pltpu.VMEM((count, width), BF),
            pltpu.VMEM((count, 3 * width), BF),
        ],
        compiler_params=pltpu.CompilerParams(vmem_limit_bytes=40 * 1024 * 1024),
        cost_estimate=pl.CostEstimate(
            flops=12 * pairs * HEAD, bytes_accessed=count * width * 30, transcendentals=pairs
        ),
    )(order, mixed, grad_att, cosine, sine)


def attention_blocks(own_place, places, mixed, grad_att, gather, scatter):
    count, width = grad_att.shape[0], grad_att.shape[1] // 4
    heads = width // HEAD
    scale = 1.0 / math.sqrt(HEAD)
    grad_att = grad_att[:, 3 * width :].astype(BF)
    cosine, sine = tables(own_place, ROT)
    cosine, sine = cosine[:, None, :], sine[:, None, :]
    kinds = [mixed[:, kind * width : (kind + 1) * width].reshape(count, heads, HEAD) for kind in range(3)]
    queries = turned(kinds[0], cosine, sine).astype(BF)
    keys = gather(turned(kinds[1], cosine, sine).astype(BF))
    values = gather(kinds[2].astype(BF))
    grad_att = grad_att.reshape(count, heads, HEAD)
    block = math.gcd(128, count)

    def one(at, carry):
        key_grad, value_grad, attended, query_grad = carry
        query = lax.dynamic_slice_in_dim(queries, at * block, block)
        grad = lax.dynamic_slice_in_dim(grad_att, at * block, block)
        place = lax.dynamic_slice_in_dim(own_place, at * block, block)
        visible = (place[:, None] >= places[None, :])[None]
        scores = jnp.einsum("qhe,khe->hqk", query, keys, preferred_element_type=F32) * scale
        scores = jnp.where(visible, scores, NEG)
        top = jnp.max(scores, axis=-1, keepdims=True)
        expo = jnp.where(visible, jnp.exp(scores - top), 0.0)
        total = jnp.sum(expo, axis=-1)
        summed = jnp.einsum("hqk,khe->qhe", expo.astype(BF), values, preferred_element_type=F32)
        attend = summed / jnp.transpose(total)[..., None]
        delta = jnp.transpose(jnp.sum(grad.astype(F32) * attend, axis=-1))
        prob = expo / total[..., None]
        dprob = jnp.einsum("qhe,khe->hqk", grad, values, preferred_element_type=F32)
        dscore = (prob * (dprob - delta[..., None])).astype(BF)
        part_q = jnp.einsum("hqk,khe->qhe", dscore, keys, preferred_element_type=F32) * scale
        key_grad += jnp.einsum("hqk,qhe->khe", dscore, query, preferred_element_type=F32) * scale
        value_grad += jnp.einsum("hqk,qhe->khe", prob.astype(BF), grad, preferred_element_type=F32)
        attended = lax.dynamic_update_slice_in_dim(attended, attend.astype(BF), at * block, 0)
        query_grad = lax.dynamic_update_slice_in_dim(query_grad, part_q, at * block, 0)
        return (key_grad, value_grad, attended, query_grad)

    zeros = jnp.zeros(keys.shape, F32)
    own = jnp.zeros((count, heads, HEAD), F32)
    key_grad, value_grad, attended, query_grad = lax.fori_loop(
        0, count // block, one, (zeros, zeros, own.astype(BF), own)
    )
    key_grad, value_grad = scatter(key_grad), scatter(value_grad)
    grad_mixed = jnp.concatenate(
        [
            turned(query_grad, cosine, -sine).astype(BF).reshape(count, width),
            turned(key_grad, cosine, -sine).astype(BF).reshape(count, width),
            value_grad.astype(BF).reshape(count, width),
            jnp.zeros((count, width), BF),
        ],
        axis=1,
    )
    attended = jnp.concatenate(
        [jnp.zeros((count, 3 * width), BF), attended.reshape(count, width)], axis=1
    )
    return attended, grad_mixed


MESH = pl.DeviceIdType.MESH
UP, DOWN, ACROSS, OTHER, CORE = range(5)


class Place:
    def __init__(self, line):
        self.line = line
        self.me = lax.axis_index("ctx")
        self.y = lax.axis_index("tp")
        self.a, self.b, self.c = self.me // 4, (self.me // 2) % 2, self.me % 2
        a, b, c, y = self.a, self.b, self.c, self.y
        self.device = {
            UP: (self.index(jnp.minimum(a + 1, line - 1), b, c), y),
            DOWN: (self.index(jnp.maximum(a - 1, 0), b, c), y),
            ACROSS: (self.index(a, 1 - b, c), y),
            OTHER: (self.me, 1 - y),
            CORE: (self.index(a, b, 1 - c), y),
        }

    def index(self, a, b, c):
        return a * 4 + b * 2 + c

    def far_first(self, turn):
        line = self.line
        high, low = line - 1 - turn, turn
        high = jnp.where(high <= self.a, high - 1, high)
        low = jnp.where(low >= self.a, low + 1, low)
        return jnp.where(self.a < line // 2, high, low)

    def greet(self):
        barrier = pltpu.get_barrier_semaphore()
        count = 4 * self.line

        def signal(step, carry):
            pl.semaphore_signal(
                barrier, inc=1, device_id=(lax.rem(self.me + step, count), self.y), device_id_type=MESH
            )
            return carry

        lax.fori_loop(1, count, signal, 0)
        pl.semaphore_signal(barrier, inc=1, device_id=self.device[OTHER], device_id_type=MESH)
        pl.semaphore_wait(barrier, count)


def remote(source, target, send, receive, device):
    return pltpu.make_async_remote_copy(
        src_ref=source, dst_ref=target, send_sem=send, recv_sem=receive, device_id=device,
        device_id_type=MESH,
    )


def exchange(place, chunks, pieces, received, send, receive, local_sem):
    count = 4 * place.line

    def copy(step, n, came):
        to = lax.rem(place.me + step, count)
        owner = lax.rem(place.me + count - step, count) if came else place.me
        return remote(
            chunks(n, to), received(n, owner), send.at[n, step], receive.at[n, step], (to, place.y)
        )

    def start():
        for n in range(pieces):
            pltpu.make_async_copy(
                chunks(n, place.me), received(n, place.me), local_sem.at[n]
            ).start()

        def one(step, carry):
            for n in range(pieces):
                copy(step, n, False).start()
            return carry

        lax.fori_loop(1, count, one, 0)

    def wait():
        def one(step, carry):
            for n in range(pieces):
                copy(step, n, True).wait()
            return carry

        lax.fori_loop(1, count, one, 0)
        for n in range(pieces):
            pltpu.make_async_copy(
                chunks(n, place.me), received(n, place.me), local_sem.at[n]
            ).wait()

    return start, wait


def collect_kernel(
    line, width, tok_ref, cot_ref, qkv_ref, out_ref, up_ref, down_ref,
    x_ref, g_ref, watt_ref, wup_ref, wdown_ref,
    packed, send, receive, own_sem, wsend, wreceive, wlocal,
):
    place = Place(line)
    a, b, c, y = place.a, place.b, place.c, place.y
    sources, targets = (tok_ref, cot_ref), (x_ref, g_ref)
    rows = tok_ref.shape[0]
    half = rows // 2
    weight_rows = up_ref.shape[0]
    hidden = wup_ref.shape[1]
    place.greet()

    def copy(t, kind, block, part, own=False):
        target = targets[t].at[pl.ds(pl.multiple_of(block * rows + part * half, half), half)]
        source = sources[t].at[pl.ds(pl.multiple_of(part * half, half), half)] if own else target
        return remote(
            source, target, send.at[t, kind, block, part], receive.at[t, block, part], place.device[kind]
        )

    def landed(t, block, part):
        copy(t, CORE, block, part).wait_recv()

    def along(t, distance):
        for sign in (0,) if distance == 0 else (1, -1):
            at = a + sign * distance

            def pass_on(sign=sign, at=at):
                block = place.index(at, b, c)
                own = distance == 0
                if not own:
                    landed(t, block, y)
                if sign <= 0:
                    pl.when(a < line - 1)(lambda: copy(t, UP, block, y, own).start())
                if sign >= 0:
                    pl.when(a > 0)(lambda: copy(t, DOWN, block, y, own).start())
                copy(t, ACROSS, block, y, own).start()
                if not own:
                    copy(t, OTHER, block, y).start()
                copy(t, CORE, block, y, own).start()
                if own:
                    copy(t, CORE, block, 1 - y, own).start()

            if distance == 0:
                pass_on()
            else:
                pl.when((at >= 0) & (at < line))(pass_on)

    def beside(t, distance):
        for sign in (0,) if distance == 0 else (1, -1):
            at = a + sign * distance

            def pass_on(at=at):
                block = place.index(at, 1 - b, c)
                landed(t, block, y)
                copy(t, OTHER, block, y).start()
                copy(t, CORE, block, y).start()

            pl.when((at >= 0) & (at < line))(pass_on)

    def from_other(t, distance):
        for column in (b, 1 - b):
            for sign in (0,) if distance == 0 else (1, -1):
                at = a + sign * distance

                def pass_on(at=at, column=column):
                    block = place.index(at, column, c)
                    landed(t, block, 1 - y)
                    copy(t, CORE, block, 1 - y).start()

                if distance == 0 and column is b:
                    continue
                pl.when((at >= 0) & (at < line))(pass_on)

    for t in range(2):
        pltpu.make_async_copy(
            sources[t], targets[t].at[pl.ds(pl.multiple_of(place.me * rows, rows), rows)], own_sem.at[t]
        ).start()
        along(t, 0)
    for owner in range(4 * line):
        columns = pl.ds(owner * width, width)
        packed[owner, :, :] = jnp.concatenate(
            [qkv_ref[:, kind, columns] for kind in range(3)] + [out_ref[:, columns]], axis=1
        )

    def chunk(n, to):
        if n == 0:
            return packed.at[to]
        return (up_ref, down_ref)[n - 1].at[:, pl.ds(pl.multiple_of(to * hidden, hidden), hidden)]

    def received(n, owner):
        here = pl.ds(pl.multiple_of(owner * weight_rows, weight_rows), weight_rows)
        return (watt_ref, wup_ref, wdown_ref)[n].at[here]

    start, wait = exchange(place, chunk, 3, received, wsend, wreceive, wlocal)
    for t in range(2):
        for distance in range(1, line):
            along(t, distance)
            beside(t, distance - 1)
        beside(t, line - 1)
    start()
    for t in range(2):
        for distance in range(line):
            from_other(t, distance)
    for t in range(2):

        def came(chip, carry, t=t):
            for part in range(2):
                landed(t, chip * 2 + (1 - c), part)
            return carry

        lax.fori_loop(0, 2 * line, came, 0)

        def left(at, carry, t=t):
            block, beyond = place.index(at, b, c), place.index(at, 1 - b, c)
            pl.when((at <= a) & (a < line - 1))(lambda: copy(t, UP, block, y).wait_send())
            pl.when((at >= a) & (a > 0))(lambda: copy(t, DOWN, block, y).wait_send())
            copy(t, ACROSS, block, y).wait_send()
            pl.when(at != a)(lambda: copy(t, OTHER, block, y).wait_send())
            copy(t, OTHER, beyond, y).wait_send()
            for part in range(2):
                copy(t, CORE, block, part).wait_send()
                copy(t, CORE, beyond, part).wait_send()
            return carry

        lax.fori_loop(0, line, left, 0)
        pltpu.make_async_copy(
            sources[t], targets[t].at[pl.ds(pl.multiple_of(place.me * rows, rows), rows)], own_sem.at[t]
        ).wait()
    wait()


def collect(tokens, cotangent, qkv_weight, out_weight, fc1_weight, fc2_weight):
    rows, features = tokens.shape
    weight_rows = fc1_weight.shape[0]
    count = lax.axis_size("ctx")
    line, width, hidden = count // 4, qkv_weight.shape[2] // count, fc1_weight.shape[1] // count
    hbm, vmem = pl.BlockSpec(memory_space=pl.ANY), pl.BlockSpec(memory_space=pltpu.VMEM)
    dma = pltpu.SemaphoreType.DMA
    return pl.pallas_call(
        functools.partial(collect_kernel, line, width),
        out_shape=[
            jax.ShapeDtypeStruct((count * rows, features), BF),
            jax.ShapeDtypeStruct((count * rows, features), BF),
            jax.ShapeDtypeStruct((count * weight_rows, 4 * width), BF),
            jax.ShapeDtypeStruct((count * weight_rows, hidden), BF),
            jax.ShapeDtypeStruct((count * weight_rows, hidden), BF),
        ],
        in_specs=[hbm, hbm, vmem, vmem, hbm, hbm],
        out_specs=[hbm] * 5,
        scratch_shapes=[
            pltpu.VMEM((count, weight_rows, 4 * width), BF),
            dma((2, 5, count, 2)),
            dma((2, count, 2)),
            dma((2,)),
            dma((3, count)),
            dma((3, count)),
            dma((3,)),
        ],
        compiler_params=pltpu.CompilerParams(
            collective_id=1, has_side_effects=True, vmem_limit_bytes=40 * 1024 * 1024
        ),
    )(tokens, cotangent, qkv_weight, out_weight, fc1_weight, fc2_weight)


def spread_kernel(
    line, att_ref, act_ref, gmix_ref, gup_ref, watt_ref, wup_ref, wdown_ref, normed_ref, g_ref, x_ref,
    sum_ref, gsum_ref, ratt_ref, rup_ref, rdown_ref, rbias_ref, norms_ref, total_ref,
    own, from_core, from_other, from_across, from_line, done, turned_s, dsend, cols, xbuf,
    gain_s, shift_s, nsend, nfrom, nline, bias_s,
    cols_sem, x_sem, csend, creceive, ysend, yreceive, xsend, xreceive, zsend, zreceive, fsend,
    freceive, wsend, wreceive, wlocal, nsend_sem, nreceive, lsend, lreceive,
):
    place = Place(line)
    a, b, c, y = place.a, place.b, place.c, place.y
    sums = (sum_ref, gsum_ref)
    features = own.shape[3]
    rows = own.shape[2] // 2
    half = rows // 2
    chips = 2 * line
    tokens = att_ref.shape[0]
    block = 2 * rows
    weight_rows = dsend.shape[1] // (2 * chips)
    pair = 2 * weight_rows
    piece = 512
    place.greet()

    def at_rows(start, size):
        return pl.ds(pl.multiple_of(start, size), size)

    mine = at_rows(c * rows + y * half, half)
    theirs = at_rows(c * rows + (1 - y) * half, half)
    both = at_rows(c * rows, rows)
    sibling = at_rows((1 - c) * rows, rows)

    def chunk(n, to):
        if n == 3:
            return bias_s
        return dsend.at[n, at_rows(to * weight_rows, weight_rows)]

    def received(n, owner):
        return (ratt_ref, rup_ref, rdown_ref, rbias_ref)[n].at[owner]

    def weight_copy(step, n, came):
        to = lax.rem(place.me + step, 2 * chips)
        owner = lax.rem(place.me + 2 * chips - step, 2 * chips) if came else place.me
        return remote(
            chunk(n, to), received(n, owner), wsend.at[n, step], wreceive.at[n, step], (to, y)
        )

    def weight_own(n):
        return pltpu.make_async_copy(chunk(n, place.me), received(n, place.me), wlocal.at[n])

    def weight_start(pieces):
        for n in pieces:
            weight_own(n).start()

        def one(step, carry):
            for n in pieces:
                weight_copy(step, n, False).start()
            return carry

        lax.fori_loop(1, 2 * chips, one, 0)

    def weight_wait(pieces):
        def one(step, carry):
            for n in pieces:
                weight_copy(step, n, True).wait()
            return carry

        lax.fori_loop(1, 2 * chips, one, 0)
        for n in pieces:
            weight_own(n).wait()

    def to_core(t, chip):
        return remote(
            own.at[t, chip, sibling], from_core.at[t, chip], csend.at[t, chip], creceive.at[t, chip],
            place.device[CORE],
        )

    def to_other(t, chip):
        return remote(
            own.at[t, chip, theirs], from_other.at[t, chip], ysend.at[t, chip], yreceive.at[t, chip],
            place.device[OTHER],
        )

    def to_across(t, at):
        return remote(
            own.at[t, at * 2 + 1 - b, mine], from_across.at[t, at], xsend.at[t, at], xreceive.at[t, at],
            place.device[ACROSS],
        )

    def to_up(t, at):
        return remote(
            own.at[t, at * 2 + b, mine], from_line.at[t, at], zsend.at[t, at], zreceive.at[t, at],
            place.device[UP],
        )

    def to_down(t, at, last):
        slot = line if last else at
        return remote(
            own.at[t, at * 2 + b, mine], from_line.at[t, slot], zsend.at[t, at], zreceive.at[t, slot],
            place.device[DOWN],
        )

    def final(t, part):
        return remote(
            done.at[t, part], done.at[t, part], fsend.at[t], freceive.at[t], place.device[OTHER]
        )

    mine_done, theirs_done = at_rows(y * half, half), at_rows((1 - y) * half, half)

    def add(t, chip, part, other):
        own[t, chip, part, :] = (own[t, chip, part, :].astype(F32) + other.astype(F32)).astype(BF)

    def order(turn):
        step = lax.rem(turn, line)
        at = jnp.where(step == line - 1, a, place.far_first(step))
        return at, at * 2 + jnp.where(turn < line, 1 - b, b)

    def columns_in(source, n, chip, slot):
        return pltpu.make_async_copy(
            source.at[:, at_rows(chip * pair, pair)], cols.at[n, slot], cols_sem.at[n, slot]
        )

    def x_in(turn, slot):
        _, chip = order(turn)
        return pltpu.make_async_copy(
            x_ref.at[at_rows(chip * block, block)], xbuf.at[slot], x_sem.at[slot]
        )

    for n, source in enumerate((normed_ref, g_ref)):
        columns_in(source, n, 0, 0).start()
    x_in(0, 0).start()

    def product(t, turn):
        _, chip = order(turn)
        here = at_rows(chip * block, block)
        left = ((att_ref, act_ref), (gmix_ref, gup_ref))[t]
        right = ((watt_ref, wdown_ref), (watt_ref, wup_ref))[t]
        first, second = left[0][here, :], left[1][here, :]
        if t == 1:
            slot = lax.rem(turn, 2)
            x_in(turn, slot).wait()

            @pl.when(turn + 1 < chips)
            def _():
                x_in(turn + 1, 1 - slot).start()

            mean = jnp.zeros((block, 1), F32)
            for at in range(0, features, piece):
                mean += jnp.sum(xbuf[slot, :, at : at + piece].astype(F32), axis=1, keepdims=True)
            mean = mean / features
            spread = jnp.zeros((block, 1), F32)
            for at in range(0, features, piece):
                center = xbuf[slot, :, at : at + piece].astype(F32) - mean
                spread += jnp.sum(center * center, axis=1, keepdims=True)
            inv_std = lax.rsqrt(spread / features + EPS)
        for at in range(0, features, piece):
            part = pl.ds(at, piece)
            value = mm(first, right[0][part, :], NT) + mm(second, right[1][part, :], NT)
            own[t, chip, :, part] = value.astype(BF)
            if t == 1:
                unit = (xbuf[slot, :, at : at + piece].astype(F32) - mean) * inv_std
                shift_s[:, part] += jnp.sum(value.reshape(block // 8, 8, piece), axis=0)
                gain_s[:, part] += jnp.sum((unit * value).reshape(block // 8, 8, piece), axis=0)
        to_core(t, chip).start()

    def stage_core(t, turn):
        _, chip = order(turn)
        to_core(t, chip).wait_recv()
        add(t, chip, both, from_core[t, chip])
        to_other(t, chip).start()

    def stage_other(t, turn):
        at, chip = order(turn)
        to_other(t, chip).wait_recv()
        add(t, chip, mine, from_other[t, chip])
        to_across(t, at).start()

    def stage_line(t):
        def one(turn, carry):
            at, chip = order(line + turn)
            to_other(t, chip).wait_recv()
            to_across(t, at).wait_recv()
            total = from_other[t, chip].astype(F32) + from_across[t, at].astype(F32)
            add(t, chip, mine, total)

            def down():
                @pl.when(a < line - 1)
                def _():
                    to_down(t, at, False).wait_recv()
                    add(t, chip, mine, from_line[t, at])

                pl.when(at == a - 1)(lambda: to_down(t, at, True).start())
                pl.when(at < a - 1)(lambda: to_down(t, at, False).start())

            def up():
                @pl.when(a > 0)
                def _():
                    to_up(t, at).wait_recv()
                    add(t, chip, mine, from_line[t, at])

                to_up(t, at).start()

            pl.when(at < a)(down)
            pl.when(at > a)(up)
            return carry

        lax.fori_loop(0, line, one, 0)
        chip = a * 2 + b

        @pl.when(a < line - 1)
        def _():
            to_down(t, a, True).wait_recv()
            add(t, chip, mine, from_line[t, line])

        @pl.when(a > 0)
        def _():
            to_up(t, a).wait_recv()
            add(t, chip, mine, from_line[t, a])

        done[t, mine_done, :] = own[t, chip, mine, :]
        final(t, mine_done).start()

    def norm_copy(step):
        kind = (CORE, OTHER, ACROSS)[step]
        return remote(
            nsend.at[step], nfrom.at[step], nsend_sem.at[step], nreceive.at[step], place.device[kind]
        )

    def norm_line(other, came):
        device = (place.index(other, b, c), y)
        return remote(
            nsend.at[3], nline.at[other if came else a], lsend.at[other],
            lreceive.at[other if came else a], device,
        )

    product(0, 0)

    def first_sum(turn, carry):
        product(0, turn)
        stage_core(0, turn - 1)
        return carry

    lax.fori_loop(1, chips, first_sum, 0)
    stage_core(0, chips - 1)

    def turn_over(at, carry):
        here = at_rows(at * 256, 256)
        for n, source in enumerate((gmix_ref, gup_ref, att_ref, act_ref)):
            turned_s[n, :, here] = source[here, :].T
        return carry

    lax.fori_loop(0, tokens // 256, turn_over, 0)
    for n, source in enumerate((gmix_ref, gup_ref)):
        wide = source.shape[1]
        total = jnp.zeros((8, wide), F32)

        def tally(at, total, source=source, wide=wide):
            return total + jnp.sum(
                source[at_rows(at * 256, 256), :].astype(F32).reshape(32, 8, wide), axis=0
            )

        total = jnp.sum(lax.fori_loop(0, tokens // 256, tally, total), axis=0, keepdims=True)
        for at in range(wide // 128):
            bias_s[pl.ds(n * 2 + at, 1), :] = total[:, at * 128 : (at + 1) * 128]
    bias_s[pl.ds(4, 4), :] = jnp.zeros((4, 128), F32)
    ones = jnp.ones((8, tokens), BF)

    def gradients(chip, carry):
        slot = lax.rem(chip, 2)
        for n, source in enumerate((normed_ref, g_ref)):
            columns_in(source, n, chip, slot).wait()

            @pl.when(chip + 1 < chips)
            def _(n=n, source=source):
                columns_in(source, n, chip + 1, 1 - slot).start()

        here = at_rows(chip * pair, pair)
        by_normed, by_grad = cols[0, slot], cols[1, slot]
        dsend[0, here, :] = (mm(turned_s[0], by_normed) + mm(turned_s[2], by_grad)).T.astype(BF)
        dsend[1, here, :] = mm(turned_s[1], by_normed).T.astype(BF)
        dsend[2, here, :] = mm(turned_s[3], by_grad).T.astype(BF)
        total_ref[:, here] = mm(ones, by_grad)
        return carry

    lax.fori_loop(0, chips, gradients, 0)
    weight_start((0, 1, 2, 3))

    gain_s[...] = jnp.zeros_like(gain_s)
    shift_s[...] = jnp.zeros_like(shift_s)
    product(1, 0)

    def second_sum(turn, carry):
        product(1, turn)
        stage_core(1, turn - 1)
        pl.when(lax.rem(turn, 2) == 1)(lambda: stage_other(0, turn // 2))
        return carry

    lax.fori_loop(1, chips, second_sum, 0)
    stage_core(1, chips - 1)
    for n, source in enumerate((gain_s, shift_s)):
        total = jnp.sum(source[...], axis=0, keepdims=True)
        for at in range(4):
            wide = features // 4
            nsend[0, pl.ds(n * 4 + at, 1), :] = total[:, at * wide : (at + 1) * wide]
    norm_copy(0).start()
    stage_line(0)
    norm_copy(0).wait_recv()
    nsend[1] = nsend[0] + nfrom[0]
    norm_copy(1).start()

    def others(turn, carry):
        stage_other(1, turn)
        return carry

    lax.fori_loop(0, line, others, 0)
    norm_copy(1).wait_recv()
    nsend[2] = nsend[1] + nfrom[1]
    norm_copy(2).start()
    norm_copy(2).wait_recv()
    nsend[3] = nsend[2] + nfrom[2]
    for other in range(line):
        pl.when(a != other)(lambda other=other: norm_line(other, False).start())
    stage_line(1)
    nline[a] = nsend[3]
    for other in range(line):
        pl.when(a != other)(lambda other=other: norm_line(other, True).wait_recv())
    total = nline[0]
    for other in range(1, line):
        total += nline[other]
    norms_ref[...] = total

    for step in range(3):
        norm_copy(step).wait_send()
    for other in range(line):
        pl.when(a != other)(lambda other=other: norm_line(other, False).wait_send())
    for t in range(2):
        final(t, theirs_done).wait_recv()
        final(t, mine_done).wait_send()
        sums[t][...] = done[t]

        def left(turn, carry, t=t):
            at, chip = order(turn)
            to_core(t, chip).wait_send()
            to_other(t, chip).wait_send()

            @pl.when(turn < line)
            def _():
                to_across(t, at).wait_send()

            @pl.when((turn >= line) & (at != a))
            def _():
                to_up(t, at).wait_send()

            return carry

        lax.fori_loop(0, chips, left, 0)
    weight_wait((0, 1, 2, 3))


def spread(attended, activated, grad_mixed, grad_up, w_att, w_up, w_down, normed, g_all, x_all):
    count = lax.axis_size("ctx")
    line = count // 4
    tokens, features = x_all.shape
    rows = tokens // count
    half = rows // 2
    chips = 2 * line
    weight_rows = w_att.shape[0] // count
    wide, hidden = w_att.shape[1], w_up.shape[1]
    hbm, vmem = pl.BlockSpec(memory_space=pl.ANY), pl.BlockSpec(memory_space=pltpu.VMEM)
    dma = pltpu.SemaphoreType.DMA
    own = jax.ShapeDtypeStruct((rows, features), BF)
    back = [
        jax.ShapeDtypeStruct((count, weight_rows, columns), BF) for columns in (wide, hidden, hidden)
    ]
    return pl.pallas_call(
        functools.partial(spread_kernel, line),
        out_shape=[own, own]
        + back
        + [
            jax.ShapeDtypeStruct((count, 8, 128), F32),
            jax.ShapeDtypeStruct((8, features // 4), F32),
            jax.ShapeDtypeStruct((8, features), F32),
        ],
        in_specs=[vmem] * 7 + [hbm] * 3,
        out_specs=[vmem, vmem, hbm, hbm, hbm, hbm, vmem, vmem],
        scratch_shapes=[
            pltpu.VMEM((2, chips, 2 * rows, features), BF),
            pltpu.VMEM((2, chips, rows, features), BF),
            pltpu.VMEM((2, chips, half, features), BF),
            pltpu.VMEM((2, line, half, features), BF),
            pltpu.VMEM((2, line + 1, half, features), BF),
            pltpu.VMEM((2, rows, features), BF),
            pltpu.VMEM((4, wide, tokens), BF),
            pltpu.VMEM((3, count * weight_rows, wide), BF),
            pltpu.VMEM((2, 2, tokens, 2 * weight_rows), BF),
            pltpu.VMEM((2, 2 * rows, features), BF),
            pltpu.VMEM((8, features), F32),
            pltpu.VMEM((8, features), F32),
            pltpu.VMEM((4, 8, features // 4), F32),
            pltpu.VMEM((3, 8, features // 4), F32),
            pltpu.VMEM((line, 8, features // 4), F32),
            pltpu.VMEM((8, 128), F32),
            dma((2, 2)),
            dma((2,)),
            dma((2, chips)),
            dma((2, chips)),
            dma((2, chips)),
            dma((2, chips)),
            dma((2, line)),
            dma((2, line)),
            dma((2, line)),
            dma((2, line + 1)),
            dma((2,)),
            dma((2,)),
            dma((4, count)),
            dma((4, count)),
            dma((4,)),
            dma((3,)),
            dma((3,)),
            dma((line,)),
            dma((line,)),
        ],
        compiler_params=pltpu.CompilerParams(
            collective_id=2, has_side_effects=True, vmem_limit_bytes=63 * 1024 * 1024
        ),
    )(attended, activated, grad_mixed, grad_up, w_att, w_up, w_down, normed, g_all, x_all)


def finish_kernel(
    tok_ref, cot_ref, gain_ref, bias_ref, branch_ref, normed_ref, datt_ref, dup_ref, ddown_ref,
    sums_ref, norms_ref, total_ref,
    out_ref, grad_ref, qkv_ref, wout_ref, up_ref, down_ref, qkvb_ref, upb_ref, gsum_ref, ssum_ref,
    bsum_ref,
):
    inputs = tok_ref[...].astype(F32)
    center = inputs - jnp.mean(inputs, axis=-1, keepdims=True)
    inv_std = lax.rsqrt(jnp.mean(center * center, axis=-1, keepdims=True) + EPS)
    unit = center * inv_std
    out_ref[...] = inputs + branch_ref[...].astype(F32) + bias_ref[...]
    grad_unit = normed_ref[...].astype(F32) * gain_ref[...]
    grad_ref[...] = cot_ref[...].astype(F32) + inv_std * (
        grad_unit
        - jnp.mean(grad_unit, axis=-1, keepdims=True)
        - unit * jnp.mean(grad_unit * unit, axis=-1, keepdims=True)
    )
    count, _, packed = datt_ref.shape
    width, hidden = packed // 4, dup_ref.shape[2]
    for owner in range(count):
        columns = pl.ds(owner * width, width)
        piece = datt_ref[owner].astype(F32)
        for kind in range(3):
            qkv_ref[:, kind, columns] = piece[:, kind * width : (kind + 1) * width]
        wout_ref[:, columns] = piece[:, 3 * width :]
        up_ref[:, pl.ds(owner * hidden, hidden)] = dup_ref[owner].astype(F32)
        down_ref[:, pl.ds(owner * hidden, hidden)] = ddown_ref[owner].astype(F32)
        for kind in range(3):
            at = kind * width
            qkvb_ref[pl.ds(kind, 1), columns] = sums_ref[owner, at // 128 : at // 128 + 1, at % 128 : at % 128 + width]
        for at in range(hidden // 128):
            upb_ref[:, pl.ds(owner * hidden + at * 128, 128)] = sums_ref[owner, 2 + at : 3 + at, :]
    wide = norms_ref.shape[1]
    for at in range(4):
        gsum_ref[:, pl.ds(at * wide, wide)] = norms_ref[at : at + 1, :]
        ssum_ref[:, pl.ds(at * wide, wide)] = norms_ref[4 + at : 5 + at, :]
    bsum_ref[...] = total_ref[0:1, :]


def finish(tokens, cotangent, gain, bias, branches, own_normed, d_att, d_up, d_down, sums, norms, total):
    count, weight_rows, packed = d_att.shape
    width, hidden = packed // 4, d_up.shape[2]
    vmem = pl.BlockSpec(memory_space=pltpu.VMEM)
    rows = jax.ShapeDtypeStruct(tokens.shape, F32)
    return pl.pallas_call(
        finish_kernel,
        out_shape=[
            rows,
            rows,
            jax.ShapeDtypeStruct((weight_rows, 3, count * width), F32),
            jax.ShapeDtypeStruct((weight_rows, count * width), F32),
            jax.ShapeDtypeStruct((weight_rows, count * hidden), F32),
            jax.ShapeDtypeStruct((weight_rows, count * hidden), F32),
            jax.ShapeDtypeStruct((3, count * width), F32),
            jax.ShapeDtypeStruct((1, count * hidden), F32),
            jax.ShapeDtypeStruct((1, tokens.shape[1]), F32),
            jax.ShapeDtypeStruct((1, tokens.shape[1]), F32),
            jax.ShapeDtypeStruct((1, tokens.shape[1]), F32),
        ],
        in_specs=[vmem] * 12,
        out_specs=[vmem] * 11,
        compiler_params=pltpu.CompilerParams(vmem_limit_bytes=50 * 1024 * 1024),
    )(
        tokens, cotangent, gain[None], bias[None], branches, own_normed, d_att, d_up, d_down, sums,
        norms, total,
    )


def gelu_tanh(value):
    return jax.nn.gelu(value, approximate=True)


def local(
    tokens, block_order, ln_gain, ln_bias, qkv_weight, qkv_bias, out_weight, fc1_weight, fc1_bias,
    fc2_weight, out_bias, cotangent,
):
    devices = lax.axis_size("ctx")
    myself = lax.axis_index("ctx")
    rows_here, features = tokens.shape
    weight_rows = qkv_weight.shape[0]
    half = devices * rows_here // block_order.shape[0]
    heads_here = qkv_weight.shape[2] // HEAD
    columns = math.gcd(devices, heads_here)
    groups = devices // columns
    mine = myself % columns
    width = qkv_weight.shape[2] // columns
    hidden = fc1_weight.shape[1] // columns
    count = columns * rows_here
    side = [[r * columns + c for c in range(columns)] for r in range(groups)]
    across = [[r * columns + c for r in range(groups)] for c in range(columns)]
    direct = groups == 1 and columns % 8 == 0 and lax.axis_size("tp") == 2

    def gathered(value, among):
        return lax.all_gather(value, "ctx", axis=0, tiled=True, axis_index_groups=among)

    def scattered(value, among):
        return lax.psum_scatter(
            value, "ctx", scatter_dimension=0, tiled=True, axis_index_groups=among
        )

    def exchanged(value):
        return lax.all_to_all(value, "ctx", split_axis=0, concat_axis=0, tiled=True)

    if direct:
        x_all, g_all, w_att, w_up, w_down = collect(
            tokens, cotangent, qkv_weight, out_weight, fc1_weight, fc2_weight
        )
    else:
        x_all, g_all = gathered(tokens, side), gathered(cotangent, side)
        kinds = jnp.concatenate([qkv_weight, out_weight[:, None]], axis=1)
        kinds = kinds.reshape(weight_rows, 4, columns, width).transpose(2, 0, 1, 3)
        packed = jnp.concatenate(
            [
                kinds.reshape(columns, weight_rows, 4 * width),
                fc1_weight.reshape(weight_rows, columns, hidden).transpose(1, 0, 2),
                fc2_weight.reshape(weight_rows, columns, hidden).transpose(1, 0, 2),
            ],
            axis=2,
        )
        packed = exchanged(jnp.tile(packed, (groups, 1, 1))).reshape(devices * weight_rows, -1)
        w_att, w_up, w_down = jnp.split(packed, [4 * width, 4 * width + hidden], axis=1)
    bias_att = lax.dynamic_slice_in_dim(qkv_bias, mine * width, width, 1).reshape(-1)
    bias_att = jnp.concatenate([bias_att, jnp.zeros((width,), F32)])
    bias_up = lax.dynamic_slice_in_dim(fc1_bias, mine * hidden, hidden, 0)

    inputs = x_all.astype(F32)
    center = inputs - jnp.mean(inputs, axis=-1, keepdims=True)
    inv_std = lax.rsqrt(jnp.mean(center * center, axis=-1, keepdims=True) + EPS)
    unit = center * inv_std
    normed = (unit * ln_gain + ln_bias).astype(BF)

    mixed = mm(normed, w_att) + bias_att
    upward = mm(normed, w_up) + bias_up
    activated, gelu_back = jax.vjp(gelu_tanh, upward)
    activated = activated.astype(BF)
    grad_att = mm(g_all, w_att)
    grad_up = gelu_back(mm(g_all, w_down))[0].astype(BF)
    if groups == 1:
        attended, grad_mixed = attention_sorted(block_order, mixed, grad_att)
    else:
        places = (block_order[:, None] * half + jnp.arange(half, dtype=jnp.int32)[None, :]).reshape(-1)
        attended, grad_mixed = attention_blocks(
            lax.dynamic_slice_in_dim(places, (myself // columns) * count, count),
            places,
            mixed,
            grad_att,
            lambda value: gathered(value, across),
            lambda value: scattered(value, across),
        )
    if direct:
        branches, own_normed, d_att, d_up, d_down, sums, norms, total = spread(
            attended, activated, grad_mixed, grad_up, w_att, w_up, w_down, normed, g_all, x_all
        )
    else:
        out_part = (mm(attended, w_att, NT) + mm(activated, w_down, NT)).astype(BF)
        normed_wide = mm(grad_mixed, w_att, NT) + mm(grad_up, w_up, NT)
        branches, own_normed = lax.psum(
            (scattered(out_part, side), scattered(normed_wide.astype(BF), side)), "tp"
        )
        back = jnp.concatenate(
            [
                (mm(normed, grad_mixed, TN) + mm(g_all, attended, TN)).astype(BF),
                mm(normed, grad_up, TN).astype(BF),
                mm(g_all, activated, TN).astype(BF),
            ],
            axis=1,
        )
        back = exchanged(back.reshape(devices, weight_rows, -1))
        back = jnp.sum(back.reshape(groups, columns, weight_rows, -1).astype(F32), axis=0)
        d_att, d_up, d_down = jnp.split(back, [4 * width, 4 * width + hidden], axis=2)
        sums = jnp.concatenate(
            [jnp.sum(grad_mixed.astype(F32), axis=0), jnp.sum(grad_up.astype(F32), axis=0)]
        ).reshape(-1, 128)
        sums = jnp.pad(sums, ((0, 8 - sums.shape[0]), (0, 0)))
        sums = gathered(lax.psum(sums, "ctx", axis_index_groups=across)[None], side)
        norms = jnp.stack([jnp.sum(unit * normed_wide, axis=0), jnp.sum(normed_wide, axis=0)])
        norms = lax.psum(norms, ("ctx", "tp")).reshape(8, -1)
        total = lax.psum(jnp.sum(g_all.astype(F32), axis=0), "ctx", axis_index_groups=across)[None]
    (
        output, input_grad, qkv_grad, out_grad, fc1_grad, fc2_grad, qkv_sums, fc1_sums, gain_sum,
        shift_sum, g_sum,
    ) = finish(
        tokens, cotangent, ln_gain, out_bias, branches, own_normed, d_att, d_up, d_down, sums, norms,
        total,
    )
    return (
        output, input_grad, gain_sum[0], shift_sum[0], qkv_grad, qkv_sums, out_grad, fc1_grad,
        fc1_sums[0], fc2_grad, g_sum[0],
    )


def solution(mesh):
    rows, tall = P("ctx", None), P("ctx", "tp")
    kinds, bias = P("ctx", None, "tp"), P(None, "tp")
    return jax.shard_map(
        local,
        mesh=mesh,
        in_specs=(rows, P(), P(), P(), kinds, bias, tall, tall, P("tp"), tall, P(), rows),
        out_specs=(rows, rows, P(), P(), kinds, bias, tall, tall, P("tp"), tall, P()),
        check_vma=False,
    )
```

```python
import functools
import math

import jax
import jax.numpy as jnp
from jax import lax
from jax.experimental import pallas as pl
from jax.experimental.pallas import tpu as pltpu
from jax.sharding import PartitionSpec as P

HEAD = 64
ROT = 32
EPS = 1e-05
NEG = -1e30
BF = jnp.bfloat16
F32 = jnp.float32
NN = (((1,), (0,)), ((), ()))
NT = (((1,), (1,)), ((), ()))
TN = (((0,), (0,)), ((), ()))


def mm(left, right, dims=NN):
    return lax.dot_general(left, right, dims, preferred_element_type=F32)


def tables(positions, width):
    freqs = 10000.0 ** (-(jnp.arange(width // 2, dtype=F32) * 2.0) / width)
    angles = positions.astype(F32)[:, None] * freqs[None, :]
    return (jnp.cos(angles), jnp.sin(angles))


def turned(value, cosine, sine):
    half = cosine.shape[-1]
    first, second = value[..., :half], value[..., half : 2 * half]
    return jnp.concatenate(
        [first * cosine - second * sine, second * cosine + first * sine, value[..., 2 * half :]],
        axis=-1,
    )


def attention_blocks(own_place, places, mixed, grad_att, gather, scatter):
    count, width = grad_att.shape[0], grad_att.shape[1] // 4
    heads = width // HEAD
    scale = 1.0 / math.sqrt(HEAD)
    grad_att = grad_att[:, 3 * width :].astype(BF)
    cosine, sine = tables(own_place, ROT)
    cosine, sine = cosine[:, None, :], sine[:, None, :]
    kinds = [mixed[:, kind * width : (kind + 1) * width].reshape(count, heads, HEAD) for kind in range(3)]
    queries = turned(kinds[0], cosine, sine).astype(BF)
    keys = gather(turned(kinds[1], cosine, sine).astype(BF))
    values = gather(kinds[2].astype(BF))
    grad_att = grad_att.reshape(count, heads, HEAD)
    block = math.gcd(128, count)

    def one(at, carry):
        key_grad, value_grad, attended, query_grad = carry
        query = lax.dynamic_slice_in_dim(queries, at * block, block)
        grad = lax.dynamic_slice_in_dim(grad_att, at * block, block)
        place = lax.dynamic_slice_in_dim(own_place, at * block, block)
        visible = (place[:, None] >= places[None, :])[None]
        scores = jnp.einsum("qhe,khe->hqk", query, keys, preferred_element_type=F32) * scale
        scores = jnp.where(visible, scores, NEG)
        top = jnp.max(scores, axis=-1, keepdims=True)
        expo = jnp.where(visible, jnp.exp(scores - top), 0.0)
        total = jnp.sum(expo, axis=-1)
        summed = jnp.einsum("hqk,khe->qhe", expo.astype(BF), values, preferred_element_type=F32)
        attend = summed / jnp.transpose(total)[..., None]
        delta = jnp.transpose(jnp.sum(grad.astype(F32) * attend, axis=-1))
        prob = expo / total[..., None]
        dprob = jnp.einsum("qhe,khe->hqk", grad, values, preferred_element_type=F32)
        dscore = (prob * (dprob - delta[..., None])).astype(BF)
        part_q = jnp.einsum("hqk,khe->qhe", dscore, keys, preferred_element_type=F32) * scale
        key_grad += jnp.einsum("hqk,qhe->khe", dscore, query, preferred_element_type=F32) * scale
        value_grad += jnp.einsum("hqk,qhe->khe", prob.astype(BF), grad, preferred_element_type=F32)
        attended = lax.dynamic_update_slice_in_dim(attended, attend.astype(BF), at * block, 0)
        query_grad = lax.dynamic_update_slice_in_dim(query_grad, part_q, at * block, 0)
        return (key_grad, value_grad, attended, query_grad)

    zeros = jnp.zeros(keys.shape, F32)
    own = jnp.zeros((count, heads, HEAD), F32)
    key_grad, value_grad, attended, query_grad = lax.fori_loop(
        0, count // block, one, (zeros, zeros, own.astype(BF), own)
    )
    key_grad, value_grad = scatter(key_grad), scatter(value_grad)
    grad_mixed = jnp.concatenate(
        [
            turned(query_grad, cosine, -sine).astype(BF).reshape(count, width),
            turned(key_grad, cosine, -sine).astype(BF).reshape(count, width),
            value_grad.astype(BF).reshape(count, width),
            jnp.zeros((count, width), BF),
        ],
        axis=1,
    )
    attended = jnp.concatenate(
        [jnp.zeros((count, 3 * width), BF), attended.reshape(count, width)], axis=1
    )
    return attended, grad_mixed


MESH = pl.DeviceIdType.MESH
UP, DOWN, ACROSS, OTHER, CORE = range(5)


def at_rows(start, size):
    return pl.ds(pl.multiple_of(start, size), size)


def remote(source, target, send, receive, device):
    return pltpu.make_async_remote_copy(
        src_ref=source, dst_ref=target, send_sem=send, recv_sem=receive, device_id=device,
        device_id_type=MESH,
    )


class Place:
    def __init__(self, line):
        self.line = line
        self.me = lax.axis_index("ctx")
        self.y = lax.axis_index("tp")
        self.a, self.b, self.c = self.me // 4, (self.me // 2) % 2, self.me % 2
        a, b, c, y = self.a, self.b, self.c, self.y
        self.device = {
            UP: (self.index(jnp.minimum(a + 1, line - 1), b, c), y),
            DOWN: (self.index(jnp.maximum(a - 1, 0), b, c), y),
            ACROSS: (self.index(a, 1 - b, c), y),
            OTHER: (self.me, 1 - y),
            CORE: (self.index(a, b, 1 - c), y),
        }

    def index(self, a, b, c):
        return a * 4 + b * 2 + c

    def far_first(self, turn):
        line = self.line
        high, low = line - 1 - turn, turn
        high = jnp.where(high <= self.a, high - 1, high)
        low = jnp.where(low >= self.a, low + 1, low)
        other = jnp.where(self.a < line // 2, high, low)
        return jnp.where(turn == line - 1, self.a, other)

    def greet(self):
        barrier = pltpu.get_barrier_semaphore()
        count = 4 * self.line

        def signal(step, carry):
            pl.semaphore_signal(
                barrier, inc=1, device_id=(lax.rem(self.me + step, count), self.y), device_id_type=MESH
            )
            return carry

        lax.fori_loop(1, count, signal, 0)
        pl.semaphore_signal(barrier, inc=1, device_id=self.device[OTHER], device_id_type=MESH)
        pl.semaphore_wait(barrier, count)


class Exchange:
    def __init__(self, place, chunk, received, send, receive, own):
        self.place, self.chunk, self.received = place, chunk, received
        self.send, self.receive, self.own = send, receive, own
        self.count = 4 * place.line

    def copy(self, step, n, came):
        place, count = self.place, self.count
        to = lax.rem(place.me + step, count)
        owner = lax.rem(place.me + count - step, count) if came else place.me
        return remote(
            self.chunk(n, to), self.received(n, owner), self.send.at[n, step], self.receive.at[n, step],
            (to, place.y),
        )

    def kept(self, n):
        me = self.place.me
        return pltpu.make_async_copy(self.chunk(n, me), self.received(n, me), self.own.at[n])

    def start(self, pieces):
        for n in pieces:
            self.kept(n).start()

        def one(step, carry):
            for n in pieces:
                self.copy(step, n, False).start()
            return carry

        lax.fori_loop(1, self.count, one, 0)

    def wait(self, pieces):
        def one(step, carry):
            for n in pieces:
                self.copy(step, n, True).wait()
            return carry

        lax.fori_loop(1, self.count, one, 0)
        for n in pieces:
            self.kept(n).wait()


def row_stats(ref, slot, features, piece):
    rows = ref.shape[1]
    mean = jnp.zeros((rows, 1), F32)
    for at in range(0, features, piece):
        mean += jnp.sum(ref[slot, :, at : at + piece].astype(F32), axis=1, keepdims=True)
    mean = mean / features
    spread = jnp.zeros((rows, 1), F32)
    for at in range(0, features, piece):
        center = ref[slot, :, at : at + piece].astype(F32) - mean
        spread += jnp.sum(center * center, axis=1, keepdims=True)
    return mean, lax.rsqrt(spread / features + EPS)


def gelu_parts(value):
    inner = math.sqrt(2.0 / math.pi) * (value + 0.044715 * value * value * value)
    return jnp.tanh(inner)


def seen(start_key, start_query, keys, queries):
    key = start_key + lax.broadcasted_iota(jnp.int32, (keys, queries), 0)
    return key <= start_query + lax.broadcasted_iota(jnp.int32, (keys, queries), 1)


def collect_kernel(
    line, order_ref, inverse_ref, tok_ref, cot_ref, qkv_ref, out_ref, up_ref, down_ref, gain_ref,
    shift_ref, batt_ref, bup_ref, angle_ref,
    x_ref, g_ref, watt_ref, wup_ref, wdown_ref, normed_ref, qkvs_ref, lse_ref, attt_ref, att_ref,
    act_ref, upward_ref, gatt_ref,
    packed, watt_s, wup_s, normed_s, mixed_s, buf, k_s, vt_s, st, att_s,
    send, receive, own_sem, wsend, wreceive, wlocal, buf_sem, out_sem,
):
    place = Place(line)
    a, b, c, y = place.a, place.b, place.c, place.y
    sources, targets = (tok_ref, cot_ref), (x_ref, g_ref)
    rows, features = tok_ref.shape
    half = rows // 2
    weight_rows = up_ref.shape[0]
    tokens = x_ref.shape[0]
    hidden = wup_ref.shape[1]
    width = watt_s.shape[1] // 4
    block = 2 * rows
    blocks = tokens // block
    piece = 512
    place.greet()

    def copy(t, kind, owner, part, own=False):
        target = targets[t].at[at_rows(owner * rows + part * half, half)]
        source = sources[t].at[at_rows(part * half, half)] if own else target
        return remote(
            source, target, send.at[t, kind, owner, part], receive.at[t, owner, part], place.device[kind]
        )

    def landed(t, owner, part):
        copy(t, CORE, owner, part).wait_recv()

    def along(t, distance):
        for sign in (0,) if distance == 0 else (1, -1):
            at = a + sign * distance

            def pass_on(sign=sign, at=at):
                owner = place.index(at, b, c)
                own = distance == 0
                if not own:
                    landed(t, owner, y)
                if sign <= 0:
                    pl.when(a < line - 1)(lambda: copy(t, UP, owner, y, own).start())
                if sign >= 0:
                    pl.when(a > 0)(lambda: copy(t, DOWN, owner, y, own).start())
                copy(t, ACROSS, owner, y, own).start()
                if not own:
                    copy(t, OTHER, owner, y).start()
                copy(t, CORE, owner, y, own).start()
                if own:
                    copy(t, CORE, owner, 1 - y, own).start()

            if distance == 0:
                pass_on()
            else:
                pl.when((at >= 0) & (at < line))(pass_on)

    def beside(t, distance):
        for sign in (0,) if distance == 0 else (1, -1):
            at = a + sign * distance

            def pass_on(at=at):
                owner = place.index(at, 1 - b, c)
                landed(t, owner, y)
                copy(t, OTHER, owner, y).start()
                copy(t, CORE, owner, y).start()

            pl.when((at >= 0) & (at < line))(pass_on)

    def from_other(t):
        for distance in range(line):
            for column in (b, 1 - b):
                for sign in (0,) if distance == 0 else (1, -1):
                    at = a + sign * distance

                    def pass_on(at=at, column=column):
                        owner = place.index(at, column, c)
                        landed(t, owner, 1 - y)
                        copy(t, CORE, owner, 1 - y).start()

                    if distance == 0 and column is b:
                        continue
                    pl.when((at >= 0) & (at < line))(pass_on)

    def own_copy(t):
        return pltpu.make_async_copy(
            sources[t], targets[t].at[at_rows(place.me * rows, rows)], own_sem.at[t]
        )

    def complete(t):
        def came(chip, carry):
            for part in range(2):
                landed(t, chip * 2 + (1 - c), part)
            return carry

        lax.fori_loop(0, 2 * line, came, 0)
        own_copy(t).wait()

    def chunk(n, to):
        if n == 0:
            return packed.at[to]
        return (up_ref, down_ref)[n - 1].at[:, at_rows(to * hidden, hidden)]

    def received(n, owner):
        return (watt_s, wup_s, wdown_ref)[n].at[at_rows(owner * weight_rows, weight_rows)]

    weights = Exchange(place, chunk, received, wsend, wreceive, wlocal)

    def spread_out(t):
        for distance in range(1, line):
            along(t, distance)
            beside(t, distance - 1)
        beside(t, line - 1)

    own_copy(0).start()
    own_copy(1).start()
    along(0, 0)
    for owner in range(4 * line):
        columns = pl.ds(owner * width, width)
        packed[owner, :, :] = jnp.concatenate(
            [qkv_ref[:, kind, columns] for kind in range(3)] + [out_ref[:, columns]], axis=1
        )
    spread_out(0)
    along(1, 0)
    weights.start((0,))
    spread_out(1)
    weights.start((1, 2))
    from_other(0)
    complete(0)
    weights.wait((0,))

    def rows_in(source, at, slot):
        return pltpu.make_async_copy(
            source.at[at_rows(at * block, block)], buf.at[slot], buf_sem.at[slot]
        )

    def normed_out(at):
        here = at_rows(at * block, block)
        return pltpu.make_async_copy(normed_s.at[here], normed_ref.at[here], out_sem)

    def step_rows(source, at):
        slot = lax.rem(at, 2)
        rows_in(source, at, slot).wait()

        @pl.when(at + 1 < blocks)
        def _():
            rows_in(source, at + 1, 1 - slot).start()

        return slot, at_rows(at * block, block)

    quarter = tokens // inverse_ref.shape[0]
    quarters = block // quarter
    rows_in(x_ref, 0, 0).start()

    def project(at, carry):
        slot, here = step_rows(x_ref, at)
        mean, inv_std = row_stats(buf, slot, features, piece)
        for start in range(0, features, piece):
            part = pl.ds(start, piece)
            unit = (buf[slot, :, start : start + piece].astype(F32) - mean) * inv_std
            normed_s[here, part] = (unit * gain_ref[:, part] + shift_ref[:, part]).astype(BF)
        mixed = mm(normed_s[here, :], watt_s[...]) + batt_ref[...]
        mixed_s[pl.ds(at * quarters, quarters)] = mixed.reshape(quarters, quarter, 4 * width)
        return carry

    lax.fori_loop(0, blocks, project, 0)
    whole_normed = pltpu.make_async_copy(normed_s, normed_ref, out_sem)
    whole_normed.start()

    wide = 2 * block
    scale = 1.0 / math.sqrt(HEAD)

    def prepare(at, carry):
        here = at_rows(at * block, block)
        mixed = jnp.concatenate(
            [mixed_s[inverse_ref[at * quarters + n]] for n in range(quarters)], axis=0
        )
        cosine, sine = angle_ref[here, : ROT // 2], angle_ref[here, ROT // 2 :]
        query = turned(mixed[:, :HEAD], cosine, sine).astype(BF) * jnp.asarray(scale, BF)
        key = turned(mixed[:, HEAD : 2 * HEAD], cosine, sine)
        value = mixed[:, 2 * HEAD : 3 * HEAD]
        k_s[here, :] = key.astype(BF)
        vt_s[:, here] = jnp.concatenate([value, value], axis=1).T[:HEAD].astype(BF)
        qkvs_ref[here, :] = jnp.concatenate(
            [query, key.astype(BF), value.astype(BF), jnp.zeros_like(query)], axis=1
        )
        return carry

    lax.fori_loop(0, blocks, prepare, 0)

    def forward(at, carry):
        here = at_rows(at * block, block)
        query = qkvs_ref[here, :][:, :HEAD]

        def scored(place_at, top, masked):
            there = at_rows(place_at * wide, wide)
            scores = mm(k_s[there, :], query, NT)
            if masked:
                scores = jnp.where(seen(place_at * wide, at * block, wide, block), scores, NEG)
            st[there, :] = scores
            return jnp.maximum(top, jnp.max(scores.reshape(wide // 8, 8, block), axis=0))

        last = at // 2
        top = lax.fori_loop(
            0, last, lambda n, top: scored(n, top, False), jnp.full((8, block), NEG, F32)
        )
        top = jnp.max(scored(last, top, True), axis=0, keepdims=True)

        def weighed(place_at, state):
            total, summed = state
            there = at_rows(place_at * wide, wide)
            expo = jnp.exp(st[there, :] - top)
            total = total + jnp.sum(expo.reshape(wide // 8, 8, block), axis=0)
            return (total, summed + mm(vt_s[:, there], expo.astype(BF)))

        total, summed = lax.fori_loop(
            0, last + 1, weighed, (jnp.zeros((8, block), F32), jnp.zeros((HEAD, block), F32))
        )
        total = jnp.sum(total, axis=0, keepdims=True)
        attended = summed * (1.0 / total)
        lse_ref[:, here] = jnp.broadcast_to(top + jnp.log(total), (8, block))
        attt_ref[:, here] = attended
        both = jnp.concatenate([attended, attended], axis=0).T.astype(BF)
        att_s[pl.ds(at * quarters, quarters)] = both.reshape(quarters, quarter, 2 * HEAD)
        return carry

    lax.fori_loop(0, blocks, forward, 0)

    def unplace(at, carry):
        attended = att_s[order_ref[at]][:, HEAD:]
        att_ref[at_rows(at * quarter, quarter), :] = jnp.concatenate(
            [jnp.zeros((quarter, 3 * HEAD), BF), attended], axis=1
        )
        return carry

    lax.fori_loop(0, tokens // quarter, unplace, 0)
    from_other(1)
    complete(1)
    rows_in(g_ref, 0, 0).start()

    def grad_in(at, carry):
        slot, here = step_rows(g_ref, at)
        grad = mm(buf[slot], watt_s[...]).astype(BF)
        gatt_ref[pl.ds(at * quarters, quarters)] = grad.reshape(quarters, quarter, 4 * width)
        return carry

    lax.fori_loop(0, blocks, grad_in, 0)
    weights.wait((1,))

    def feed(at, carry):
        here = at_rows(at * block, block)
        upward = mm(normed_s[here, :], wup_s[...]) + bup_ref[...]
        upward_ref[here, :] = upward
        act_ref[here, :] = (0.5 * upward * (1.0 + gelu_parts(upward))).astype(BF)
        return carry

    lax.fori_loop(0, blocks, feed, 0)
    watt_ref[...] = watt_s[...]
    wup_ref[...] = wup_s[...]
    for t in range(2):

        def left(at, carry, t=t):
            owner, beyond = place.index(at, b, c), place.index(at, 1 - b, c)
            pl.when((at <= a) & (a < line - 1))(lambda: copy(t, UP, owner, y).wait_send())
            pl.when((at >= a) & (a > 0))(lambda: copy(t, DOWN, owner, y).wait_send())
            copy(t, ACROSS, owner, y).wait_send()
            pl.when(at != a)(lambda: copy(t, OTHER, owner, y).wait_send())
            copy(t, OTHER, beyond, y).wait_send()
            for part in range(2):
                copy(t, CORE, owner, part).wait_send()
                copy(t, CORE, beyond, part).wait_send()
            return carry

        lax.fori_loop(0, line, left, 0)
    whole_normed.wait()
    weights.wait((2,))


def collect(
    order, inverse, tokens, cotangent, qkv_weight, out_weight, fc1_weight, fc2_weight, gain, shift,
    bias_att, bias_up, angles,
):
    rows, features = tokens.shape
    weight_rows = fc1_weight.shape[0]
    count = lax.axis_size("ctx")
    line, width, hidden = count // 4, qkv_weight.shape[2] // count, fc1_weight.shape[1] // count
    total, depth = count * rows, count * weight_rows
    halves = order.shape[0]
    hbm, vmem = pl.BlockSpec(memory_space=pl.ANY), pl.BlockSpec(memory_space=pltpu.VMEM)
    smem = pl.BlockSpec(memory_space=pltpu.SMEM)
    dma = pltpu.SemaphoreType.DMA
    shape = jax.ShapeDtypeStruct
    return pl.pallas_call(
        functools.partial(collect_kernel, line),
        out_shape=[
            shape((total, features), BF),
            shape((total, features), BF),
            shape((depth, 4 * width), BF),
            shape((depth, hidden), BF),
            shape((depth, hidden), BF),
            shape((total, features), BF),
            shape((total, 4 * width), BF),
            shape((8, total), F32),
            shape((width, total), F32),
            shape((total, 4 * width), BF),
            shape((total, hidden), BF),
            shape((total, hidden), F32),
            shape((halves, total // halves, 4 * width), BF),
        ],
        in_specs=[smem, smem, hbm, hbm, vmem, vmem, hbm, hbm] + [vmem] * 5,
        out_specs=[hbm, hbm, vmem, vmem, hbm, hbm] + [vmem] * 7,
        scratch_shapes=[
            pltpu.VMEM((count, weight_rows, 4 * width), BF),
            pltpu.VMEM((depth, 4 * width), BF),
            pltpu.VMEM((depth, hidden), BF),
            pltpu.VMEM((total, features), BF),
            pltpu.VMEM((halves, total // halves, 4 * width), F32),
            pltpu.VMEM((2, 2 * rows, features), BF),
            pltpu.VMEM((total, width), BF),
            pltpu.VMEM((width, total), BF),
            pltpu.VMEM((total, 2 * rows), F32),
            pltpu.VMEM((halves, total // halves, 2 * width), BF),
            dma((2, 5, count, 2)),
            dma((2, count, 2)),
            dma((2,)),
            dma((3, count)),
            dma((3, count)),
            dma((3,)),
            dma((2,)),
            dma,
        ],
        compiler_params=pltpu.CompilerParams(
            collective_id=1, has_side_effects=True, vmem_limit_bytes=56 * 1024 * 1024
        ),
    )(
        order, inverse, tokens, cotangent, qkv_weight, out_weight, fc1_weight, fc2_weight, gain, shift,
        bias_att, bias_up, angles,
    )


def spread_kernel(
    line, order_ref, inverse_ref, att_ref, act_ref, upward_ref, gatt_ref, qkvs_ref, lse_ref, attt_ref,
    watt_ref, wup_ref, wdown_ref, angle_ref, normed_ref, g_ref, x_ref,
    sum_ref, gsum_ref, ratt_ref, rup_ref, rdown_ref, rbias_ref, norms_ref, total_ref,
    fresh, own, from_core, from_other, from_across, from_line, done, turned_s, dsend, cols, buf,
    gain_s, shift_s, nsend, nfrom, nline, bias_s, gmix_s, gup_s, kt_s, dkv_s, gm_s,
    cols_sem, buf_sem, csend, creceive, ysend, yreceive, xsend, xreceive, zsend, zreceive, fsend,
    freceive, wsend, wreceive, wlocal, nsend_sem, nreceive, lsend, lreceive,
):
    place = Place(line)
    a, b, c, y = place.a, place.b, place.c, place.y
    sums = (sum_ref, gsum_ref)
    rows, features = own.shape[2:]
    half = rows // 2
    chips = 2 * line
    tokens = att_ref.shape[0]
    block = 2 * rows
    blocks = tokens // block
    weight_rows = dsend.shape[1] // (2 * chips)
    pair = 2 * weight_rows
    piece = 512
    place.greet()
    mine, theirs = at_rows(y * half, half), at_rows((1 - y) * half, half)
    both, sibling = at_rows(c * rows, rows), at_rows((1 - c) * rows, rows)

    def chunk(n, to):
        if n == 3:
            return bias_s
        return dsend.at[n, at_rows(to * weight_rows, weight_rows)]

    def received(n, owner):
        return (ratt_ref, rup_ref, rdown_ref, rbias_ref)[n].at[owner]

    weights = Exchange(place, chunk, received, wsend, wreceive, wlocal)

    def order(turn):
        at = place.far_first(turn // 2)
        return at, at * 2 + jnp.where(lax.rem(turn, 2) == 0, 1 - b, b)

    def to_core(t, turn):
        return remote(
            fresh.at[lax.rem(turn, 2), sibling], from_core.at[t, order(turn)[1]], csend.at[t, turn],
            creceive.at[t, order(turn)[1]], place.device[CORE],
        )

    def to_other(t, chip):
        return remote(
            own.at[t, chip, theirs], from_other.at[t, chip], ysend.at[t, chip], yreceive.at[t, chip],
            place.device[OTHER],
        )

    def to_across(t, at):
        return remote(
            own.at[t, at * 2 + 1 - b, mine], from_across.at[t, at], xsend.at[t, at], xreceive.at[t, at],
            place.device[ACROSS],
        )

    def to_up(t, at):
        return remote(
            own.at[t, at * 2 + b, mine], from_line.at[t, at], zsend.at[t, at], zreceive.at[t, at],
            place.device[UP],
        )

    def to_down(t, at, last):
        slot = line if last else at
        return remote(
            own.at[t, at * 2 + b, mine], from_line.at[t, slot], zsend.at[t, at], zreceive.at[t, slot],
            place.device[DOWN],
        )

    def final(t, part):
        return remote(
            done.at[t, part], done.at[t, part], fsend.at[t], freceive.at[t], place.device[OTHER]
        )

    def add(t, chip, part, other):
        own[t, chip, part, :] = (own[t, chip, part, :].astype(F32) + other.astype(F32)).astype(BF)

    def columns_in(source, n, chip, slot):
        return pltpu.make_async_copy(
            source.at[:, at_rows(chip * pair, pair)], cols.at[n, slot], cols_sem.at[n, slot]
        )

    def rows_in(source, at, slot):
        return pltpu.make_async_copy(
            source.at[at_rows(at * block, block)], buf.at[slot], buf_sem.at[slot]
        )

    rows_in(g_ref, 0, 0).start()
    for n, source in enumerate((normed_ref, g_ref)):
        columns_in(source, n, 0, 0).start()

    def product(t, turn):
        _, chip = order(turn)
        here = at_rows(chip * block, block)
        fresh_at = lax.rem(turn, 2)
        left = ((att_ref, act_ref), (gmix_s, gup_s))[t]
        right = ((watt_ref, wdown_ref), (watt_ref, wup_ref))[t]
        first, second = left[0][here, :], left[1][here, :]
        if t == 1:
            slot = lax.rem(turn, 2)
            rows_in(x_ref, chip, slot).wait()

            @pl.when(turn + 1 < chips)
            def _():
                rows_in(x_ref, order(turn + 1)[1], 1 - slot).start()

            mean, inv_std = row_stats(buf, slot, features, piece)
        for start in range(0, features, piece):
            part = pl.ds(start, piece)
            value = mm(first, right[0][part, :], NT) + mm(second, right[1][part, :], NT)
            fresh[fresh_at, :, part] = value.astype(BF)
            if t == 1:
                unit = (buf[slot, :, start : start + piece].astype(F32) - mean) * inv_std
                shift_s[:, part] += jnp.sum(value.reshape(block // 8, 8, piece), axis=0)
                gain_s[:, part] += jnp.sum((unit * value).reshape(block // 8, 8, piece), axis=0)
        to_core(t, turn).start()

    def stage_core(t, turn):
        _, chip = order(turn)
        to_core(t, turn).wait_recv()
        own[t, chip, :, :] = (
            fresh[lax.rem(turn, 2), both, :].astype(F32) + from_core[t, chip].astype(F32)
        ).astype(BF)
        to_other(t, chip).start()
        to_core(t, turn).wait_send()

    def stage_other(t, nth):
        at = place.far_first(nth)
        chip = at * 2 + 1 - b
        to_other(t, chip).wait_recv()
        add(t, chip, mine, from_other[t, chip])
        to_across(t, at).start()

    def stage_line(t, nth):
        at = place.far_first(nth)
        chip = at * 2 + b
        to_other(t, chip).wait_recv()
        to_across(t, at).wait_recv()
        add(t, chip, mine, from_other[t, chip].astype(F32) + from_across[t, at].astype(F32))

        def down():
            @pl.when(a < line - 1)
            def _():
                to_down(t, at, False).wait_recv()
                add(t, chip, mine, from_line[t, at])

            pl.when(at == a - 1)(lambda: to_down(t, at, True).start())
            pl.when(at < a - 1)(lambda: to_down(t, at, False).start())

        def up():
            @pl.when(a > 0)
            def _():
                to_up(t, at).wait_recv()
                add(t, chip, mine, from_line[t, at])

            to_up(t, at).start()

        if nth < line - 1:
            pl.when(at < a)(down)
            pl.when(at > a)(up)
            return

        @pl.when(a < line - 1)
        def _():
            to_down(t, at, True).wait_recv()
            add(t, chip, mine, from_line[t, line])

        @pl.when(a > 0)
        def _():
            to_up(t, at).wait_recv()
            add(t, chip, mine, from_line[t, at])

        done[t, mine, :] = own[t, chip, mine, :]
        final(t, mine).start()

    def stages(t):
        steps = [functools.partial(stage_other, t, 0)]
        for nth in range(1, line):
            steps.append(functools.partial(stage_other, t, nth))
            steps.append(functools.partial(stage_line, t, nth - 1))
        steps.append(functools.partial(stage_line, t, line - 1))
        return steps

    def norm_copy(step):
        kind = (CORE, OTHER, ACROSS)[step]
        return remote(
            nsend.at[step], nfrom.at[step], nsend_sem.at[step], nreceive.at[step], place.device[kind]
        )

    def norm_line(other, came):
        return remote(
            nsend.at[3], nline.at[other if came else a], lsend.at[other],
            lreceive.at[other if came else a], (place.index(other, b, c), y),
        )

    product(0, 0)

    def first_sum(turn, carry):
        product(0, turn)
        stage_core(0, turn - 1)
        return carry

    lax.fori_loop(1, chips, first_sum, 0)
    stage_core(0, chips - 1)
    pending = stages(0)

    def feed_back(at, carry):
        slot = lax.rem(at, 2)
        rows_in(g_ref, at, slot).wait()

        @pl.when(at + 1 < blocks)
        def _():
            rows_in(g_ref, at + 1, 1 - slot).start()

        here = at_rows(at * block, block)
        upward = upward_ref[here, :]
        tanh = gelu_parts(upward)
        slope = 0.5 * (1.0 + tanh) + 0.5 * upward * (1.0 - tanh * tanh) * (
            math.sqrt(2.0 / math.pi) * (1.0 + 3 * 0.044715 * upward * upward)
        )
        gup_s[here, :] = (mm(buf[slot], wdown_ref[...]) * slope).astype(BF)
        return carry

    lax.fori_loop(0, blocks // 2, feed_back, 0)
    pending.pop(0)()
    lax.fori_loop(blocks // 2, blocks, feed_back, 0)
    rows_in(x_ref, order(0)[1], 0).start()

    def turn_over(pieces):
        def one(at, carry):
            here = at_rows(at * 256, 256)
            for n, source in pieces:
                turned_s[n, :, here] = source[here, :].T
            return carry

        lax.fori_loop(0, tokens // 256, one, 0)

    turn_over(((1, gup_s), (2, att_ref), (3, act_ref)))
    ones = jnp.ones((8, tokens), BF)

    def gradients(chip, carry):
        slot = lax.rem(chip, 2)
        for n, source in enumerate((normed_ref, g_ref)):
            columns_in(source, n, chip, slot).wait()

            @pl.when(chip + 1 < chips)
            def _(n=n, source=source):
                columns_in(source, n, chip + 1, 1 - slot).start()

        here = at_rows(chip * pair, pair)
        by_normed, by_grad = cols[0, slot], cols[1, slot]
        dsend[0, here, :] = mm(turned_s[2], by_grad).T.astype(BF)
        dsend[1, here, :] = mm(turned_s[1], by_normed).T.astype(BF)
        dsend[2, here, :] = mm(turned_s[3], by_grad).T.astype(BF)
        total_ref[:, here] = mm(ones, by_grad)
        return carry

    lax.fori_loop(0, chips // 2, gradients, 0)
    pending.pop(0)()
    lax.fori_loop(chips // 2, chips, gradients, 0)
    weights.start((1, 2))
    columns_in(normed_ref, 0, 0, 0).start()
    pending.pop(0)()

    quarter = tokens // inverse_ref.shape[0]
    quarters = block // quarter
    wide = 2 * block
    scale = 1.0 / math.sqrt(HEAD)

    def prepare(at, carry):
        here = at_rows(at * block, block)
        key = qkvs_ref[here, :][:, : 2 * HEAD].astype(F32)
        kt_s[:, here] = key.T[HEAD:].astype(BF)
        dkv_s[here, :] = jnp.zeros((block, 2 * HEAD), F32)
        return carry

    lax.fori_loop(0, blocks, prepare, 0)

    def backward(at, carry):
        here = at_rows(at * block, block)
        query = qkvs_ref[here, :][:, :HEAD]
        grad = jnp.concatenate(
            [gatt_ref[inverse_ref[at * quarters + n]] for n in range(quarters)], axis=0
        )
        left = lax.broadcasted_iota(jnp.int32, (block, 2 * HEAD), 1) < HEAD
        grad_wide = grad[:, 2 * HEAD :].astype(F32)
        grad_right = jnp.where(left, 0.0, grad_wide).astype(BF)
        query_left = jnp.concatenate([query, jnp.zeros_like(query)], axis=1)
        grad = grad[:, 3 * HEAD :]
        delta = jnp.sum(grad_wide.T[HEAD:] * attt_ref[:, here], axis=0, keepdims=True)
        lse = lse_ref[0:1, here]

        def back(place_at, query_grad, masked):
            there = at_rows(place_at * wide, wide)
            keyvalue = qkvs_ref[there, :]
            scores = mm(keyvalue[:, HEAD : 2 * HEAD], query, NT)
            if masked:
                scores = jnp.where(seen(place_at * wide, at * block, wide, block), scores, NEG)
            prob = jnp.exp(scores - lse)
            dprob = mm(keyvalue[:, 2 * HEAD : 3 * HEAD], grad, NT)
            dscore = (prob * (dprob - delta)).astype(BF)
            dkv_s[there, :] += mm(dscore, query_left) + mm(prob.astype(BF), grad_right)
            return query_grad + mm(kt_s[:, there], dscore)

        last = at // 2
        query_grad = lax.fori_loop(
            0, last, lambda n, total: back(n, total, False), jnp.zeros((HEAD, block), F32)
        )
        query_grad = back(last, query_grad, True)
        query_grad = jnp.concatenate([query_grad, query_grad], axis=0).T[:, :HEAD]
        query_grad = turned(
            query_grad * scale, angle_ref[here, : ROT // 2], -angle_ref[here, ROT // 2 :]
        ).astype(BF)
        gm_s[pl.ds(at * quarters, quarters), :, pl.ds(0, HEAD)] = query_grad.reshape(
            quarters, quarter, HEAD
        )
        return carry

    done_blocks = 0
    for upto in (blocks // 2, blocks * 3 // 4, blocks * 7 // 8, blocks):
        lax.fori_loop(done_blocks, upto, backward, 0)
        done_blocks = upto
        pending.pop(0)()

    def finish_keys(at, carry):
        here = at_rows(at * block, block)
        keyvalue = jnp.concatenate(
            [
                turned(
                    dkv_s[here, :][:, :HEAD], angle_ref[here, : ROT // 2], -angle_ref[here, ROT // 2 :]
                ).astype(BF),
                dkv_s[here, :][:, HEAD:].astype(BF),
            ],
            axis=1,
        )
        gm_s[pl.ds(at * quarters, quarters), :, pl.ds(HEAD, 2 * HEAD)] = keyvalue.reshape(
            quarters, quarter, 2 * HEAD
        )
        return carry

    lax.fori_loop(0, blocks, finish_keys, 0)

    def unplace(at, carry):
        gmix_s[at_rows(at * quarter, quarter), :] = jnp.concatenate(
            [gm_s[order_ref[at]], jnp.zeros((quarter, HEAD), BF)], axis=1
        )
        return carry

    lax.fori_loop(0, tokens // quarter, unplace, 0)
    turn_over(((0, gmix_s),))
    for n, source in enumerate((gmix_s, gup_s)):
        columns = source.shape[1]

        def tally(at, total, source=source, columns=columns):
            return total + jnp.sum(
                source[at_rows(at * 256, 256), :].astype(F32).reshape(32, 8, columns), axis=0
            )

        total = lax.fori_loop(0, tokens // 256, tally, jnp.zeros((8, columns), F32))
        total = jnp.sum(total, axis=0, keepdims=True)
        for at in range(columns // 128):
            bias_s[pl.ds(n * 2 + at, 1), :] = total[:, at * 128 : (at + 1) * 128]
    bias_s[pl.ds(4, 4), :] = jnp.zeros((4, 128), F32)

    gain_s[...] = jnp.zeros_like(gain_s)
    shift_s[...] = jnp.zeros_like(shift_s)

    def gradients_att(chip):
        slot = lax.rem(chip, 2)
        columns_in(normed_ref, 0, chip, slot).wait()

        @pl.when(chip + 1 < chips)
        def _():
            columns_in(normed_ref, 0, chip + 1, 1 - slot).start()

        here = at_rows(chip * pair, pair)
        more = mm(turned_s[0], cols[0, slot]).T
        dsend[0, here, :] = (dsend[0, here, :].astype(F32) + more).astype(BF)

    product(1, 0)

    def second_sum(turn, carry):
        product(1, turn)
        stage_core(1, turn - 1)
        gradients_att(turn - 1)
        return carry

    lax.fori_loop(1, chips, second_sum, 0)
    stage_core(1, chips - 1)
    gradients_att(chips - 1)
    weights.start((0, 3))
    for step in pending:
        step()
    for n, source in enumerate((gain_s, shift_s)):
        total = jnp.sum(source[...], axis=0, keepdims=True)
        span = features // 4
        for at in range(4):
            nsend[0, pl.ds(n * 4 + at, 1), :] = total[:, at * span : (at + 1) * span]
    norm_copy(0).start()
    pending = stages(1)
    pending.pop(0)()
    norm_copy(0).wait_recv()
    nsend[1] = nsend[0] + nfrom[0]
    norm_copy(1).start()
    pending.pop(0)()
    pending.pop(0)()
    norm_copy(1).wait_recv()
    nsend[2] = nsend[1] + nfrom[1]
    norm_copy(2).start()
    pending.pop(0)()
    pending.pop(0)()
    norm_copy(2).wait_recv()
    nsend[3] = nsend[2] + nfrom[2]
    nline[a] = nsend[3]
    for other in range(line):
        pl.when(a != other)(lambda other=other: norm_line(other, False).start())
    for step in pending:
        step()
    for other in range(line):
        pl.when(a != other)(lambda other=other: norm_line(other, True).wait_recv())
    total = nline[0]
    for other in range(1, line):
        total += nline[other]
    norms_ref[...] = total

    for step in range(3):
        norm_copy(step).wait_send()
    for other in range(line):
        pl.when(a != other)(lambda other=other: norm_line(other, False).wait_send())
    for t in range(2):
        final(t, theirs).wait_recv()
        final(t, mine).wait_send()
        sums[t][...] = done[t]

        def left(at, carry, t=t):
            to_other(t, at * 2).wait_send()
            to_other(t, at * 2 + 1).wait_send()
            to_across(t, at).wait_send()
            pl.when(at != a)(lambda: to_up(t, at).wait_send())
            return carry

        lax.fori_loop(0, line, left, 0)
    weights.wait((0, 1, 2, 3))


def spread(
    order, inverse, attended, activated, upward, grad_att, qkvs, lse, attended_t, w_att, w_up, w_down,
    angles, normed, g_all, x_all,
):
    count = lax.axis_size("ctx")
    line = count // 4
    tokens, features = x_all.shape
    rows = tokens // count
    half = rows // 2
    chips = 2 * line
    weight_rows = w_att.shape[0] // count
    wide, hidden = w_att.shape[1], w_up.shape[1]
    hbm, vmem = pl.BlockSpec(memory_space=pl.ANY), pl.BlockSpec(memory_space=pltpu.VMEM)
    smem = pl.BlockSpec(memory_space=pltpu.SMEM)
    dma = pltpu.SemaphoreType.DMA
    own = jax.ShapeDtypeStruct((rows, features), BF)
    back = [
        jax.ShapeDtypeStruct((count, weight_rows, columns), BF) for columns in (wide, hidden, hidden)
    ]
    return pl.pallas_call(
        functools.partial(spread_kernel, line),
        out_shape=[own, own]
        + back
        + [
            jax.ShapeDtypeStruct((count, 8, 128), F32),
            jax.ShapeDtypeStruct((8, features // 4), F32),
            jax.ShapeDtypeStruct((8, features), F32),
        ],
        in_specs=[smem, smem] + [vmem] * 11 + [hbm] * 3,
        out_specs=[vmem, vmem, hbm, hbm, hbm, hbm, vmem, vmem],
        scratch_shapes=[
            pltpu.VMEM((2, 2 * rows, features), BF),
            pltpu.VMEM((2, chips, rows, features), BF),
            pltpu.VMEM((2, chips, rows, features), BF),
            pltpu.VMEM((2, chips, half, features), BF),
            pltpu.VMEM((2, line, half, features), BF),
            pltpu.VMEM((2, line + 1, half, features), BF),
            pltpu.VMEM((2, rows, features), BF),
            pltpu.VMEM((4, wide, tokens), BF),
            pltpu.VMEM((3, count * weight_rows, wide), BF),
            pltpu.VMEM((2, 2, tokens, 2 * weight_rows), BF),
            pltpu.VMEM((2, 2 * rows, features), BF),
            pltpu.VMEM((8, features), F32),
            pltpu.VMEM((8, features), F32),
            pltpu.VMEM((4, 8, features // 4), F32),
            pltpu.VMEM((3, 8, features // 4), F32),
            pltpu.VMEM((line, 8, features // 4), F32),
            pltpu.VMEM((8, 128), F32),
            pltpu.VMEM((tokens, wide), BF),
            pltpu.VMEM((tokens, hidden), BF),
            pltpu.VMEM((HEAD, tokens), BF),
            pltpu.VMEM((tokens, 2 * HEAD), F32),
            pltpu.VMEM((order.shape[0], tokens // order.shape[0], 3 * HEAD), BF),
            dma((2, 2)),
            dma((2,)),
            dma((2, chips)),
            dma((2, chips)),
            dma((2, chips)),
            dma((2, chips)),
            dma((2, line)),
            dma((2, line)),
            dma((2, line)),
            dma((2, line + 1)),
            dma((2,)),
            dma((2,)),
            dma((4, count)),
            dma((4, count)),
            dma((4,)),
            dma((3,)),
            dma((3,)),
            dma((line,)),
            dma((line,)),
        ],
        compiler_params=pltpu.CompilerParams(
            collective_id=2, has_side_effects=True, vmem_limit_bytes=63 * 1024 * 1024
        ),
    )(
        order, inverse, attended, activated, upward, grad_att, qkvs, lse, attended_t, w_att, w_up,
        w_down, angles, normed, g_all, x_all,
    )


def finish_kernel(
    tok_ref, cot_ref, gain_ref, bias_ref, branch_ref, normed_ref, datt_ref, dup_ref, ddown_ref,
    sums_ref, norms_ref, total_ref,
    out_ref, grad_ref, qkv_ref, wout_ref, up_ref, down_ref, qkvb_ref, upb_ref, gsum_ref, ssum_ref,
    bsum_ref,
):
    inputs = tok_ref[...].astype(F32)
    center = inputs - jnp.mean(inputs, axis=-1, keepdims=True)
    inv_std = lax.rsqrt(jnp.mean(center * center, axis=-1, keepdims=True) + EPS)
    unit = center * inv_std
    out_ref[...] = inputs + branch_ref[...].astype(F32) + bias_ref[...]
    grad_unit = normed_ref[...].astype(F32) * gain_ref[...]
    grad_ref[...] = cot_ref[...].astype(F32) + inv_std * (
        grad_unit
        - jnp.mean(grad_unit, axis=-1, keepdims=True)
        - unit * jnp.mean(grad_unit * unit, axis=-1, keepdims=True)
    )
    count, _, packed = datt_ref.shape
    width, hidden = packed // 4, dup_ref.shape[2]
    for owner in range(count):
        columns = pl.ds(owner * width, width)
        piece = datt_ref[owner].astype(F32)
        for kind in range(3):
            qkv_ref[:, kind, columns] = piece[:, kind * width : (kind + 1) * width]
        wout_ref[:, columns] = piece[:, 3 * width :]
        up_ref[:, pl.ds(owner * hidden, hidden)] = dup_ref[owner].astype(F32)
        down_ref[:, pl.ds(owner * hidden, hidden)] = ddown_ref[owner].astype(F32)
        for kind in range(3):
            at = kind * width
            qkvb_ref[pl.ds(kind, 1), columns] = sums_ref[owner, at // 128 : at // 128 + 1, at % 128 : at % 128 + width]
        for at in range(hidden // 128):
            upb_ref[:, pl.ds(owner * hidden + at * 128, 128)] = sums_ref[owner, 2 + at : 3 + at, :]
    wide = norms_ref.shape[1]
    for at in range(4):
        gsum_ref[:, pl.ds(at * wide, wide)] = norms_ref[at : at + 1, :]
        ssum_ref[:, pl.ds(at * wide, wide)] = norms_ref[4 + at : 5 + at, :]
    bsum_ref[...] = total_ref[0:1, :]


def finish(tokens, cotangent, gain, bias, branches, own_normed, d_att, d_up, d_down, sums, norms, total):
    count, weight_rows, packed = d_att.shape
    width, hidden = packed // 4, d_up.shape[2]
    vmem = pl.BlockSpec(memory_space=pltpu.VMEM)
    rows = jax.ShapeDtypeStruct(tokens.shape, F32)
    return pl.pallas_call(
        finish_kernel,
        out_shape=[
            rows,
            rows,
            jax.ShapeDtypeStruct((weight_rows, 3, count * width), F32),
            jax.ShapeDtypeStruct((weight_rows, count * width), F32),
            jax.ShapeDtypeStruct((weight_rows, count * hidden), F32),
            jax.ShapeDtypeStruct((weight_rows, count * hidden), F32),
            jax.ShapeDtypeStruct((3, count * width), F32),
            jax.ShapeDtypeStruct((1, count * hidden), F32),
            jax.ShapeDtypeStruct((1, tokens.shape[1]), F32),
            jax.ShapeDtypeStruct((1, tokens.shape[1]), F32),
            jax.ShapeDtypeStruct((1, tokens.shape[1]), F32),
        ],
        in_specs=[vmem] * 12,
        out_specs=[vmem] * 11,
        compiler_params=pltpu.CompilerParams(vmem_limit_bytes=50 * 1024 * 1024),
    )(
        tokens, cotangent, gain[None], bias[None], branches, own_normed, d_att, d_up, d_down, sums,
        norms, total,
    )


def gelu_tanh(value):
    return jax.nn.gelu(value, approximate=True)


def local(
    tokens, block_order, ln_gain, ln_bias, qkv_weight, qkv_bias, out_weight, fc1_weight, fc1_bias,
    fc2_weight, out_bias, cotangent,
):
    devices = lax.axis_size("ctx")
    myself = lax.axis_index("ctx")
    heads_here = qkv_weight.shape[2] // HEAD
    columns = math.gcd(devices, heads_here)
    mine = myself % columns
    width = qkv_weight.shape[2] // columns
    hidden = fc1_weight.shape[1] // columns
    bias_att = lax.dynamic_slice_in_dim(qkv_bias, mine * width, width, 1).reshape(-1)
    bias_att = jnp.concatenate([bias_att, jnp.zeros((width,), F32)])[None]
    bias_up = lax.dynamic_slice_in_dim(fc1_bias, mine * hidden, hidden, 0)[None]
    if devices == columns and columns % 8 == 0 and width == HEAD and lax.axis_size("tp") == 2:
        halves = block_order.shape[0]
        counted = jnp.arange(halves, dtype=jnp.int32)
        inverse = jnp.sum(
            jnp.where(block_order[None, :] == counted[:, None], counted[None, :], 0), axis=1
        )
        angles = tables(jnp.arange(devices * tokens.shape[0], dtype=jnp.int32), ROT)
        angles = jnp.concatenate(angles, axis=1)
        (
            x_all, g_all, w_att, w_up, w_down, normed, qkvs, lse, attended_t, attended, activated,
            upward, grad_att,
        ) = collect(
            block_order, inverse, tokens, cotangent, qkv_weight, out_weight, fc1_weight, fc2_weight,
            ln_gain[None], ln_bias[None], bias_att, bias_up, angles,
        )
        parts = spread(
            block_order, inverse, attended, activated, upward, grad_att, qkvs, lse, attended_t, w_att,
            w_up, w_down, angles, normed, g_all, x_all,
        )
    else:
        parts = by_groups(
            tokens, block_order, ln_gain, ln_bias, qkv_weight, out_weight, fc1_weight, fc2_weight,
            cotangent, bias_att, bias_up,
        )
    (
        output, input_grad, qkv_grad, out_grad, fc1_grad, fc2_grad, qkv_sums, fc1_sums, gain_sum,
        shift_sum, g_sum,
    ) = finish(tokens, cotangent, ln_gain, out_bias, *parts)
    return (
        output, input_grad, gain_sum[0], shift_sum[0], qkv_grad, qkv_sums, out_grad, fc1_grad,
        fc1_sums[0], fc2_grad, g_sum[0],
    )


def by_groups(
    tokens, block_order, ln_gain, ln_bias, qkv_weight, out_weight, fc1_weight, fc2_weight, cotangent,
    bias_att, bias_up,
):
    devices = lax.axis_size("ctx")
    myself = lax.axis_index("ctx")
    rows_here = tokens.shape[0]
    weight_rows = qkv_weight.shape[0]
    half = devices * rows_here // block_order.shape[0]
    columns = math.gcd(devices, qkv_weight.shape[2] // HEAD)
    groups = devices // columns
    width, hidden = qkv_weight.shape[2] // columns, fc1_weight.shape[1] // columns
    count = columns * rows_here
    side = [[r * columns + c for c in range(columns)] for r in range(groups)]
    across = [[r * columns + c for r in range(groups)] for c in range(columns)]

    def gathered(value, among):
        return lax.all_gather(value, "ctx", axis=0, tiled=True, axis_index_groups=among)

    def scattered(value, among):
        return lax.psum_scatter(
            value, "ctx", scatter_dimension=0, tiled=True, axis_index_groups=among
        )

    def exchanged(value):
        return lax.all_to_all(value, "ctx", split_axis=0, concat_axis=0, tiled=True)

    x_all, g_all = gathered(tokens, side), gathered(cotangent, side)
    kinds = jnp.concatenate([qkv_weight, out_weight[:, None]], axis=1)
    kinds = kinds.reshape(weight_rows, 4, columns, width).transpose(2, 0, 1, 3)
    packed = jnp.concatenate(
        [
            kinds.reshape(columns, weight_rows, 4 * width),
            fc1_weight.reshape(weight_rows, columns, hidden).transpose(1, 0, 2),
            fc2_weight.reshape(weight_rows, columns, hidden).transpose(1, 0, 2),
        ],
        axis=2,
    )
    packed = exchanged(jnp.tile(packed, (groups, 1, 1))).reshape(devices * weight_rows, -1)
    w_att, w_up, w_down = jnp.split(packed, [4 * width, 4 * width + hidden], axis=1)

    inputs = x_all.astype(F32)
    center = inputs - jnp.mean(inputs, axis=-1, keepdims=True)
    inv_std = lax.rsqrt(jnp.mean(center * center, axis=-1, keepdims=True) + EPS)
    unit = center * inv_std
    normed = (unit * ln_gain + ln_bias).astype(BF)
    upward = mm(normed, w_up) + bias_up
    activated, gelu_back = jax.vjp(gelu_tanh, upward)
    activated = activated.astype(BF)
    grad_up = gelu_back(mm(g_all, w_down))[0].astype(BF)
    places = (block_order[:, None] * half + jnp.arange(half, dtype=jnp.int32)[None, :]).reshape(-1)
    attended, grad_mixed = attention_blocks(
        lax.dynamic_slice_in_dim(places, (myself // columns) * count, count),
        places,
        mm(normed, w_att) + bias_att,
        mm(g_all, w_att),
        lambda value: gathered(value, across),
        lambda value: scattered(value, across),
    )
    out_part = (mm(attended, w_att, NT) + mm(activated, w_down, NT)).astype(BF)
    normed_wide = mm(grad_mixed, w_att, NT) + mm(grad_up, w_up, NT)
    branches, own_normed = lax.psum(
        (scattered(out_part, side), scattered(normed_wide.astype(BF), side)), "tp"
    )
    back = jnp.concatenate(
        [
            (mm(normed, grad_mixed, TN) + mm(g_all, attended, TN)).astype(BF),
            mm(normed, grad_up, TN).astype(BF),
            mm(g_all, activated, TN).astype(BF),
        ],
        axis=1,
    )
    back = exchanged(back.reshape(devices, weight_rows, -1))
    back = jnp.sum(back.reshape(groups, columns, weight_rows, -1).astype(F32), axis=0)
    sums = jnp.concatenate(
        [jnp.sum(grad_mixed.astype(F32), axis=0), jnp.sum(grad_up.astype(F32), axis=0)]
    ).reshape(-1, 128)
    sums = jnp.pad(sums, ((0, 8 - sums.shape[0]), (0, 0)))
    sums = gathered(lax.psum(sums, "ctx", axis_index_groups=across)[None], side)
    norms = jnp.stack([jnp.sum(unit * normed_wide, axis=0), jnp.sum(normed_wide, axis=0)])
    norms = lax.psum(norms, ("ctx", "tp")).reshape(8, -1)
    total = lax.psum(jnp.sum(g_all.astype(F32), axis=0), "ctx", axis_index_groups=across)[None]
    return (
        branches, own_normed, *jnp.split(back, [4 * width, 4 * width + hidden], axis=2), sums, norms,
        total,
    )


def solution(mesh):
    rows, tall = P("ctx", None), P("ctx", "tp")
    kinds, bias = P("ctx", None, "tp"), P(None, "tp")
    return jax.shard_map(
        local,
        mesh=mesh,
        in_specs=(rows, P(), P(), P(), kinds, bias, tall, tall, P("tp"), tall, P(), rows),
        out_specs=(rows, rows, P(), P(), kinds, bias, tall, tall, P("tp"), tall, P()),
        check_vma=False,
    )
```

```python
import functools
import math

import jax
import jax.numpy as jnp
from jax import lax
from jax.experimental import pallas as pl
from jax.experimental.pallas import tpu as pltpu
from jax.sharding import PartitionSpec as P

HEAD = 64
ROT = 32
EPS = 1e-05
NEG = -1e30
BF = jnp.bfloat16
F32 = jnp.float32
NN = (((1,), (0,)), ((), ()))
NT = (((1,), (1,)), ((), ()))
TN = (((0,), (0,)), ((), ()))


def mm(left, right, dims=NN):
    return lax.dot_general(left, right, dims, preferred_element_type=F32)


def tables(positions, width):
    freqs = 10000.0 ** (-(jnp.arange(width // 2, dtype=F32) * 2.0) / width)
    angles = positions.astype(F32)[:, None] * freqs[None, :]
    return (jnp.cos(angles), jnp.sin(angles))


def turned(value, cosine, sine):
    half = cosine.shape[-1]
    first, second = value[..., :half], value[..., half : 2 * half]
    return jnp.concatenate(
        [first * cosine - second * sine, second * cosine + first * sine, value[..., 2 * half :]],
        axis=-1,
    )


def attention_blocks(own_place, places, mixed, grad_att, gather, scatter):
    count, width = grad_att.shape[0], grad_att.shape[1] // 4
    heads = width // HEAD
    scale = 1.0 / math.sqrt(HEAD)
    grad_att = grad_att[:, 3 * width :].astype(BF)
    cosine, sine = tables(own_place, ROT)
    cosine, sine = cosine[:, None, :], sine[:, None, :]
    kinds = [mixed[:, kind * width : (kind + 1) * width].reshape(count, heads, HEAD) for kind in range(3)]
    queries = turned(kinds[0], cosine, sine).astype(BF)
    keys = gather(turned(kinds[1], cosine, sine).astype(BF))
    values = gather(kinds[2].astype(BF))
    grad_att = grad_att.reshape(count, heads, HEAD)
    block = math.gcd(128, count)

    def one(at, carry):
        key_grad, value_grad, attended, query_grad = carry
        query = lax.dynamic_slice_in_dim(queries, at * block, block)
        grad = lax.dynamic_slice_in_dim(grad_att, at * block, block)
        place = lax.dynamic_slice_in_dim(own_place, at * block, block)
        visible = (place[:, None] >= places[None, :])[None]
        scores = jnp.einsum("qhe,khe->hqk", query, keys, preferred_element_type=F32) * scale
        scores = jnp.where(visible, scores, NEG)
        top = jnp.max(scores, axis=-1, keepdims=True)
        expo = jnp.where(visible, jnp.exp(scores - top), 0.0)
        total = jnp.sum(expo, axis=-1)
        summed = jnp.einsum("hqk,khe->qhe", expo.astype(BF), values, preferred_element_type=F32)
        attend = summed / jnp.transpose(total)[..., None]
        delta = jnp.transpose(jnp.sum(grad.astype(F32) * attend, axis=-1))
        prob = expo / total[..., None]
        dprob = jnp.einsum("qhe,khe->hqk", grad, values, preferred_element_type=F32)
        dscore = (prob * (dprob - delta[..., None])).astype(BF)
        part_q = jnp.einsum("hqk,khe->qhe", dscore, keys, preferred_element_type=F32) * scale
        key_grad += jnp.einsum("hqk,qhe->khe", dscore, query, preferred_element_type=F32) * scale
        value_grad += jnp.einsum("hqk,qhe->khe", prob.astype(BF), grad, preferred_element_type=F32)
        attended = lax.dynamic_update_slice_in_dim(attended, attend.astype(BF), at * block, 0)
        query_grad = lax.dynamic_update_slice_in_dim(query_grad, part_q, at * block, 0)
        return (key_grad, value_grad, attended, query_grad)

    zeros = jnp.zeros(keys.shape, F32)
    own = jnp.zeros((count, heads, HEAD), F32)
    key_grad, value_grad, attended, query_grad = lax.fori_loop(
        0, count // block, one, (zeros, zeros, own.astype(BF), own)
    )
    key_grad, value_grad = scatter(key_grad), scatter(value_grad)
    grad_mixed = jnp.concatenate(
        [
            turned(query_grad, cosine, -sine).astype(BF).reshape(count, width),
            turned(key_grad, cosine, -sine).astype(BF).reshape(count, width),
            value_grad.astype(BF).reshape(count, width),
            jnp.zeros((count, width), BF),
        ],
        axis=1,
    )
    attended = jnp.concatenate(
        [jnp.zeros((count, 3 * width), BF), attended.reshape(count, width)], axis=1
    )
    return attended, grad_mixed


MESH = pl.DeviceIdType.MESH
UP, DOWN, ACROSS, OTHER, CORE = range(5)


def at_rows(start, size):
    return pl.ds(pl.multiple_of(start, size), size)


def remote(source, target, send, receive, device):
    return pltpu.make_async_remote_copy(
        src_ref=source, dst_ref=target, send_sem=send, recv_sem=receive, device_id=device,
        device_id_type=MESH,
    )


class Place:
    def __init__(self, line):
        self.line = line
        self.me = lax.axis_index("ctx")
        self.y = lax.axis_index("tp")
        self.a, self.b, self.c = self.me // 4, (self.me // 2) % 2, self.me % 2
        a, b, c, y = self.a, self.b, self.c, self.y
        self.device = {
            UP: (self.index(jnp.minimum(a + 1, line - 1), b, c), y),
            DOWN: (self.index(jnp.maximum(a - 1, 0), b, c), y),
            ACROSS: (self.index(a, 1 - b, c), y),
            OTHER: (self.me, 1 - y),
            CORE: (self.index(a, b, 1 - c), y),
        }

    def index(self, a, b, c):
        return a * 4 + b * 2 + c

    def far_first(self, turn):
        line = self.line
        high, low = line - 1 - turn, turn
        high = jnp.where(high <= self.a, high - 1, high)
        low = jnp.where(low >= self.a, low + 1, low)
        other = jnp.where(self.a < line // 2, high, low)
        return jnp.where(turn == line - 1, self.a, other)

    def greet(self):
        barrier = pltpu.get_barrier_semaphore()
        count = 4 * self.line

        def signal(step, carry):
            pl.semaphore_signal(
                barrier, inc=1, device_id=(lax.rem(self.me + step, count), self.y), device_id_type=MESH
            )
            return carry

        lax.fori_loop(1, count, signal, 0)
        pl.semaphore_signal(barrier, inc=1, device_id=self.device[OTHER], device_id_type=MESH)
        pl.semaphore_wait(barrier, count)


def flipped(value, mask, bits):
    result = 0
    for bit in range(bits):
        part = (value // 2**bit) % 2
        result = result + 2**bit * (1 - part if mask >> bit & 1 else part)
    return result


class Exchange:
    def __init__(self, place, chunk, received, send, receive, own):
        self.place, self.chunk, self.received = place, chunk, received
        self.send, self.receive, self.own = send, receive, own
        self.count = 4 * place.line
        bits = self.count.bit_length() - 1
        self.partners = [
            (mask, flipped(place.me, mask, bits)) for mask in range(self.count - 1, 0, -1)
        ]

    def copy(self, partner, n, came):
        mask, to = partner
        return remote(
            self.chunk(n, to), self.received(n, to if came else self.place.me), self.send.at[n, mask],
            self.receive.at[n, mask], (to, self.place.y),
        )

    def kept(self, n):
        me = self.place.me
        return pltpu.make_async_copy(self.chunk(n, me), self.received(n, me), self.own.at[n])

    def keep(self, pieces):
        for n in pieces:
            self.kept(n).start()

    def start(self, pieces, wanted=lambda at, mask: True):
        for at, partner in enumerate(self.partners):
            for n in pieces:
                if wanted(at, partner[0]):
                    self.copy(partner, n, False).start()

    def wait(self, pieces):
        for partner in self.partners:
            for n in pieces:
                self.copy(partner, n, True).wait()
        for n in pieces:
            self.kept(n).wait()


def row_stats(load, rows, features, piece):
    mean = jnp.zeros((rows, 1), F32)
    for at in range(0, features, piece):
        mean += jnp.sum(load(at), axis=1, keepdims=True)
    mean = mean / features
    spread = jnp.zeros((rows, 1), F32)
    for at in range(0, features, piece):
        center = load(at) - mean
        spread += jnp.sum(center * center, axis=1, keepdims=True)
    return mean, lax.rsqrt(spread / features + EPS)


class Stream:
    def __init__(self, copy, depth, total):
        self.copy, self.depth, self.total = copy, depth, total

    def prime(self):
        for at in range(min(self.depth - 1, self.total)):
            self.copy(at, at).start()

    def step(self, at):
        slot = lax.rem(at, self.depth)
        self.copy(at, slot).wait()
        later = at + self.depth - 1

        @pl.when(later < self.total)
        def _():
            self.copy(later, lax.rem(later, self.depth)).start()

        return slot


def gelu_parts(value):
    inner = math.sqrt(2.0 / math.pi) * (value + 0.044715 * value * value * value)
    return jnp.tanh(inner)


def seen(start_key, start_query, keys, queries):
    key = start_key + lax.broadcasted_iota(jnp.int32, (keys, queries), 0)
    return key <= start_query + lax.broadcasted_iota(jnp.int32, (keys, queries), 1)


def collect_kernel(
    line, order_ref, inverse_ref, tok_ref, cot_ref, qkv_ref, out_ref, up_ref, down_ref, gain_ref,
    shift_ref, batt_ref, bup_ref, angle_ref,
    x_out, g_out, watt_out, wup_out, wdown_ref, normed_out, qkvs_out, lse_out, attt_out, att_out,
    act_out, upward_out, gatt_out,
    x_ref, g_ref, watt_s, wup_s, normed_s, qkvs_ref, lse_ref, attt_ref, att_ref, act_ref, upward_ref,
    gatt_ref, packed, mixed_s, k_s, vt_s, st, att_s,
    send, receive, own_sem, wsend, wreceive, wlocal, out_sem,
):
    place = Place(line)
    a, b, c, y = place.a, place.b, place.c, place.y
    sources, targets = (tok_ref, cot_ref), (x_ref, g_ref)
    rows, features = tok_ref.shape
    half = rows // 2
    weight_rows = up_ref.shape[0]
    tokens = x_ref.shape[0]
    hidden = wup_s.shape[1]
    width = watt_s.shape[1] // 4
    block = 2 * rows
    blocks = tokens // block
    piece = 512
    place.greet()
    shipped = []

    def ship(source, target):
        shipped.append(pltpu.make_async_copy(source, target, out_sem.at[len(shipped)]))
        shipped[-1].start()

    def copy(t, kind, owner, part, own=False):
        target = targets[t].at[at_rows(owner * rows + part * half, half)]
        source = sources[t].at[at_rows(part * half, half)] if own else target
        return remote(
            source, target, send.at[t, kind, owner, part], receive.at[t, owner, part], place.device[kind]
        )

    def landed(t, owner, part):
        copy(t, CORE, owner, part).wait_recv()

    def along(t, distance):
        for sign in (0,) if distance == 0 else (1, -1):
            at = a + sign * distance

            def pass_on(sign=sign, at=at):
                owner = place.index(at, b, c)
                own = distance == 0
                if not own:
                    landed(t, owner, y)
                if sign <= 0:
                    pl.when(a < line - 1)(lambda: copy(t, UP, owner, y, own).start())
                if sign >= 0:
                    pl.when(a > 0)(lambda: copy(t, DOWN, owner, y, own).start())
                copy(t, ACROSS, owner, y, own).start()
                if not own:
                    copy(t, OTHER, owner, y).start()
                copy(t, CORE, owner, y, own).start()
                if own:
                    copy(t, CORE, owner, 1 - y, own).start()

            if distance == 0:
                pass_on()
            else:
                pl.when((at >= 0) & (at < line))(pass_on)

    def beside(t, distance):
        for sign in (0,) if distance == 0 else (1, -1):
            at = a + sign * distance

            def pass_on(at=at):
                owner = place.index(at, 1 - b, c)
                landed(t, owner, y)
                copy(t, OTHER, owner, y).start()
                copy(t, CORE, owner, y).start()

            pl.when((at >= 0) & (at < line))(pass_on)

    def from_other(t):
        for distance in range(line):
            for column in (b, 1 - b):
                for sign in (0,) if distance == 0 else (1, -1):
                    at = a + sign * distance

                    def pass_on(at=at, column=column):
                        owner = place.index(at, column, c)
                        landed(t, owner, 1 - y)
                        copy(t, CORE, owner, 1 - y).start()

                    if distance == 0 and column is b:
                        continue
                    pl.when((at >= 0) & (at < line))(pass_on)

    def own_copy(t):
        return pltpu.make_async_copy(
            sources[t], targets[t].at[at_rows(place.me * rows, rows)], own_sem.at[t]
        )

    def complete(t):
        def came(chip, carry):
            for part in range(2):
                landed(t, chip * 2 + (1 - c), part)
            return carry

        lax.fori_loop(0, 2 * line, came, 0)
        own_copy(t).wait()

    def chunk(n, to):
        if n == 0:
            return packed.at[to]
        return (up_ref, down_ref)[n - 1].at[:, at_rows(to * hidden, hidden)]

    def received(n, owner):
        return (watt_s, wup_s, wdown_ref)[n].at[at_rows(owner * weight_rows, weight_rows)]

    weights = Exchange(place, chunk, received, wsend, wreceive, wlocal)

    own_copy(0).start()
    own_copy(1).start()
    along(0, 0)
    for owner in range(4 * line):
        columns = pl.ds(owner * width, width)
        packed[owner, :, :] = jnp.concatenate(
            [qkv_ref[kind, :, columns] for kind in range(3)] + [out_ref[:, columns]], axis=1
        )
    weights.keep((0, 1, 2))
    for distance in range(1, line):
        along(0, distance)
        beside(0, distance - 1)
    beside(0, line - 1)
    along(1, 0)
    weights.start((0,))
    for distance in range(1, line - 1):
        along(1, distance)
        beside(1, distance - 1)
    weights.start((1, 2), lambda at, mask: not mask & 2)
    from_other(0)
    complete(0)
    weights.wait((0,))
    ship(x_ref, x_out)
    ship(watt_s, watt_out)

    quarter = tokens // inverse_ref.shape[0]
    quarters = block // quarter

    def project(at, carry):
        here = at_rows(at * block, block)

        def load(start):
            return x_ref[here, pl.ds(start, piece)].astype(F32)

        mean, inv_std = row_stats(load, block, features, piece)
        for start in range(0, features, piece):
            part = pl.ds(start, piece)
            unit = (load(start) - mean) * inv_std
            normed_s[here, part] = (unit * gain_ref[:, part] + shift_ref[:, part]).astype(BF)
        mixed = mm(normed_s[here, :], watt_s[...]) + batt_ref[...]
        mixed_s[pl.ds(at * quarters, quarters)] = mixed.reshape(quarters, quarter, 4 * width)
        return carry

    lax.fori_loop(0, blocks // 2, project, 0)
    along(1, line - 1)
    beside(1, line - 2)
    lax.fori_loop(blocks // 2, blocks, project, 0)
    ship(normed_s, normed_out)
    beside(1, line - 1)
    weights.start((1, 2), lambda at, mask: mask & 2)

    wide = 2 * block
    scale = 1.0 / math.sqrt(HEAD)

    def prepare(at, carry):
        here = at_rows(at * block, block)
        mixed = jnp.concatenate(
            [mixed_s[inverse_ref[at * quarters + n]] for n in range(quarters)], axis=0
        )
        cosine, sine = angle_ref[here, : ROT // 2], angle_ref[here, ROT // 2 :]
        query = turned(mixed[:, :HEAD], cosine, sine).astype(BF) * jnp.asarray(scale, BF)
        key = turned(mixed[:, HEAD : 2 * HEAD], cosine, sine)
        value = mixed[:, 2 * HEAD : 3 * HEAD]
        k_s[here, :] = key.astype(BF)
        vt_s[:, here] = jnp.concatenate([value, value], axis=1).T[:HEAD].astype(BF)
        qkvs_ref[here, :] = jnp.concatenate(
            [query, key.astype(BF), value.astype(BF), jnp.zeros_like(query)], axis=1
        )
        return carry

    lax.fori_loop(0, blocks, prepare, 0)

    def forward(at, carry):
        here = at_rows(at * block, block)
        query = qkvs_ref[here, :][:, :HEAD]

        def scored(place_at, top, masked):
            there = at_rows(place_at * wide, wide)
            scores = mm(k_s[there, :], query, NT)
            if masked:
                scores = jnp.where(seen(place_at * wide, at * block, wide, block), scores, NEG)
            st[there, :] = scores
            return jnp.maximum(top, jnp.max(scores.reshape(wide // 8, 8, block), axis=0))

        last = at // 2
        top = lax.fori_loop(
            0, last, lambda n, top: scored(n, top, False), jnp.full((8, block), NEG, F32)
        )
        top = jnp.max(scored(last, top, True), axis=0, keepdims=True)

        def weighed(place_at, state):
            total, summed = state
            there = at_rows(place_at * wide, wide)
            expo = jnp.exp(st[there, :] - top)
            total = total + jnp.sum(expo.reshape(wide // 8, 8, block), axis=0)
            return (total, summed + mm(vt_s[:, there], expo.astype(BF)))

        total, summed = lax.fori_loop(
            0, last + 1, weighed, (jnp.zeros((8, block), F32), jnp.zeros((HEAD, block), F32))
        )
        total = jnp.sum(total, axis=0, keepdims=True)
        attended = summed * (1.0 / total)
        lse_ref[:, here] = jnp.broadcast_to(top + jnp.log(total), (8, block))
        attt_ref[:, here] = attended
        both = jnp.concatenate([attended, attended], axis=0).T.astype(BF)
        att_s[pl.ds(at * quarters, quarters)] = both.reshape(quarters, quarter, 2 * HEAD)
        return carry

    lax.fori_loop(0, blocks, forward, 0)
    for source, target in ((qkvs_ref, qkvs_out), (lse_ref, lse_out), (attt_ref, attt_out)):
        ship(source, target)

    def unplace(at, carry):
        attended = att_s[order_ref[at]][:, HEAD:]
        att_ref[at_rows(at * quarter, quarter), :] = jnp.concatenate(
            [jnp.zeros((quarter, 3 * HEAD), BF), attended], axis=1
        )
        return carry

    lax.fori_loop(0, tokens // quarter, unplace, 0)
    ship(att_ref, att_out)
    from_other(1)
    complete(1)
    ship(g_ref, g_out)

    def grad_in(at, carry):
        grad = mm(g_ref[at_rows(at * block, block), :], watt_s[...]).astype(BF)
        gatt_ref[pl.ds(at * quarters, quarters)] = grad.reshape(quarters, quarter, 4 * width)
        return carry

    lax.fori_loop(0, blocks, grad_in, 0)
    ship(gatt_ref, gatt_out)
    weights.wait((1,))
    ship(wup_s, wup_out)

    def feed(at, carry):
        here = at_rows(at * block, block)
        upward = mm(normed_s[here, :], wup_s[...]) + bup_ref[...]
        upward_ref[here, :] = upward
        act_ref[here, :] = (0.5 * upward * (1.0 + gelu_parts(upward))).astype(BF)
        return carry

    lax.fori_loop(0, blocks, feed, 0)
    ship(upward_ref, upward_out)
    ship(act_ref, act_out)
    for t in range(2):

        def left(at, carry, t=t):
            owner, beyond = place.index(at, b, c), place.index(at, 1 - b, c)
            pl.when((at <= a) & (a < line - 1))(lambda: copy(t, UP, owner, y).wait_send())
            pl.when((at >= a) & (a > 0))(lambda: copy(t, DOWN, owner, y).wait_send())
            copy(t, ACROSS, owner, y).wait_send()
            pl.when(at != a)(lambda: copy(t, OTHER, owner, y).wait_send())
            copy(t, OTHER, beyond, y).wait_send()
            for part in range(2):
                copy(t, CORE, owner, part).wait_send()
                copy(t, CORE, beyond, part).wait_send()
            return carry

        lax.fori_loop(0, line, left, 0)
    weights.wait((2,))
    for result in shipped:
        result.wait()


def collect(
    order, inverse, tokens, cotangent, qkv_weight, out_weight, fc1_weight, fc2_weight, gain, shift,
    bias_att, bias_up, angles,
):
    rows, features = tokens.shape
    weight_rows = fc1_weight.shape[0]
    count = lax.axis_size("ctx")
    line, width, hidden = count // 4, qkv_weight.shape[2] // count, fc1_weight.shape[1] // count
    total, depth = count * rows, count * weight_rows
    halves = order.shape[0]
    hbm, vmem = pl.BlockSpec(memory_space=pl.ANY), pl.BlockSpec(memory_space=pltpu.VMEM)
    smem = pl.BlockSpec(memory_space=pltpu.SMEM)
    dma = pltpu.SemaphoreType.DMA
    shape = jax.ShapeDtypeStruct
    return pl.pallas_call(
        functools.partial(collect_kernel, line),
        out_shape=[
            shape((total, features), BF),
            shape((total, features), BF),
            shape((depth, 4 * width), BF),
            shape((depth, hidden), BF),
            shape((depth, hidden), BF),
            shape((total, features), BF),
            shape((total, 4 * width), BF),
            shape((8, total), F32),
            shape((width, total), F32),
            shape((total, 4 * width), BF),
            shape((total, hidden), BF),
            shape((total, hidden), F32),
            shape((halves, total // halves, 4 * width), BF),
        ],
        in_specs=[smem, smem, hbm, hbm, vmem, vmem, hbm, hbm] + [vmem] * 5,
        out_specs=[hbm] * 13,
        scratch_shapes=[
            pltpu.VMEM((total, features), BF),
            pltpu.VMEM((total, features), BF),
            pltpu.VMEM((depth, 4 * width), BF),
            pltpu.VMEM((depth, hidden), BF),
            pltpu.VMEM((total, features), BF),
            pltpu.VMEM((total, 4 * width), BF),
            pltpu.VMEM((8, total), F32),
            pltpu.VMEM((width, total), F32),
            pltpu.VMEM((total, 4 * width), BF),
            pltpu.VMEM((total, hidden), BF),
            pltpu.VMEM((total, hidden), F32),
            pltpu.VMEM((halves, total // halves, 4 * width), BF),
            pltpu.VMEM((count, weight_rows, 4 * width), BF),
            pltpu.VMEM((halves, total // halves, 4 * width), F32),
            pltpu.VMEM((total, width), BF),
            pltpu.VMEM((width, total), BF),
            pltpu.VMEM((total, 2 * rows), F32),
            pltpu.VMEM((halves, total // halves, 2 * width), BF),
            dma((2, 5, count, 2)),
            dma((2, count, 2)),
            dma((2,)),
            dma((3, count)),
            dma((3, count)),
            dma((3,)),
            dma((12,)),
        ],
        compiler_params=pltpu.CompilerParams(
            collective_id=1, has_side_effects=True, vmem_limit_bytes=60 * 1024 * 1024
        ),
    )(
        order, inverse, tokens, cotangent, qkv_weight.transpose(1, 0, 2), out_weight, fc1_weight,
        fc2_weight, gain, shift, bias_att, bias_up, angles,
    )


def spread_kernel(
    line, order_ref, inverse_ref, att_ref, act_ref, watt_ref, wdown_ref, lse_ref, angle_ref,
    upward_in, gatt_in, qkvs_in, attt_in, wup_in, normed_ref, g_ref, x_ref,
    sum_ref, gsum_ref, ratt_ref, rup_ref, rdown_ref, rbias_ref, norms_ref, total_ref,
    upward_ref, gatt_ref, qkvs_ref, attt_ref, wup_ref,
    fresh, own, from_core, from_other, from_across, from_beyond, from_line, done, turned_s, dsend, cols,
    buf, gain_s, shift_s, nsend, nfrom, nline, bias_s, gmix_s, gup_s, kt_s, dkv_s, gm_s,
    in_sem, cols_sem, buf_sem, csend, creceive, credit, ysend, yreceive, xsend, xreceive, bsend,
    breceive, zsend, zreceive, fsend, freceive, wsend, wreceive, wlocal, nsend_sem, nreceive, lsend,
    lreceive,
):
    place = Place(line)
    a, b, c, y = place.a, place.b, place.c, place.y
    sums = (sum_ref, gsum_ref)
    rows, features = own.shape[2:]
    half = rows // 2
    chips = 2 * line
    tokens = att_ref.shape[0]
    block = 2 * rows
    blocks = tokens // block
    weight_rows = dsend.shape[1] // (2 * chips)
    pair = 2 * weight_rows
    piece = 512
    ring = from_core.shape[0]
    shortcut = 2 if line > 2 else -1
    place.greet()
    late = [
        pltpu.make_async_copy(source, target, in_sem.at[n])
        for n, (source, target) in enumerate(
            (
                (upward_in, upward_ref), (gatt_in, gatt_ref), (qkvs_in, qkvs_ref), (attt_in, attt_ref),
                (wup_in, wup_ref),
            )
        )
    ]
    for operand in late:
        operand.start()
    mine, theirs = at_rows(y * half, half), at_rows((1 - y) * half, half)
    both, sibling = at_rows(c * rows, rows), at_rows((1 - c) * rows, rows)

    def chunk(n, to):
        if n == 3:
            return bias_s
        return dsend.at[n, at_rows(to * weight_rows, weight_rows)]

    def received(n, owner):
        return (ratt_ref, rup_ref, rdown_ref, rbias_ref)[n].at[owner]

    weights = Exchange(place, chunk, received, wsend, wreceive, wlocal)

    def order(turn):
        at = place.far_first(turn // 2)
        return at, at * 2 + jnp.where(lax.rem(turn, 2) == 0, 1 - b, b)

    def to_core(t, turn):
        return remote(
            fresh.at[lax.rem(turn, 2), sibling], from_core.at[lax.rem(turn, ring)], csend.at[t, turn],
            creceive.at[lax.rem(turn, ring)], place.device[CORE],
        )

    def to_other(t, chip):
        return remote(
            own.at[t, chip, theirs], from_other.at[t, chip], ysend.at[t, chip], yreceive.at[t, chip],
            place.device[OTHER],
        )

    def to_across(t, at):
        return remote(
            own.at[t, at * 2 + 1 - b, mine], from_across.at[t, at], xsend.at[t, at], xreceive.at[t, at],
            place.device[ACROSS],
        )

    def to_beyond(t):
        at = place.far_first(shortcut)
        return remote(
            own.at[t, at * 2 + 1 - b], from_beyond.at[t], bsend.at[t], breceive.at[t], place.device[ACROSS]
        )

    def to_up(t, at):
        return remote(
            own.at[t, at * 2 + b, mine], from_line.at[t, at], zsend.at[t, at], zreceive.at[t, at],
            place.device[UP],
        )

    def to_down(t, at, last):
        slot = line if last else at
        return remote(
            own.at[t, at * 2 + b, mine], from_line.at[t, slot], zsend.at[t, at], zreceive.at[t, slot],
            place.device[DOWN],
        )

    def final(t, part):
        return remote(
            done.at[t, part], done.at[t, part], fsend.at[t], freceive.at[t], place.device[OTHER]
        )

    def add(t, chip, part, other):
        own[t, chip, part, :] = (own[t, chip, part, :].astype(F32) + other.astype(F32)).astype(BF)

    def columns_of(n, source):
        return Stream(
            lambda chip, slot: pltpu.make_async_copy(
                source.at[:, at_rows(chip * pair, pair)], cols.at[n, slot], cols_sem.at[n, slot]
            ),
            cols.shape[1],
            chips,
        )

    def rows_of(source, chip_of):
        return Stream(
            lambda at, slot: pltpu.make_async_copy(
                source.at[at_rows(chip_of(at) * block, block)], buf.at[slot], buf_sem.at[slot]
            ),
            buf.shape[0],
            blocks,
        )

    g_rows, x_rows = rows_of(g_ref, lambda at: at), rows_of(x_ref, lambda at: order(at)[1])
    normed_columns, g_columns = columns_of(0, normed_ref), columns_of(1, g_ref)
    g_rows.prime()
    normed_columns.prime()
    g_columns.prime()

    def product(t, turn):
        _, chip = order(turn)
        here = at_rows(chip * block, block)
        fresh_at = lax.rem(turn, 2)
        left = ((att_ref, act_ref), (gmix_s, gup_s))[t]
        right = ((watt_ref, wdown_ref), (watt_ref, wup_ref))[t]
        first, second = left[0][here, :], left[1][here, :]
        if t == 1:
            slot = x_rows.step(turn)

            def load(start):
                return buf[slot, :, pl.ds(start, piece)].astype(F32)

            mean, inv_std = row_stats(load, block, features, piece)
        for start in range(0, features, piece):
            part = pl.ds(start, piece)
            value = mm(first, right[0][part, :], NT) + mm(second, right[1][part, :], NT)
            fresh[fresh_at, :, part] = value.astype(BF)
            if t == 1:
                unit = (load(start) - mean) * inv_std
                shift_s[:, part] += jnp.sum(value.reshape(block // 8, 8, piece), axis=0)
                gain_s[:, part] += jnp.sum((unit * value).reshape(block // 8, 8, piece), axis=0)
        if t == 1:
            pl.semaphore_wait(credit, 1)
        else:
            pl.when(turn >= ring)(lambda: pl.semaphore_wait(credit, 1))
        to_core(t, turn).start()

    def stage_core(t, turn):
        _, chip = order(turn)
        to_core(t, turn).wait_recv()
        own[t, chip, :, :] = (
            fresh[lax.rem(turn, 2), both, :].astype(F32)
            + from_core[lax.rem(turn, ring)].astype(F32)
        ).astype(BF)

        def give():
            pl.semaphore_signal(
                credit, inc=1, device_id=place.device[CORE], device_id_type=MESH
            )

        if t == 0:
            give()
        else:
            pl.when(turn < chips - ring)(give)
        if shortcut < 0:
            to_other(t, chip).start()
        else:
            pl.when(turn == 2 * shortcut)(lambda: to_beyond(t).start())
            pl.when(turn // 2 != shortcut)(lambda: to_other(t, chip).start())
        to_core(t, turn).wait_send()

    def stage_beyond(t):
        chip = place.far_first(shortcut) * 2 + b
        to_beyond(t).wait_recv()
        add(t, chip, pl.ds(0, rows), from_beyond[t])
        to_other(t, chip).start()

    def stage_other(t, nth):
        if nth == shortcut:
            return
        at = place.far_first(nth)
        chip = at * 2 + 1 - b
        to_other(t, chip).wait_recv()
        add(t, chip, mine, from_other[t, chip])
        to_across(t, at).start()

    def stage_line(t, nth):
        at = place.far_first(nth)
        chip = at * 2 + b
        to_other(t, chip).wait_recv()
        if nth == shortcut:
            add(t, chip, mine, from_other[t, chip])
        else:
            to_across(t, at).wait_recv()
            add(t, chip, mine, from_other[t, chip].astype(F32) + from_across[t, at].astype(F32))

        def down():
            @pl.when(a < line - 1)
            def _():
                to_down(t, at, False).wait_recv()
                add(t, chip, mine, from_line[t, at])

            pl.when(at == a - 1)(lambda: to_down(t, at, True).start())
            pl.when(at < a - 1)(lambda: to_down(t, at, False).start())

        def up():
            @pl.when(a > 0)
            def _():
                to_up(t, at).wait_recv()
                add(t, chip, mine, from_line[t, at])

            to_up(t, at).start()

        if nth < line - 1:
            pl.when(at < a)(down)
            pl.when(at > a)(up)
            return

        @pl.when(a < line - 1)
        def _():
            to_down(t, at, True).wait_recv()
            add(t, chip, mine, from_line[t, line])

        @pl.when(a > 0)
        def _():
            to_up(t, at).wait_recv()
            add(t, chip, mine, from_line[t, at])

        done[t, mine, :] = own[t, chip, mine, :]
        final(t, mine).start()

    def norm_copy(step):
        kind = (CORE, OTHER, ACROSS)[step]
        return remote(
            nsend.at[step], nfrom.at[step], nsend_sem.at[step], nreceive.at[step], place.device[kind]
        )

    def norm_line(other, came):
        return remote(
            nsend.at[3], nline.at[other if came else a], lsend.at[other],
            lreceive.at[other if came else a], (place.index(other, b, c), y),
        )

    product(0, 0)

    def first_sum(turn, carry):
        product(0, turn)
        stage_core(0, turn - 1)
        return carry

    lax.fori_loop(1, chips, first_sum, 0)
    stage_core(0, chips - 1)

    late[0].wait()

    def feed_back(at, carry):
        slot = g_rows.step(at)
        here = at_rows(at * block, block)
        upward = upward_ref[here, :]
        tanh = gelu_parts(upward)
        slope = 0.5 * (1.0 + tanh) + 0.5 * upward * (1.0 - tanh * tanh) * (
            math.sqrt(2.0 / math.pi) * (1.0 + 3 * 0.044715 * upward * upward)
        )
        gup_s[here, :] = (mm(buf[slot], wdown_ref[...]) * slope).astype(BF)
        return carry

    lax.fori_loop(0, blocks // 2, feed_back, 0)
    stage_other(0, 0)
    lax.fori_loop(blocks // 2, blocks, feed_back, 0)
    if shortcut >= 0:
        stage_beyond(0)
    x_rows.prime()

    def turn_over(pieces):
        def one(at, carry):
            here = at_rows(at * 256, 256)
            for n, source in pieces:
                turned_s[n, :, here] = source[here, :].T
            return carry

        lax.fori_loop(0, tokens // 256, one, 0)

    turn_over(((1, gup_s), (2, att_ref), (3, act_ref)))
    ones = jnp.ones((8, tokens), BF)

    def gradients(chip, carry):
        slot = normed_columns.step(chip)
        g_columns.step(chip)
        here = at_rows(chip * pair, pair)
        by_normed, by_grad = cols[0, slot], cols[1, slot]
        dsend[0, here, :] = mm(turned_s[2], by_grad).T.astype(BF)
        dsend[1, here, :] = mm(turned_s[1], by_normed).T.astype(BF)
        dsend[2, here, :] = mm(turned_s[3], by_grad).T.astype(BF)
        total_ref[:, here] = mm(ones, by_grad)
        return carry

    lax.fori_loop(0, chips // 2, gradients, 0)
    stage_other(0, 1)
    lax.fori_loop(chips // 2, chips, gradients, 0)
    weights.keep((1, 2))
    weights.start((1, 2))
    normed_columns.prime()
    for operand in late[1:]:
        operand.wait()
    others_left = list(range(2, line))

    quarter = tokens // inverse_ref.shape[0]
    quarters = block // quarter
    wide = 2 * block
    scale = 1.0 / math.sqrt(HEAD)

    def prepare(at, carry):
        here = at_rows(at * block, block)
        key = qkvs_ref[here, :][:, : 2 * HEAD].astype(F32)
        kt_s[:, here] = key.T[HEAD:].astype(BF)
        dkv_s[here, :] = jnp.zeros((block, 2 * HEAD), F32)
        return carry

    lax.fori_loop(0, blocks, prepare, 0)

    def backward(at, carry):
        here = at_rows(at * block, block)
        query = qkvs_ref[here, :][:, :HEAD]
        grad = jnp.concatenate(
            [gatt_ref[inverse_ref[at * quarters + n]] for n in range(quarters)], axis=0
        )
        left = lax.broadcasted_iota(jnp.int32, (block, 2 * HEAD), 1) < HEAD
        grad_wide = grad[:, 2 * HEAD :].astype(F32)
        grad_right = jnp.where(left, 0.0, grad_wide).astype(BF)
        query_left = jnp.concatenate([query, jnp.zeros_like(query)], axis=1)
        grad = grad[:, 3 * HEAD :]
        delta = jnp.sum(grad_wide.T[HEAD:] * attt_ref[:, here], axis=0, keepdims=True)
        lse = lse_ref[0:1, here]

        def back(place_at, query_grad, masked):
            there = at_rows(place_at * wide, wide)
            keyvalue = qkvs_ref[there, :]
            scores = mm(keyvalue[:, HEAD : 2 * HEAD], query, NT)
            if masked:
                scores = jnp.where(seen(place_at * wide, at * block, wide, block), scores, NEG)
            prob = jnp.exp(scores - lse)
            dprob = mm(keyvalue[:, 2 * HEAD : 3 * HEAD], grad, NT)
            dscore = (prob * (dprob - delta)).astype(BF)
            dkv_s[there, :] += mm(dscore, query_left) + mm(prob.astype(BF), grad_right)
            return query_grad + mm(kt_s[:, there], dscore)

        last = at // 2
        query_grad = lax.fori_loop(
            0, last, lambda n, total: back(n, total, False), jnp.zeros((HEAD, block), F32)
        )
        query_grad = back(last, query_grad, True)
        query_grad = jnp.concatenate([query_grad, query_grad], axis=0).T[:, :HEAD]
        query_grad = turned(
            query_grad * scale, angle_ref[here, : ROT // 2], -angle_ref[here, ROT // 2 :]
        ).astype(BF)
        gm_s[pl.ds(at * quarters, quarters), :, pl.ds(0, HEAD)] = query_grad.reshape(
            quarters, quarter, HEAD
        )
        return carry

    lax.fori_loop(0, blocks // 2, backward, 0)
    for nth in others_left[:-1]:
        stage_other(0, nth)
    lax.fori_loop(blocks // 2, blocks, backward, 0)
    stage_other(0, line - 1)

    def finish_keys(at, carry):
        here = at_rows(at * block, block)
        keyvalue = jnp.concatenate(
            [
                turned(
                    dkv_s[here, :][:, :HEAD], angle_ref[here, : ROT // 2], -angle_ref[here, ROT // 2 :]
                ).astype(BF),
                dkv_s[here, :][:, HEAD:].astype(BF),
            ],
            axis=1,
        )
        gm_s[pl.ds(at * quarters, quarters), :, pl.ds(HEAD, 2 * HEAD)] = keyvalue.reshape(
            quarters, quarter, 2 * HEAD
        )
        return carry

    lax.fori_loop(0, blocks, finish_keys, 0)

    def unplace(at, carry):
        gmix_s[at_rows(at * quarter, quarter), :] = jnp.concatenate(
            [gm_s[order_ref[at]], jnp.zeros((quarter, HEAD), BF)], axis=1
        )
        return carry

    lax.fori_loop(0, tokens // quarter, unplace, 0)
    turn_over(((0, gmix_s),))
    for n, source in enumerate((gmix_s, gup_s)):
        columns = source.shape[1]

        def tally(at, total, source=source, columns=columns):
            return total + jnp.sum(
                source[at_rows(at * 256, 256), :].astype(F32).reshape(32, 8, columns), axis=0
            )

        total = lax.fori_loop(0, tokens // 256, tally, jnp.zeros((8, columns), F32))
        total = jnp.sum(total, axis=0, keepdims=True)
        for at in range(columns // 128):
            bias_s[pl.ds(n * 2 + at, 1), :] = total[:, at * 128 : (at + 1) * 128]
    bias_s[pl.ds(4, 4), :] = jnp.zeros((4, 128), F32)

    gain_s[...] = jnp.zeros_like(gain_s)
    shift_s[...] = jnp.zeros_like(shift_s)

    def gradients_att(chip):
        slot = normed_columns.step(chip)
        here = at_rows(chip * pair, pair)
        more = mm(turned_s[0], cols[0, slot]).T
        dsend[0, here, :] = (dsend[0, here, :].astype(F32) + more).astype(BF)

    product(1, 0)

    def second_sum(turn, carry):
        product(1, turn)
        stage_core(1, turn - 1)
        gradients_att(turn - 1)
        return carry

    lax.fori_loop(1, chips, second_sum, 0)
    stage_core(1, chips - 1)
    gradients_att(chips - 1)
    for n, source in enumerate((gain_s, shift_s)):
        total = jnp.sum(source[...], axis=0, keepdims=True)
        span = features // 4
        for at in range(4):
            nsend[0, pl.ds(n * 4 + at, 1), :] = total[:, at * span : (at + 1) * span]
    norm_copy(0).start()
    if shortcut >= 0:
        stage_beyond(1)
    weights.keep((0, 3))
    share = -(-2 * chips // line)
    for nth in range(line):
        if nth < line - 1:
            stage_other(1, nth)
        stage_line(0, nth)
        weights.start((0, 3), lambda at, mask, nth=nth: at // share == nth)
    norm_copy(0).wait_recv()
    nsend[1] = nsend[0] + nfrom[0]
    norm_copy(1).start()
    stage_line(1, 0)
    norm_copy(1).wait_recv()
    nsend[2] = nsend[1] + nfrom[1]
    norm_copy(2).start()
    stage_line(1, 1)
    norm_copy(2).wait_recv()
    nsend[3] = nsend[2] + nfrom[2]
    nline[a] = nsend[3]
    for other in range(line):
        pl.when(a != other)(lambda other=other: norm_line(other, False).start())
    stage_other(1, line - 1)
    for nth in range(2, line):
        stage_line(1, nth)
    for other in range(line):
        pl.when(a != other)(lambda other=other: norm_line(other, True).wait_recv())
    total = nline[0]
    for other in range(1, line):
        total += nline[other]
    norms_ref[...] = total

    for step in range(3):
        norm_copy(step).wait_send()
    for other in range(line):
        pl.when(a != other)(lambda other=other: norm_line(other, False).wait_send())
    for t in range(2):
        final(t, theirs).wait_recv()
        final(t, mine).wait_send()
        sums[t][...] = done[t]

        def left(at, carry, t=t):
            to_other(t, at * 2 + b).wait_send()
            pl.when(at != a)(lambda: to_up(t, at).wait_send())

            def also():
                to_other(t, at * 2 + 1 - b).wait_send()
                to_across(t, at).wait_send()

            if shortcut < 0:
                also()
            else:
                pl.when(at != place.far_first(shortcut))(also)
            return carry

        lax.fori_loop(0, line, left, 0)
        if shortcut >= 0:
            to_beyond(t).wait_send()
    weights.wait((0, 1, 2, 3))


def spread(
    order, inverse, attended, activated, upward, grad_att, qkvs, lse, attended_t, w_att, w_up, w_down,
    angles, normed, g_all, x_all,
):
    count = lax.axis_size("ctx")
    line = count // 4
    tokens, features = x_all.shape
    rows = tokens // count
    half = rows // 2
    chips = 2 * line
    weight_rows = w_att.shape[0] // count
    wide, hidden = w_att.shape[1], w_up.shape[1]
    hbm, vmem = pl.BlockSpec(memory_space=pl.ANY), pl.BlockSpec(memory_space=pltpu.VMEM)
    smem = pl.BlockSpec(memory_space=pltpu.SMEM)
    dma = pltpu.SemaphoreType.DMA
    own = jax.ShapeDtypeStruct((rows, features), BF)
    back = [
        jax.ShapeDtypeStruct((count, weight_rows, columns), BF) for columns in (wide, hidden, hidden)
    ]
    return pl.pallas_call(
        functools.partial(spread_kernel, line),
        out_shape=[own, own]
        + back
        + [
            jax.ShapeDtypeStruct((count, 8, 128), F32),
            jax.ShapeDtypeStruct((8, features // 4), F32),
            jax.ShapeDtypeStruct((8, features), F32),
        ],
        in_specs=[smem, smem] + [vmem] * 6 + [hbm] * 8,
        out_specs=[vmem, vmem, hbm, hbm, hbm, hbm, vmem, vmem],
        scratch_shapes=[
            pltpu.VMEM(upward.shape, F32),
            pltpu.VMEM(grad_att.shape, BF),
            pltpu.VMEM(qkvs.shape, BF),
            pltpu.VMEM(attended_t.shape, F32),
            pltpu.VMEM(w_up.shape, BF),
            pltpu.VMEM((2, 2 * rows, features), BF),
            pltpu.VMEM((2, chips, rows, features), BF),
            pltpu.VMEM((4, rows, features), BF),
            pltpu.VMEM((2, chips, half, features), BF),
            pltpu.VMEM((2, line, half, features), BF),
            pltpu.VMEM((2, rows, features), BF),
            pltpu.VMEM((2, line + 1, half, features), BF),
            pltpu.VMEM((2, rows, features), BF),
            pltpu.VMEM((4, wide, tokens), BF),
            pltpu.VMEM((3, count * weight_rows, wide), BF),
            pltpu.VMEM((2, 3, tokens, 2 * weight_rows), BF),
            pltpu.VMEM((3, 2 * rows, features), BF),
            pltpu.VMEM((8, features), F32),
            pltpu.VMEM((8, features), F32),
            pltpu.VMEM((4, 8, features // 4), F32),
            pltpu.VMEM((3, 8, features // 4), F32),
            pltpu.VMEM((line, 8, features // 4), F32),
            pltpu.VMEM((8, 128), F32),
            pltpu.VMEM((tokens, wide), BF),
            pltpu.VMEM((tokens, hidden), BF),
            pltpu.VMEM((HEAD, tokens), BF),
            pltpu.VMEM((tokens, 2 * HEAD), F32),
            pltpu.VMEM((order.shape[0], tokens // order.shape[0], 3 * HEAD), BF),
            dma((5,)),
            dma((2, 3)),
            dma((3,)),
            dma((2, chips)),
            dma((4,)),
            pltpu.SemaphoreType.REGULAR,
            dma((2, chips)),
            dma((2, chips)),
            dma((2, line)),
            dma((2, line)),
            dma((2,)),
            dma((2,)),
            dma((2, line)),
            dma((2, line + 1)),
            dma((2,)),
            dma((2,)),
            dma((4, count)),
            dma((4, count)),
            dma((4,)),
            dma((3,)),
            dma((3,)),
            dma((line,)),
            dma((line,)),
        ],
        compiler_params=pltpu.CompilerParams(
            collective_id=2, has_side_effects=True, vmem_limit_bytes=63 * 1024 * 1024
        ),
    )(
        order, inverse, attended, activated, w_att, w_down, lse, angles, upward, grad_att, qkvs,
        attended_t, w_up, normed, g_all, x_all,
    )


def finish_kernel(
    tok_ref, cot_ref, gain_ref, bias_ref, branch_ref, normed_ref, datt_ref, dup_ref, ddown_ref,
    sums_ref, norms_ref, total_ref,
    out_ref, grad_ref, qkv_ref, wout_ref, up_ref, down_ref, qkvb_ref, upb_ref, gsum_ref, ssum_ref,
    bsum_ref,
):
    inputs = tok_ref[...].astype(F32)
    center = inputs - jnp.mean(inputs, axis=-1, keepdims=True)
    inv_std = lax.rsqrt(jnp.mean(center * center, axis=-1, keepdims=True) + EPS)
    unit = center * inv_std
    out_ref[...] = inputs + branch_ref[...].astype(F32) + bias_ref[...]
    grad_unit = normed_ref[...].astype(F32) * gain_ref[...]
    grad_ref[...] = cot_ref[...].astype(F32) + inv_std * (
        grad_unit
        - jnp.mean(grad_unit, axis=-1, keepdims=True)
        - unit * jnp.mean(grad_unit * unit, axis=-1, keepdims=True)
    )
    count, _, packed = datt_ref.shape
    width, hidden = packed // 4, dup_ref.shape[2]
    pieces = [datt_ref[owner].astype(F32) for owner in range(count)]

    def together(kind):
        return jnp.concatenate(
            [piece[:, kind * width : (kind + 1) * width] for piece in pieces], axis=1
        )

    for kind in range(3):
        qkv_ref[kind, :, :] = together(kind)
        at = kind * width
        qkvb_ref[kind : kind + 1, :] = jnp.concatenate(
            [
                sums_ref[owner, at // 128 : at // 128 + 1, at % 128 : at % 128 + width]
                for owner in range(count)
            ],
            axis=1,
        )
    wout_ref[...] = together(3)
    for owner in range(count):
        columns = pl.ds(owner * hidden, hidden)
        up_ref[:, columns] = dup_ref[owner].astype(F32)
        down_ref[:, columns] = ddown_ref[owner].astype(F32)
        for at in range(hidden // 128):
            upb_ref[:, pl.ds(owner * hidden + at * 128, 128)] = sums_ref[owner, 2 + at : 3 + at, :]
    wide = norms_ref.shape[1]
    for at in range(4):
        gsum_ref[:, pl.ds(at * wide, wide)] = norms_ref[at : at + 1, :]
        ssum_ref[:, pl.ds(at * wide, wide)] = norms_ref[4 + at : 5 + at, :]
    bsum_ref[...] = total_ref[0:1, :]


def finish(tokens, cotangent, gain, bias, branches, own_normed, d_att, d_up, d_down, sums, norms, total):
    count, weight_rows, packed = d_att.shape
    rows, features = tokens.shape
    width, hidden = packed // 4, d_up.shape[2]
    owners = max(128 // width, count * 16 // rows)
    steps = count // owners
    by_rows = pl.BlockSpec((rows // steps, features), lambda at: (at, 0))
    line = pl.BlockSpec((1, features), lambda at: (0, 0))

    def whole(array):
        return pl.BlockSpec(array.shape, lambda at: (0,) * array.ndim)

    def by_owner(array):
        return pl.BlockSpec((owners, *array.shape[1:]), lambda at: (at, 0, 0))

    def by_columns(*lead):
        return lambda columns: pl.BlockSpec(
            (*lead, owners * columns), lambda at: (*(0,) * len(lead), at)
        )

    shape = jax.ShapeDtypeStruct
    return pl.pallas_call(
        finish_kernel,
        grid=(steps,),
        out_shape=[
            shape(tokens.shape, F32),
            shape(tokens.shape, F32),
            shape((3, weight_rows, count * width), F32),
            shape((weight_rows, count * width), F32),
            shape((weight_rows, count * hidden), F32),
            shape((weight_rows, count * hidden), F32),
            shape((3, count * width), F32),
            shape((1, count * hidden), F32),
            shape((1, features), F32),
            shape((1, features), F32),
            shape((1, features), F32),
        ],
        in_specs=[by_rows, by_rows, line, line, by_rows, by_rows]
        + [by_owner(array) for array in (d_att, d_up, d_down, sums)]
        + [whole(norms), whole(total)],
        out_specs=[
            by_rows,
            by_rows,
            by_columns(3, weight_rows)(width),
            by_columns(weight_rows)(width),
            by_columns(weight_rows)(hidden),
            by_columns(weight_rows)(hidden),
            by_columns(3)(width),
            by_columns(1)(hidden),
            line,
            line,
            line,
        ],
        compiler_params=pltpu.CompilerParams(vmem_limit_bytes=63 * 1024 * 1024),
    )(
        tokens, cotangent, gain[None], bias[None], branches, own_normed, d_att, d_up, d_down, sums,
        norms, total,
    )


def gelu_tanh(value):
    return jax.nn.gelu(value, approximate=True)


def local(
    tokens, block_order, ln_gain, ln_bias, qkv_weight, qkv_bias, out_weight, fc1_weight, fc1_bias,
    fc2_weight, out_bias, cotangent,
):
    devices = lax.axis_size("ctx")
    myself = lax.axis_index("ctx")
    heads_here = qkv_weight.shape[2] // HEAD
    columns = math.gcd(devices, heads_here)
    mine = myself % columns
    width = qkv_weight.shape[2] // columns
    hidden = fc1_weight.shape[1] // columns
    bias_att = lax.dynamic_slice_in_dim(qkv_bias, mine * width, width, 1).reshape(-1)
    bias_att = jnp.concatenate([bias_att, jnp.zeros((width,), F32)])[None]
    bias_up = lax.dynamic_slice_in_dim(fc1_bias, mine * hidden, hidden, 0)[None]
    if devices == columns and columns % 8 == 0 and width == HEAD and lax.axis_size("tp") == 2:
        halves = block_order.shape[0]
        counted = jnp.arange(halves, dtype=jnp.int32)
        inverse = jnp.sum(
            jnp.where(block_order[None, :] == counted[:, None], counted[None, :], 0), axis=1
        )
        angles = tables(jnp.arange(devices * tokens.shape[0], dtype=jnp.int32), ROT)
        angles = jnp.concatenate(angles, axis=1)
        (
            x_all, g_all, w_att, w_up, w_down, normed, qkvs, lse, attended_t, attended, activated,
            upward, grad_att,
        ) = collect(
            block_order, inverse, tokens, cotangent, qkv_weight, out_weight, fc1_weight, fc2_weight,
            ln_gain[None], ln_bias[None], bias_att, bias_up, angles,
        )
        parts = spread(
            block_order, inverse, attended, activated, upward, grad_att, qkvs, lse, attended_t, w_att,
            w_up, w_down, angles, normed, g_all, x_all,
        )
    else:
        parts = by_groups(
            tokens, block_order, ln_gain, ln_bias, qkv_weight, out_weight, fc1_weight, fc2_weight,
            cotangent, bias_att, bias_up,
        )
    (
        output, input_grad, qkv_grad, out_grad, fc1_grad, fc2_grad, qkv_sums, fc1_sums, gain_sum,
        shift_sum, g_sum,
    ) = finish(tokens, cotangent, ln_gain, out_bias, *parts)
    return (
        output, input_grad, gain_sum[0], shift_sum[0], qkv_grad.transpose(1, 0, 2), qkv_sums, out_grad,
        fc1_grad, fc1_sums[0], fc2_grad, g_sum[0],
    )


def by_groups(
    tokens, block_order, ln_gain, ln_bias, qkv_weight, out_weight, fc1_weight, fc2_weight, cotangent,
    bias_att, bias_up,
):
    devices = lax.axis_size("ctx")
    myself = lax.axis_index("ctx")
    rows_here = tokens.shape[0]
    weight_rows = qkv_weight.shape[0]
    half = devices * rows_here // block_order.shape[0]
    columns = math.gcd(devices, qkv_weight.shape[2] // HEAD)
    groups = devices // columns
    width, hidden = qkv_weight.shape[2] // columns, fc1_weight.shape[1] // columns
    count = columns * rows_here
    side = [[r * columns + c for c in range(columns)] for r in range(groups)]
    across = [[r * columns + c for r in range(groups)] for c in range(columns)]

    def gathered(value, among):
        return lax.all_gather(value, "ctx", axis=0, tiled=True, axis_index_groups=among)

    def scattered(value, among):
        return lax.psum_scatter(
            value, "ctx", scatter_dimension=0, tiled=True, axis_index_groups=among
        )

    def exchanged(value):
        return lax.all_to_all(value, "ctx", split_axis=0, concat_axis=0, tiled=True)

    x_all, g_all = gathered(tokens, side), gathered(cotangent, side)
    kinds = jnp.concatenate([qkv_weight, out_weight[:, None]], axis=1)
    kinds = kinds.reshape(weight_rows, 4, columns, width).transpose(2, 0, 1, 3)
    packed = jnp.concatenate(
        [
            kinds.reshape(columns, weight_rows, 4 * width),
            fc1_weight.reshape(weight_rows, columns, hidden).transpose(1, 0, 2),
            fc2_weight.reshape(weight_rows, columns, hidden).transpose(1, 0, 2),
        ],
        axis=2,
    )
    packed = exchanged(jnp.tile(packed, (groups, 1, 1))).reshape(devices * weight_rows, -1)
    w_att, w_up, w_down = jnp.split(packed, [4 * width, 4 * width + hidden], axis=1)

    inputs = x_all.astype(F32)
    center = inputs - jnp.mean(inputs, axis=-1, keepdims=True)
    inv_std = lax.rsqrt(jnp.mean(center * center, axis=-1, keepdims=True) + EPS)
    unit = center * inv_std
    normed = (unit * ln_gain + ln_bias).astype(BF)
    upward = mm(normed, w_up) + bias_up
    activated, gelu_back = jax.vjp(gelu_tanh, upward)
    activated = activated.astype(BF)
    grad_up = gelu_back(mm(g_all, w_down))[0].astype(BF)
    places = (block_order[:, None] * half + jnp.arange(half, dtype=jnp.int32)[None, :]).reshape(-1)
    attended, grad_mixed = attention_blocks(
        lax.dynamic_slice_in_dim(places, (myself // columns) * count, count),
        places,
        mm(normed, w_att) + bias_att,
        mm(g_all, w_att),
        lambda value: gathered(value, across),
        lambda value: scattered(value, across),
    )
    out_part = (mm(attended, w_att, NT) + mm(activated, w_down, NT)).astype(BF)
    normed_wide = mm(grad_mixed, w_att, NT) + mm(grad_up, w_up, NT)
    branches, own_normed = lax.psum(
        (scattered(out_part, side), scattered(normed_wide.astype(BF), side)), "tp"
    )
    back = jnp.concatenate(
        [
            (mm(normed, grad_mixed, TN) + mm(g_all, attended, TN)).astype(BF),
            mm(normed, grad_up, TN).astype(BF),
            mm(g_all, activated, TN).astype(BF),
        ],
        axis=1,
    )
    back = exchanged(back.reshape(devices, weight_rows, -1))
    back = jnp.sum(back.reshape(groups, columns, weight_rows, -1).astype(F32), axis=0)
    sums = jnp.concatenate(
        [jnp.sum(grad_mixed.astype(F32), axis=0), jnp.sum(grad_up.astype(F32), axis=0)]
    ).reshape(-1, 128)
    sums = jnp.pad(sums, ((0, 8 - sums.shape[0]), (0, 0)))
    sums = gathered(lax.psum(sums, "ctx", axis_index_groups=across)[None], side)
    norms = jnp.stack([jnp.sum(unit * normed_wide, axis=0), jnp.sum(normed_wide, axis=0)])
    norms = lax.psum(norms, ("ctx", "tp")).reshape(8, -1)
    total = lax.psum(jnp.sum(g_all.astype(F32), axis=0), "ctx", axis_index_groups=across)[None]
    return (
        branches, own_normed, *jnp.split(back, [4 * width, 4 * width + hidden], axis=2), sums, norms,
        total,
    )


def solution(mesh):
    rows, tall = P("ctx", None), P("ctx", "tp")
    kinds, bias = P("ctx", None, "tp"), P(None, "tp")
    return jax.shard_map(
        local,
        mesh=mesh,
        in_specs=(rows, P(), P(), P(), kinds, bias, tall, tall, P("tp"), tall, P(), rows),
        out_specs=(rows, rows, P(), P(), kinds, bias, tall, tall, P("tp"), tall, P()),
        check_vma=False,
    )
```

```python
import functools
import math

import jax
import jax.numpy as jnp
import numpy as np
from jax import lax
from jax.experimental import pallas as pl
from jax.experimental.pallas import tpu as pltpu
from jax.sharding import PartitionSpec as P

HEAD = 64
ROT = 32
EPS = 1e-05
NEG = -1e30
BF = jnp.bfloat16
F32 = jnp.float32
NN = (((1,), (0,)), ((), ()))
NT = (((1,), (1,)), ((), ()))
TN = (((0,), (0,)), ((), ()))


def mm(left, right, dims=NN):
    return lax.dot_general(left, right, dims, preferred_element_type=F32)


def tables(positions, width):
    freqs = 10000.0 ** (-(jnp.arange(width // 2, dtype=F32) * 2.0) / width)
    angles = positions.astype(F32)[:, None] * freqs[None, :]
    return (jnp.cos(angles), jnp.sin(angles))


def turned(value, cosine, sine):
    half = cosine.shape[-1]
    first, second = value[..., :half], value[..., half : 2 * half]
    return jnp.concatenate(
        [first * cosine - second * sine, second * cosine + first * sine, value[..., 2 * half :]],
        axis=-1,
    )


def attention_blocks(own_place, places, mixed, grad_att, gather, scatter):
    count, width = grad_att.shape[0], grad_att.shape[1] // 4
    heads = width // HEAD
    scale = 1.0 / math.sqrt(HEAD)
    grad_att = grad_att[:, 3 * width :].astype(BF)
    cosine, sine = tables(own_place, ROT)
    cosine, sine = cosine[:, None, :], sine[:, None, :]
    kinds = [mixed[:, kind * width : (kind + 1) * width].reshape(count, heads, HEAD) for kind in range(3)]
    queries = turned(kinds[0], cosine, sine).astype(BF)
    keys = gather(turned(kinds[1], cosine, sine).astype(BF))
    values = gather(kinds[2].astype(BF))
    grad_att = grad_att.reshape(count, heads, HEAD)
    block = math.gcd(128, count)

    def one(at, carry):
        key_grad, value_grad, attended, query_grad = carry
        query = lax.dynamic_slice_in_dim(queries, at * block, block)
        grad = lax.dynamic_slice_in_dim(grad_att, at * block, block)
        place = lax.dynamic_slice_in_dim(own_place, at * block, block)
        visible = (place[:, None] >= places[None, :])[None]
        scores = jnp.einsum("qhe,khe->hqk", query, keys, preferred_element_type=F32) * scale
        scores = jnp.where(visible, scores, NEG)
        top = jnp.max(scores, axis=-1, keepdims=True)
        expo = jnp.where(visible, jnp.exp(scores - top), 0.0)
        total = jnp.sum(expo, axis=-1)
        summed = jnp.einsum("hqk,khe->qhe", expo.astype(BF), values, preferred_element_type=F32)
        attend = summed / jnp.transpose(total)[..., None]
        delta = jnp.transpose(jnp.sum(grad.astype(F32) * attend, axis=-1))
        prob = expo / total[..., None]
        dprob = jnp.einsum("qhe,khe->hqk", grad, values, preferred_element_type=F32)
        dscore = (prob * (dprob - delta[..., None])).astype(BF)
        part_q = jnp.einsum("hqk,khe->qhe", dscore, keys, preferred_element_type=F32) * scale
        key_grad += jnp.einsum("hqk,qhe->khe", dscore, query, preferred_element_type=F32) * scale
        value_grad += jnp.einsum("hqk,qhe->khe", prob.astype(BF), grad, preferred_element_type=F32)
        attended = lax.dynamic_update_slice_in_dim(attended, attend.astype(BF), at * block, 0)
        query_grad = lax.dynamic_update_slice_in_dim(query_grad, part_q, at * block, 0)
        return (key_grad, value_grad, attended, query_grad)

    zeros = jnp.zeros(keys.shape, F32)
    own = jnp.zeros((count, heads, HEAD), F32)
    key_grad, value_grad, attended, query_grad = lax.fori_loop(
        0, count // block, one, (zeros, zeros, own.astype(BF), own)
    )
    key_grad, value_grad = scatter(key_grad), scatter(value_grad)
    grad_mixed = jnp.concatenate(
        [
            turned(query_grad, cosine, -sine).astype(BF).reshape(count, width),
            turned(key_grad, cosine, -sine).astype(BF).reshape(count, width),
            value_grad.astype(BF).reshape(count, width),
            jnp.zeros((count, width), BF),
        ],
        axis=1,
    )
    attended = jnp.concatenate(
        [jnp.zeros((count, 3 * width), BF), attended.reshape(count, width)], axis=1
    )
    return attended, grad_mixed


MESH = pl.DeviceIdType.MESH
UP, DOWN, ACROSS, OTHER, CORE = range(5)


def at_rows(start, size):
    return pl.ds(pl.multiple_of(start, size), size)


def remote(source, target, send, receive, device):
    return pltpu.make_async_remote_copy(
        src_ref=source, dst_ref=target, send_sem=send, recv_sem=receive, device_id=device,
        device_id_type=MESH,
    )


class Place:
    def __init__(self, line):
        self.line = line
        self.me = lax.axis_index("ctx")
        self.y = lax.axis_index("tp")
        self.a, self.b, self.c = self.me // 4, (self.me // 2) % 2, self.me % 2
        a, b, c, y = self.a, self.b, self.c, self.y
        self.device = {
            UP: (self.index(jnp.minimum(a + 1, line - 1), b, c), y),
            DOWN: (self.index(jnp.maximum(a - 1, 0), b, c), y),
            ACROSS: (self.index(a, 1 - b, c), y),
            OTHER: (self.me, 1 - y),
            CORE: (self.index(a, b, 1 - c), y),
        }

    def index(self, a, b, c):
        return a * 4 + b * 2 + c

    def far_first(self, turn):
        line = self.line
        high, low = line - 1 - turn, turn
        high = jnp.where(high <= self.a, high - 1, high)
        low = jnp.where(low >= self.a, low + 1, low)
        other = jnp.where(self.a < line // 2, high, low)
        return jnp.where(turn == line - 1, self.a, other)

    def greet(self):
        barrier = pltpu.get_barrier_semaphore()
        count = 4 * self.line

        def signal(step, carry):
            pl.semaphore_signal(
                barrier, inc=1, device_id=(lax.rem(self.me + step, count), self.y), device_id_type=MESH
            )
            return carry

        lax.fori_loop(1, count, signal, 0)
        pl.semaphore_signal(barrier, inc=1, device_id=self.device[OTHER], device_id_type=MESH)
        pl.semaphore_wait(barrier, count)


def flipped(value, mask, bits):
    result = 0
    for bit in range(bits):
        part = (value // 2**bit) % 2
        result = result + 2**bit * (1 - part if mask >> bit & 1 else part)
    return result


class Exchange:
    def __init__(self, place, chunk, received, send, receive, own):
        self.place, self.chunk, self.received = place, chunk, received
        self.send, self.receive, self.own = send, receive, own
        self.count = 4 * place.line
        bits = self.count.bit_length() - 1
        self.partners = [
            (mask, flipped(place.me, mask, bits)) for mask in range(self.count - 1, 0, -1)
        ]

    def copy(self, partner, n, came):
        mask, to = partner
        return remote(
            self.chunk(n, to), self.received(n, to if came else self.place.me), self.send.at[n, mask],
            self.receive.at[n, mask], (to, self.place.y),
        )

    def kept(self, n):
        me = self.place.me
        return pltpu.make_async_copy(self.chunk(n, me), self.received(n, me), self.own.at[n])

    def keep(self, pieces):
        for n in pieces:
            self.kept(n).start()

    def start(self, pieces):
        for partner in self.partners:
            for n in pieces:
                self.copy(partner, n, False).start()

    def wait(self, pieces):
        for partner in self.partners:
            for n in pieces:
                self.copy(partner, n, True).wait()
        for n in pieces:
            self.kept(n).wait()


def row_stats(load, rows, features, piece):
    mean = jnp.zeros((rows, 1), F32)
    for at in range(0, features, piece):
        mean += jnp.sum(load(at), axis=1, keepdims=True)
    mean = mean / features
    spread = jnp.zeros((rows, 1), F32)
    for at in range(0, features, piece):
        center = load(at) - mean
        spread += jnp.sum(center * center, axis=1, keepdims=True)
    return mean, lax.rsqrt(spread / features + EPS)


class Stream:
    def __init__(self, copy, depth, total):
        self.copy, self.depth, self.total = copy, depth, total

    def prime(self):
        for at in range(min(self.depth - 1, self.total)):
            self.copy(at, at).start()

    def step(self, at):
        slot = lax.rem(at, self.depth)
        self.copy(at, slot).wait()
        later = at + self.depth - 1

        @pl.when(later < self.total)
        def _():
            self.copy(later, lax.rem(later, self.depth)).start()

        return slot


def gelu_parts(value):
    inner = math.sqrt(2.0 / math.pi) * (value + 0.044715 * value * value * value)
    return jnp.tanh(inner)


def seen(start_key, start_query, keys, queries):
    key = start_key + lax.broadcasted_iota(jnp.int32, (keys, queries), 0)
    return key <= start_query + lax.broadcasted_iota(jnp.int32, (keys, queries), 1)


def collect_kernel(
    line, order_ref, tok_ref, cot_ref, qkv_ref, out_ref, up_ref, down_ref, gain_ref,
    shift_ref, batt_ref, bup_ref, angle_ref,
    x_out, g_out, watt_out, wup_out, wdown_ref, normed_out, qkvs_out, lse_out, attt_out, att_out,
    act_out, upward_out, gatt_out, inverse_ref,
    x_ref, g_ref, watt_s, wup_s, normed_s, qkvs_ref, lse_ref, attt_ref, att_ref, act_ref, upward_ref,
    gatt_ref, packed, mixed_s, k_s, vt_s, st, att_s,
    send, receive, own_sem, wsend, wreceive, wlocal, out_sem,
):
    place = Place(line)
    a, b, c, y = place.a, place.b, place.c, place.y
    sources, targets = (tok_ref, cot_ref), (x_ref, g_ref)
    rows, features = tok_ref.shape
    half = rows // 2
    weight_rows = up_ref.shape[0]
    tokens = x_ref.shape[0]
    hidden = wup_s.shape[1]
    width = watt_s.shape[1] // 4
    block = 2 * rows
    blocks = tokens // block
    piece = 512
    place.greet()
    shipped = []

    def ship(source, target):
        shipped.append(pltpu.make_async_copy(source, target, out_sem.at[len(shipped)]))
        shipped[-1].start()

    def copy(t, kind, owner, part, own=False):
        target = targets[t].at[at_rows(owner * rows + part * half, half)]
        source = sources[t].at[at_rows(part * half, half)] if own else target
        return remote(
            source, target, send.at[t, kind, owner, part], receive.at[t, owner, part], place.device[kind]
        )

    def landed(t, owner, part):
        copy(t, CORE, owner, part).wait_recv()

    def along(t, distance):
        for sign in (0,) if distance == 0 else (1, -1):
            at = a + sign * distance

            def pass_on(sign=sign, at=at):
                owner = place.index(at, b, c)
                own = distance == 0
                if not own:
                    landed(t, owner, y)
                if sign <= 0:
                    pl.when(a < line - 1)(lambda: copy(t, UP, owner, y, own).start())
                if sign >= 0:
                    pl.when(a > 0)(lambda: copy(t, DOWN, owner, y, own).start())
                copy(t, ACROSS, owner, y, own).start()
                if not own:
                    copy(t, OTHER, owner, y).start()
                copy(t, CORE, owner, y, own).start()
                if own:
                    copy(t, CORE, owner, 1 - y, own).start()

            if distance == 0:
                pass_on()
            else:
                pl.when((at >= 0) & (at < line))(pass_on)

    def beside(t, distance):
        for sign in (0,) if distance == 0 else (1, -1):
            at = a + sign * distance

            def pass_on(at=at):
                owner = place.index(at, 1 - b, c)
                landed(t, owner, y)
                copy(t, OTHER, owner, y).start()
                copy(t, CORE, owner, y).start()

            pl.when((at >= 0) & (at < line))(pass_on)

    def from_other(t):
        for distance in range(line):
            for column in (b, 1 - b):
                for sign in (0,) if distance == 0 else (1, -1):
                    at = a + sign * distance

                    def pass_on(at=at, column=column):
                        owner = place.index(at, column, c)
                        landed(t, owner, 1 - y)
                        copy(t, CORE, owner, 1 - y).start()

                    if distance == 0 and column is b:
                        continue
                    pl.when((at >= 0) & (at < line))(pass_on)

    def own_copy(t):
        return pltpu.make_async_copy(
            sources[t], targets[t].at[at_rows(place.me * rows, rows)], own_sem.at[t]
        )

    def complete(t):
        def came(chip, carry):
            for part in range(2):
                landed(t, chip * 2 + (1 - c), part)
            return carry

        lax.fori_loop(0, 2 * line, came, 0)
        own_copy(t).wait()

    def chunk(n, to):
        if n == 0:
            return packed.at[to]
        return (up_ref, down_ref)[n - 1].at[:, at_rows(to * hidden, hidden)]

    def received(n, owner):
        return (watt_s, wup_s, wdown_ref)[n].at[at_rows(owner * weight_rows, weight_rows)]

    weights = Exchange(place, chunk, received, wsend, wreceive, wlocal)

    own_copy(0).start()
    own_copy(1).start()
    along(0, 0)
    for owner in range(4 * line):
        columns = pl.ds(owner * width, width)
        packed[owner, :, :] = jnp.concatenate(
            [qkv_ref[kind, :, columns] for kind in range(3)] + [out_ref[:, columns]], axis=1
        )
    weights.keep((0, 1, 2))
    ordered = [order_ref[at] for at in range(order_ref.shape[0])]

    def invert(wanted, carry):
        found = jnp.int32(0)
        for at, held in enumerate(ordered):
            found = jnp.where(held == wanted, at, found)
        inverse_ref[wanted] = found
        return carry

    for distance in range(1, line):
        along(0, distance)
        beside(0, distance - 1)
    beside(0, line - 1)
    along(1, 0)
    weights.start((0,))
    lax.fori_loop(0, len(ordered), invert, 0)
    for distance in range(1, line - 1):
        along(1, distance)
        beside(1, distance - 1)
    from_other(0)
    complete(0)
    weights.wait((0,))
    ship(x_ref, x_out)
    ship(watt_s, watt_out)

    quarter = tokens // inverse_ref.shape[0]
    quarters = block // quarter

    def project(at, carry):
        here = at_rows(at * block, block)

        def load(start):
            return x_ref[here, pl.ds(start, piece)].astype(F32)

        mean, inv_std = row_stats(load, block, features, piece)
        for start in range(0, features, piece):
            part = pl.ds(start, piece)
            unit = (load(start) - mean) * inv_std
            normed_s[here, part] = (unit * gain_ref[:, part] + shift_ref[:, part]).astype(BF)
        mixed = mm(normed_s[here, :], watt_s[...]) + batt_ref[...]
        mixed_s[pl.ds(at * quarters, quarters)] = mixed.reshape(quarters, quarter, 4 * width)
        return carry

    lax.fori_loop(0, blocks // 2, project, 0)
    along(1, line - 1)
    beside(1, line - 2)
    weights.start((1,))
    lax.fori_loop(blocks // 2, blocks, project, 0)
    ship(normed_s, normed_out)
    beside(1, line - 1)
    weights.start((2,))

    wide = 2 * block
    scale = 1.0 / math.sqrt(HEAD)

    def prepare(at, carry):
        here = at_rows(at * block, block)
        mixed = jnp.concatenate(
            [mixed_s[inverse_ref[at * quarters + n]] for n in range(quarters)], axis=0
        )
        cosine, sine = angle_ref[here, : ROT // 2], angle_ref[here, ROT // 2 :]
        query = turned(mixed[:, :HEAD], cosine, sine).astype(BF) * jnp.asarray(scale, BF)
        key = turned(mixed[:, HEAD : 2 * HEAD], cosine, sine)
        value = mixed[:, 2 * HEAD : 3 * HEAD]
        k_s[here, :] = key.astype(BF)
        vt_s[:, here] = jnp.concatenate([value, value], axis=1).T[:HEAD].astype(BF)
        qkvs_ref[here, :] = jnp.concatenate(
            [query, key.astype(BF), value.astype(BF), jnp.zeros_like(query)], axis=1
        )
        return carry

    lax.fori_loop(0, blocks, prepare, 0)

    def forward(at, carry):
        here = at_rows(at * block, block)
        query = qkvs_ref[here, :][:, :HEAD]

        def scored(place_at, top, masked):
            there = at_rows(place_at * wide, wide)
            scores = mm(k_s[there, :], query, NT)
            if masked:
                scores = jnp.where(seen(place_at * wide, at * block, wide, block), scores, NEG)
            st[there, :] = scores
            return jnp.maximum(top, jnp.max(scores.reshape(wide // 8, 8, block), axis=0))

        last = at // 2
        top = lax.fori_loop(
            0, last, lambda n, top: scored(n, top, False), jnp.full((8, block), NEG, F32)
        )
        top = jnp.max(scored(last, top, True), axis=0, keepdims=True)

        def weighed(place_at, state):
            total, summed = state
            there = at_rows(place_at * wide, wide)
            expo = jnp.exp(st[there, :] - top)
            total = total + jnp.sum(expo.reshape(wide // 8, 8, block), axis=0)
            return (total, summed + mm(vt_s[:, there], expo.astype(BF)))

        total, summed = lax.fori_loop(
            0, last + 1, weighed, (jnp.zeros((8, block), F32), jnp.zeros((HEAD, block), F32))
        )
        total = jnp.sum(total, axis=0, keepdims=True)
        attended = summed * (1.0 / total)
        lse_ref[:, here] = jnp.broadcast_to(top + jnp.log(total), (8, block))
        attt_ref[:, here] = attended
        both = jnp.concatenate([attended, attended], axis=0).T.astype(BF)
        att_s[pl.ds(at * quarters, quarters)] = both.reshape(quarters, quarter, 2 * HEAD)
        return carry

    lax.fori_loop(0, blocks, forward, 0)
    for source, target in ((qkvs_ref, qkvs_out), (lse_ref, lse_out), (attt_ref, attt_out)):
        ship(source, target)

    def unplace(at, carry):
        attended = att_s[order_ref[at]][:, HEAD:]
        att_ref[at_rows(at * quarter, quarter), :] = jnp.concatenate(
            [jnp.zeros((quarter, 3 * HEAD), BF), attended], axis=1
        )
        return carry

    lax.fori_loop(0, tokens // quarter, unplace, 0)
    ship(att_ref, att_out)
    from_other(1)
    complete(1)
    ship(g_ref, g_out)

    def grad_in(at, carry):
        grad = mm(g_ref[at_rows(at * block, block), :], watt_s[...]).astype(BF)
        gatt_ref[pl.ds(at * quarters, quarters)] = grad.reshape(quarters, quarter, 4 * width)
        return carry

    lax.fori_loop(0, blocks, grad_in, 0)
    ship(gatt_ref, gatt_out)
    weights.wait((1,))
    ship(wup_s, wup_out)

    def feed(at, carry):
        here = at_rows(at * block, block)
        upward = mm(normed_s[here, :], wup_s[...]) + bup_ref[...]
        upward_ref[here, :] = upward
        act_ref[here, :] = (0.5 * upward * (1.0 + gelu_parts(upward))).astype(BF)
        return carry

    lax.fori_loop(0, blocks, feed, 0)
    ship(upward_ref, upward_out)
    ship(act_ref, act_out)
    for t in range(2):

        def left(at, carry, t=t):
            owner, beyond = place.index(at, b, c), place.index(at, 1 - b, c)
            pl.when((at <= a) & (a < line - 1))(lambda: copy(t, UP, owner, y).wait_send())
            pl.when((at >= a) & (a > 0))(lambda: copy(t, DOWN, owner, y).wait_send())
            copy(t, ACROSS, owner, y).wait_send()
            pl.when(at != a)(lambda: copy(t, OTHER, owner, y).wait_send())
            copy(t, OTHER, beyond, y).wait_send()
            for part in range(2):
                copy(t, CORE, owner, part).wait_send()
                copy(t, CORE, beyond, part).wait_send()
            return carry

        lax.fori_loop(0, line, left, 0)
    weights.wait((2,))
    for result in shipped:
        result.wait()


def collect(
    order, tokens, cotangent, qkv_weight, out_weight, fc1_weight, fc2_weight, gain, shift, bias_att,
    bias_up, angles,
):
    rows, features = tokens.shape
    weight_rows = fc1_weight.shape[0]
    count = lax.axis_size("ctx")
    line, width, hidden = count // 4, qkv_weight.shape[2] // count, fc1_weight.shape[1] // count
    total, depth = count * rows, count * weight_rows
    halves = order.shape[0]
    hbm, vmem = pl.BlockSpec(memory_space=pl.ANY), pl.BlockSpec(memory_space=pltpu.VMEM)
    smem = pl.BlockSpec(memory_space=pltpu.SMEM)
    dma = pltpu.SemaphoreType.DMA
    shape = jax.ShapeDtypeStruct
    return pl.pallas_call(
        functools.partial(collect_kernel, line),
        out_shape=[
            shape((total, features), BF),
            shape((total, features), BF),
            shape((depth, 4 * width), BF),
            shape((depth, hidden), BF),
            shape((depth, hidden), BF),
            shape((total, features), BF),
            shape((total, 4 * width), BF),
            shape((8, total), F32),
            shape((width, total), F32),
            shape((total, 4 * width), BF),
            shape((total, hidden), BF),
            shape((total, hidden), F32),
            shape((halves, total // halves, 4 * width), BF),
            shape((halves,), jnp.int32),
        ],
        in_specs=[smem, hbm, hbm, vmem, vmem, hbm, hbm] + [vmem] * 5,
        out_specs=[hbm] * 13 + [smem],
        scratch_shapes=[
            pltpu.VMEM((total, features), BF),
            pltpu.VMEM((total, features), BF),
            pltpu.VMEM((depth, 4 * width), BF),
            pltpu.VMEM((depth, hidden), BF),
            pltpu.VMEM((total, features), BF),
            pltpu.VMEM((total, 4 * width), BF),
            pltpu.VMEM((8, total), F32),
            pltpu.VMEM((width, total), F32),
            pltpu.VMEM((total, 4 * width), BF),
            pltpu.VMEM((total, hidden), BF),
            pltpu.VMEM((total, hidden), F32),
            pltpu.VMEM((halves, total // halves, 4 * width), BF),
            pltpu.VMEM((count, weight_rows, 4 * width), BF),
            pltpu.VMEM((halves, total // halves, 4 * width), F32),
            pltpu.VMEM((total, width), BF),
            pltpu.VMEM((width, total), BF),
            pltpu.VMEM((total, 2 * rows), F32),
            pltpu.VMEM((halves, total // halves, 2 * width), BF),
            dma((2, 5, count, 2)),
            dma((2, count, 2)),
            dma((2,)),
            dma((3, count)),
            dma((3, count)),
            dma((3,)),
            dma((12,)),
        ],
        compiler_params=pltpu.CompilerParams(
            collective_id=1, has_side_effects=True, vmem_limit_bytes=60 * 1024 * 1024
        ),
    )(
        order, tokens, cotangent, qkv_weight.transpose(1, 0, 2), out_weight, fc1_weight,
        fc2_weight, gain, shift, bias_att, bias_up, angles,
    )


def spread_kernel(
    line, order_ref, inverse_ref, att_ref, act_ref, watt_ref, wdown_ref, lse_ref, angle_ref,
    upward_in, gatt_in, qkvs_in, attt_in, wup_in, normed_ref, g_ref, x_ref,
    sum_ref, gsum_ref, ratt_ref, rup_ref, rdown_ref, rbias_ref, norms_ref, total_ref,
    upward_ref, gatt_ref, qkvs_ref, attt_ref, wup_ref,
    fresh, own, from_core, from_other, from_across, from_beyond, from_line, done, turned_s, dsend, cols,
    buf, gain_s, shift_s, nsend, nfrom, nline, bias_s, gmix_s, gup_s, kt_s, dkv_s, gm_s,
    in_sem, cols_sem, buf_sem, csend, creceive, credit, ysend, yreceive, xsend, xreceive, bsend,
    breceive, zsend, zreceive, fsend, freceive, wsend, wreceive, wlocal, nsend_sem, nreceive, lsend,
    lreceive,
):
    place = Place(line)
    a, b, c, y = place.a, place.b, place.c, place.y
    sums = (sum_ref, gsum_ref)
    rows, features = own.shape[2:]
    half = rows // 2
    chips = 2 * line
    tokens = att_ref.shape[0]
    block = 2 * rows
    blocks = tokens // block
    weight_rows = dsend.shape[1] // (2 * chips)
    pair = 2 * weight_rows
    piece = 512
    ring = from_core.shape[0]
    shortcuts = tuple(range(line - from_beyond.shape[1], line))
    place.greet()
    late = [
        pltpu.make_async_copy(source, target, in_sem.at[n])
        for n, (source, target) in enumerate(
            (
                (upward_in, upward_ref), (gatt_in, gatt_ref), (qkvs_in, qkvs_ref), (attt_in, attt_ref),
                (wup_in, wup_ref),
            )
        )
    ]
    for operand in late:
        operand.start()
    mine, theirs = at_rows(y * half, half), at_rows((1 - y) * half, half)
    both, sibling = at_rows(c * rows, rows), at_rows((1 - c) * rows, rows)

    def chunk(n, to):
        if n == 3:
            return bias_s
        return dsend.at[n, at_rows(to * weight_rows, weight_rows)]

    def received(n, owner):
        return (ratt_ref, rup_ref, rdown_ref, rbias_ref)[n].at[owner]

    weights = Exchange(place, chunk, received, wsend, wreceive, wlocal)

    def order(turn):
        at = place.far_first(turn // 2)
        return at, at * 2 + jnp.where(lax.rem(turn, 2) == 0, 1 - b, b)

    def to_core(t, turn):
        return remote(
            fresh.at[lax.rem(turn, 2), sibling], from_core.at[lax.rem(turn, ring)], csend.at[t, turn],
            creceive.at[lax.rem(turn, ring)], place.device[CORE],
        )

    def to_other(t, chip):
        return remote(
            own.at[t, chip, theirs], from_other.at[t, chip], ysend.at[t, chip], yreceive.at[t, chip],
            place.device[OTHER],
        )

    def to_across(t, at):
        return remote(
            own.at[t, at * 2 + 1 - b, mine], from_across.at[t, at], xsend.at[t, at], xreceive.at[t, at],
            place.device[ACROSS],
        )

    def to_beyond(t, nth):
        at, slot = place.far_first(nth), nth - shortcuts[0]
        return remote(
            own.at[t, at * 2 + 1 - b], from_beyond.at[t, slot], bsend.at[t, slot],
            breceive.at[t, slot], place.device[ACROSS],
        )

    def to_up(t, at):
        return remote(
            own.at[t, at * 2 + b, mine], from_line.at[t, at], zsend.at[t, at], zreceive.at[t, at],
            place.device[UP],
        )

    def to_down(t, at, last):
        slot = line if last else at
        return remote(
            own.at[t, at * 2 + b, mine], from_line.at[t, slot], zsend.at[t, at], zreceive.at[t, slot],
            place.device[DOWN],
        )

    def final(t, part):
        return remote(
            done.at[t, part], done.at[t, part], fsend.at[t], freceive.at[t], place.device[OTHER]
        )

    def add(t, chip, part, other):
        own[t, chip, part, :] = (own[t, chip, part, :].astype(F32) + other.astype(F32)).astype(BF)

    def columns_of(n, source):
        return Stream(
            lambda chip, slot: pltpu.make_async_copy(
                source.at[:, at_rows(chip * pair, pair)], cols.at[n, slot], cols_sem.at[n, slot]
            ),
            cols.shape[1],
            chips,
        )

    def rows_of(source, chip_of):
        return Stream(
            lambda at, slot: pltpu.make_async_copy(
                source.at[at_rows(chip_of(at) * block, block)], buf.at[slot], buf_sem.at[slot]
            ),
            buf.shape[0],
            blocks,
        )

    g_rows, x_rows = rows_of(g_ref, lambda at: at), rows_of(x_ref, lambda at: order(at)[1])
    normed_columns, g_columns = columns_of(0, normed_ref), columns_of(1, g_ref)
    g_rows.prime()
    normed_columns.prime()
    g_columns.prime()

    def product(t, turn):
        _, chip = order(turn)
        here = at_rows(chip * block, block)
        fresh_at = lax.rem(turn, 2)
        left = ((att_ref, act_ref), (gmix_s, gup_s))[t]
        right = ((watt_ref, wdown_ref), (watt_ref, wup_ref))[t]
        first, second = left[0][here, :], left[1][here, :]
        if t == 1:
            slot = x_rows.step(turn)

            def load(start):
                return buf[slot, :, pl.ds(start, piece)].astype(F32)

            mean, inv_std = row_stats(load, block, features, piece)
        for start in range(0, features, piece):
            part = pl.ds(start, piece)
            value = mm(first, right[0][part, :], NT) + mm(second, right[1][part, :], NT)
            fresh[fresh_at, :, part] = value.astype(BF)
            if t == 1:
                unit = (load(start) - mean) * inv_std
                shift_s[:, part] += jnp.sum(value.reshape(block // 8, 8, piece), axis=0)
                gain_s[:, part] += jnp.sum((unit * value).reshape(block // 8, 8, piece), axis=0)
        if t == 1:
            pl.semaphore_wait(credit, 1)
        else:
            pl.when(turn >= ring)(lambda: pl.semaphore_wait(credit, 1))
        to_core(t, turn).start()

    def stage_core(t, turn):
        _, chip = order(turn)
        to_core(t, turn).wait_recv()
        own[t, chip, :, :] = (
            fresh[lax.rem(turn, 2), both, :].astype(F32)
            + from_core[lax.rem(turn, ring)].astype(F32)
        ).astype(BF)

        def give():
            pl.semaphore_signal(
                credit, inc=1, device_id=place.device[CORE], device_id_type=MESH
            )

        if t == 0:
            give()
        else:
            pl.when(turn < chips - ring)(give)
        pl.when(turn < 2 * shortcuts[0])(lambda: to_other(t, chip).start())
        for nth in shortcuts:
            pl.when(turn == 2 * nth)(lambda nth=nth: to_beyond(t, nth).start())
        to_core(t, turn).wait_send()

    def stage_beyond(t):
        for nth in shortcuts:
            chip = place.far_first(nth) * 2 + b
            to_beyond(t, nth).wait_recv()
            add(t, chip, pl.ds(0, rows), from_beyond[t, nth - shortcuts[0]])
            to_other(t, chip).start()

    def stage_other(t, nth):
        if nth in shortcuts:
            return
        at = place.far_first(nth)
        chip = at * 2 + 1 - b
        to_other(t, chip).wait_recv()
        add(t, chip, mine, from_other[t, chip])
        to_across(t, at).start()

    def stage_line(t, nth):
        at = place.far_first(nth)
        chip = at * 2 + b
        to_other(t, chip).wait_recv()
        if nth in shortcuts:
            add(t, chip, mine, from_other[t, chip])
        else:
            to_across(t, at).wait_recv()
            add(t, chip, mine, from_other[t, chip].astype(F32) + from_across[t, at].astype(F32))

        def down():
            @pl.when(a < line - 1)
            def _():
                to_down(t, at, False).wait_recv()
                add(t, chip, mine, from_line[t, at])

            pl.when(at == a - 1)(lambda: to_down(t, at, True).start())
            pl.when(at < a - 1)(lambda: to_down(t, at, False).start())

        def up():
            @pl.when(a > 0)
            def _():
                to_up(t, at).wait_recv()
                add(t, chip, mine, from_line[t, at])

            to_up(t, at).start()

        if nth < line - 1:
            pl.when(at < a)(down)
            pl.when(at > a)(up)
            return

        @pl.when(a < line - 1)
        def _():
            to_down(t, at, True).wait_recv()
            add(t, chip, mine, from_line[t, line])

        @pl.when(a > 0)
        def _():
            to_up(t, at).wait_recv()
            add(t, chip, mine, from_line[t, at])

        done[t, mine, :] = own[t, chip, mine, :]
        final(t, mine).start()

    def norm_copy(step):
        kind = (CORE, OTHER, ACROSS)[step]
        return remote(
            nsend.at[step], nfrom.at[step], nsend_sem.at[step], nreceive.at[step], place.device[kind]
        )

    def norm_line(other, came):
        return remote(
            nsend.at[3], nline.at[other if came else a], lsend.at[other],
            lreceive.at[other if came else a], (place.index(other, b, c), y),
        )

    product(0, 0)

    def first_sum(turn, carry):
        product(0, turn)
        stage_core(0, turn - 1)
        return carry

    lax.fori_loop(1, chips, first_sum, 0)
    stage_core(0, chips - 1)

    def turn_over(pieces):
        def one(at, carry):
            here = at_rows(at * 256, 256)
            for n, source in pieces:
                turned_s[n, :, here] = source[here, :].T
            return carry

        lax.fori_loop(0, tokens // 256, one, 0)

    turn_over(((2, att_ref), (3, act_ref)))
    ones = jnp.ones((8, tokens), BF)

    def gradients_down(chip, carry):
        slot = g_columns.step(chip)
        here = at_rows(chip * pair, pair)
        by_grad = cols[1, slot]
        dsend[2, here, :] = mm(turned_s[3], by_grad).T.astype(BF)
        dsend[0, here, :] = mm(turned_s[2], by_grad).T.astype(BF)
        total_ref[:, here] = mm(ones, by_grad)
        return carry

    lax.fori_loop(0, chips, gradients_down, 0)
    weights.keep((2,))
    weights.start((2,))

    late[0].wait()

    def feed_back(at, carry):
        slot = g_rows.step(at)
        here = at_rows(at * block, block)
        upward = upward_ref[here, :]
        tanh = gelu_parts(upward)
        slope = 0.5 * (1.0 + tanh) + 0.5 * upward * (1.0 - tanh * tanh) * (
            math.sqrt(2.0 / math.pi) * (1.0 + 3 * 0.044715 * upward * upward)
        )
        gup_s[here, :] = (mm(buf[slot], wdown_ref[...]) * slope).astype(BF)
        return carry

    lax.fori_loop(0, blocks, feed_back, 0)
    stage_other(0, 0)
    x_rows.prime()

    turn_over(((1, gup_s),))

    def gradients_up(chip, carry):
        slot = normed_columns.step(chip)
        dsend[1, at_rows(chip * pair, pair), :] = mm(turned_s[1], cols[0, slot]).T.astype(BF)
        return carry

    lax.fori_loop(0, chips, gradients_up, 0)
    weights.keep((1,))
    weights.start((1,))
    stage_other(0, 1)
    normed_columns.prime()
    for operand in late[1:]:
        operand.wait()

    quarter = tokens // inverse_ref.shape[0]
    quarters = block // quarter
    wide = 2 * block
    scale = 1.0 / math.sqrt(HEAD)

    def prepare(at, carry):
        here = at_rows(at * block, block)
        key = qkvs_ref[here, :][:, : 2 * HEAD].astype(F32)
        kt_s[:, here] = key.T[HEAD:].astype(BF)
        dkv_s[here, :] = jnp.zeros((block, 2 * HEAD), F32)
        return carry

    lax.fori_loop(0, blocks, prepare, 0)

    def backward(at, carry):
        here = at_rows(at * block, block)
        query = qkvs_ref[here, :][:, :HEAD]
        grad = jnp.concatenate(
            [gatt_ref[inverse_ref[at * quarters + n]] for n in range(quarters)], axis=0
        )
        left = lax.broadcasted_iota(jnp.int32, (block, 2 * HEAD), 1) < HEAD
        grad_wide = grad[:, 2 * HEAD :].astype(F32)
        grad_right = jnp.where(left, 0.0, grad_wide).astype(BF)
        query_left = jnp.concatenate([query, jnp.zeros_like(query)], axis=1)
        grad = grad[:, 3 * HEAD :]
        delta = jnp.sum(grad_wide.T[HEAD:] * attt_ref[:, here], axis=0, keepdims=True)
        lse = lse_ref[0:1, here]

        def back(place_at, query_grad, masked):
            there = at_rows(place_at * wide, wide)
            keyvalue = qkvs_ref[there, :]
            scores = mm(keyvalue[:, HEAD : 2 * HEAD], query, NT)
            if masked:
                scores = jnp.where(seen(place_at * wide, at * block, wide, block), scores, NEG)
            prob = jnp.exp(scores - lse)
            dprob = mm(keyvalue[:, 2 * HEAD : 3 * HEAD], grad, NT)
            dscore = (prob * (dprob - delta)).astype(BF)
            dkv_s[there, :] += mm(dscore, query_left) + mm(prob.astype(BF), grad_right)
            return query_grad + mm(kt_s[:, there], dscore)

        last = at // 2
        query_grad = lax.fori_loop(
            0, last, lambda n, total: back(n, total, False), jnp.zeros((HEAD, block), F32)
        )
        query_grad = back(last, query_grad, True)
        query_grad = jnp.concatenate([query_grad, query_grad], axis=0).T[:, :HEAD]
        query_grad = turned(
            query_grad * scale, angle_ref[here, : ROT // 2], -angle_ref[here, ROT // 2 :]
        ).astype(BF)
        gm_s[pl.ds(at * quarters, quarters), :, pl.ds(0, HEAD)] = query_grad.reshape(
            quarters, quarter, HEAD
        )
        return carry

    lax.fori_loop(0, blocks // 2, backward, 0)
    stage_beyond(0)
    for nth in range(2, line - 1):
        stage_other(0, nth)
    lax.fori_loop(blocks // 2, blocks, backward, 0)
    if line > 2:
        stage_other(0, line - 1)

    def finish_keys(at, carry):
        here = at_rows(at * block, block)
        keyvalue = jnp.concatenate(
            [
                turned(
                    dkv_s[here, :][:, :HEAD], angle_ref[here, : ROT // 2], -angle_ref[here, ROT // 2 :]
                ).astype(BF),
                dkv_s[here, :][:, HEAD:].astype(BF),
            ],
            axis=1,
        )
        gm_s[pl.ds(at * quarters, quarters), :, pl.ds(HEAD, 2 * HEAD)] = keyvalue.reshape(
            quarters, quarter, 2 * HEAD
        )
        return carry

    lax.fori_loop(0, blocks, finish_keys, 0)

    def unplace(at, carry):
        gmix_s[at_rows(at * quarter, quarter), :] = jnp.concatenate(
            [gm_s[order_ref[at]], jnp.zeros((quarter, HEAD), BF)], axis=1
        )
        return carry

    lax.fori_loop(0, tokens // quarter, unplace, 0)
    turn_over(((0, gmix_s),))
    for n, source in enumerate((gmix_s, gup_s)):
        columns = source.shape[1]

        def tally(at, total, source=source, columns=columns):
            return total + jnp.sum(
                source[at_rows(at * 256, 256), :].astype(F32).reshape(32, 8, columns), axis=0
            )

        total = lax.fori_loop(0, tokens // 256, tally, jnp.zeros((8, columns), F32))
        total = jnp.sum(total, axis=0, keepdims=True)
        for at in range(columns // 128):
            bias_s[pl.ds(n * 2 + at, 1), :] = total[:, at * 128 : (at + 1) * 128]
    bias_s[pl.ds(4, 4), :] = jnp.zeros((4, 128), F32)

    gain_s[...] = jnp.zeros_like(gain_s)
    shift_s[...] = jnp.zeros_like(shift_s)

    def gradients_att(chip):
        slot = normed_columns.step(chip)
        here = at_rows(chip * pair, pair)
        more = mm(turned_s[0], cols[0, slot]).T
        dsend[0, here, :] = (dsend[0, here, :].astype(F32) + more).astype(BF)

    product(1, 0)

    def second_sum(turn, carry):
        product(1, turn)
        stage_core(1, turn - 1)
        return carry

    def second_sum_too(turn, carry):
        second_sum(turn, carry)
        gradients_att(2 * turn - 2)
        gradients_att(2 * turn - 1)
        return carry

    lax.fori_loop(1, chips // 2 + 1, second_sum_too, 0)
    weights.keep((0, 3))
    weights.start((0, 3))
    lax.fori_loop(chips // 2 + 1, chips, second_sum, 0)
    stage_core(1, chips - 1)
    for n, source in enumerate((gain_s, shift_s)):
        total = jnp.sum(source[...], axis=0, keepdims=True)
        span = features // 4
        for at in range(4):
            nsend[0, pl.ds(n * 4 + at, 1), :] = total[:, at * span : (at + 1) * span]
    norm_copy(0).start()
    stage_beyond(1)
    for nth in range(line):
        if nth < line - 1:
            stage_other(1, nth)
        stage_line(0, nth)
    norm_copy(0).wait_recv()
    nsend[1] = nsend[0] + nfrom[0]
    norm_copy(1).start()
    stage_line(1, 0)
    norm_copy(1).wait_recv()
    nsend[2] = nsend[1] + nfrom[1]
    norm_copy(2).start()
    stage_line(1, 1)
    norm_copy(2).wait_recv()
    nsend[3] = nsend[2] + nfrom[2]
    nline[a] = nsend[3]
    for other in range(line):
        pl.when(a != other)(lambda other=other: norm_line(other, False).start())
    stage_other(1, line - 1)
    for nth in range(2, line):
        stage_line(1, nth)
    for other in range(line):
        pl.when(a != other)(lambda other=other: norm_line(other, True).wait_recv())
    total = nline[0]
    for other in range(1, line):
        total += nline[other]
    norms_ref[...] = total

    for step in range(3):
        norm_copy(step).wait_send()
    for other in range(line):
        pl.when(a != other)(lambda other=other: norm_line(other, False).wait_send())
    for t in range(2):
        final(t, theirs).wait_recv()
        final(t, mine).wait_send()
        sums[t][...] = done[t]

        def left(at, carry, t=t):
            to_other(t, at * 2 + b).wait_send()
            pl.when(at != a)(lambda: to_up(t, at).wait_send())

            def also():
                to_other(t, at * 2 + 1 - b).wait_send()
                to_across(t, at).wait_send()

            shorter = at == place.far_first(shortcuts[0])
            for nth in shortcuts[1:]:
                shorter = shorter | (at == place.far_first(nth))
            pl.when(jnp.logical_not(shorter))(also)
            return carry

        lax.fori_loop(0, line, left, 0)
        for nth in shortcuts:
            to_beyond(t, nth).wait_send()
    weights.wait((0, 1, 2, 3))


def spread(
    order, inverse, attended, activated, upward, grad_att, qkvs, lse, attended_t, w_att, w_up, w_down,
    angles, normed, g_all, x_all,
):
    count = lax.axis_size("ctx")
    line = count // 4
    tokens, features = x_all.shape
    rows = tokens // count
    half = rows // 2
    chips = 2 * line
    weight_rows = w_att.shape[0] // count
    wide, hidden = w_att.shape[1], w_up.shape[1]
    hbm, vmem = pl.BlockSpec(memory_space=pl.ANY), pl.BlockSpec(memory_space=pltpu.VMEM)
    smem = pl.BlockSpec(memory_space=pltpu.SMEM)
    dma = pltpu.SemaphoreType.DMA
    own = jax.ShapeDtypeStruct((rows, features), BF)
    back = [
        jax.ShapeDtypeStruct((count, weight_rows, columns), BF) for columns in (wide, hidden, hidden)
    ]
    return pl.pallas_call(
        functools.partial(spread_kernel, line),
        out_shape=[own, own]
        + back
        + [
            jax.ShapeDtypeStruct((count, 8, 128), F32),
            jax.ShapeDtypeStruct((8, features // 4), F32),
            jax.ShapeDtypeStruct((8, features), F32),
        ],
        in_specs=[smem, smem] + [vmem] * 6 + [hbm] * 8,
        out_specs=[vmem, vmem, hbm, hbm, hbm, hbm, vmem, vmem],
        scratch_shapes=[
            pltpu.VMEM(upward.shape, F32),
            pltpu.VMEM(grad_att.shape, BF),
            pltpu.VMEM(qkvs.shape, BF),
            pltpu.VMEM(attended_t.shape, F32),
            pltpu.VMEM(w_up.shape, BF),
            pltpu.VMEM((2, 2 * rows, features), BF),
            pltpu.VMEM((2, chips, rows, features), BF),
            pltpu.VMEM((4, rows, features), BF),
            pltpu.VMEM((2, chips, half, features), BF),
            pltpu.VMEM((2, line, half, features), BF),
            pltpu.VMEM((2, 1, rows, features), BF),
            pltpu.VMEM((2, line + 1, half, features), BF),
            pltpu.VMEM((2, rows, features), BF),
            pltpu.VMEM((4, wide, tokens), BF),
            pltpu.VMEM((3, count * weight_rows, wide), BF),
            pltpu.VMEM((2, 3, tokens, 2 * weight_rows), BF),
            pltpu.VMEM((3, 2 * rows, features), BF),
            pltpu.VMEM((8, features), F32),
            pltpu.VMEM((8, features), F32),
            pltpu.VMEM((4, 8, features // 4), F32),
            pltpu.VMEM((3, 8, features // 4), F32),
            pltpu.VMEM((line, 8, features // 4), F32),
            pltpu.VMEM((8, 128), F32),
            pltpu.VMEM((tokens, wide), BF),
            pltpu.VMEM((tokens, hidden), BF),
            pltpu.VMEM((HEAD, tokens), BF),
            pltpu.VMEM((tokens, 2 * HEAD), F32),
            pltpu.VMEM((order.shape[0], tokens // order.shape[0], 3 * HEAD), BF),
            dma((5,)),
            dma((2, 3)),
            dma((3,)),
            dma((2, chips)),
            dma((4,)),
            pltpu.SemaphoreType.REGULAR,
            dma((2, chips)),
            dma((2, chips)),
            dma((2, line)),
            dma((2, line)),
            dma((2, 1)),
            dma((2, 1)),
            dma((2, line)),
            dma((2, line + 1)),
            dma((2,)),
            dma((2,)),
            dma((4, count)),
            dma((4, count)),
            dma((4,)),
            dma((3,)),
            dma((3,)),
            dma((line,)),
            dma((line,)),
        ],
        compiler_params=pltpu.CompilerParams(
            collective_id=2, has_side_effects=True, vmem_limit_bytes=63 * 1024 * 1024
        ),
    )(
        order, inverse, attended, activated, w_att, w_down, lse, angles, upward, grad_att, qkvs,
        attended_t, w_up, normed, g_all, x_all,
    )


def finish_kernel(
    tok_ref, cot_ref, gain_ref, bias_ref, branch_ref, normed_ref, datt_ref, dup_ref, ddown_ref,
    sums_ref, norms_ref, total_ref,
    out_ref, grad_ref, qkv_ref, wout_ref, up_ref, down_ref, qkvb_ref, upb_ref, gsum_ref, ssum_ref,
    bsum_ref,
):
    inputs = tok_ref[...].astype(F32)
    center = inputs - jnp.mean(inputs, axis=-1, keepdims=True)
    inv_std = lax.rsqrt(jnp.mean(center * center, axis=-1, keepdims=True) + EPS)
    unit = center * inv_std
    out_ref[...] = inputs + branch_ref[...].astype(F32) + bias_ref[...]
    grad_unit = normed_ref[...].astype(F32) * gain_ref[...]
    grad_ref[...] = cot_ref[...].astype(F32) + inv_std * (
        grad_unit
        - jnp.mean(grad_unit, axis=-1, keepdims=True)
        - unit * jnp.mean(grad_unit * unit, axis=-1, keepdims=True)
    )
    count, _, packed = datt_ref.shape
    width, hidden = packed // 4, dup_ref.shape[2]
    pieces = [datt_ref[owner].astype(F32) for owner in range(count)]

    def together(kind):
        return jnp.concatenate(
            [piece[:, kind * width : (kind + 1) * width] for piece in pieces], axis=1
        )

    for kind in range(3):
        qkv_ref[kind, :, :] = together(kind)
        at = kind * width
        qkvb_ref[kind : kind + 1, :] = jnp.concatenate(
            [
                sums_ref[owner, at // 128 : at // 128 + 1, at % 128 : at % 128 + width]
                for owner in range(count)
            ],
            axis=1,
        )
    wout_ref[...] = together(3)
    for owner in range(count):
        columns = pl.ds(owner * hidden, hidden)
        up_ref[:, columns] = dup_ref[owner].astype(F32)
        down_ref[:, columns] = ddown_ref[owner].astype(F32)
        for at in range(hidden // 128):
            upb_ref[:, pl.ds(owner * hidden + at * 128, 128)] = sums_ref[owner, 2 + at : 3 + at, :]
    wide = norms_ref.shape[1]
    for at in range(4):
        gsum_ref[:, pl.ds(at * wide, wide)] = norms_ref[at : at + 1, :]
        ssum_ref[:, pl.ds(at * wide, wide)] = norms_ref[4 + at : 5 + at, :]
    bsum_ref[...] = total_ref[0:1, :]


def finish(tokens, cotangent, gain, bias, branches, own_normed, d_att, d_up, d_down, sums, norms, total):
    count, weight_rows, packed = d_att.shape
    rows, features = tokens.shape
    width, hidden = packed // 4, d_up.shape[2]
    owners = max(128 // width, count // 2)
    steps = count // owners
    by_rows = pl.BlockSpec((rows // steps, features), lambda at: (at, 0))
    line = pl.BlockSpec((1, features), lambda at: (0, 0))

    def whole(array):
        return pl.BlockSpec(array.shape, lambda at: (0,) * array.ndim)

    def by_owner(array):
        return pl.BlockSpec((owners, *array.shape[1:]), lambda at: (at, 0, 0))

    def by_columns(*lead):
        return lambda columns: pl.BlockSpec(
            (*lead, owners * columns), lambda at: (*(0,) * len(lead), at)
        )

    shape = jax.ShapeDtypeStruct
    return pl.pallas_call(
        finish_kernel,
        grid=(steps,),
        out_shape=[
            shape(tokens.shape, F32),
            shape(tokens.shape, F32),
            shape((3, weight_rows, count * width), F32),
            shape((weight_rows, count * width), F32),
            shape((weight_rows, count * hidden), F32),
            shape((weight_rows, count * hidden), F32),
            shape((3, count * width), F32),
            shape((1, count * hidden), F32),
            shape((1, features), F32),
            shape((1, features), F32),
            shape((1, features), F32),
        ],
        in_specs=[by_rows, by_rows, line, line, by_rows, by_rows]
        + [by_owner(array) for array in (d_att, d_up, d_down, sums)]
        + [whole(norms), whole(total)],
        out_specs=[
            by_rows,
            by_rows,
            by_columns(3, weight_rows)(width),
            by_columns(weight_rows)(width),
            by_columns(weight_rows)(hidden),
            by_columns(weight_rows)(hidden),
            by_columns(3)(width),
            by_columns(1)(hidden),
            line,
            line,
            line,
        ],
        compiler_params=pltpu.CompilerParams(vmem_limit_bytes=63 * 1024 * 1024),
    )(
        tokens, cotangent, gain[None], bias[None], branches, own_normed, d_att, d_up, d_down, sums,
        norms, total,
    )


def gelu_tanh(value):
    return jax.nn.gelu(value, approximate=True)


def local(
    tokens, block_order, ln_gain, ln_bias, qkv_weight, qkv_bias, out_weight, fc1_weight, fc1_bias,
    fc2_weight, out_bias, cotangent,
):
    devices = lax.axis_size("ctx")
    myself = lax.axis_index("ctx")
    heads_here = qkv_weight.shape[2] // HEAD
    columns = math.gcd(devices, heads_here)
    mine = myself % columns
    width = qkv_weight.shape[2] // columns
    hidden = fc1_weight.shape[1] // columns
    bias_att = lax.dynamic_slice_in_dim(qkv_bias, mine * width, width, 1).reshape(-1)
    bias_att = jnp.concatenate([bias_att, jnp.zeros((width,), F32)])[None]
    bias_up = lax.dynamic_slice_in_dim(fc1_bias, mine * hidden, hidden, 0)[None]
    if devices == columns and columns % 8 == 0 and width == HEAD and lax.axis_size("tp") == 2:
        freqs = 10000.0 ** (-np.arange(0, ROT, 2, dtype=np.float32) / ROT)
        angles = np.arange(devices * tokens.shape[0], dtype=np.float32)[:, None] * freqs[None, :]
        angles = jnp.asarray(np.concatenate([np.cos(angles), np.sin(angles)], axis=1), F32)
        (
            x_all, g_all, w_att, w_up, w_down, normed, qkvs, lse, attended_t, attended, activated,
            upward, grad_att, inverse,
        ) = collect(
            block_order, tokens, cotangent, qkv_weight, out_weight, fc1_weight, fc2_weight,
            ln_gain[None], ln_bias[None], bias_att, bias_up, angles,
        )
        parts = spread(
            block_order, inverse, attended, activated, upward, grad_att, qkvs, lse, attended_t, w_att,
            w_up, w_down, angles, normed, g_all, x_all,
        )
    else:
        parts = by_groups(
            tokens, block_order, ln_gain, ln_bias, qkv_weight, out_weight, fc1_weight, fc2_weight,
            cotangent, bias_att, bias_up,
        )
    (
        output, input_grad, qkv_grad, out_grad, fc1_grad, fc2_grad, qkv_sums, fc1_sums, gain_sum,
        shift_sum, g_sum,
    ) = finish(tokens, cotangent, ln_gain, out_bias, *parts)
    return (
        output, input_grad, gain_sum[0], shift_sum[0], qkv_grad.transpose(1, 0, 2), qkv_sums, out_grad,
        fc1_grad, fc1_sums[0], fc2_grad, g_sum[0],
    )


def by_groups(
    tokens, block_order, ln_gain, ln_bias, qkv_weight, out_weight, fc1_weight, fc2_weight, cotangent,
    bias_att, bias_up,
):
    devices = lax.axis_size("ctx")
    myself = lax.axis_index("ctx")
    rows_here = tokens.shape[0]
    weight_rows = qkv_weight.shape[0]
    half = devices * rows_here // block_order.shape[0]
    columns = math.gcd(devices, qkv_weight.shape[2] // HEAD)
    groups = devices // columns
    width, hidden = qkv_weight.shape[2] // columns, fc1_weight.shape[1] // columns
    count = columns * rows_here
    side = [[r * columns + c for c in range(columns)] for r in range(groups)]
    across = [[r * columns + c for r in range(groups)] for c in range(columns)]

    def gathered(value, among):
        return lax.all_gather(value, "ctx", axis=0, tiled=True, axis_index_groups=among)

    def scattered(value, among):
        return lax.psum_scatter(
            value, "ctx", scatter_dimension=0, tiled=True, axis_index_groups=among
        )

    def exchanged(value):
        return lax.all_to_all(value, "ctx", split_axis=0, concat_axis=0, tiled=True)

    x_all, g_all = gathered(tokens, side), gathered(cotangent, side)
    kinds = jnp.concatenate([qkv_weight, out_weight[:, None]], axis=1)
    kinds = kinds.reshape(weight_rows, 4, columns, width).transpose(2, 0, 1, 3)
    packed = jnp.concatenate(
        [
            kinds.reshape(columns, weight_rows, 4 * width),
            fc1_weight.reshape(weight_rows, columns, hidden).transpose(1, 0, 2),
            fc2_weight.reshape(weight_rows, columns, hidden).transpose(1, 0, 2),
        ],
        axis=2,
    )
    packed = exchanged(jnp.tile(packed, (groups, 1, 1))).reshape(devices * weight_rows, -1)
    w_att, w_up, w_down = jnp.split(packed, [4 * width, 4 * width + hidden], axis=1)

    inputs = x_all.astype(F32)
    center = inputs - jnp.mean(inputs, axis=-1, keepdims=True)
    inv_std = lax.rsqrt(jnp.mean(center * center, axis=-1, keepdims=True) + EPS)
    unit = center * inv_std
    normed = (unit * ln_gain + ln_bias).astype(BF)
    upward = mm(normed, w_up) + bias_up
    activated, gelu_back = jax.vjp(gelu_tanh, upward)
    activated = activated.astype(BF)
    grad_up = gelu_back(mm(g_all, w_down))[0].astype(BF)
    places = (block_order[:, None] * half + jnp.arange(half, dtype=jnp.int32)[None, :]).reshape(-1)
    attended, grad_mixed = attention_blocks(
        lax.dynamic_slice_in_dim(places, (myself // columns) * count, count),
        places,
        mm(normed, w_att) + bias_att,
        mm(g_all, w_att),
        lambda value: gathered(value, across),
        lambda value: scattered(value, across),
    )
    out_part = (mm(attended, w_att, NT) + mm(activated, w_down, NT)).astype(BF)
    normed_wide = mm(grad_mixed, w_att, NT) + mm(grad_up, w_up, NT)
    branches, own_normed = lax.psum(
        (scattered(out_part, side), scattered(normed_wide.astype(BF), side)), "tp"
    )
    back = jnp.concatenate(
        [
            (mm(normed, grad_mixed, TN) + mm(g_all, attended, TN)).astype(BF),
            mm(normed, grad_up, TN).astype(BF),
            mm(g_all, activated, TN).astype(BF),
        ],
        axis=1,
    )
    back = exchanged(back.reshape(devices, weight_rows, -1))
    back = jnp.sum(back.reshape(groups, columns, weight_rows, -1).astype(F32), axis=0)
    sums = jnp.concatenate(
        [jnp.sum(grad_mixed.astype(F32), axis=0), jnp.sum(grad_up.astype(F32), axis=0)]
    ).reshape(-1, 128)
    sums = jnp.pad(sums, ((0, 8 - sums.shape[0]), (0, 0)))
    sums = gathered(lax.psum(sums, "ctx", axis_index_groups=across)[None], side)
    norms = jnp.stack([jnp.sum(unit * normed_wide, axis=0), jnp.sum(normed_wide, axis=0)])
    norms = lax.psum(norms, ("ctx", "tp")).reshape(8, -1)
    total = lax.psum(jnp.sum(g_all.astype(F32), axis=0), "ctx", axis_index_groups=across)[None]
    return (
        branches, own_normed, *jnp.split(back, [4 * width, 4 * width + hidden], axis=2), sums, norms,
        total,
    )


def solution(mesh):
    rows, tall = P("ctx", None), P("ctx", "tp")
    kinds, bias = P("ctx", None, "tp"), P(None, "tp")
    return jax.shard_map(
        local,
        mesh=mesh,
        in_specs=(rows, P(), P(), P(), kinds, bias, tall, tall, P("tp"), tall, P(), rows),
        out_specs=(rows, rows, P(), P(), kinds, bias, tall, tall, P("tp"), tall, P()),
        check_vma=False,
    )
```

```python
import functools
import math

import jax
import jax.numpy as jnp
import numpy as np
from jax import lax
from jax.experimental import pallas as pl
from jax.experimental.pallas import tpu as pltpu
from jax.sharding import PartitionSpec as P

HEAD = 64
ROT = 32
EPS = 1e-05
NEG = -1e30
BF = jnp.bfloat16
F32 = jnp.float32
NN = (((1,), (0,)), ((), ()))
NT = (((1,), (1,)), ((), ()))
TN = (((0,), (0,)), ((), ()))


def mm(left, right, dims=NN):
    return lax.dot_general(left, right, dims, preferred_element_type=F32)


def tables(positions, width):
    freqs = 10000.0 ** (-(jnp.arange(width // 2, dtype=F32) * 2.0) / width)
    angles = positions.astype(F32)[:, None] * freqs[None, :]
    return (jnp.cos(angles), jnp.sin(angles))


def turned(value, cosine, sine):
    half = cosine.shape[-1]
    first, second = value[..., :half], value[..., half : 2 * half]
    return jnp.concatenate(
        [first * cosine - second * sine, second * cosine + first * sine, value[..., 2 * half :]],
        axis=-1,
    )


def attention_blocks(own_place, places, mixed, grad_att, gather, scatter):
    count, width = grad_att.shape[0], grad_att.shape[1] // 4
    heads = width // HEAD
    scale = 1.0 / math.sqrt(HEAD)
    grad_att = grad_att[:, 3 * width :].astype(BF)
    cosine, sine = tables(own_place, ROT)
    cosine, sine = cosine[:, None, :], sine[:, None, :]
    kinds = [mixed[:, kind * width : (kind + 1) * width].reshape(count, heads, HEAD) for kind in range(3)]
    queries = turned(kinds[0], cosine, sine).astype(BF)
    keys = gather(turned(kinds[1], cosine, sine).astype(BF))
    values = gather(kinds[2].astype(BF))
    grad_att = grad_att.reshape(count, heads, HEAD)
    block = math.gcd(128, count)

    def one(at, carry):
        key_grad, value_grad, attended, query_grad = carry
        query = lax.dynamic_slice_in_dim(queries, at * block, block)
        grad = lax.dynamic_slice_in_dim(grad_att, at * block, block)
        place = lax.dynamic_slice_in_dim(own_place, at * block, block)
        visible = (place[:, None] >= places[None, :])[None]
        scores = jnp.einsum("qhe,khe->hqk", query, keys, preferred_element_type=F32) * scale
        scores = jnp.where(visible, scores, NEG)
        top = jnp.max(scores, axis=-1, keepdims=True)
        expo = jnp.where(visible, jnp.exp(scores - top), 0.0)
        total = jnp.sum(expo, axis=-1)
        summed = jnp.einsum("hqk,khe->qhe", expo.astype(BF), values, preferred_element_type=F32)
        attend = summed / jnp.transpose(total)[..., None]
        delta = jnp.transpose(jnp.sum(grad.astype(F32) * attend, axis=-1))
        prob = expo / total[..., None]
        dprob = jnp.einsum("qhe,khe->hqk", grad, values, preferred_element_type=F32)
        dscore = (prob * (dprob - delta[..., None])).astype(BF)
        part_q = jnp.einsum("hqk,khe->qhe", dscore, keys, preferred_element_type=F32) * scale
        key_grad += jnp.einsum("hqk,qhe->khe", dscore, query, preferred_element_type=F32) * scale
        value_grad += jnp.einsum("hqk,qhe->khe", prob.astype(BF), grad, preferred_element_type=F32)
        attended = lax.dynamic_update_slice_in_dim(attended, attend.astype(BF), at * block, 0)
        query_grad = lax.dynamic_update_slice_in_dim(query_grad, part_q, at * block, 0)
        return (key_grad, value_grad, attended, query_grad)

    zeros = jnp.zeros(keys.shape, F32)
    own = jnp.zeros((count, heads, HEAD), F32)
    key_grad, value_grad, attended, query_grad = lax.fori_loop(
        0, count // block, one, (zeros, zeros, own.astype(BF), own)
    )
    key_grad, value_grad = scatter(key_grad), scatter(value_grad)
    grad_mixed = jnp.concatenate(
        [
            turned(query_grad, cosine, -sine).astype(BF).reshape(count, width),
            turned(key_grad, cosine, -sine).astype(BF).reshape(count, width),
            value_grad.astype(BF).reshape(count, width),
            jnp.zeros((count, width), BF),
        ],
        axis=1,
    )
    attended = jnp.concatenate(
        [jnp.zeros((count, 3 * width), BF), attended.reshape(count, width)], axis=1
    )
    return attended, grad_mixed


MESH = pl.DeviceIdType.MESH
UP, DOWN, ACROSS, OTHER, CORE = range(5)


def at_rows(start, size):
    return pl.ds(pl.multiple_of(start, size), size)


def remote(source, target, send, receive, device):
    return pltpu.make_async_remote_copy(
        src_ref=source, dst_ref=target, send_sem=send, recv_sem=receive, device_id=device,
        device_id_type=MESH,
    )


class Place:
    def __init__(self, line):
        self.line = line
        self.me = lax.axis_index("ctx")
        self.y = lax.axis_index("tp")
        self.a, self.b, self.c = self.me // 4, (self.me // 2) % 2, self.me % 2
        a, b, c, y = self.a, self.b, self.c, self.y
        self.device = {
            UP: (self.index(jnp.minimum(a + 1, line - 1), b, c), y),
            DOWN: (self.index(jnp.maximum(a - 1, 0), b, c), y),
            ACROSS: (self.index(a, 1 - b, c), y),
            OTHER: (self.me, 1 - y),
            CORE: (self.index(a, b, 1 - c), y),
        }

    def index(self, a, b, c):
        return a * 4 + b * 2 + c

    def far_first(self, turn):
        line = self.line
        high, low = line - 1 - turn, turn
        high = jnp.where(high <= self.a, high - 1, high)
        low = jnp.where(low >= self.a, low + 1, low)
        other = jnp.where(self.a < line // 2, high, low)
        return jnp.where(turn == line - 1, self.a, other)

    def greet(self):
        barrier = pltpu.get_barrier_semaphore()
        count = 4 * self.line

        def signal(step, carry):
            pl.semaphore_signal(
                barrier, inc=1, device_id=(lax.rem(self.me + step, count), self.y), device_id_type=MESH
            )
            return carry

        lax.fori_loop(1, count, signal, 0)
        pl.semaphore_signal(barrier, inc=1, device_id=self.device[OTHER], device_id_type=MESH)
        pl.semaphore_wait(barrier, count)


def flipped(value, mask, bits):
    result = 0
    for bit in range(bits):
        one, other = (value // 2**bit) % 2, (mask // 2**bit) % 2
        result = result + 2**bit * (one + other - 2 * one * other)
    return result


class Exchange:
    def __init__(self, place, chunk, received, send, receive, own):
        self.place, self.chunk, self.received = place, chunk, received
        self.send, self.receive, self.own = send, receive, own
        self.count = 4 * place.line
        self.bits = self.count.bit_length() - 1
        self.partners = [self.partner(mask) for mask in range(self.count - 1, 0, -1)]

    def partner(self, mask):
        return mask, flipped(self.place.me, mask, self.bits)

    def chip(self, turn):
        return flipped(self.place.me // 2, self.count // 2 - 1 - turn, self.bits - 1)

    def start_chip(self, pieces, turn):
        mask = self.count - 2 - 2 * turn
        for n in pieces:
            self.copy(self.partner(mask + 1), n, False).start()
            pl.when(mask > 0)(lambda n=n: self.copy(self.partner(mask), n, False).start())
            pl.when(mask == 0)(lambda n=n: self.kept(n).start())

    def copy(self, partner, n, came):
        mask, to = partner
        return remote(
            self.chunk(n, to), self.received(n, to if came else self.place.me), self.send.at[n, mask],
            self.receive.at[n, mask], (to, self.place.y),
        )

    def kept(self, n):
        me = self.place.me
        return pltpu.make_async_copy(self.chunk(n, me), self.received(n, me), self.own.at[n])

    def keep(self, pieces):
        for n in pieces:
            self.kept(n).start()

    def start(self, pieces):
        for partner in self.partners:
            for n in pieces:
                self.copy(partner, n, False).start()

    def wait(self, pieces):
        for partner in self.partners:
            for n in pieces:
                self.copy(partner, n, True).wait()
        for n in pieces:
            self.kept(n).wait()


def row_stats(load, rows, features, piece):
    mean = jnp.zeros((rows, 1), F32)
    for at in range(0, features, piece):
        mean += jnp.sum(load(at), axis=1, keepdims=True)
    mean = mean / features
    spread = jnp.zeros((rows, 1), F32)
    for at in range(0, features, piece):
        center = load(at) - mean
        spread += jnp.sum(center * center, axis=1, keepdims=True)
    return mean, lax.rsqrt(spread / features + EPS)


class Stream:
    def __init__(self, copy, depth, total):
        self.copy, self.depth, self.total = copy, depth, total

    def prime(self):
        for at in range(min(self.depth - 1, self.total)):
            self.copy(at, at).start()

    def step(self, at):
        slot = lax.rem(at, self.depth)
        self.copy(at, slot).wait()
        later = at + self.depth - 1

        @pl.when(later < self.total)
        def _():
            self.copy(later, lax.rem(later, self.depth)).start()

        return slot


def gelu_parts(value):
    inner = math.sqrt(2.0 / math.pi) * (value + 0.044715 * value * value * value)
    return jnp.tanh(inner)


def seen(start_key, start_query, keys, queries):
    key = start_key + lax.broadcasted_iota(jnp.int32, (keys, queries), 0)
    return key <= start_query + lax.broadcasted_iota(jnp.int32, (keys, queries), 1)


def collect_kernel(
    line, order_ref, tok_ref, cot_ref, qkv_ref, out_ref, up_ref, down_ref, gain_ref,
    shift_ref, batt_ref, bup_ref, angle_ref,
    x_out, g_out, watt_out, wup_out, wdown_ref, normed_out, qkvs_out, lse_out, attt_out, att_out,
    act_out, upward_out, gatt_out, inverse_ref,
    x_ref, g_ref, watt_s, wup_s, normed_s, qkvs_ref, lse_ref, attt_ref, att_ref, act_ref, upward_ref,
    gatt_ref, packed, mixed_s, k_s, vt_s, st, att_s,
    send, receive, own_sem, wsend, wreceive, wlocal, out_sem,
):
    place = Place(line)
    a, b, c, y = place.a, place.b, place.c, place.y
    sources, targets = (tok_ref, cot_ref), (x_ref, g_ref)
    rows, features = tok_ref.shape
    half = rows // 2
    weight_rows = up_ref.shape[0]
    tokens = x_ref.shape[0]
    hidden = wup_s.shape[1]
    width = watt_s.shape[1] // 4
    block = 2 * rows
    blocks = tokens // block
    piece = 512
    place.greet()
    shipped = []

    def ship(source, target):
        shipped.append(pltpu.make_async_copy(source, target, out_sem.at[len(shipped)]))
        shipped[-1].start()

    def copy(t, kind, owner, part, own=False):
        target = targets[t].at[at_rows(owner * rows + part * half, half)]
        source = sources[t].at[at_rows(part * half, half)] if own else target
        return remote(
            source, target, send.at[t, kind, owner, part], receive.at[t, owner, part], place.device[kind]
        )

    def landed(t, owner, part):
        copy(t, CORE, owner, part).wait_recv()

    def along(t, distance):
        for sign in (0,) if distance == 0 else (1, -1):
            at = a + sign * distance

            def pass_on(sign=sign, at=at):
                owner = place.index(at, b, c)
                own = distance == 0
                if not own:
                    landed(t, owner, y)
                if sign <= 0:
                    pl.when(a < line - 1)(lambda: copy(t, UP, owner, y, own).start())
                if sign >= 0:
                    pl.when(a > 0)(lambda: copy(t, DOWN, owner, y, own).start())
                copy(t, ACROSS, owner, y, own).start()
                if not own:
                    copy(t, OTHER, owner, y).start()
                copy(t, CORE, owner, y, own).start()
                if own:
                    copy(t, CORE, owner, 1 - y, own).start()

            if distance == 0:
                pass_on()
            else:
                pl.when((at >= 0) & (at < line))(pass_on)

    def beside(t, distance):
        for sign in (0,) if distance == 0 else (1, -1):
            at = a + sign * distance

            def pass_on(at=at):
                owner = place.index(at, 1 - b, c)
                landed(t, owner, y)
                copy(t, OTHER, owner, y).start()
                copy(t, CORE, owner, y).start()

            pl.when((at >= 0) & (at < line))(pass_on)

    def from_other(t):
        for distance in range(line):
            for column in (b, 1 - b):
                for sign in (0,) if distance == 0 else (1, -1):
                    at = a + sign * distance

                    def pass_on(at=at, column=column):
                        owner = place.index(at, column, c)
                        landed(t, owner, 1 - y)
                        copy(t, CORE, owner, 1 - y).start()

                    if distance == 0 and column is b:
                        continue
                    pl.when((at >= 0) & (at < line))(pass_on)

    def own_copy(t):
        return pltpu.make_async_copy(
            sources[t], targets[t].at[at_rows(place.me * rows, rows)], own_sem.at[t]
        )

    def complete(t):
        def came(chip, carry):
            for part in range(2):
                landed(t, chip * 2 + (1 - c), part)
            return carry

        lax.fori_loop(0, 2 * line, came, 0)
        own_copy(t).wait()

    def chunk(n, to):
        if n == 0:
            return packed.at[to]
        return (up_ref, down_ref)[n - 1].at[:, at_rows(to * hidden, hidden)]

    def received(n, owner):
        return (watt_s, wup_s, wdown_ref)[n].at[at_rows(owner * weight_rows, weight_rows)]

    weights = Exchange(place, chunk, received, wsend, wreceive, wlocal)

    own_copy(0).start()
    own_copy(1).start()
    along(0, 0)
    for owner in range(4 * line):
        columns = pl.ds(owner * width, width)
        packed[owner, :, :] = jnp.concatenate(
            [qkv_ref[kind, :, columns] for kind in range(3)] + [out_ref[:, columns]], axis=1
        )
    weights.keep((0, 1, 2))
    ordered = [order_ref[at] for at in range(order_ref.shape[0])]

    def invert(wanted, carry):
        found = jnp.int32(0)
        for at, held in enumerate(ordered):
            found = jnp.where(held == wanted, at, found)
        inverse_ref[wanted] = found
        return carry

    for distance in range(1, line):
        along(0, distance)
        beside(0, distance - 1)
    beside(0, line - 1)
    along(1, 0)
    weights.start((0,))
    lax.fori_loop(0, len(ordered), invert, 0)
    for distance in range(1, line - 1):
        along(1, distance)
        beside(1, distance - 1)
    from_other(0)
    complete(0)
    weights.wait((0,))
    ship(x_ref, x_out)
    ship(watt_s, watt_out)

    quarter = tokens // inverse_ref.shape[0]
    quarters = block // quarter

    shared = batt_ref[:, at_rows(place.me // 2 * 2 * width, 2 * width)]
    shared = jnp.where(c == 0, shared[:, :width], shared[:, width:])
    bias_att = jnp.concatenate(
        [shared[kind : kind + 1] for kind in range(3)] + [jnp.zeros((1, width), F32)], axis=1
    )
    bias_up = bup_ref[:, at_rows(place.me * hidden, hidden)]

    def project(at, carry):
        here = at_rows(at * block, block)

        def load(start):
            return x_ref[here, pl.ds(start, piece)].astype(F32)

        mean, inv_std = row_stats(load, block, features, piece)
        for start in range(0, features, piece):
            part = pl.ds(start, piece)
            unit = (load(start) - mean) * inv_std
            normed_s[here, part] = (unit * gain_ref[:, part] + shift_ref[:, part]).astype(BF)
        mixed = mm(normed_s[here, :], watt_s[...]) + bias_att
        mixed_s[pl.ds(at * quarters, quarters)] = mixed.reshape(quarters, quarter, 4 * width)
        return carry

    lax.fori_loop(0, blocks // 2, project, 0)
    along(1, line - 1)
    beside(1, line - 2)
    weights.start((1,))
    lax.fori_loop(blocks // 2, blocks, project, 0)
    ship(normed_s, normed_out)
    beside(1, line - 1)
    weights.start((2,))

    wide = 2 * block
    scale = 1.0 / math.sqrt(HEAD)

    def prepare(at, carry):
        here = at_rows(at * block, block)
        mixed = jnp.concatenate(
            [mixed_s[inverse_ref[at * quarters + n]] for n in range(quarters)], axis=0
        )
        cosine, sine = angle_ref[here, : ROT // 2], angle_ref[here, ROT // 2 :]
        query = turned(mixed[:, :HEAD], cosine, sine).astype(BF) * jnp.asarray(scale, BF)
        key = turned(mixed[:, HEAD : 2 * HEAD], cosine, sine)
        value = mixed[:, 2 * HEAD : 3 * HEAD]
        k_s[here, :] = key.astype(BF)
        vt_s[:, here] = jnp.concatenate([value, value], axis=1).T[:HEAD].astype(BF)
        qkvs_ref[here, :] = jnp.concatenate(
            [query, key.astype(BF), value.astype(BF), jnp.zeros_like(query)], axis=1
        )
        return carry

    lax.fori_loop(0, blocks, prepare, 0)

    def forward(at, carry):
        here = at_rows(at * block, block)
        query = qkvs_ref[here, :][:, :HEAD]

        def scored(place_at, top, masked):
            there = at_rows(place_at * wide, wide)
            scores = mm(k_s[there, :], query, NT)
            if masked:
                scores = jnp.where(seen(place_at * wide, at * block, wide, block), scores, NEG)
            st[there, :] = scores
            return jnp.maximum(top, jnp.max(scores.reshape(wide // 8, 8, block), axis=0))

        last = at // 2
        top = lax.fori_loop(
            0, last, lambda n, top: scored(n, top, False), jnp.full((8, block), NEG, F32)
        )
        top = jnp.max(scored(last, top, True), axis=0, keepdims=True)

        def weighed(place_at, state):
            total, summed = state
            there = at_rows(place_at * wide, wide)
            expo = jnp.exp(st[there, :] - top)
            total = total + jnp.sum(expo.reshape(wide // 8, 8, block), axis=0)
            return (total, summed + mm(vt_s[:, there], expo.astype(BF)))

        total, summed = lax.fori_loop(
            0, last + 1, weighed, (jnp.zeros((8, block), F32), jnp.zeros((HEAD, block), F32))
        )
        total = jnp.sum(total, axis=0, keepdims=True)
        attended = summed * (1.0 / total)
        lse_ref[:, here] = jnp.broadcast_to(top + jnp.log(total), (8, block))
        attt_ref[:, here] = attended
        both = jnp.concatenate([attended, attended], axis=0).T.astype(BF)
        att_s[pl.ds(at * quarters, quarters)] = both.reshape(quarters, quarter, 2 * HEAD)
        return carry

    lax.fori_loop(0, blocks, forward, 0)
    for source, target in ((qkvs_ref, qkvs_out), (lse_ref, lse_out), (attt_ref, attt_out)):
        ship(source, target)

    def unplace(at, carry):
        attended = att_s[order_ref[at]][:, HEAD:]
        att_ref[at_rows(at * quarter, quarter), :] = jnp.concatenate(
            [jnp.zeros((quarter, 3 * HEAD), BF), attended], axis=1
        )
        return carry

    lax.fori_loop(0, tokens // quarter, unplace, 0)
    ship(att_ref, att_out)
    from_other(1)
    complete(1)
    ship(g_ref, g_out)

    def grad_in(at, carry):
        grad = mm(g_ref[at_rows(at * block, block), :], watt_s[...]).astype(BF)
        gatt_ref[pl.ds(at * quarters, quarters)] = grad.reshape(quarters, quarter, 4 * width)
        return carry

    lax.fori_loop(0, blocks, grad_in, 0)
    ship(gatt_ref, gatt_out)
    weights.wait((1,))
    ship(wup_s, wup_out)

    def feed(at, carry):
        here = at_rows(at * block, block)
        upward = mm(normed_s[here, :], wup_s[...]) + bias_up
        upward_ref[here, :] = upward
        act_ref[here, :] = (0.5 * upward * (1.0 + gelu_parts(upward))).astype(BF)
        return carry

    lax.fori_loop(0, blocks, feed, 0)
    ship(upward_ref, upward_out)
    ship(act_ref, act_out)
    for t in range(2):

        def left(at, carry, t=t):
            owner, beyond = place.index(at, b, c), place.index(at, 1 - b, c)
            pl.when((at <= a) & (a < line - 1))(lambda: copy(t, UP, owner, y).wait_send())
            pl.when((at >= a) & (a > 0))(lambda: copy(t, DOWN, owner, y).wait_send())
            copy(t, ACROSS, owner, y).wait_send()
            pl.when(at != a)(lambda: copy(t, OTHER, owner, y).wait_send())
            copy(t, OTHER, beyond, y).wait_send()
            for part in range(2):
                copy(t, CORE, owner, part).wait_send()
                copy(t, CORE, beyond, part).wait_send()
            return carry

        lax.fori_loop(0, line, left, 0)
    weights.wait((2,))
    for result in shipped:
        result.wait()


def collect(
    order, tokens, cotangent, qkv_weight, out_weight, fc1_weight, fc2_weight, gain, shift, bias_att,
    bias_up, angles,
):
    rows, features = tokens.shape
    weight_rows = fc1_weight.shape[0]
    count = lax.axis_size("ctx")
    line, width, hidden = count // 4, qkv_weight.shape[2] // count, fc1_weight.shape[1] // count
    total, depth = count * rows, count * weight_rows
    halves = order.shape[0]
    hbm, vmem = pl.BlockSpec(memory_space=pl.ANY), pl.BlockSpec(memory_space=pltpu.VMEM)
    smem = pl.BlockSpec(memory_space=pltpu.SMEM)
    dma = pltpu.SemaphoreType.DMA
    shape = jax.ShapeDtypeStruct
    return pl.pallas_call(
        functools.partial(collect_kernel, line),
        out_shape=[
            shape((total, features), BF),
            shape((total, features), BF),
            shape((depth, 4 * width), BF),
            shape((depth, hidden), BF),
            shape((depth, hidden), BF),
            shape((total, features), BF),
            shape((total, 4 * width), BF),
            shape((8, total), F32),
            shape((width, total), F32),
            shape((total, 4 * width), BF),
            shape((total, hidden), BF),
            shape((total, hidden), F32),
            shape((halves, total // halves, 4 * width), BF),
            shape((halves,), jnp.int32),
        ],
        in_specs=[smem, hbm, hbm, vmem, vmem, hbm, hbm] + [vmem] * 5,
        out_specs=[hbm] * 13 + [smem],
        scratch_shapes=[
            pltpu.VMEM((total, features), BF),
            pltpu.VMEM((total, features), BF),
            pltpu.VMEM((depth, 4 * width), BF),
            pltpu.VMEM((depth, hidden), BF),
            pltpu.VMEM((total, features), BF),
            pltpu.VMEM((total, 4 * width), BF),
            pltpu.VMEM((8, total), F32),
            pltpu.VMEM((width, total), F32),
            pltpu.VMEM((total, 4 * width), BF),
            pltpu.VMEM((total, hidden), BF),
            pltpu.VMEM((total, hidden), F32),
            pltpu.VMEM((halves, total // halves, 4 * width), BF),
            pltpu.VMEM((count, weight_rows, 4 * width), BF),
            pltpu.VMEM((halves, total // halves, 4 * width), F32),
            pltpu.VMEM((total, width), BF),
            pltpu.VMEM((width, total), BF),
            pltpu.VMEM((total, 2 * rows), F32),
            pltpu.VMEM((halves, total // halves, 2 * width), BF),
            dma((2, 5, count, 2)),
            dma((2, count, 2)),
            dma((2,)),
            dma((3, count)),
            dma((3, count)),
            dma((3,)),
            dma((12,)),
        ],
        compiler_params=pltpu.CompilerParams(
            collective_id=1, has_side_effects=True, vmem_limit_bytes=60 * 1024 * 1024
        ),
    )(
        order, tokens, cotangent, qkv_weight.transpose(1, 0, 2), out_weight, fc1_weight,
        fc2_weight, gain, shift, bias_att, bias_up, angles,
    )


def spread_kernel(
    line, order_ref, inverse_ref, att_ref, act_ref, lse_ref, angle_ref,
    watt_in, wdown_in, upward_in, gatt_in, qkvs_in, attt_in, wup_in, normed_ref, g_ref, x_ref,
    sum_ref, gsum_ref, ratt_ref, rup_ref, rdown_ref, rbias_ref, norms_ref, total_ref,
    weights_s, upward_ref, gatt_ref, qkvs_ref, attt_ref,
    fresh, own, from_core, from_other, from_across, from_beyond, from_line, done, turned_s, dsend, cols,
    buf, gain_s, shift_s, nsend, nfrom, nline, bias_s, gmix_s, gup_s, kt_s, dkv_s, gm_s,
    in_sem, cols_sem, buf_sem, csend, creceive, credit, ysend, yreceive, xsend, xreceive, bsend,
    breceive, zsend, zreceive, fsend, freceive, wsend, wreceive, wlocal, nsend_sem, nreceive, lsend,
    lreceive,
):
    place = Place(line)
    a, b, c, y = place.a, place.b, place.c, place.y
    sums = (sum_ref, gsum_ref)
    rows, features = own.shape[2:]
    half = rows // 2
    chips = 2 * line
    tokens = att_ref.shape[0]
    block = 2 * rows
    blocks = tokens // block
    weight_rows = dsend.shape[1] // (2 * chips)
    pair = 2 * weight_rows
    piece = 512
    ring = from_core.shape[0]
    shortcuts = tuple(range(line - from_beyond.shape[1], line))
    place.greet()
    wide, hidden = watt_in.shape[1], wup_in.shape[1]
    late = [
        pltpu.make_async_copy(source, target, in_sem.at[n])
        for n, (source, target) in enumerate(
            (
                (wdown_in, weights_s.at[:, pl.ds(0, hidden)]),
                (watt_in, weights_s.at[:, pl.ds(hidden, wide)]),
                (upward_in, upward_ref),
                (gatt_in, gatt_ref),
                (qkvs_in, qkvs_ref),
                (attt_in, attt_ref),
                (wup_in, weights_s.at[:, pl.ds(hidden + wide, hidden)]),
            )
        )
    ]
    for operand in late:
        operand.start()
    mine, theirs = at_rows(y * half, half), at_rows((1 - y) * half, half)
    both, sibling = at_rows(c * rows, rows), at_rows((1 - c) * rows, rows)

    def chunk(n, to):
        if n == 3:
            return bias_s
        return dsend.at[n, at_rows(to * weight_rows, weight_rows)]

    def received(n, owner):
        return (ratt_ref, rup_ref, rdown_ref, rbias_ref)[n].at[owner]

    weights = Exchange(place, chunk, received, wsend, wreceive, wlocal)

    def order(turn):
        at = place.far_first(turn // 2)
        return at, at * 2 + jnp.where(lax.rem(turn, 2) == 0, 1 - b, b)

    def to_core(t, turn):
        return remote(
            fresh.at[lax.rem(turn, 2), sibling], from_core.at[lax.rem(turn, ring)], csend.at[t, turn],
            creceive.at[lax.rem(turn, ring)], place.device[CORE],
        )

    def to_other(t, chip):
        return remote(
            own.at[t, chip, theirs], from_other.at[t, chip], ysend.at[t, chip], yreceive.at[t, chip],
            place.device[OTHER],
        )

    def to_across(t, at):
        return remote(
            own.at[t, at * 2 + 1 - b, mine], from_across.at[t, at], xsend.at[t, at], xreceive.at[t, at],
            place.device[ACROSS],
        )

    def to_beyond(t, nth):
        at, slot = place.far_first(nth), nth - shortcuts[0]
        return remote(
            own.at[t, at * 2 + 1 - b], from_beyond.at[t, slot], bsend.at[t, slot],
            breceive.at[t, slot], place.device[ACROSS],
        )

    def to_up(t, at):
        return remote(
            own.at[t, at * 2 + b, mine], from_line.at[t, at], zsend.at[t, at], zreceive.at[t, at],
            place.device[UP],
        )

    def to_down(t, at, last):
        slot = line if last else at
        return remote(
            own.at[t, at * 2 + b, mine], from_line.at[t, slot], zsend.at[t, at], zreceive.at[t, slot],
            place.device[DOWN],
        )

    def final(t, part):
        return remote(
            done.at[t, part], done.at[t, part], fsend.at[t], freceive.at[t], place.device[OTHER]
        )

    def add(t, chip, part, other):
        own[t, chip, part, :] = (own[t, chip, part, :].astype(F32) + other.astype(F32)).astype(BF)

    def columns_of(n, source):
        return Stream(
            lambda at, slot: pltpu.make_async_copy(
                source.at[:, at_rows(weights.chip(at) * pair, pair)],
                cols.at[n, slot],
                cols_sem.at[n, slot],
            ),
            cols.shape[1],
            chips,
        )

    def rows_of(source, chip_of):
        return Stream(
            lambda at, slot: pltpu.make_async_copy(
                source.at[at_rows(chip_of(at) * block, block)], buf.at[slot], buf_sem.at[slot]
            ),
            buf.shape[0],
            blocks,
        )

    g_rows, x_rows = rows_of(g_ref, lambda at: at), rows_of(x_ref, lambda at: order(at)[1])
    normed_columns, g_columns = columns_of(0, normed_ref), columns_of(1, g_ref)
    g_rows.prime()
    normed_columns.prime()
    g_columns.prime()

    def product(t, turn):
        _, chip = order(turn)
        here = at_rows(chip * block, block)
        fresh_at = lax.rem(turn, 2)
        left = ((act_ref, att_ref), (gmix_s, gup_s))[t]
        left = jnp.concatenate([left[0][here, :], left[1][here, :]], axis=1)
        right = pl.ds((0, hidden)[t], hidden + wide)
        if t == 1:
            slot = x_rows.step(turn)

            def load(start):
                return buf[slot, :, pl.ds(start, piece)].astype(F32)

            mean, inv_std = row_stats(load, block, features, piece)
        for start in range(0, features, piece):
            part = pl.ds(start, piece)
            value = mm(left, weights_s[part, right], NT)
            fresh[fresh_at, :, part] = value.astype(BF)
            if t == 1:
                unit = (load(start) - mean) * inv_std
                shift_s[:, part] += jnp.sum(value.reshape(block // 8, 8, piece), axis=0)
                gain_s[:, part] += jnp.sum((unit * value).reshape(block // 8, 8, piece), axis=0)
        if t == 1:
            pl.semaphore_wait(credit, 1)
        else:
            pl.when(turn >= ring)(lambda: pl.semaphore_wait(credit, 1))
        to_core(t, turn).start()

    def stage_core(t, turn):
        _, chip = order(turn)
        to_core(t, turn).wait_recv()
        own[t, chip, :, :] = (
            fresh[lax.rem(turn, 2), both, :].astype(F32)
            + from_core[lax.rem(turn, ring)].astype(F32)
        ).astype(BF)

        def give():
            pl.semaphore_signal(
                credit, inc=1, device_id=place.device[CORE], device_id_type=MESH
            )

        if t == 0:
            give()
        else:
            pl.when(turn < chips - ring)(give)
        pl.when(turn < 2 * shortcuts[0])(lambda: to_other(t, chip).start())
        for nth in shortcuts:
            pl.when(turn == 2 * nth)(lambda nth=nth: to_beyond(t, nth).start())
        to_core(t, turn).wait_send()

    def stage_beyond(t):
        for nth in shortcuts:
            chip = place.far_first(nth) * 2 + b
            to_beyond(t, nth).wait_recv()
            add(t, chip, pl.ds(0, rows), from_beyond[t, nth - shortcuts[0]])
            to_other(t, chip).start()

    def stage_other(t, nth):
        if nth in shortcuts:
            return
        at = place.far_first(nth)
        chip = at * 2 + 1 - b
        to_other(t, chip).wait_recv()
        add(t, chip, mine, from_other[t, chip])
        to_across(t, at).start()

    def stage_line(t, nth):
        at = place.far_first(nth)
        chip = at * 2 + b
        to_other(t, chip).wait_recv()
        if nth in shortcuts:
            add(t, chip, mine, from_other[t, chip])
        else:
            to_across(t, at).wait_recv()
            add(t, chip, mine, from_other[t, chip].astype(F32) + from_across[t, at].astype(F32))

        def down():
            @pl.when(a < line - 1)
            def _():
                to_down(t, at, False).wait_recv()
                add(t, chip, mine, from_line[t, at])

            pl.when(at == a - 1)(lambda: to_down(t, at, True).start())
            pl.when(at < a - 1)(lambda: to_down(t, at, False).start())

        def up():
            @pl.when(a > 0)
            def _():
                to_up(t, at).wait_recv()
                add(t, chip, mine, from_line[t, at])

            to_up(t, at).start()

        if nth < line - 1:
            pl.when(at < a)(down)
            pl.when(at > a)(up)
            return

        @pl.when(a < line - 1)
        def _():
            to_down(t, at, True).wait_recv()
            add(t, chip, mine, from_line[t, line])

        @pl.when(a > 0)
        def _():
            to_up(t, at).wait_recv()
            add(t, chip, mine, from_line[t, at])

        done[t, mine, :] = own[t, chip, mine, :]
        final(t, mine).start()

    def norm_copy(step):
        kind = (CORE, OTHER, ACROSS)[step]
        return remote(
            nsend.at[step], nfrom.at[step], nsend_sem.at[step], nreceive.at[step], place.device[kind]
        )

    def norm_line(other, came):
        return remote(
            nsend.at[3], nline.at[other if came else a], lsend.at[other],
            lreceive.at[other if came else a], (place.index(other, b, c), y),
        )

    for operand in late[:2]:
        operand.wait()
    product(0, 0)

    def turn_over(pieces):
        def one(at, carry):
            here = at_rows(at * 256, 256)
            for n, source in pieces:
                turned_s[n, :, here] = source[here, :].T
            return carry

        lax.fori_loop(0, tokens // 256, one, 0)

    turn_over(((2, att_ref), (3, act_ref)))
    ones = jnp.ones((8, tokens), BF)

    def gradients_down(turn):
        slot = g_columns.step(turn)
        here = at_rows(weights.chip(turn) * pair, pair)
        by_grad = cols[1, slot]
        dsend[2, here, :] = mm(turned_s[3], by_grad).T.astype(BF)
        dsend[0, here, :] = mm(turned_s[2], by_grad).T.astype(BF)
        total_ref[:, here] = mm(ones, by_grad)
        weights.start_chip((2,), turn)

    def first_sum(turn, carry):
        product(0, turn)
        stage_core(0, turn - 1)
        gradients_down(turn - 1)
        return carry

    lax.fori_loop(1, chips, first_sum, 0)
    stage_core(0, chips - 1)
    gradients_down(chips - 1)

    late[2].wait()

    def feed_back(at, carry):
        slot = g_rows.step(at)
        here = at_rows(at * block, block)
        upward = upward_ref[here, :]
        tanh = gelu_parts(upward)
        slope = 0.5 * (1.0 + tanh) + 0.5 * upward * (1.0 - tanh * tanh) * (
            math.sqrt(2.0 / math.pi) * (1.0 + 3 * 0.044715 * upward * upward)
        )
        gup_s[here, :] = (mm(buf[slot], weights_s[:, pl.ds(0, hidden)]) * slope).astype(BF)
        return carry

    lax.fori_loop(0, blocks, feed_back, 0)
    stage_other(0, 0)
    x_rows.prime()

    turn_over(((1, gup_s),))

    def gradients_up(turn, carry):
        slot = normed_columns.step(turn)
        here = at_rows(weights.chip(turn) * pair, pair)
        dsend[1, here, :] = mm(turned_s[1], cols[0, slot]).T.astype(BF)
        weights.start_chip((1,), turn)
        return carry

    lax.fori_loop(0, chips, gradients_up, 0)
    stage_other(0, 1)
    normed_columns.prime()
    for operand in late[3:]:
        operand.wait()

    quarter = tokens // inverse_ref.shape[0]
    quarters = block // quarter
    span = 2 * block
    scale = 1.0 / math.sqrt(HEAD)

    def prepare(at, carry):
        here = at_rows(at * block, block)
        key = qkvs_ref[here, :][:, : 2 * HEAD].astype(F32)
        kt_s[:, here] = key.T[HEAD:].astype(BF)
        dkv_s[here, :] = jnp.zeros((block, 2 * HEAD), F32)
        return carry

    lax.fori_loop(0, blocks, prepare, 0)

    def backward(at, carry):
        here = at_rows(at * span, span)
        query = qkvs_ref[here, :][:, :HEAD]
        grad = jnp.concatenate(
            [gatt_ref[inverse_ref[at * 2 * quarters + n]] for n in range(2 * quarters)], axis=0
        )
        left = lax.broadcasted_iota(jnp.int32, (span, 2 * HEAD), 1) < HEAD
        grad_wide = grad[:, 2 * HEAD :].astype(F32)
        grad_right = jnp.where(left, 0.0, grad_wide).astype(BF)
        query_left = jnp.concatenate([query, jnp.zeros_like(query)], axis=1)
        beside_each = jnp.concatenate([query_left, grad_right], axis=0)
        grad = grad[:, 3 * HEAD :]
        delta = jnp.sum(grad_wide.T[HEAD:] * attt_ref[:, here], axis=0, keepdims=True)
        lse = lse_ref[0:1, here]

        def back(place_at, query_grad, masked):
            there = at_rows(place_at * span, span)
            keyvalue = qkvs_ref[there, :]
            scores = mm(keyvalue[:, HEAD : 2 * HEAD], query, NT)
            if masked:
                scores = jnp.where(seen(0, 0, span, span), scores, NEG)
            prob = jnp.exp(scores - lse)
            dprob = mm(keyvalue[:, 2 * HEAD : 3 * HEAD], grad, NT)
            dscore = (prob * (dprob - delta)).astype(BF)
            dkv_s[there, :] += mm(
                jnp.concatenate([dscore, prob.astype(BF)], axis=1), beside_each
            )
            return query_grad + mm(kt_s[:, there], dscore)

        query_grad = lax.fori_loop(
            0, at, lambda n, total: back(n, total, False), jnp.zeros((HEAD, span), F32)
        )
        query_grad = back(at, query_grad, True)
        query_grad = jnp.concatenate([query_grad, query_grad], axis=0).T[:, :HEAD]
        query_grad = turned(
            query_grad * scale, angle_ref[here, : ROT // 2], -angle_ref[here, ROT // 2 :]
        ).astype(BF)
        gm_s[pl.ds(at * 2 * quarters, 2 * quarters), :, pl.ds(0, HEAD)] = query_grad.reshape(
            2 * quarters, quarter, HEAD
        )
        return carry

    lax.fori_loop(0, blocks // 4, backward, 0)
    stage_beyond(0)
    for nth in range(2, line - 1):
        stage_other(0, nth)
    lax.fori_loop(blocks // 4, blocks // 2, backward, 0)
    if line > 2:
        stage_other(0, line - 1)

    def finish_keys(at, carry):
        here = at_rows(at * block, block)
        keyvalue = jnp.concatenate(
            [
                turned(
                    dkv_s[here, :][:, :HEAD], angle_ref[here, : ROT // 2], -angle_ref[here, ROT // 2 :]
                ).astype(BF),
                dkv_s[here, :][:, HEAD:].astype(BF),
            ],
            axis=1,
        )
        gm_s[pl.ds(at * quarters, quarters), :, pl.ds(HEAD, 2 * HEAD)] = keyvalue.reshape(
            quarters, quarter, 2 * HEAD
        )
        return carry

    lax.fori_loop(0, blocks, finish_keys, 0)

    def unplace(at, carry):
        gmix_s[at_rows(at * quarter, quarter), :] = jnp.concatenate(
            [gm_s[order_ref[at]], jnp.zeros((quarter, HEAD), BF)], axis=1
        )
        return carry

    lax.fori_loop(0, tokens // quarter, unplace, 0)
    turn_over(((0, gmix_s),))
    for n, source in enumerate((gmix_s, gup_s)):
        columns = source.shape[1]

        def tally(at, total, source=source, columns=columns):
            return total + jnp.sum(
                source[at_rows(at * 256, 256), :].astype(F32).reshape(32, 8, columns), axis=0
            )

        total = lax.fori_loop(0, tokens // 256, tally, jnp.zeros((8, columns), F32))
        total = jnp.sum(total, axis=0, keepdims=True)
        for at in range(columns // 128):
            bias_s[pl.ds(n * 2 + at, 1), :] = total[:, at * 128 : (at + 1) * 128]
    bias_s[pl.ds(4, 4), :] = jnp.zeros((4, 128), F32)

    gain_s[...] = jnp.zeros_like(gain_s)
    shift_s[...] = jnp.zeros_like(shift_s)

    def gradients_att(turn, carry):
        slot = normed_columns.step(turn)
        here = at_rows(weights.chip(turn) * pair, pair)
        more = mm(turned_s[0], cols[0, slot]).T
        dsend[0, here, :] = (dsend[0, here, :].astype(F32) + more).astype(BF)
        weights.start_chip((0, 3), turn)
        return carry

    lax.fori_loop(0, chips, gradients_att, 0)
    product(1, 0)

    def second_sum(turn, carry):
        product(1, turn)
        stage_core(1, turn - 1)
        return carry

    lax.fori_loop(1, chips, second_sum, 0)
    stage_core(1, chips - 1)
    for n, source in enumerate((gain_s, shift_s)):
        total = jnp.sum(source[...], axis=0, keepdims=True)
        quarter_of = features // 4
        for at in range(4):
            nsend[0, pl.ds(n * 4 + at, 1), :] = total[:, at * quarter_of : (at + 1) * quarter_of]
    norm_copy(0).start()
    stage_other(1, 0)
    stage_line(0, 0)
    stage_line(0, 1)
    stage_other(1, 1)
    stage_line(0, 2)
    stage_line(1, 0)
    norm_copy(0).wait_recv()
    nsend[1] = nsend[0] + nfrom[0]
    norm_copy(1).start()
    stage_beyond(1)
    stage_other(1, 2)
    norm_copy(1).wait_recv()
    nsend[2] = nsend[1] + nfrom[1]
    norm_copy(2).start()
    stage_line(1, 1)
    stage_line(0, 3)
    norm_copy(2).wait_recv()
    nsend[3] = nsend[2] + nfrom[2]
    nline[a] = nsend[3]
    for other in range(line):
        pl.when(a != other)(lambda other=other: norm_line(other, False).start())
    stage_line(1, 2)
    stage_line(1, 3)
    for other in range(line):
        pl.when(a != other)(lambda other=other: norm_line(other, True).wait_recv())
    total = nline[0]
    for other in range(1, line):
        total += nline[other]
    norms_ref[...] = total

    for step in range(3):
        norm_copy(step).wait_send()
    for other in range(line):
        pl.when(a != other)(lambda other=other: norm_line(other, False).wait_send())
    for t in range(2):
        final(t, theirs).wait_recv()
        final(t, mine).wait_send()
        sums[t][...] = done[t]

        def left(at, carry, t=t):
            to_other(t, at * 2 + b).wait_send()
            pl.when(at != a)(lambda: to_up(t, at).wait_send())

            def also():
                to_other(t, at * 2 + 1 - b).wait_send()
                to_across(t, at).wait_send()

            shorter = at == place.far_first(shortcuts[0])
            for nth in shortcuts[1:]:
                shorter = shorter | (at == place.far_first(nth))
            pl.when(jnp.logical_not(shorter))(also)
            return carry

        lax.fori_loop(0, line, left, 0)
        for nth in shortcuts:
            to_beyond(t, nth).wait_send()
    weights.wait((0, 1, 2, 3))


def spread(
    order, inverse, attended, activated, upward, grad_att, qkvs, lse, attended_t, w_att, w_up, w_down,
    angles, normed, g_all, x_all,
):
    count = lax.axis_size("ctx")
    line = count // 4
    tokens, features = x_all.shape
    rows = tokens // count
    half = rows // 2
    chips = 2 * line
    weight_rows = w_att.shape[0] // count
    wide, hidden = w_att.shape[1], w_up.shape[1]
    hbm, vmem = pl.BlockSpec(memory_space=pl.ANY), pl.BlockSpec(memory_space=pltpu.VMEM)
    smem = pl.BlockSpec(memory_space=pltpu.SMEM)
    dma = pltpu.SemaphoreType.DMA
    own = jax.ShapeDtypeStruct((rows, features), BF)
    back = [
        jax.ShapeDtypeStruct((count, weight_rows, columns), BF) for columns in (wide, hidden, hidden)
    ]
    return pl.pallas_call(
        functools.partial(spread_kernel, line),
        out_shape=[own, own]
        + back
        + [
            jax.ShapeDtypeStruct((count, 8, 128), F32),
            jax.ShapeDtypeStruct((8, features // 4), F32),
            jax.ShapeDtypeStruct((8, features), F32),
        ],
        in_specs=[smem, smem] + [vmem] * 4 + [hbm] * 10,
        out_specs=[vmem, vmem, hbm, hbm, hbm, hbm, vmem, vmem],
        scratch_shapes=[
            pltpu.VMEM((count * weight_rows, wide + 2 * hidden), BF),
            pltpu.VMEM(upward.shape, F32),
            pltpu.VMEM(grad_att.shape, BF),
            pltpu.VMEM(qkvs.shape, BF),
            pltpu.VMEM(attended_t.shape, F32),
            pltpu.VMEM((2, 2 * rows, features), BF),
            pltpu.VMEM((2, chips, rows, features), BF),
            pltpu.VMEM((4, rows, features), BF),
            pltpu.VMEM((2, chips, half, features), BF),
            pltpu.VMEM((2, line, half, features), BF),
            pltpu.VMEM((2, 1, rows, features), BF),
            pltpu.VMEM((2, line + 1, half, features), BF),
            pltpu.VMEM((2, rows, features), BF),
            pltpu.VMEM((4, wide, tokens), BF),
            pltpu.VMEM((3, count * weight_rows, wide), BF),
            pltpu.VMEM((2, 3, tokens, 2 * weight_rows), BF),
            pltpu.VMEM((3, 2 * rows, features), BF),
            pltpu.VMEM((8, features), F32),
            pltpu.VMEM((8, features), F32),
            pltpu.VMEM((4, 8, features // 4), F32),
            pltpu.VMEM((3, 8, features // 4), F32),
            pltpu.VMEM((line, 8, features // 4), F32),
            pltpu.VMEM((8, 128), F32),
            pltpu.VMEM((tokens, wide), BF),
            pltpu.VMEM((tokens, hidden), BF),
            pltpu.VMEM((HEAD, tokens), BF),
            pltpu.VMEM((tokens, 2 * HEAD), F32),
            pltpu.VMEM((order.shape[0], tokens // order.shape[0], 3 * HEAD), BF),
            dma((7,)),
            dma((2, 3)),
            dma((3,)),
            dma((2, chips)),
            dma((4,)),
            pltpu.SemaphoreType.REGULAR,
            dma((2, chips)),
            dma((2, chips)),
            dma((2, line)),
            dma((2, line)),
            dma((2, 1)),
            dma((2, 1)),
            dma((2, line)),
            dma((2, line + 1)),
            dma((2,)),
            dma((2,)),
            dma((4, count)),
            dma((4, count)),
            dma((4,)),
            dma((3,)),
            dma((3,)),
            dma((line,)),
            dma((line,)),
        ],
        compiler_params=pltpu.CompilerParams(
            collective_id=2, has_side_effects=True, vmem_limit_bytes=63 * 1024 * 1024
        ),
    )(
        order, inverse, attended, activated, lse, angles, w_att, w_down, upward, grad_att, qkvs,
        attended_t, w_up, normed, g_all, x_all,
    )


def finish_kernel(
    tok_ref, cot_ref, gain_ref, bias_ref, branch_ref, normed_ref, datt_ref, dup_ref, ddown_ref,
    sums_ref, norms_ref, total_ref,
    out_ref, grad_ref, qkv_ref, wout_ref, up_ref, down_ref, qkvb_ref, upb_ref, gsum_ref, ssum_ref,
    bsum_ref,
):
    inputs = tok_ref[...].astype(F32)
    center = inputs - jnp.mean(inputs, axis=-1, keepdims=True)
    inv_std = lax.rsqrt(jnp.mean(center * center, axis=-1, keepdims=True) + EPS)
    unit = center * inv_std
    out_ref[...] = inputs + branch_ref[...].astype(F32) + bias_ref[...]
    grad_unit = normed_ref[...].astype(F32) * gain_ref[...]
    grad_ref[...] = cot_ref[...].astype(F32) + inv_std * (
        grad_unit
        - jnp.mean(grad_unit, axis=-1, keepdims=True)
        - unit * jnp.mean(grad_unit * unit, axis=-1, keepdims=True)
    )
    count, _, packed = datt_ref.shape
    width, hidden = packed // 4, dup_ref.shape[2]
    pieces = [datt_ref[owner].astype(F32) for owner in range(count)]

    def together(kind):
        return jnp.concatenate(
            [piece[:, kind * width : (kind + 1) * width] for piece in pieces], axis=1
        )

    for kind in range(3):
        qkv_ref[kind, :, :] = together(kind)
        at = kind * width
        qkvb_ref[kind : kind + 1, :] = jnp.concatenate(
            [
                sums_ref[owner, at // 128 : at // 128 + 1, at % 128 : at % 128 + width]
                for owner in range(count)
            ],
            axis=1,
        )
    wout_ref[...] = together(3)
    for owner in range(count):
        columns = pl.ds(owner * hidden, hidden)
        up_ref[:, columns] = dup_ref[owner].astype(F32)
        down_ref[:, columns] = ddown_ref[owner].astype(F32)
        for at in range(hidden // 128):
            upb_ref[:, pl.ds(owner * hidden + at * 128, 128)] = sums_ref[owner, 2 + at : 3 + at, :]
    wide = norms_ref.shape[1]
    for at in range(4):
        gsum_ref[:, pl.ds(at * wide, wide)] = norms_ref[at : at + 1, :]
        ssum_ref[:, pl.ds(at * wide, wide)] = norms_ref[4 + at : 5 + at, :]
    bsum_ref[...] = total_ref[0:1, :]


def finish(tokens, cotangent, gain, bias, branches, own_normed, d_att, d_up, d_down, sums, norms, total):
    count, weight_rows, packed = d_att.shape
    rows, features = tokens.shape
    width, hidden = packed // 4, d_up.shape[2]
    owners = max(128 // width, count // 2)
    steps = count // owners
    by_rows = pl.BlockSpec((rows // steps, features), lambda at: (at, 0))
    line = pl.BlockSpec((1, features), lambda at: (0, 0))

    def whole(array):
        return pl.BlockSpec(array.shape, lambda at: (0,) * array.ndim)

    def by_owner(array):
        return pl.BlockSpec((owners, *array.shape[1:]), lambda at: (at, 0, 0))

    def by_columns(*lead):
        return lambda columns: pl.BlockSpec(
            (*lead, owners * columns), lambda at: (*(0,) * len(lead), at)
        )

    shape = jax.ShapeDtypeStruct
    return pl.pallas_call(
        finish_kernel,
        grid=(steps,),
        out_shape=[
            shape(tokens.shape, F32),
            shape(tokens.shape, F32),
            shape((3, weight_rows, count * width), F32),
            shape((weight_rows, count * width), F32),
            shape((weight_rows, count * hidden), F32),
            shape((weight_rows, count * hidden), F32),
            shape((3, count * width), F32),
            shape((1, count * hidden), F32),
            shape((1, features), F32),
            shape((1, features), F32),
            shape((1, features), F32),
        ],
        in_specs=[by_rows, by_rows, line, line, by_rows, by_rows]
        + [by_owner(array) for array in (d_att, d_up, d_down, sums)]
        + [whole(norms), whole(total)],
        out_specs=[
            by_rows,
            by_rows,
            by_columns(3, weight_rows)(width),
            by_columns(weight_rows)(width),
            by_columns(weight_rows)(hidden),
            by_columns(weight_rows)(hidden),
            by_columns(3)(width),
            by_columns(1)(hidden),
            line,
            line,
            line,
        ],
        compiler_params=pltpu.CompilerParams(vmem_limit_bytes=63 * 1024 * 1024),
    )(
        tokens, cotangent, gain[None], bias[None], branches, own_normed, d_att, d_up, d_down, sums,
        norms, total,
    )


def gelu_tanh(value):
    return jax.nn.gelu(value, approximate=True)


def local(
    tokens, block_order, ln_gain, ln_bias, qkv_weight, qkv_bias, out_weight, fc1_weight, fc1_bias,
    fc2_weight, out_bias, cotangent,
):
    devices = lax.axis_size("ctx")
    myself = lax.axis_index("ctx")
    heads_here = qkv_weight.shape[2] // HEAD
    columns = math.gcd(devices, heads_here)
    mine = myself % columns
    width = qkv_weight.shape[2] // columns
    hidden = fc1_weight.shape[1] // columns
    if devices == columns and columns % 8 == 0 and width == HEAD and lax.axis_size("tp") == 2:
        freqs = 10000.0 ** (-np.arange(0, ROT, 2, dtype=np.float32) / ROT)
        angles = np.arange(devices * tokens.shape[0], dtype=np.float32)[:, None] * freqs[None, :]
        angles = jnp.asarray(np.concatenate([np.cos(angles), np.sin(angles)], axis=1), F32)
        (
            x_all, g_all, w_att, w_up, w_down, normed, qkvs, lse, attended_t, attended, activated,
            upward, grad_att, inverse,
        ) = collect(
            block_order, tokens, cotangent, qkv_weight, out_weight, fc1_weight, fc2_weight,
            ln_gain[None], ln_bias[None], qkv_bias, fc1_bias[None], angles,
        )
        parts = spread(
            block_order, inverse, attended, activated, upward, grad_att, qkvs, lse, attended_t, w_att,
            w_up, w_down, angles, normed, g_all, x_all,
        )
    else:
        bias_att = lax.dynamic_slice_in_dim(qkv_bias, mine * width, width, 1).reshape(-1)
        bias_att = jnp.concatenate([bias_att, jnp.zeros((width,), F32)])[None]
        bias_up = lax.dynamic_slice_in_dim(fc1_bias, mine * hidden, hidden, 0)[None]
        parts = by_groups(
            tokens, block_order, ln_gain, ln_bias, qkv_weight, out_weight, fc1_weight, fc2_weight,
            cotangent, bias_att, bias_up,
        )
    (
        output, input_grad, qkv_grad, out_grad, fc1_grad, fc2_grad, qkv_sums, fc1_sums, gain_sum,
        shift_sum, g_sum,
    ) = finish(tokens, cotangent, ln_gain, out_bias, *parts)
    return (
        output, input_grad, gain_sum[0], shift_sum[0], qkv_grad.transpose(1, 0, 2), qkv_sums, out_grad,
        fc1_grad, fc1_sums[0], fc2_grad, g_sum[0],
    )


def by_groups(
    tokens, block_order, ln_gain, ln_bias, qkv_weight, out_weight, fc1_weight, fc2_weight, cotangent,
    bias_att, bias_up,
):
    devices = lax.axis_size("ctx")
    myself = lax.axis_index("ctx")
    rows_here = tokens.shape[0]
    weight_rows = qkv_weight.shape[0]
    half = devices * rows_here // block_order.shape[0]
    columns = math.gcd(devices, qkv_weight.shape[2] // HEAD)
    groups = devices // columns
    width, hidden = qkv_weight.shape[2] // columns, fc1_weight.shape[1] // columns
    count = columns * rows_here
    side = [[r * columns + c for c in range(columns)] for r in range(groups)]
    across = [[r * columns + c for r in range(groups)] for c in range(columns)]

    def gathered(value, among):
        return lax.all_gather(value, "ctx", axis=0, tiled=True, axis_index_groups=among)

    def scattered(value, among):
        return lax.psum_scatter(
            value, "ctx", scatter_dimension=0, tiled=True, axis_index_groups=among
        )

    def exchanged(value):
        return lax.all_to_all(value, "ctx", split_axis=0, concat_axis=0, tiled=True)

    x_all, g_all = gathered(tokens, side), gathered(cotangent, side)
    kinds = jnp.concatenate([qkv_weight, out_weight[:, None]], axis=1)
    kinds = kinds.reshape(weight_rows, 4, columns, width).transpose(2, 0, 1, 3)
    packed = jnp.concatenate(
        [
            kinds.reshape(columns, weight_rows, 4 * width),
            fc1_weight.reshape(weight_rows, columns, hidden).transpose(1, 0, 2),
            fc2_weight.reshape(weight_rows, columns, hidden).transpose(1, 0, 2),
        ],
        axis=2,
    )
    packed = exchanged(jnp.tile(packed, (groups, 1, 1))).reshape(devices * weight_rows, -1)
    w_att, w_up, w_down = jnp.split(packed, [4 * width, 4 * width + hidden], axis=1)

    inputs = x_all.astype(F32)
    center = inputs - jnp.mean(inputs, axis=-1, keepdims=True)
    inv_std = lax.rsqrt(jnp.mean(center * center, axis=-1, keepdims=True) + EPS)
    unit = center * inv_std
    normed = (unit * ln_gain + ln_bias).astype(BF)
    upward = mm(normed, w_up) + bias_up
    activated, gelu_back = jax.vjp(gelu_tanh, upward)
    activated = activated.astype(BF)
    grad_up = gelu_back(mm(g_all, w_down))[0].astype(BF)
    places = (block_order[:, None] * half + jnp.arange(half, dtype=jnp.int32)[None, :]).reshape(-1)
    attended, grad_mixed = attention_blocks(
        lax.dynamic_slice_in_dim(places, (myself // columns) * count, count),
        places,
        mm(normed, w_att) + bias_att,
        mm(g_all, w_att),
        lambda value: gathered(value, across),
        lambda value: scattered(value, across),
    )
    out_part = (mm(attended, w_att, NT) + mm(activated, w_down, NT)).astype(BF)
    normed_wide = mm(grad_mixed, w_att, NT) + mm(grad_up, w_up, NT)
    branches, own_normed = lax.psum(
        (scattered(out_part, side), scattered(normed_wide.astype(BF), side)), "tp"
    )
    back = jnp.concatenate(
        [
            (mm(normed, grad_mixed, TN) + mm(g_all, attended, TN)).astype(BF),
            mm(normed, grad_up, TN).astype(BF),
            mm(g_all, activated, TN).astype(BF),
        ],
        axis=1,
    )
    back = exchanged(back.reshape(devices, weight_rows, -1))
    back = jnp.sum(back.reshape(groups, columns, weight_rows, -1).astype(F32), axis=0)
    sums = jnp.concatenate(
        [jnp.sum(grad_mixed.astype(F32), axis=0), jnp.sum(grad_up.astype(F32), axis=0)]
    ).reshape(-1, 128)
    sums = jnp.pad(sums, ((0, 8 - sums.shape[0]), (0, 0)))
    sums = gathered(lax.psum(sums, "ctx", axis_index_groups=across)[None], side)
    norms = jnp.stack([jnp.sum(unit * normed_wide, axis=0), jnp.sum(normed_wide, axis=0)])
    norms = lax.psum(norms, ("ctx", "tp")).reshape(8, -1)
    total = lax.psum(jnp.sum(g_all.astype(F32), axis=0), "ctx", axis_index_groups=across)[None]
    return (
        branches, own_normed, *jnp.split(back, [4 * width, 4 * width + hidden], axis=2), sums, norms,
        total,
    )


def solution(mesh):
    rows, tall = P("ctx", None), P("ctx", "tp")
    kinds, bias = P("ctx", None, "tp"), P(None, "tp")
    return jax.shard_map(
        local,
        mesh=mesh,
        in_specs=(rows, P(), P(), P(), kinds, bias, tall, tall, P("tp"), tall, P(), rows),
        out_specs=(rows, rows, P(), P(), kinds, bias, tall, tall, P("tp"), tall, P()),
        check_vma=False,
    )
```

```python
import functools
import math

import jax
import jax.numpy as jnp
import numpy as np
from jax import lax
from jax.experimental import pallas as pl
from jax.experimental.pallas import tpu as pltpu
from jax.sharding import PartitionSpec as P

HEAD = 64
ROT = 32
EPS = 1e-05
NEG = -1e30
BF = jnp.bfloat16
F32 = jnp.float32
NN = (((1,), (0,)), ((), ()))
NT = (((1,), (1,)), ((), ()))
TN = (((0,), (0,)), ((), ()))


def mm(left, right, dims=NN):
    return lax.dot_general(left, right, dims, preferred_element_type=F32)


def tables(positions, width):
    freqs = 10000.0 ** (-(jnp.arange(width // 2, dtype=F32) * 2.0) / width)
    angles = positions.astype(F32)[:, None] * freqs[None, :]
    return (jnp.cos(angles), jnp.sin(angles))


def turned(value, cosine, sine):
    half = cosine.shape[-1]
    first, second = value[..., :half], value[..., half : 2 * half]
    return jnp.concatenate(
        [first * cosine - second * sine, second * cosine + first * sine, value[..., 2 * half :]],
        axis=-1,
    )


def attention_blocks(own_place, places, mixed, grad_att, gather, scatter):
    count, width = grad_att.shape[0], grad_att.shape[1] // 4
    heads = width // HEAD
    scale = 1.0 / math.sqrt(HEAD)
    grad_att = grad_att[:, 3 * width :].astype(BF)
    cosine, sine = tables(own_place, ROT)
    cosine, sine = cosine[:, None, :], sine[:, None, :]
    kinds = [mixed[:, kind * width : (kind + 1) * width].reshape(count, heads, HEAD) for kind in range(3)]
    queries = turned(kinds[0], cosine, sine).astype(BF)
    keys = gather(turned(kinds[1], cosine, sine).astype(BF))
    values = gather(kinds[2].astype(BF))
    grad_att = grad_att.reshape(count, heads, HEAD)
    block = math.gcd(128, count)

    def one(at, carry):
        key_grad, value_grad, attended, query_grad = carry
        query = lax.dynamic_slice_in_dim(queries, at * block, block)
        grad = lax.dynamic_slice_in_dim(grad_att, at * block, block)
        place = lax.dynamic_slice_in_dim(own_place, at * block, block)
        visible = (place[:, None] >= places[None, :])[None]
        scores = jnp.einsum("qhe,khe->hqk", query, keys, preferred_element_type=F32) * scale
        scores = jnp.where(visible, scores, NEG)
        top = jnp.max(scores, axis=-1, keepdims=True)
        expo = jnp.where(visible, jnp.exp(scores - top), 0.0)
        total = jnp.sum(expo, axis=-1)
        summed = jnp.einsum("hqk,khe->qhe", expo.astype(BF), values, preferred_element_type=F32)
        attend = summed / jnp.transpose(total)[..., None]
        delta = jnp.transpose(jnp.sum(grad.astype(F32) * attend, axis=-1))
        prob = expo / total[..., None]
        dprob = jnp.einsum("qhe,khe->hqk", grad, values, preferred_element_type=F32)
        dscore = (prob * (dprob - delta[..., None])).astype(BF)
        part_q = jnp.einsum("hqk,khe->qhe", dscore, keys, preferred_element_type=F32) * scale
        key_grad += jnp.einsum("hqk,qhe->khe", dscore, query, preferred_element_type=F32) * scale
        value_grad += jnp.einsum("hqk,qhe->khe", prob.astype(BF), grad, preferred_element_type=F32)
        attended = lax.dynamic_update_slice_in_dim(attended, attend.astype(BF), at * block, 0)
        query_grad = lax.dynamic_update_slice_in_dim(query_grad, part_q, at * block, 0)
        return (key_grad, value_grad, attended, query_grad)

    zeros = jnp.zeros(keys.shape, F32)
    own = jnp.zeros((count, heads, HEAD), F32)
    key_grad, value_grad, attended, query_grad = lax.fori_loop(
        0, count // block, one, (zeros, zeros, own.astype(BF), own)
    )
    key_grad, value_grad = scatter(key_grad), scatter(value_grad)
    grad_mixed = jnp.concatenate(
        [
            turned(query_grad, cosine, -sine).astype(BF).reshape(count, width),
            turned(key_grad, cosine, -sine).astype(BF).reshape(count, width),
            value_grad.astype(BF).reshape(count, width),
            jnp.zeros((count, width), BF),
        ],
        axis=1,
    )
    attended = jnp.concatenate(
        [jnp.zeros((count, 3 * width), BF), attended.reshape(count, width)], axis=1
    )
    return attended, grad_mixed


MESH = pl.DeviceIdType.MESH
UP, DOWN, ACROSS, OTHER, CORE = range(5)


def at_rows(start, size):
    return pl.ds(pl.multiple_of(start, size), size)


def remote(source, target, send, receive, device):
    return pltpu.make_async_remote_copy(
        src_ref=source, dst_ref=target, send_sem=send, recv_sem=receive, device_id=device,
        device_id_type=MESH,
    )


class Place:
    def __init__(self, line):
        self.line = line
        self.me = lax.axis_index("ctx")
        self.y = lax.axis_index("tp")
        self.a, self.b, self.c = self.me // 4, (self.me // 2) % 2, self.me % 2
        a, b, c, y = self.a, self.b, self.c, self.y
        self.device = {
            UP: (self.index(jnp.minimum(a + 1, line - 1), b, c), y),
            DOWN: (self.index(jnp.maximum(a - 1, 0), b, c), y),
            ACROSS: (self.index(a, 1 - b, c), y),
            OTHER: (self.me, 1 - y),
            CORE: (self.index(a, b, 1 - c), y),
        }

    def index(self, a, b, c):
        return a * 4 + b * 2 + c

    def far_first(self, turn):
        line = self.line
        high, low = line - 1 - turn, turn
        high = jnp.where(high <= self.a, high - 1, high)
        low = jnp.where(low >= self.a, low + 1, low)
        other = jnp.where(self.a < line // 2, high, low)
        return jnp.where(turn == line - 1, self.a, other)

    def greet(self):
        barrier = pltpu.get_barrier_semaphore()
        count = 4 * self.line

        def signal(step, carry):
            pl.semaphore_signal(
                barrier, inc=1, device_id=(lax.rem(self.me + step, count), self.y), device_id_type=MESH
            )
            return carry

        lax.fori_loop(1, count, signal, 0)
        pl.semaphore_signal(barrier, inc=1, device_id=self.device[OTHER], device_id_type=MESH)
        pl.semaphore_wait(barrier, count)


def flipped(value, mask, bits):
    result = 0
    for bit in range(bits):
        one, other = (value // 2**bit) % 2, (mask // 2**bit) % 2
        result = result + 2**bit * (one + other - 2 * one * other)
    return result


class Exchange:
    def __init__(self, place, chunk, received, send, receive, own):
        self.place, self.chunk, self.received = place, chunk, received
        self.send, self.receive, self.own = send, receive, own
        self.count = 4 * place.line
        self.bits = self.count.bit_length() - 1
        self.partners = [self.partner(mask) for mask in range(self.count - 1, 0, -1)]

    def partner(self, mask):
        return mask, flipped(self.place.me, mask, self.bits)

    def chip(self, turn):
        return flipped(self.place.me // 2, self.count // 2 - 1 - turn, self.bits - 1)

    def start_chip(self, pieces, turn):
        mask = self.count - 2 - 2 * turn
        for n in pieces:
            self.copy(self.partner(mask + 1), n, False).start()
            pl.when(mask > 0)(lambda n=n: self.copy(self.partner(mask), n, False).start())
            pl.when(mask == 0)(lambda n=n: self.kept(n).start())

    def copy(self, partner, n, came):
        mask, to = partner
        return remote(
            self.chunk(n, to), self.received(n, to if came else self.place.me), self.send.at[n, mask],
            self.receive.at[n, mask], (to, self.place.y),
        )

    def kept(self, n):
        me = self.place.me
        return pltpu.make_async_copy(self.chunk(n, me), self.received(n, me), self.own.at[n])

    def keep(self, pieces):
        for n in pieces:
            self.kept(n).start()

    def start(self, pieces):
        for partner in self.partners:
            for n in pieces:
                self.copy(partner, n, False).start()

    def wait(self, pieces):
        for partner in self.partners:
            for n in pieces:
                self.copy(partner, n, True).wait()
        for n in pieces:
            self.kept(n).wait()


def row_stats(load, rows, features, piece):
    mean = jnp.zeros((rows, 1), F32)
    for at in range(0, features, piece):
        mean += jnp.sum(load(at), axis=1, keepdims=True)
    mean = mean / features
    spread = jnp.zeros((rows, 1), F32)
    for at in range(0, features, piece):
        center = load(at) - mean
        spread += jnp.sum(center * center, axis=1, keepdims=True)
    return mean, lax.rsqrt(spread / features + EPS)


class Stream:
    def __init__(self, copy, depth, total):
        self.copy, self.depth, self.total = copy, depth, total

    def prime(self):
        for at in range(min(self.depth - 1, self.total)):
            self.copy(at, at).start()

    def step(self, at):
        slot = lax.rem(at, self.depth)
        self.copy(at, slot).wait()
        later = at + self.depth - 1

        @pl.when(later < self.total)
        def _():
            self.copy(later, lax.rem(later, self.depth)).start()

        return slot


def gelu_parts(value):
    inner = math.sqrt(2.0 / math.pi) * (value + 0.044715 * value * value * value)
    return jnp.tanh(inner)


def seen(start_key, start_query, keys, queries):
    key = start_key + lax.broadcasted_iota(jnp.int32, (keys, queries), 0)
    return key <= start_query + lax.broadcasted_iota(jnp.int32, (keys, queries), 1)


def collect_kernel(
    line, order_ref, tok_ref, cot_ref, qkv_ref, out_ref, up_ref, down_ref, gain_ref,
    shift_ref, batt_ref, bup_ref, angle_ref,
    x_out, g_out, watt_out, wup_out, wdown_ref, normed_out, qkvs_out, lse_out, attt_out, att_out,
    act_out, upward_out, gatt_out, inverse_ref,
    x_ref, g_ref, watt_s, wup_s, normed_s, qkvs_ref, lse_ref, attt_ref, att_ref, act_ref, upward_ref,
    gatt_ref, packed, mixed_s, k_s, vt_s, st, att_s,
    send, receive, own_sem, wsend, wreceive, wlocal, out_sem,
):
    place = Place(line)
    a, b, c, y = place.a, place.b, place.c, place.y
    sources, targets = (tok_ref, cot_ref), (x_ref, g_ref)
    rows, features = tok_ref.shape
    half = rows // 2
    weight_rows = up_ref.shape[0]
    tokens = x_ref.shape[0]
    hidden = wup_s.shape[1]
    width = watt_s.shape[1] // 4
    block = 2 * rows
    blocks = tokens // block
    piece = 512
    place.greet()
    shipped = []

    def ship(source, target):
        shipped.append(pltpu.make_async_copy(source, target, out_sem.at[len(shipped)]))
        shipped[-1].start()

    def copy(t, kind, owner, part, own=False):
        target = targets[t].at[at_rows(owner * rows + part * half, half)]
        source = sources[t].at[at_rows(part * half, half)] if own else target
        return remote(
            source, target, send.at[t, kind, owner, part], receive.at[t, owner, part], place.device[kind]
        )

    def landed(t, owner, part):
        copy(t, CORE, owner, part).wait_recv()

    def along(t, distance):
        for sign in (0,) if distance == 0 else (1, -1):
            at = a + sign * distance

            def pass_on(sign=sign, at=at):
                owner = place.index(at, b, c)
                own = distance == 0
                if not own:
                    landed(t, owner, y)
                if sign <= 0:
                    pl.when(a < line - 1)(lambda: copy(t, UP, owner, y, own).start())
                if sign >= 0:
                    pl.when(a > 0)(lambda: copy(t, DOWN, owner, y, own).start())
                copy(t, ACROSS, owner, y, own).start()
                if not own:
                    copy(t, OTHER, owner, y).start()
                copy(t, CORE, owner, y, own).start()
                if own:
                    copy(t, CORE, owner, 1 - y, own).start()

            if distance == 0:
                pass_on()
            else:
                pl.when((at >= 0) & (at < line))(pass_on)

    def beside(t, distance):
        for sign in (0,) if distance == 0 else (1, -1):
            at = a + sign * distance

            def pass_on(at=at):
                owner = place.index(at, 1 - b, c)
                landed(t, owner, y)
                copy(t, OTHER, owner, y).start()
                copy(t, CORE, owner, y).start()

            pl.when((at >= 0) & (at < line))(pass_on)

    def from_other(t):
        for distance in range(line):
            for column in (b, 1 - b):
                for sign in (0,) if distance == 0 else (1, -1):
                    at = a + sign * distance

                    def pass_on(at=at, column=column):
                        owner = place.index(at, column, c)
                        landed(t, owner, 1 - y)
                        copy(t, CORE, owner, 1 - y).start()

                    if distance == 0 and column is b:
                        continue
                    pl.when((at >= 0) & (at < line))(pass_on)

    def own_copy(t):
        return pltpu.make_async_copy(
            sources[t], targets[t].at[at_rows(place.me * rows, rows)], own_sem.at[t]
        )

    def complete(t):
        def came(chip, carry):
            for part in range(2):
                landed(t, chip * 2 + (1 - c), part)
            return carry

        lax.fori_loop(0, 2 * line, came, 0)
        own_copy(t).wait()

    def chunk(n, to):
        if n == 0:
            return packed.at[to]
        return (up_ref, down_ref)[n - 1].at[:, at_rows(to * hidden, hidden)]

    def received(n, owner):
        return (watt_s, wup_s, wdown_ref)[n].at[at_rows(owner * weight_rows, weight_rows)]

    weights = Exchange(place, chunk, received, wsend, wreceive, wlocal)

    own_copy(0).start()
    own_copy(1).start()
    along(0, 0)
    for owner in range(4 * line):
        columns = pl.ds(owner * width, width)
        packed[owner, :, :] = jnp.concatenate(
            [qkv_ref[kind, :, columns] for kind in range(3)] + [out_ref[:, columns]], axis=1
        )
    weights.keep((0, 1, 2))
    ordered = [order_ref[at] for at in range(order_ref.shape[0])]

    def invert(wanted, carry):
        found = jnp.int32(0)
        for at, held in enumerate(ordered):
            found = jnp.where(held == wanted, at, found)
        inverse_ref[wanted] = found
        return carry

    for distance in range(1, line):
        along(0, distance)
        if distance == line - 1:
            along(1, 0)
        beside(0, distance - 1)
    beside(0, line - 1)
    lax.fori_loop(0, len(ordered), invert, 0)
    for distance in range(1, line - 1):
        along(1, distance)
        if distance == 1:
            weights.start((0,))
        beside(1, distance - 1)
    from_other(0)
    complete(0)
    weights.wait((0,))
    ship(x_ref, x_out)
    ship(watt_s, watt_out)

    quarter = tokens // inverse_ref.shape[0]
    quarters = block // quarter

    shared = batt_ref[:, at_rows(place.me // 2 * 2 * width, 2 * width)]
    shared = jnp.where(c == 0, shared[:, :width], shared[:, width:])
    bias_att = jnp.concatenate(
        [shared[kind : kind + 1] for kind in range(3)] + [jnp.zeros((1, width), F32)], axis=1
    )
    bias_up = bup_ref[:, at_rows(place.me * hidden, hidden)]

    def project(at, carry):
        here = at_rows(at * block, block)

        def load(start):
            return x_ref[here, pl.ds(start, piece)].astype(F32)

        mean, inv_std = row_stats(load, block, features, piece)
        for start in range(0, features, piece):
            part = pl.ds(start, piece)
            unit = (load(start) - mean) * inv_std
            normed_s[here, part] = (unit * gain_ref[:, part] + shift_ref[:, part]).astype(BF)
        mixed = mm(normed_s[here, :], watt_s[...]) + bias_att
        mixed_s[pl.ds(at * quarters, quarters)] = mixed.reshape(quarters, quarter, 4 * width)
        return carry

    lax.fori_loop(0, blocks // 2, project, 0)
    along(1, line - 1)
    beside(1, line - 2)
    weights.start((1,))
    lax.fori_loop(blocks // 2, blocks, project, 0)
    ship(normed_s, normed_out)
    beside(1, line - 1)
    weights.start((2,))

    wide = 2 * block
    scale = 1.0 / math.sqrt(HEAD)

    def prepare(at, carry):
        here = at_rows(at * block, block)
        mixed = jnp.concatenate(
            [mixed_s[inverse_ref[at * quarters + n]] for n in range(quarters)], axis=0
        )
        cosine, sine = angle_ref[here, : ROT // 2], angle_ref[here, ROT // 2 :]
        query = turned(mixed[:, :HEAD], cosine, sine).astype(BF) * jnp.asarray(scale, BF)
        key = turned(mixed[:, HEAD : 2 * HEAD], cosine, sine)
        value = mixed[:, 2 * HEAD : 3 * HEAD]
        k_s[here, :] = key.astype(BF)
        vt_s[:, here] = jnp.concatenate([value, value], axis=1).T[:HEAD].astype(BF)
        qkvs_ref[here, :] = jnp.concatenate(
            [query, key.astype(BF), value.astype(BF), jnp.zeros_like(query)], axis=1
        )
        return carry

    lax.fori_loop(0, blocks, prepare, 0)

    def forward(at, carry):
        here = at_rows(at * block, block)
        query = qkvs_ref[here, :][:, :HEAD]

        def scored(place_at, top, masked):
            there = at_rows(place_at * wide, wide)
            scores = mm(k_s[there, :], query, NT)
            if masked:
                scores = jnp.where(seen(place_at * wide, at * block, wide, block), scores, NEG)
            st[there, :] = scores
            return jnp.maximum(top, jnp.max(scores.reshape(wide // 8, 8, block), axis=0))

        last = at // 2
        top = lax.fori_loop(
            0, last, lambda n, top: scored(n, top, False), jnp.full((8, block), NEG, F32)
        )
        top = jnp.max(scored(last, top, True), axis=0, keepdims=True)

        def weighed(place_at, state):
            total, summed = state
            there = at_rows(place_at * wide, wide)
            expo = jnp.exp(st[there, :] - top)
            total = total + jnp.sum(expo.reshape(wide // 8, 8, block), axis=0)
            return (total, summed + mm(vt_s[:, there], expo.astype(BF)))

        total, summed = lax.fori_loop(
            0, last + 1, weighed, (jnp.zeros((8, block), F32), jnp.zeros((HEAD, block), F32))
        )
        total = jnp.sum(total, axis=0, keepdims=True)
        attended = summed * (1.0 / total)
        lse_ref[:, here] = jnp.broadcast_to(top + jnp.log(total), (8, block))
        attt_ref[:, here] = attended
        both = jnp.concatenate([attended, attended], axis=0).T.astype(BF)
        att_s[pl.ds(at * quarters, quarters)] = both.reshape(quarters, quarter, 2 * HEAD)
        return carry

    lax.fori_loop(0, blocks, forward, 0)
    for source, target in ((qkvs_ref, qkvs_out), (lse_ref, lse_out), (attt_ref, attt_out)):
        ship(source, target)

    def unplace(at, carry):
        attended = att_s[order_ref[at]][:, HEAD:]
        att_ref[at_rows(at * quarter, quarter), :] = jnp.concatenate(
            [jnp.zeros((quarter, 3 * HEAD), BF), attended], axis=1
        )
        return carry

    lax.fori_loop(0, tokens // quarter, unplace, 0)
    ship(att_ref, att_out)
    from_other(1)
    complete(1)
    ship(g_ref, g_out)

    def grad_in(at, carry):
        grad = mm(g_ref[at_rows(at * block, block), :], watt_s[...]).astype(BF)
        gatt_ref[pl.ds(at * quarters, quarters)] = grad.reshape(quarters, quarter, 4 * width)
        return carry

    lax.fori_loop(0, blocks, grad_in, 0)
    ship(gatt_ref, gatt_out)
    weights.wait((1,))
    ship(wup_s, wup_out)

    def feed(at, carry):
        here = at_rows(at * block, block)
        upward = mm(normed_s[here, :], wup_s[...]) + bias_up
        upward_ref[here, :] = upward
        act_ref[here, :] = (0.5 * upward * (1.0 + gelu_parts(upward))).astype(BF)
        return carry

    lax.fori_loop(0, blocks, feed, 0)
    ship(upward_ref, upward_out)
    ship(act_ref, act_out)
    for t in range(2):

        def left(at, carry, t=t):
            owner, beyond = place.index(at, b, c), place.index(at, 1 - b, c)
            pl.when((at <= a) & (a < line - 1))(lambda: copy(t, UP, owner, y).wait_send())
            pl.when((at >= a) & (a > 0))(lambda: copy(t, DOWN, owner, y).wait_send())
            copy(t, ACROSS, owner, y).wait_send()
            pl.when(at != a)(lambda: copy(t, OTHER, owner, y).wait_send())
            copy(t, OTHER, beyond, y).wait_send()
            for part in range(2):
                copy(t, CORE, owner, part).wait_send()
                copy(t, CORE, beyond, part).wait_send()
            return carry

        lax.fori_loop(0, line, left, 0)
    weights.wait((2,))
    for result in shipped:
        result.wait()


def collect(
    order, tokens, cotangent, qkv_weight, out_weight, fc1_weight, fc2_weight, gain, shift, bias_att,
    bias_up, angles,
):
    rows, features = tokens.shape
    weight_rows = fc1_weight.shape[0]
    count = lax.axis_size("ctx")
    line, width, hidden = count // 4, qkv_weight.shape[2] // count, fc1_weight.shape[1] // count
    total, depth = count * rows, count * weight_rows
    halves = order.shape[0]
    hbm, vmem = pl.BlockSpec(memory_space=pl.ANY), pl.BlockSpec(memory_space=pltpu.VMEM)
    smem = pl.BlockSpec(memory_space=pltpu.SMEM)
    dma = pltpu.SemaphoreType.DMA
    shape = jax.ShapeDtypeStruct
    return pl.pallas_call(
        functools.partial(collect_kernel, line),
        out_shape=[
            shape((total, features), BF),
            shape((total, features), BF),
            shape((depth, 4 * width), BF),
            shape((depth, hidden), BF),
            shape((depth, hidden), BF),
            shape((total, features), BF),
            shape((total, 4 * width), BF),
            shape((8, total), F32),
            shape((width, total), F32),
            shape((total, 4 * width), BF),
            shape((total, hidden), BF),
            shape((total, hidden), F32),
            shape((halves, total // halves, 4 * width), BF),
            shape((halves,), jnp.int32),
        ],
        in_specs=[smem, hbm, hbm, vmem, vmem, hbm, hbm] + [vmem] * 5,
        out_specs=[hbm] * 13 + [smem],
        scratch_shapes=[
            pltpu.VMEM((total, features), BF),
            pltpu.VMEM((total, features), BF),
            pltpu.VMEM((depth, 4 * width), BF),
            pltpu.VMEM((depth, hidden), BF),
            pltpu.VMEM((total, features), BF),
            pltpu.VMEM((total, 4 * width), BF),
            pltpu.VMEM((8, total), F32),
            pltpu.VMEM((width, total), F32),
            pltpu.VMEM((total, 4 * width), BF),
            pltpu.VMEM((total, hidden), BF),
            pltpu.VMEM((total, hidden), F32),
            pltpu.VMEM((halves, total // halves, 4 * width), BF),
            pltpu.VMEM((count, weight_rows, 4 * width), BF),
            pltpu.VMEM((halves, total // halves, 4 * width), F32),
            pltpu.VMEM((total, width), BF),
            pltpu.VMEM((width, total), BF),
            pltpu.VMEM((total, 2 * rows), F32),
            pltpu.VMEM((halves, total // halves, 2 * width), BF),
            dma((2, 5, count, 2)),
            dma((2, count, 2)),
            dma((2,)),
            dma((3, count)),
            dma((3, count)),
            dma((3,)),
            dma((12,)),
        ],
        compiler_params=pltpu.CompilerParams(
            collective_id=1, has_side_effects=True, vmem_limit_bytes=60 * 1024 * 1024
        ),
    )(
        order, tokens, cotangent, qkv_weight.transpose(1, 0, 2), out_weight, fc1_weight,
        fc2_weight, gain, shift, bias_att, bias_up, angles,
    )


def spread_kernel(
    line, order_ref, inverse_ref, att_ref, act_ref, lse_ref, angle_ref,
    watt_in, wdown_in, upward_in, gatt_in, qkvs_in, attt_in, wup_in, normed_ref, g_ref, x_ref,
    sum_ref, gsum_ref, ratt_ref, rup_ref, rdown_ref, rbias_ref, norms_ref, total_ref,
    weights_s, upward_ref, gatt_ref, qkvs_ref, attt_ref,
    fresh, own, from_core, from_other, from_across, from_beyond, from_line, done, turned_s, dsend, cols,
    buf, gain_s, shift_s, nsend, nfrom, nline, bias_s, gmix_s, gup_s, kt_s, dkv_s, gm_s,
    in_sem, cols_sem, buf_sem, csend, creceive, credit, ysend, yreceive, xsend, xreceive, bsend,
    breceive, zsend, zreceive, fsend, freceive, wsend, wreceive, wlocal, nsend_sem, nreceive, lsend,
    lreceive,
):
    place = Place(line)
    a, b, c, y = place.a, place.b, place.c, place.y
    sums = (sum_ref, gsum_ref)
    rows, features = own.shape[2:]
    half = rows // 2
    chips = 2 * line
    tokens = att_ref.shape[0]
    block = 2 * rows
    blocks = tokens // block
    weight_rows = dsend.shape[1] // (2 * chips)
    pair = 2 * weight_rows
    piece = 512
    ring = from_core.shape[0]
    shortcuts = tuple(range(line - from_beyond.shape[1], line))
    place.greet()
    wide, hidden = watt_in.shape[1], wup_in.shape[1]
    late = [
        pltpu.make_async_copy(source, target, in_sem.at[n])
        for n, (source, target) in enumerate(
            (
                (wdown_in, weights_s.at[:, pl.ds(0, hidden)]),
                (watt_in, weights_s.at[:, pl.ds(hidden, wide)]),
                (upward_in, upward_ref),
                (gatt_in, gatt_ref),
                (qkvs_in, qkvs_ref),
                (attt_in, attt_ref),
                (wup_in, weights_s.at[:, pl.ds(hidden + wide, hidden)]),
            )
        )
    ]
    for operand in late:
        operand.start()
    mine, theirs = at_rows(y * half, half), at_rows((1 - y) * half, half)
    both, sibling = at_rows(c * rows, rows), at_rows((1 - c) * rows, rows)

    def chunk(n, to):
        if n == 3:
            return bias_s
        return dsend.at[n, at_rows(to * weight_rows, weight_rows)]

    def received(n, owner):
        return (ratt_ref, rup_ref, rdown_ref, rbias_ref)[n].at[owner]

    weights = Exchange(place, chunk, received, wsend, wreceive, wlocal)

    def order(turn):
        at = place.far_first(turn // 2)
        return at, at * 2 + jnp.where(lax.rem(turn, 2) == 0, 1 - b, b)

    def to_core(t, turn):
        return remote(
            fresh.at[lax.rem(turn, 2), sibling], from_core.at[lax.rem(turn, ring)], csend.at[t, turn],
            creceive.at[lax.rem(turn, ring)], place.device[CORE],
        )

    def to_other(t, chip):
        return remote(
            own.at[t, chip, theirs], from_other.at[t, chip], ysend.at[t, chip], yreceive.at[t, chip],
            place.device[OTHER],
        )

    def to_across(t, at):
        return remote(
            own.at[t, at * 2 + 1 - b, mine], from_across.at[t, at], xsend.at[t, at], xreceive.at[t, at],
            place.device[ACROSS],
        )

    def to_beyond(t, nth):
        at, slot = place.far_first(nth), nth - shortcuts[0]
        return remote(
            own.at[t, at * 2 + 1 - b], from_beyond.at[t, slot], bsend.at[t, slot],
            breceive.at[t, slot], place.device[ACROSS],
        )

    def to_up(t, at):
        return remote(
            own.at[t, at * 2 + b, mine], from_line.at[t, at], zsend.at[t, at], zreceive.at[t, at],
            place.device[UP],
        )

    def to_down(t, at, last):
        slot = line if last else at
        return remote(
            own.at[t, at * 2 + b, mine], from_line.at[t, slot], zsend.at[t, at], zreceive.at[t, slot],
            place.device[DOWN],
        )

    def final(t, part):
        return remote(
            done.at[t, part], done.at[t, part], fsend.at[t], freceive.at[t], place.device[OTHER]
        )

    def add(t, chip, part, other):
        own[t, chip, part, :] = (own[t, chip, part, :].astype(F32) + other.astype(F32)).astype(BF)

    def columns_of(n, source):
        return Stream(
            lambda at, slot: pltpu.make_async_copy(
                source.at[:, at_rows(weights.chip(at) * pair, pair)],
                cols.at[n, slot],
                cols_sem.at[n, slot],
            ),
            cols.shape[1],
            chips,
        )

    def rows_of(source, chip_of):
        return Stream(
            lambda at, slot: pltpu.make_async_copy(
                source.at[at_rows(chip_of(at) * block, block)], buf.at[slot], buf_sem.at[slot]
            ),
            buf.shape[0],
            blocks,
        )

    g_rows, x_rows = rows_of(g_ref, lambda at: at), rows_of(x_ref, lambda at: order(at)[1])
    normed_columns, g_columns = columns_of(0, normed_ref), columns_of(1, g_ref)
    g_rows.prime()
    normed_columns.prime()
    g_columns.prime()

    def product(t, turn):
        _, chip = order(turn)
        here = at_rows(chip * block, block)
        fresh_at = lax.rem(turn, 2)
        left = ((act_ref, att_ref), (gmix_s, gup_s))[t]
        left = jnp.concatenate([left[0][here, :], left[1][here, :]], axis=1)
        right = pl.ds((0, hidden)[t], hidden + wide)
        if t == 1:
            slot = x_rows.step(turn)

            def load(start):
                return buf[slot, :, pl.ds(start, piece)].astype(F32)

            mean, inv_std = row_stats(load, block, features, piece)
        for start in range(0, features, piece):
            part = pl.ds(start, piece)
            value = mm(left, weights_s[part, right], NT)
            fresh[fresh_at, :, part] = value.astype(BF)
            if t == 1:
                unit = (load(start) - mean) * inv_std
                shift_s[:, part] += jnp.sum(value.reshape(block // 8, 8, piece), axis=0)
                gain_s[:, part] += jnp.sum((unit * value).reshape(block // 8, 8, piece), axis=0)
        if t == 1:
            pl.semaphore_wait(credit, 1)
        else:
            pl.when(turn >= ring)(lambda: pl.semaphore_wait(credit, 1))
        to_core(t, turn).start()

    def stage_core(t, turn):
        _, chip = order(turn)
        to_core(t, turn).wait_recv()
        own[t, chip, :, :] = (
            fresh[lax.rem(turn, 2), both, :].astype(F32)
            + from_core[lax.rem(turn, ring)].astype(F32)
        ).astype(BF)

        def give():
            pl.semaphore_signal(
                credit, inc=1, device_id=place.device[CORE], device_id_type=MESH
            )

        if t == 0:
            give()
        else:
            pl.when(turn < chips - ring)(give)
        pl.when(turn < 2 * shortcuts[0])(lambda: to_other(t, chip).start())
        for nth in shortcuts:
            pl.when(turn == 2 * nth)(lambda nth=nth: to_beyond(t, nth).start())
        to_core(t, turn).wait_send()

    def stage_beyond(t):
        for nth in shortcuts:
            chip = place.far_first(nth) * 2 + b
            to_beyond(t, nth).wait_recv()
            add(t, chip, pl.ds(0, rows), from_beyond[t, nth - shortcuts[0]])
            to_other(t, chip).start()

    def stage_other(t, nth):
        if nth in shortcuts:
            return
        at = place.far_first(nth)
        chip = at * 2 + 1 - b
        to_other(t, chip).wait_recv()
        add(t, chip, mine, from_other[t, chip])
        to_across(t, at).start()

    def stage_line(t, nth):
        at = place.far_first(nth)
        chip = at * 2 + b
        to_other(t, chip).wait_recv()
        if nth in shortcuts:
            add(t, chip, mine, from_other[t, chip])
        else:
            to_across(t, at).wait_recv()
            add(t, chip, mine, from_other[t, chip].astype(F32) + from_across[t, at].astype(F32))

        def down():
            @pl.when(a < line - 1)
            def _():
                to_down(t, at, False).wait_recv()
                add(t, chip, mine, from_line[t, at])

            pl.when(at == a - 1)(lambda: to_down(t, at, True).start())
            pl.when(at < a - 1)(lambda: to_down(t, at, False).start())

        def up():
            @pl.when(a > 0)
            def _():
                to_up(t, at).wait_recv()
                add(t, chip, mine, from_line[t, at])

            to_up(t, at).start()

        if nth < line - 1:
            pl.when(at < a)(down)
            pl.when(at > a)(up)
            return

        @pl.when(a < line - 1)
        def _():
            to_down(t, at, True).wait_recv()
            add(t, chip, mine, from_line[t, line])

        @pl.when(a > 0)
        def _():
            to_up(t, at).wait_recv()
            add(t, chip, mine, from_line[t, at])

        done[t, mine, :] = own[t, chip, mine, :]
        final(t, mine).start()

    def norm_copy(step):
        kind = (CORE, OTHER, ACROSS)[step]
        return remote(
            nsend.at[step], nfrom.at[step], nsend_sem.at[step], nreceive.at[step], place.device[kind]
        )

    def norm_line(other, came):
        return remote(
            nsend.at[3], nline.at[other if came else a], lsend.at[other],
            lreceive.at[other if came else a], (place.index(other, b, c), y),
        )

    for operand in late[:2]:
        operand.wait()
    product(0, 0)

    def turn_over(pieces):
        def one(at, carry):
            here = at_rows(at * 256, 256)
            for n, source in pieces:
                turned_s[n, :, here] = source[here, :].T
            return carry

        lax.fori_loop(0, tokens // 256, one, 0)

    turn_over(((2, att_ref), (3, act_ref)))
    ones = jnp.ones((8, tokens), BF)

    def gradients_down(turn):
        slot = g_columns.step(turn)
        here = at_rows(weights.chip(turn) * pair, pair)
        by_grad = cols[1, slot]
        dsend[2, here, :] = mm(turned_s[3], by_grad).T.astype(BF)
        dsend[0, here, :] = mm(turned_s[2], by_grad).T.astype(BF)
        total_ref[:, here] = mm(ones, by_grad)
        weights.start_chip((2,), turn)

    def first_sum(turn, carry):
        product(0, turn)
        stage_core(0, turn - 1)
        gradients_down(turn - 1)
        return carry

    lax.fori_loop(1, chips, first_sum, 0)
    stage_core(0, chips - 1)
    gradients_down(chips - 1)

    late[2].wait()

    def feed_back(at, carry):
        slot = g_rows.step(at)
        here = at_rows(at * block, block)
        upward = upward_ref[here, :]
        tanh = gelu_parts(upward)
        slope = 0.5 * (1.0 + tanh) + 0.5 * upward * (1.0 - tanh * tanh) * (
            math.sqrt(2.0 / math.pi) * (1.0 + 3 * 0.044715 * upward * upward)
        )
        gup_s[here, :] = (mm(buf[slot], weights_s[:, pl.ds(0, hidden)]) * slope).astype(BF)
        return carry

    lax.fori_loop(0, blocks, feed_back, 0)
    stage_other(0, 0)
    x_rows.prime()

    turn_over(((1, gup_s),))

    def gradients_up(turn, carry):
        slot = normed_columns.step(turn)
        here = at_rows(weights.chip(turn) * pair, pair)
        dsend[1, here, :] = mm(turned_s[1], cols[0, slot]).T.astype(BF)
        weights.start_chip((1,), turn)
        return carry

    lax.fori_loop(0, chips, gradients_up, 0)
    stage_other(0, 1)
    normed_columns.prime()
    for operand in late[3:]:
        operand.wait()

    quarter = tokens // inverse_ref.shape[0]
    quarters = block // quarter
    span = 2 * block
    scale = 1.0 / math.sqrt(HEAD)

    def prepare(at, carry):
        here = at_rows(at * block, block)
        key = qkvs_ref[here, :][:, : 2 * HEAD].astype(F32)
        kt_s[:, here] = key.T[HEAD:].astype(BF)
        dkv_s[here, :] = jnp.zeros((block, 2 * HEAD), F32)
        return carry

    lax.fori_loop(0, blocks, prepare, 0)

    def backward(at, carry):
        here = at_rows(at * span, span)
        query = qkvs_ref[here, :][:, :HEAD]
        grad = jnp.concatenate(
            [gatt_ref[inverse_ref[at * 2 * quarters + n]] for n in range(2 * quarters)], axis=0
        )
        left = lax.broadcasted_iota(jnp.int32, (span, 2 * HEAD), 1) < HEAD
        grad_wide = grad[:, 2 * HEAD :].astype(F32)
        grad_right = jnp.where(left, 0.0, grad_wide).astype(BF)
        query_left = jnp.concatenate([query, jnp.zeros_like(query)], axis=1)
        beside_each = jnp.concatenate([query_left, grad_right], axis=0)
        grad = grad[:, 3 * HEAD :]
        delta = jnp.sum(grad_wide.T[HEAD:] * attt_ref[:, here], axis=0, keepdims=True)
        lse = lse_ref[0:1, here]

        def back(place_at, query_grad, masked):
            there = at_rows(place_at * span, span)
            keyvalue = qkvs_ref[there, :]
            scores = mm(keyvalue[:, HEAD : 2 * HEAD], query, NT)
            if masked:
                scores = jnp.where(seen(0, 0, span, span), scores, NEG)
            prob = jnp.exp(scores - lse)
            dprob = mm(keyvalue[:, 2 * HEAD : 3 * HEAD], grad, NT)
            dscore = (prob * (dprob - delta)).astype(BF)
            dkv_s[there, :] += mm(
                jnp.concatenate([dscore, prob.astype(BF)], axis=1), beside_each
            )
            return query_grad + mm(kt_s[:, there], dscore)

        query_grad = lax.fori_loop(
            0, at, lambda n, total: back(n, total, False), jnp.zeros((HEAD, span), F32)
        )
        query_grad = back(at, query_grad, True)
        query_grad = jnp.concatenate([query_grad, query_grad], axis=0).T[:, :HEAD]
        query_grad = turned(
            query_grad * scale, angle_ref[here, : ROT // 2], -angle_ref[here, ROT // 2 :]
        ).astype(BF)
        gm_s[pl.ds(at * 2 * quarters, 2 * quarters), :, pl.ds(0, HEAD)] = query_grad.reshape(
            2 * quarters, quarter, HEAD
        )
        return carry

    lax.fori_loop(0, blocks // 4, backward, 0)
    stage_beyond(0)
    for nth in range(2, line - 1):
        stage_other(0, nth)
    lax.fori_loop(blocks // 4, blocks // 2, backward, 0)
    if line > 2:
        stage_other(0, line - 1)

    def finish_keys(at, carry):
        here = at_rows(at * block, block)
        keyvalue = jnp.concatenate(
            [
                turned(
                    dkv_s[here, :][:, :HEAD], angle_ref[here, : ROT // 2], -angle_ref[here, ROT // 2 :]
                ).astype(BF),
                dkv_s[here, :][:, HEAD:].astype(BF),
            ],
            axis=1,
        )
        gm_s[pl.ds(at * quarters, quarters), :, pl.ds(HEAD, 2 * HEAD)] = keyvalue.reshape(
            quarters, quarter, 2 * HEAD
        )
        return carry

    lax.fori_loop(0, blocks, finish_keys, 0)

    def unplace(at, carry):
        gmix_s[at_rows(at * quarter, quarter), :] = jnp.concatenate(
            [gm_s[order_ref[at]], jnp.zeros((quarter, HEAD), BF)], axis=1
        )
        return carry

    lax.fori_loop(0, tokens // quarter, unplace, 0)
    turn_over(((0, gmix_s),))
    for n, source in enumerate((gmix_s, gup_s)):
        columns = source.shape[1]

        def tally(at, total, source=source, columns=columns):
            return total + jnp.sum(
                source[at_rows(at * 256, 256), :].astype(F32).reshape(32, 8, columns), axis=0
            )

        total = lax.fori_loop(0, tokens // 256, tally, jnp.zeros((8, columns), F32))
        total = jnp.sum(total, axis=0, keepdims=True)
        for at in range(columns // 128):
            bias_s[pl.ds(n * 2 + at, 1), :] = total[:, at * 128 : (at + 1) * 128]
    bias_s[pl.ds(4, 4), :] = jnp.zeros((4, 128), F32)

    gain_s[...] = jnp.zeros_like(gain_s)
    shift_s[...] = jnp.zeros_like(shift_s)

    def gradients_att(turn, carry):
        slot = normed_columns.step(turn)
        here = at_rows(weights.chip(turn) * pair, pair)
        more = mm(turned_s[0], cols[0, slot]).T
        dsend[0, here, :] = (dsend[0, here, :].astype(F32) + more).astype(BF)
        weights.start_chip((0, 3), turn)
        return carry

    lax.fori_loop(0, chips, gradients_att, 0)
    product(1, 0)

    def second_sum(turn, carry):
        product(1, turn)
        stage_core(1, turn - 1)
        return carry

    lax.fori_loop(1, chips, second_sum, 0)
    stage_core(1, chips - 1)
    for n, source in enumerate((gain_s, shift_s)):
        total = jnp.sum(source[...], axis=0, keepdims=True)
        quarter_of = features // 4
        for at in range(4):
            nsend[0, pl.ds(n * 4 + at, 1), :] = total[:, at * quarter_of : (at + 1) * quarter_of]
    norm_copy(0).start()
    stage_other(1, 0)
    stage_line(0, 0)
    stage_line(0, 1)
    stage_other(1, 1)
    stage_line(0, 2)
    stage_line(1, 0)
    norm_copy(0).wait_recv()
    nsend[1] = nsend[0] + nfrom[0]
    norm_copy(1).start()
    stage_beyond(1)
    stage_other(1, 2)
    norm_copy(1).wait_recv()
    nsend[2] = nsend[1] + nfrom[1]
    norm_copy(2).start()
    stage_line(1, 1)
    stage_line(0, 3)
    norm_copy(2).wait_recv()
    nsend[3] = nsend[2] + nfrom[2]
    nline[a] = nsend[3]
    for other in range(line):
        pl.when(a != other)(lambda other=other: norm_line(other, False).start())
    stage_line(1, 2)
    stage_line(1, 3)
    for other in range(line):
        pl.when(a != other)(lambda other=other: norm_line(other, True).wait_recv())
    total = nline[0]
    for other in range(1, line):
        total += nline[other]
    norms_ref[...] = total

    for step in range(3):
        norm_copy(step).wait_send()
    for other in range(line):
        pl.when(a != other)(lambda other=other: norm_line(other, False).wait_send())
    for t in range(2):
        final(t, theirs).wait_recv()
        final(t, mine).wait_send()
        sums[t][...] = done[t]

        def left(at, carry, t=t):
            to_other(t, at * 2 + b).wait_send()
            pl.when(at != a)(lambda: to_up(t, at).wait_send())

            def also():
                to_other(t, at * 2 + 1 - b).wait_send()
                to_across(t, at).wait_send()

            shorter = at == place.far_first(shortcuts[0])
            for nth in shortcuts[1:]:
                shorter = shorter | (at == place.far_first(nth))
            pl.when(jnp.logical_not(shorter))(also)
            return carry

        lax.fori_loop(0, line, left, 0)
        for nth in shortcuts:
            to_beyond(t, nth).wait_send()
    weights.wait((0, 1, 2, 3))


def spread(
    order, inverse, attended, activated, upward, grad_att, qkvs, lse, attended_t, w_att, w_up, w_down,
    angles, normed, g_all, x_all,
):
    count = lax.axis_size("ctx")
    line = count // 4
    tokens, features = x_all.shape
    rows = tokens // count
    half = rows // 2
    chips = 2 * line
    weight_rows = w_att.shape[0] // count
    wide, hidden = w_att.shape[1], w_up.shape[1]
    hbm, vmem = pl.BlockSpec(memory_space=pl.ANY), pl.BlockSpec(memory_space=pltpu.VMEM)
    smem = pl.BlockSpec(memory_space=pltpu.SMEM)
    dma = pltpu.SemaphoreType.DMA
    own = jax.ShapeDtypeStruct((rows, features), BF)
    back = [
        jax.ShapeDtypeStruct((count, weight_rows, columns), BF) for columns in (wide, hidden, hidden)
    ]
    return pl.pallas_call(
        functools.partial(spread_kernel, line),
        out_shape=[own, own]
        + back
        + [
            jax.ShapeDtypeStruct((count, 8, 128), F32),
            jax.ShapeDtypeStruct((8, features // 4), F32),
            jax.ShapeDtypeStruct((8, features), F32),
        ],
        in_specs=[smem, smem] + [vmem] * 4 + [hbm] * 10,
        out_specs=[vmem, vmem, hbm, hbm, hbm, hbm, vmem, vmem],
        scratch_shapes=[
            pltpu.VMEM((count * weight_rows, wide + 2 * hidden), BF),
            pltpu.VMEM(upward.shape, F32),
            pltpu.VMEM(grad_att.shape, BF),
            pltpu.VMEM(qkvs.shape, BF),
            pltpu.VMEM(attended_t.shape, F32),
            pltpu.VMEM((2, 2 * rows, features), BF),
            pltpu.VMEM((2, chips, rows, features), BF),
            pltpu.VMEM((4, rows, features), BF),
            pltpu.VMEM((2, chips, half, features), BF),
            pltpu.VMEM((2, line, half, features), BF),
            pltpu.VMEM((2, 1, rows, features), BF),
            pltpu.VMEM((2, line + 1, half, features), BF),
            pltpu.VMEM((2, rows, features), BF),
            pltpu.VMEM((4, wide, tokens), BF),
            pltpu.VMEM((3, count * weight_rows, wide), BF),
            pltpu.VMEM((2, 3, tokens, 2 * weight_rows), BF),
            pltpu.VMEM((3, 2 * rows, features), BF),
            pltpu.VMEM((8, features), F32),
            pltpu.VMEM((8, features), F32),
            pltpu.VMEM((4, 8, features // 4), F32),
            pltpu.VMEM((3, 8, features // 4), F32),
            pltpu.VMEM((line, 8, features // 4), F32),
            pltpu.VMEM((8, 128), F32),
            pltpu.VMEM((tokens, wide), BF),
            pltpu.VMEM((tokens, hidden), BF),
            pltpu.VMEM((HEAD, tokens), BF),
            pltpu.VMEM((tokens, 2 * HEAD), F32),
            pltpu.VMEM((order.shape[0], tokens // order.shape[0], 3 * HEAD), BF),
            dma((7,)),
            dma((2, 3)),
            dma((3,)),
            dma((2, chips)),
            dma((4,)),
            pltpu.SemaphoreType.REGULAR,
            dma((2, chips)),
            dma((2, chips)),
            dma((2, line)),
            dma((2, line)),
            dma((2, 1)),
            dma((2, 1)),
            dma((2, line)),
            dma((2, line + 1)),
            dma((2,)),
            dma((2,)),
            dma((4, count)),
            dma((4, count)),
            dma((4,)),
            dma((3,)),
            dma((3,)),
            dma((line,)),
            dma((line,)),
        ],
        compiler_params=pltpu.CompilerParams(
            collective_id=2, has_side_effects=True, vmem_limit_bytes=63 * 1024 * 1024
        ),
    )(
        order, inverse, attended, activated, lse, angles, w_att, w_down, upward, grad_att, qkvs,
        attended_t, w_up, normed, g_all, x_all,
    )


def finish_kernel(
    tok_ref, cot_ref, gain_ref, bias_ref, branch_ref, normed_ref, datt_ref, dup_ref, ddown_ref,
    sums_ref, norms_ref, total_ref,
    out_ref, grad_ref, qkv_ref, wout_ref, up_ref, down_ref, qkvb_ref, upb_ref, gsum_ref, ssum_ref,
    bsum_ref,
):
    inputs = tok_ref[...].astype(F32)
    center = inputs - jnp.mean(inputs, axis=-1, keepdims=True)
    inv_std = lax.rsqrt(jnp.mean(center * center, axis=-1, keepdims=True) + EPS)
    unit = center * inv_std
    out_ref[...] = inputs + branch_ref[...].astype(F32) + bias_ref[...]
    grad_unit = normed_ref[...].astype(F32) * gain_ref[...]
    grad_ref[...] = cot_ref[...].astype(F32) + inv_std * (
        grad_unit
        - jnp.mean(grad_unit, axis=-1, keepdims=True)
        - unit * jnp.mean(grad_unit * unit, axis=-1, keepdims=True)
    )
    count, _, packed = datt_ref.shape
    width, hidden = packed // 4, dup_ref.shape[2]
    pieces = [datt_ref[owner].astype(F32) for owner in range(count)]

    def together(kind):
        return jnp.concatenate(
            [piece[:, kind * width : (kind + 1) * width] for piece in pieces], axis=1
        )

    for kind in range(3):
        qkv_ref[kind, :, :] = together(kind)
        at = kind * width
        qkvb_ref[kind : kind + 1, :] = jnp.concatenate(
            [
                sums_ref[owner, at // 128 : at // 128 + 1, at % 128 : at % 128 + width]
                for owner in range(count)
            ],
            axis=1,
        )
    wout_ref[...] = together(3)
    for owner in range(count):
        columns = pl.ds(owner * hidden, hidden)
        up_ref[:, columns] = dup_ref[owner].astype(F32)
        down_ref[:, columns] = ddown_ref[owner].astype(F32)
        for at in range(hidden // 128):
            upb_ref[:, pl.ds(owner * hidden + at * 128, 128)] = sums_ref[owner, 2 + at : 3 + at, :]
    wide = norms_ref.shape[1]
    for at in range(4):
        gsum_ref[:, pl.ds(at * wide, wide)] = norms_ref[at : at + 1, :]
        ssum_ref[:, pl.ds(at * wide, wide)] = norms_ref[4 + at : 5 + at, :]
    bsum_ref[...] = total_ref[0:1, :]


def finish(tokens, cotangent, gain, bias, branches, own_normed, d_att, d_up, d_down, sums, norms, total):
    count, weight_rows, packed = d_att.shape
    rows, features = tokens.shape
    width, hidden = packed // 4, d_up.shape[2]
    owners = max(128 // width, count // 2)
    steps = count // owners
    by_rows = pl.BlockSpec((rows // steps, features), lambda at: (at, 0))
    line = pl.BlockSpec((1, features), lambda at: (0, 0))

    def whole(array):
        return pl.BlockSpec(array.shape, lambda at: (0,) * array.ndim)

    def by_owner(array):
        return pl.BlockSpec((owners, *array.shape[1:]), lambda at: (at, 0, 0))

    def by_columns(*lead):
        return lambda columns: pl.BlockSpec(
            (*lead, owners * columns), lambda at: (*(0,) * len(lead), at)
        )

    shape = jax.ShapeDtypeStruct
    return pl.pallas_call(
        finish_kernel,
        grid=(steps,),
        out_shape=[
            shape(tokens.shape, F32),
            shape(tokens.shape, F32),
            shape((3, weight_rows, count * width), F32),
            shape((weight_rows, count * width), F32),
            shape((weight_rows, count * hidden), F32),
            shape((weight_rows, count * hidden), F32),
            shape((3, count * width), F32),
            shape((1, count * hidden), F32),
            shape((1, features), F32),
            shape((1, features), F32),
            shape((1, features), F32),
        ],
        in_specs=[by_rows, by_rows, line, line, by_rows, by_rows]
        + [by_owner(array) for array in (d_att, d_up, d_down, sums)]
        + [whole(norms), whole(total)],
        out_specs=[
            by_rows,
            by_rows,
            by_columns(3, weight_rows)(width),
            by_columns(weight_rows)(width),
            by_columns(weight_rows)(hidden),
            by_columns(weight_rows)(hidden),
            by_columns(3)(width),
            by_columns(1)(hidden),
            line,
            line,
            line,
        ],
        compiler_params=pltpu.CompilerParams(vmem_limit_bytes=63 * 1024 * 1024),
    )(
        tokens, cotangent, gain[None], bias[None], branches, own_normed, d_att, d_up, d_down, sums,
        norms, total,
    )


def gelu_tanh(value):
    return jax.nn.gelu(value, approximate=True)


def local(
    tokens, block_order, ln_gain, ln_bias, qkv_weight, qkv_bias, out_weight, fc1_weight, fc1_bias,
    fc2_weight, out_bias, cotangent,
):
    devices = lax.axis_size("ctx")
    myself = lax.axis_index("ctx")
    heads_here = qkv_weight.shape[2] // HEAD
    columns = math.gcd(devices, heads_here)
    mine = myself % columns
    width = qkv_weight.shape[2] // columns
    hidden = fc1_weight.shape[1] // columns
    if devices == columns and columns % 8 == 0 and width == HEAD and lax.axis_size("tp") == 2:
        freqs = 10000.0 ** (-np.arange(0, ROT, 2, dtype=np.float32) / ROT)
        angles = np.arange(devices * tokens.shape[0], dtype=np.float32)[:, None] * freqs[None, :]
        angles = jnp.asarray(np.concatenate([np.cos(angles), np.sin(angles)], axis=1), F32)
        (
            x_all, g_all, w_att, w_up, w_down, normed, qkvs, lse, attended_t, attended, activated,
            upward, grad_att, inverse,
        ) = collect(
            block_order, tokens, cotangent, qkv_weight, out_weight, fc1_weight, fc2_weight,
            ln_gain[None], ln_bias[None], qkv_bias, fc1_bias[None], angles,
        )
        parts = spread(
            block_order, inverse, attended, activated, upward, grad_att, qkvs, lse, attended_t, w_att,
            w_up, w_down, angles, normed, g_all, x_all,
        )
    else:
        bias_att = lax.dynamic_slice_in_dim(qkv_bias, mine * width, width, 1).reshape(-1)
        bias_att = jnp.concatenate([bias_att, jnp.zeros((width,), F32)])[None]
        bias_up = lax.dynamic_slice_in_dim(fc1_bias, mine * hidden, hidden, 0)[None]
        parts = by_groups(
            tokens, block_order, ln_gain, ln_bias, qkv_weight, out_weight, fc1_weight, fc2_weight,
            cotangent, bias_att, bias_up,
        )
    (
        output, input_grad, qkv_grad, out_grad, fc1_grad, fc2_grad, qkv_sums, fc1_sums, gain_sum,
        shift_sum, g_sum,
    ) = finish(tokens, cotangent, ln_gain, out_bias, *parts)
    return (
        output, input_grad, gain_sum[0], shift_sum[0], qkv_grad.transpose(1, 0, 2), qkv_sums, out_grad,
        fc1_grad, fc1_sums[0], fc2_grad, g_sum[0],
    )


def by_groups(
    tokens, block_order, ln_gain, ln_bias, qkv_weight, out_weight, fc1_weight, fc2_weight, cotangent,
    bias_att, bias_up,
):
    devices = lax.axis_size("ctx")
    myself = lax.axis_index("ctx")
    rows_here = tokens.shape[0]
    weight_rows = qkv_weight.shape[0]
    half = devices * rows_here // block_order.shape[0]
    columns = math.gcd(devices, qkv_weight.shape[2] // HEAD)
    groups = devices // columns
    width, hidden = qkv_weight.shape[2] // columns, fc1_weight.shape[1] // columns
    count = columns * rows_here
    side = [[r * columns + c for c in range(columns)] for r in range(groups)]
    across = [[r * columns + c for r in range(groups)] for c in range(columns)]

    def gathered(value, among):
        return lax.all_gather(value, "ctx", axis=0, tiled=True, axis_index_groups=among)

    def scattered(value, among):
        return lax.psum_scatter(
            value, "ctx", scatter_dimension=0, tiled=True, axis_index_groups=among
        )

    def exchanged(value):
        return lax.all_to_all(value, "ctx", split_axis=0, concat_axis=0, tiled=True)

    x_all, g_all = gathered(tokens, side), gathered(cotangent, side)
    kinds = jnp.concatenate([qkv_weight, out_weight[:, None]], axis=1)
    kinds = kinds.reshape(weight_rows, 4, columns, width).transpose(2, 0, 1, 3)
    packed = jnp.concatenate(
        [
            kinds.reshape(columns, weight_rows, 4 * width),
            fc1_weight.reshape(weight_rows, columns, hidden).transpose(1, 0, 2),
            fc2_weight.reshape(weight_rows, columns, hidden).transpose(1, 0, 2),
        ],
        axis=2,
    )
    packed = exchanged(jnp.tile(packed, (groups, 1, 1))).reshape(devices * weight_rows, -1)
    w_att, w_up, w_down = jnp.split(packed, [4 * width, 4 * width + hidden], axis=1)

    inputs = x_all.astype(F32)
    center = inputs - jnp.mean(inputs, axis=-1, keepdims=True)
    inv_std = lax.rsqrt(jnp.mean(center * center, axis=-1, keepdims=True) + EPS)
    unit = center * inv_std
    normed = (unit * ln_gain + ln_bias).astype(BF)
    upward = mm(normed, w_up) + bias_up
    activated, gelu_back = jax.vjp(gelu_tanh, upward)
    activated = activated.astype(BF)
    grad_up = gelu_back(mm(g_all, w_down))[0].astype(BF)
    places = (block_order[:, None] * half + jnp.arange(half, dtype=jnp.int32)[None, :]).reshape(-1)
    attended, grad_mixed = attention_blocks(
        lax.dynamic_slice_in_dim(places, (myself // columns) * count, count),
        places,
        mm(normed, w_att) + bias_att,
        mm(g_all, w_att),
        lambda value: gathered(value, across),
        lambda value: scattered(value, across),
    )
    out_part = (mm(attended, w_att, NT) + mm(activated, w_down, NT)).astype(BF)
    normed_wide = mm(grad_mixed, w_att, NT) + mm(grad_up, w_up, NT)
    branches, own_normed = lax.psum(
        (scattered(out_part, side), scattered(normed_wide.astype(BF), side)), "tp"
    )
    back = jnp.concatenate(
        [
            (mm(normed, grad_mixed, TN) + mm(g_all, attended, TN)).astype(BF),
            mm(normed, grad_up, TN).astype(BF),
            mm(g_all, activated, TN).astype(BF),
        ],
        axis=1,
    )
    back = exchanged(back.reshape(devices, weight_rows, -1))
    back = jnp.sum(back.reshape(groups, columns, weight_rows, -1).astype(F32), axis=0)
    sums = jnp.concatenate(
        [jnp.sum(grad_mixed.astype(F32), axis=0), jnp.sum(grad_up.astype(F32), axis=0)]
    ).reshape(-1, 128)
    sums = jnp.pad(sums, ((0, 8 - sums.shape[0]), (0, 0)))
    sums = gathered(lax.psum(sums, "ctx", axis_index_groups=across)[None], side)
    norms = jnp.stack([jnp.sum(unit * normed_wide, axis=0), jnp.sum(normed_wide, axis=0)])
    norms = lax.psum(norms, ("ctx", "tp")).reshape(8, -1)
    total = lax.psum(jnp.sum(g_all.astype(F32), axis=0), "ctx", axis_index_groups=across)[None]
    return (
        branches, own_normed, *jnp.split(back, [4 * width, 4 * width + hidden], axis=2), sums, norms,
        total,
    )


def solution(mesh):
    rows, tall = P("ctx", None), P("ctx", "tp")
    kinds, bias = P("ctx", None, "tp"), P(None, "tp")
    return jax.shard_map(
        local,
        mesh=mesh,
        in_specs=(rows, P(), P(), P(), kinds, bias, tall, tall, P("tp"), tall, P(), rows),
        out_specs=(rows, rows, P(), P(), kinds, bias, tall, tall, P("tp"), tall, P()),
        check_vma=False,
    )
```

```python
import functools
import math

import jax
import jax.numpy as jnp
import numpy as np
from jax import lax
from jax.experimental import pallas as pl
from jax.experimental.pallas import tpu as pltpu
from jax.sharding import PartitionSpec as P

HEAD = 64
ROT = 32
EPS = 1e-05
NEG = -1e30
BF = jnp.bfloat16
F32 = jnp.float32
NN = (((1,), (0,)), ((), ()))
NT = (((1,), (1,)), ((), ()))
TN = (((0,), (0,)), ((), ()))


def mm(left, right, dims=NN):
    return lax.dot_general(left, right, dims, preferred_element_type=F32)


def tables(positions, width):
    freqs = 10000.0 ** (-(jnp.arange(width // 2, dtype=F32) * 2.0) / width)
    angles = positions.astype(F32)[:, None] * freqs[None, :]
    return (jnp.cos(angles), jnp.sin(angles))


def turned(value, cosine, sine):
    half = cosine.shape[-1]
    first, second = value[..., :half], value[..., half : 2 * half]
    return jnp.concatenate(
        [first * cosine - second * sine, second * cosine + first * sine, value[..., 2 * half :]],
        axis=-1,
    )


def attention_blocks(own_place, places, mixed, grad_att, gather, scatter):
    count, width = grad_att.shape[0], grad_att.shape[1] // 4
    heads = width // HEAD
    scale = 1.0 / math.sqrt(HEAD)
    grad_att = grad_att[:, 3 * width :].astype(BF)
    cosine, sine = tables(own_place, ROT)
    cosine, sine = cosine[:, None, :], sine[:, None, :]
    kinds = [mixed[:, kind * width : (kind + 1) * width].reshape(count, heads, HEAD) for kind in range(3)]
    queries = turned(kinds[0], cosine, sine).astype(BF)
    keys = gather(turned(kinds[1], cosine, sine).astype(BF))
    values = gather(kinds[2].astype(BF))
    grad_att = grad_att.reshape(count, heads, HEAD)
    block = math.gcd(128, count)

    def one(at, carry):
        key_grad, value_grad, attended, query_grad = carry
        query = lax.dynamic_slice_in_dim(queries, at * block, block)
        grad = lax.dynamic_slice_in_dim(grad_att, at * block, block)
        place = lax.dynamic_slice_in_dim(own_place, at * block, block)
        visible = (place[:, None] >= places[None, :])[None]
        scores = jnp.einsum("qhe,khe->hqk", query, keys, preferred_element_type=F32) * scale
        scores = jnp.where(visible, scores, NEG)
        top = jnp.max(scores, axis=-1, keepdims=True)
        expo = jnp.where(visible, jnp.exp(scores - top), 0.0)
        total = jnp.sum(expo, axis=-1)
        summed = jnp.einsum("hqk,khe->qhe", expo.astype(BF), values, preferred_element_type=F32)
        attend = summed / jnp.transpose(total)[..., None]
        delta = jnp.transpose(jnp.sum(grad.astype(F32) * attend, axis=-1))
        prob = expo / total[..., None]
        dprob = jnp.einsum("qhe,khe->hqk", grad, values, preferred_element_type=F32)
        dscore = (prob * (dprob - delta[..., None])).astype(BF)
        part_q = jnp.einsum("hqk,khe->qhe", dscore, keys, preferred_element_type=F32) * scale
        key_grad += jnp.einsum("hqk,qhe->khe", dscore, query, preferred_element_type=F32) * scale
        value_grad += jnp.einsum("hqk,qhe->khe", prob.astype(BF), grad, preferred_element_type=F32)
        attended = lax.dynamic_update_slice_in_dim(attended, attend.astype(BF), at * block, 0)
        query_grad = lax.dynamic_update_slice_in_dim(query_grad, part_q, at * block, 0)
        return (key_grad, value_grad, attended, query_grad)

    zeros = jnp.zeros(keys.shape, F32)
    own = jnp.zeros((count, heads, HEAD), F32)
    key_grad, value_grad, attended, query_grad = lax.fori_loop(
        0, count // block, one, (zeros, zeros, own.astype(BF), own)
    )
    key_grad, value_grad = scatter(key_grad), scatter(value_grad)
    grad_mixed = jnp.concatenate(
        [
            turned(query_grad, cosine, -sine).astype(BF).reshape(count, width),
            turned(key_grad, cosine, -sine).astype(BF).reshape(count, width),
            value_grad.astype(BF).reshape(count, width),
            jnp.zeros((count, width), BF),
        ],
        axis=1,
    )
    attended = jnp.concatenate(
        [jnp.zeros((count, 3 * width), BF), attended.reshape(count, width)], axis=1
    )
    return attended, grad_mixed


MESH = pl.DeviceIdType.MESH
UP, DOWN, ACROSS, OTHER, CORE = range(5)


def at_rows(start, size):
    return pl.ds(pl.multiple_of(start, size), size)


def remote(source, target, send, receive, device):
    return pltpu.make_async_remote_copy(
        src_ref=source, dst_ref=target, send_sem=send, recv_sem=receive, device_id=device,
        device_id_type=MESH,
    )


class Place:
    def __init__(self, line):
        self.line = line
        self.me = lax.axis_index("ctx")
        self.y = lax.axis_index("tp")
        self.a, self.b, self.c = self.me // 4, (self.me // 2) % 2, self.me % 2
        a, b, c, y = self.a, self.b, self.c, self.y
        self.device = {
            UP: (self.index(jnp.minimum(a + 1, line - 1), b, c), y),
            DOWN: (self.index(jnp.maximum(a - 1, 0), b, c), y),
            ACROSS: (self.index(a, 1 - b, c), y),
            OTHER: (self.me, 1 - y),
            CORE: (self.index(a, b, 1 - c), y),
        }

    def index(self, a, b, c):
        return a * 4 + b * 2 + c

    def far_first(self, turn):
        line = self.line
        high, low = line - 1 - turn, turn
        high = jnp.where(high <= self.a, high - 1, high)
        low = jnp.where(low >= self.a, low + 1, low)
        other = jnp.where(self.a < line // 2, high, low)
        return jnp.where(turn == line - 1, self.a, other)

    def greet(self):
        barrier = pltpu.get_barrier_semaphore()
        count = 4 * self.line

        def signal(step, carry):
            pl.semaphore_signal(
                barrier, inc=1, device_id=(lax.rem(self.me + step, count), self.y), device_id_type=MESH
            )
            return carry

        lax.fori_loop(1, count, signal, 0)
        pl.semaphore_signal(barrier, inc=1, device_id=self.device[OTHER], device_id_type=MESH)
        pl.semaphore_wait(barrier, count)


def flipped(value, mask, bits):
    result = 0
    for bit in range(bits):
        one, other = (value // 2**bit) % 2, (mask // 2**bit) % 2
        result = result + 2**bit * (one + other - 2 * one * other)
    return result


class Exchange:
    def __init__(self, place, chunk, received, send, receive, own):
        self.place, self.chunk, self.received = place, chunk, received
        self.send, self.receive, self.own = send, receive, own
        self.count = 4 * place.line
        self.bits = self.count.bit_length() - 1
        self.partners = [self.partner(mask) for mask in range(self.count - 1, 0, -1)]

    def partner(self, mask):
        return mask, flipped(self.place.me, mask, self.bits)

    def chip(self, turn):
        return flipped(self.place.me // 2, self.count // 2 - 1 - turn, self.bits - 1)

    def start_chip(self, pieces, turn):
        mask = self.count - 2 - 2 * turn
        for n in pieces:
            self.copy(self.partner(mask + 1), n, False).start()
            pl.when(mask > 0)(lambda n=n: self.copy(self.partner(mask), n, False).start())
            pl.when(mask == 0)(lambda n=n: self.kept(n).start())

    def copy(self, partner, n, came):
        mask, to = partner
        return remote(
            self.chunk(n, to), self.received(n, to if came else self.place.me), self.send.at[n, mask],
            self.receive.at[n, mask], (to, self.place.y),
        )

    def kept(self, n):
        me = self.place.me
        return pltpu.make_async_copy(self.chunk(n, me), self.received(n, me), self.own.at[n])

    def keep(self, pieces):
        for n in pieces:
            self.kept(n).start()

    def start(self, pieces):
        for partner in self.partners:
            for n in pieces:
                self.copy(partner, n, False).start()

    def wait(self, pieces):
        for partner in self.partners:
            for n in pieces:
                self.copy(partner, n, True).wait()
        for n in pieces:
            self.kept(n).wait()


def row_stats(load, rows, features, piece):
    mean = jnp.zeros((rows, 1), F32)
    for at in range(0, features, piece):
        mean += jnp.sum(load(at), axis=1, keepdims=True)
    mean = mean / features
    spread = jnp.zeros((rows, 1), F32)
    for at in range(0, features, piece):
        center = load(at) - mean
        spread += jnp.sum(center * center, axis=1, keepdims=True)
    return mean, lax.rsqrt(spread / features + EPS)


class Stream:
    def __init__(self, copy, depth, total):
        self.copy, self.depth, self.total = copy, depth, total

    def prime(self):
        for at in range(min(self.depth - 1, self.total)):
            self.copy(at, at).start()

    def step(self, at):
        slot = lax.rem(at, self.depth)
        self.copy(at, slot).wait()
        later = at + self.depth - 1

        @pl.when(later < self.total)
        def _():
            self.copy(later, lax.rem(later, self.depth)).start()

        return slot


def gelu_parts(value):
    inner = math.sqrt(2.0 / math.pi) * (value + 0.044715 * value * value * value)
    return jnp.tanh(inner)


def seen(start_key, start_query, keys, queries):
    key = start_key + lax.broadcasted_iota(jnp.int32, (keys, queries), 0)
    return key <= start_query + lax.broadcasted_iota(jnp.int32, (keys, queries), 1)


def collect_kernel(
    line, order_ref, tok_ref, cot_ref, qkv_ref, out_ref, up_ref, down_ref, gain_ref,
    shift_ref, batt_ref, bup_ref, angle_ref,
    x_out, g_out, watt_out, wup_out, wdown_ref, normed_out, qkvs_out, lse_out, attt_out, att_out,
    act_out, upward_out, gatt_out, inverse_ref,
    x_ref, g_ref, watt_s, wup_s, normed_s, qkvs_ref, lse_ref, attt_ref, att_ref, act_ref, upward_ref,
    gatt_ref, packed, mixed_s, k_s, vt_s, st, att_s,
    send, receive, own_sem, wsend, wreceive, wlocal, out_sem,
):
    place = Place(line)
    a, b, c, y = place.a, place.b, place.c, place.y
    sources, targets = (tok_ref, cot_ref), (x_ref, g_ref)
    rows, features = tok_ref.shape
    half = rows // 2
    weight_rows = up_ref.shape[0]
    tokens = x_ref.shape[0]
    hidden = wup_s.shape[1]
    width = watt_s.shape[1] // 4
    block = 2 * rows
    blocks = tokens // block
    piece = 512
    place.greet()
    shipped = []

    def ship(source, target):
        shipped.append(pltpu.make_async_copy(source, target, out_sem.at[len(shipped)]))
        shipped[-1].start()

    def copy(t, kind, owner, part, own=False):
        target = targets[t].at[at_rows(owner * rows + part * half, half)]
        source = sources[t].at[at_rows(part * half, half)] if own else target
        return remote(
            source, target, send.at[t, kind, owner, part], receive.at[t, owner, part], place.device[kind]
        )

    def landed(t, owner, part):
        copy(t, CORE, owner, part).wait_recv()

    def along(t, distance):
        for sign in (0,) if distance == 0 else (1, -1):
            at = a + sign * distance

            def pass_on(sign=sign, at=at):
                owner = place.index(at, b, c)
                own = distance == 0
                if not own:
                    landed(t, owner, y)
                if sign <= 0:
                    pl.when(a < line - 1)(lambda: copy(t, UP, owner, y, own).start())
                if sign >= 0:
                    pl.when(a > 0)(lambda: copy(t, DOWN, owner, y, own).start())
                copy(t, ACROSS, owner, y, own).start()
                if not own:
                    copy(t, OTHER, owner, y).start()
                copy(t, CORE, owner, y, own).start()
                if own:
                    copy(t, CORE, owner, 1 - y, own).start()

            if distance == 0:
                pass_on()
            else:
                pl.when((at >= 0) & (at < line))(pass_on)

    def beside(t, distance):
        for sign in (0,) if distance == 0 else (1, -1):
            at = a + sign * distance

            def pass_on(at=at):
                owner = place.index(at, 1 - b, c)
                landed(t, owner, y)
                copy(t, OTHER, owner, y).start()
                copy(t, CORE, owner, y).start()

            pl.when((at >= 0) & (at < line))(pass_on)

    def from_other(t):
        for distance in range(line):
            for column in (b, 1 - b):
                for sign in (0,) if distance == 0 else (1, -1):
                    at = a + sign * distance

                    def pass_on(at=at, column=column):
                        owner = place.index(at, column, c)
                        landed(t, owner, 1 - y)
                        copy(t, CORE, owner, 1 - y).start()

                    if distance == 0 and column is b:
                        continue
                    pl.when((at >= 0) & (at < line))(pass_on)

    def own_copy(t):
        return pltpu.make_async_copy(
            sources[t], targets[t].at[at_rows(place.me * rows, rows)], own_sem.at[t]
        )

    def complete(t):
        def came(chip, carry):
            for part in range(2):
                landed(t, chip * 2 + (1 - c), part)
            return carry

        lax.fori_loop(0, 2 * line, came, 0)
        own_copy(t).wait()

    def chunk(n, to):
        if n == 0:
            return packed.at[to]
        return (up_ref, down_ref)[n - 1].at[:, at_rows(to * hidden, hidden)]

    def received(n, owner):
        return (watt_s, wup_s, wdown_ref)[n].at[at_rows(owner * weight_rows, weight_rows)]

    weights = Exchange(place, chunk, received, wsend, wreceive, wlocal)

    own_copy(0).start()
    own_copy(1).start()
    along(0, 0)
    for owner in range(4 * line):
        columns = pl.ds(owner * width, width)
        packed[owner, :, :] = jnp.concatenate(
            [qkv_ref[kind, :, columns] for kind in range(3)] + [out_ref[:, columns]], axis=1
        )
    weights.keep((0, 1, 2))
    ordered = [order_ref[at] for at in range(order_ref.shape[0])]

    def invert(wanted, carry):
        found = jnp.int32(0)
        for at, held in enumerate(ordered):
            found = jnp.where(held == wanted, at, found)
        inverse_ref[wanted] = found
        return carry

    for distance in range(1, line):
        along(0, distance)
        if distance == line - 2:
            along(1, 0)
        beside(0, distance - 1)
    beside(0, line - 1)
    lax.fori_loop(0, len(ordered), invert, 0)
    for distance in range(1, line - 1):
        along(1, distance)
        beside(1, distance - 1)
        if distance == 1:
            weights.start((0,))
    from_other(0)
    complete(0)
    weights.wait((0,))
    ship(x_ref, x_out)
    ship(watt_s, watt_out)

    quarter = tokens // inverse_ref.shape[0]
    quarters = block // quarter

    shared = batt_ref[:, at_rows(place.me // 2 * 2 * width, 2 * width)]
    shared = jnp.where(c == 0, shared[:, :width], shared[:, width:])
    bias_att = jnp.concatenate(
        [shared[kind : kind + 1] for kind in range(3)] + [jnp.zeros((1, width), F32)], axis=1
    )
    bias_up = bup_ref[:, at_rows(place.me * hidden, hidden)]

    def project(at, carry):
        here = at_rows(at * block, block)

        def load(start):
            return x_ref[here, pl.ds(start, piece)].astype(F32)

        mean, inv_std = row_stats(load, block, features, piece)
        for start in range(0, features, piece):
            part = pl.ds(start, piece)
            unit = (load(start) - mean) * inv_std
            normed_s[here, part] = (unit * gain_ref[:, part] + shift_ref[:, part]).astype(BF)
        mixed = mm(normed_s[here, :], watt_s[...]) + bias_att
        mixed_s[pl.ds(at * quarters, quarters)] = mixed.reshape(quarters, quarter, 4 * width)
        return carry

    lax.fori_loop(0, blocks // 2, project, 0)
    along(1, line - 1)
    beside(1, line - 2)
    weights.start((1,))
    lax.fori_loop(blocks // 2, blocks, project, 0)
    ship(normed_s, normed_out)
    beside(1, line - 1)
    weights.start((2,))

    wide = 2 * block
    scale = 1.0 / math.sqrt(HEAD)

    def prepare(at, carry):
        here = at_rows(at * block, block)
        mixed = jnp.concatenate(
            [mixed_s[inverse_ref[at * quarters + n]] for n in range(quarters)], axis=0
        )
        cosine, sine = angle_ref[here, : ROT // 2], angle_ref[here, ROT // 2 :]
        query = turned(mixed[:, :HEAD], cosine, sine).astype(BF) * jnp.asarray(scale, BF)
        key = turned(mixed[:, HEAD : 2 * HEAD], cosine, sine)
        value = mixed[:, 2 * HEAD : 3 * HEAD]
        k_s[here, :] = key.astype(BF)
        vt_s[:, here] = jnp.concatenate([value, value], axis=1).T[:HEAD].astype(BF)
        qkvs_ref[here, :] = jnp.concatenate(
            [query, key.astype(BF), value.astype(BF), jnp.zeros_like(query)], axis=1
        )
        return carry

    lax.fori_loop(0, blocks, prepare, 0)

    def forward(at, carry):
        here = at_rows(at * block, block)
        query = qkvs_ref[here, :][:, :HEAD]

        def scored(place_at, top, masked):
            there = at_rows(place_at * wide, wide)
            scores = mm(k_s[there, :], query, NT)
            if masked:
                scores = jnp.where(seen(place_at * wide, at * block, wide, block), scores, NEG)
            st[there, :] = scores
            return jnp.maximum(top, jnp.max(scores.reshape(wide // 8, 8, block), axis=0))

        last = at // 2
        top = lax.fori_loop(
            0, last, lambda n, top: scored(n, top, False), jnp.full((8, block), NEG, F32)
        )
        top = jnp.max(scored(last, top, True), axis=0, keepdims=True)

        def weighed(place_at, state):
            total, summed = state
            there = at_rows(place_at * wide, wide)
            expo = jnp.exp(st[there, :] - top)
            total = total + jnp.sum(expo.reshape(wide // 8, 8, block), axis=0)
            return (total, summed + mm(vt_s[:, there], expo.astype(BF)))

        total, summed = lax.fori_loop(
            0, last + 1, weighed, (jnp.zeros((8, block), F32), jnp.zeros((HEAD, block), F32))
        )
        total = jnp.sum(total, axis=0, keepdims=True)
        attended = summed * (1.0 / total)
        lse_ref[:, here] = jnp.broadcast_to(top + jnp.log(total), (8, block))
        attt_ref[:, here] = attended
        both = jnp.concatenate([attended, attended], axis=0).T.astype(BF)
        att_s[pl.ds(at * quarters, quarters)] = both.reshape(quarters, quarter, 2 * HEAD)
        return carry

    lax.fori_loop(0, blocks, forward, 0)
    for source, target in ((qkvs_ref, qkvs_out), (lse_ref, lse_out), (attt_ref, attt_out)):
        ship(source, target)

    def unplace(at, carry):
        attended = att_s[order_ref[at]][:, HEAD:]
        att_ref[at_rows(at * quarter, quarter), :] = jnp.concatenate(
            [jnp.zeros((quarter, 3 * HEAD), BF), attended], axis=1
        )
        return carry

    lax.fori_loop(0, tokens // quarter, unplace, 0)
    ship(att_ref, att_out)
    from_other(1)
    complete(1)
    ship(g_ref, g_out)

    def grad_in(at, carry):
        grad = mm(g_ref[at_rows(at * block, block), :], watt_s[...]).astype(BF)
        gatt_ref[pl.ds(at * quarters, quarters)] = grad.reshape(quarters, quarter, 4 * width)
        return carry

    lax.fori_loop(0, blocks, grad_in, 0)
    ship(gatt_ref, gatt_out)
    weights.wait((1,))
    ship(wup_s, wup_out)

    def feed(at, carry):
        here = at_rows(at * block, block)
        upward = mm(normed_s[here, :], wup_s[...]) + bias_up
        upward_ref[here, :] = upward
        act_ref[here, :] = (0.5 * upward * (1.0 + gelu_parts(upward))).astype(BF)
        return carry

    lax.fori_loop(0, blocks, feed, 0)
    ship(upward_ref, upward_out)
    ship(act_ref, act_out)
    for t in range(2):

        def left(at, carry, t=t):
            owner, beyond = place.index(at, b, c), place.index(at, 1 - b, c)
            pl.when((at <= a) & (a < line - 1))(lambda: copy(t, UP, owner, y).wait_send())
            pl.when((at >= a) & (a > 0))(lambda: copy(t, DOWN, owner, y).wait_send())
            copy(t, ACROSS, owner, y).wait_send()
            pl.when(at != a)(lambda: copy(t, OTHER, owner, y).wait_send())
            copy(t, OTHER, beyond, y).wait_send()
            for part in range(2):
                copy(t, CORE, owner, part).wait_send()
                copy(t, CORE, beyond, part).wait_send()
            return carry

        lax.fori_loop(0, line, left, 0)
    weights.wait((2,))
    for result in shipped:
        result.wait()


def collect(
    order, tokens, cotangent, qkv_weight, out_weight, fc1_weight, fc2_weight, gain, shift, bias_att,
    bias_up, angles,
):
    rows, features = tokens.shape
    weight_rows = fc1_weight.shape[0]
    count = lax.axis_size("ctx")
    line, width, hidden = count // 4, qkv_weight.shape[2] // count, fc1_weight.shape[1] // count
    total, depth = count * rows, count * weight_rows
    halves = order.shape[0]
    hbm, vmem = pl.BlockSpec(memory_space=pl.ANY), pl.BlockSpec(memory_space=pltpu.VMEM)
    smem = pl.BlockSpec(memory_space=pltpu.SMEM)
    dma = pltpu.SemaphoreType.DMA
    shape = jax.ShapeDtypeStruct
    return pl.pallas_call(
        functools.partial(collect_kernel, line),
        out_shape=[
            shape((total, features), BF),
            shape((total, features), BF),
            shape((depth, 4 * width), BF),
            shape((depth, hidden), BF),
            shape((depth, hidden), BF),
            shape((total, features), BF),
            shape((total, 4 * width), BF),
            shape((8, total), F32),
            shape((width, total), F32),
            shape((total, 4 * width), BF),
            shape((total, hidden), BF),
            shape((total, hidden), F32),
            shape((halves, total // halves, 4 * width), BF),
            shape((halves,), jnp.int32),
        ],
        in_specs=[smem, hbm, hbm, vmem, vmem, hbm, hbm] + [vmem] * 5,
        out_specs=[hbm] * 13 + [smem],
        scratch_shapes=[
            pltpu.VMEM((total, features), BF),
            pltpu.VMEM((total, features), BF),
            pltpu.VMEM((depth, 4 * width), BF),
            pltpu.VMEM((depth, hidden), BF),
            pltpu.VMEM((total, features), BF),
            pltpu.VMEM((total, 4 * width), BF),
            pltpu.VMEM((8, total), F32),
            pltpu.VMEM((width, total), F32),
            pltpu.VMEM((total, 4 * width), BF),
            pltpu.VMEM((total, hidden), BF),
            pltpu.VMEM((total, hidden), F32),
            pltpu.VMEM((halves, total // halves, 4 * width), BF),
            pltpu.VMEM((count, weight_rows, 4 * width), BF),
            pltpu.VMEM((halves, total // halves, 4 * width), F32),
            pltpu.VMEM((total, width), BF),
            pltpu.VMEM((width, total), BF),
            pltpu.VMEM((total, 2 * rows), F32),
            pltpu.VMEM((halves, total // halves, 2 * width), BF),
            dma((2, 5, count, 2)),
            dma((2, count, 2)),
            dma((2,)),
            dma((3, count)),
            dma((3, count)),
            dma((3,)),
            dma((12,)),
        ],
        compiler_params=pltpu.CompilerParams(
            collective_id=1, has_side_effects=True, vmem_limit_bytes=60 * 1024 * 1024
        ),
    )(
        order, tokens, cotangent, qkv_weight.transpose(1, 0, 2), out_weight, fc1_weight,
        fc2_weight, gain, shift, bias_att, bias_up, angles,
    )


def spread_kernel(
    line, order_ref, inverse_ref, att_ref, act_ref, lse_ref, angle_ref,
    watt_in, wdown_in, upward_in, gatt_in, qkvs_in, attt_in, wup_in, normed_ref, g_ref, x_ref,
    sum_ref, gsum_ref, ratt_ref, rup_ref, rdown_ref, rbias_ref, norms_ref, total_ref,
    weights_s, upward_ref, gatt_ref, qkvs_ref, attt_ref,
    fresh, own, from_core, from_other, from_across, from_beyond, from_line, done, turned_s, dsend, cols,
    buf, gain_s, shift_s, nsend, nfrom, nline, bias_s, gmix_s, gup_s, kt_s, dkv_s, gm_s,
    in_sem, cols_sem, buf_sem, csend, creceive, credit, ysend, yreceive, xsend, xreceive, bsend,
    breceive, zsend, zreceive, fsend, freceive, wsend, wreceive, wlocal, nsend_sem, nreceive, lsend,
    lreceive,
):
    place = Place(line)
    a, b, c, y = place.a, place.b, place.c, place.y
    sums = (sum_ref, gsum_ref)
    rows, features = own.shape[2:]
    half = rows // 2
    chips = 2 * line
    tokens = att_ref.shape[0]
    block = 2 * rows
    blocks = tokens // block
    weight_rows = dsend.shape[1] // (2 * chips)
    pair = 2 * weight_rows
    piece = 512
    ring = from_core.shape[0]
    shortcuts = tuple(range(line - from_beyond.shape[1], line))
    place.greet()
    wide, hidden = watt_in.shape[1], wup_in.shape[1]
    late = [
        pltpu.make_async_copy(source, target, in_sem.at[n])
        for n, (source, target) in enumerate(
            (
                (wdown_in, weights_s.at[:, pl.ds(0, hidden)]),
                (watt_in, weights_s.at[:, pl.ds(hidden, wide)]),
                (upward_in, upward_ref),
                (gatt_in, gatt_ref),
                (qkvs_in, qkvs_ref),
                (attt_in, attt_ref),
                (wup_in, weights_s.at[:, pl.ds(hidden + wide, hidden)]),
            )
        )
    ]
    for operand in late:
        operand.start()
    mine, theirs = at_rows(y * half, half), at_rows((1 - y) * half, half)
    both, sibling = at_rows(c * rows, rows), at_rows((1 - c) * rows, rows)

    def chunk(n, to):
        if n == 3:
            return bias_s
        return dsend.at[n, at_rows(to * weight_rows, weight_rows)]

    def received(n, owner):
        return (ratt_ref, rup_ref, rdown_ref, rbias_ref)[n].at[owner]

    weights = Exchange(place, chunk, received, wsend, wreceive, wlocal)

    def order(turn):
        at = place.far_first(turn // 2)
        return at, at * 2 + jnp.where(lax.rem(turn, 2) == 0, 1 - b, b)

    def to_core(t, turn):
        return remote(
            fresh.at[lax.rem(turn, 2), sibling], from_core.at[lax.rem(turn, ring)], csend.at[t, turn],
            creceive.at[lax.rem(turn, ring)], place.device[CORE],
        )

    def to_other(t, chip):
        return remote(
            own.at[t, chip, theirs], from_other.at[t, chip], ysend.at[t, chip], yreceive.at[t, chip],
            place.device[OTHER],
        )

    def to_across(t, at):
        return remote(
            own.at[t, at * 2 + 1 - b, mine], from_across.at[t, at], xsend.at[t, at], xreceive.at[t, at],
            place.device[ACROSS],
        )

    def to_beyond(t, nth):
        at, slot = place.far_first(nth), nth - shortcuts[0]
        return remote(
            own.at[t, at * 2 + 1 - b], from_beyond.at[t, slot], bsend.at[t, slot],
            breceive.at[t, slot], place.device[ACROSS],
        )

    def to_up(t, at):
        return remote(
            own.at[t, at * 2 + b, mine], from_line.at[t, at], zsend.at[t, at], zreceive.at[t, at],
            place.device[UP],
        )

    def to_down(t, at, last):
        slot = line if last else at
        return remote(
            own.at[t, at * 2 + b, mine], from_line.at[t, slot], zsend.at[t, at], zreceive.at[t, slot],
            place.device[DOWN],
        )

    def final(t, part):
        return remote(
            done.at[t, part], done.at[t, part], fsend.at[t], freceive.at[t], place.device[OTHER]
        )

    def add(t, chip, part, other):
        own[t, chip, part, :] = (own[t, chip, part, :].astype(F32) + other.astype(F32)).astype(BF)

    def columns_of(n, source):
        return Stream(
            lambda at, slot: pltpu.make_async_copy(
                source.at[:, at_rows(weights.chip(at) * pair, pair)],
                cols.at[n, slot],
                cols_sem.at[n, slot],
            ),
            cols.shape[1],
            chips,
        )

    def rows_of(source, chip_of):
        return Stream(
            lambda at, slot: pltpu.make_async_copy(
                source.at[at_rows(chip_of(at) * block, block)], buf.at[slot], buf_sem.at[slot]
            ),
            buf.shape[0],
            blocks,
        )

    g_rows, x_rows = rows_of(g_ref, lambda at: at), rows_of(x_ref, lambda at: order(at)[1])
    normed_columns, g_columns = columns_of(0, normed_ref), columns_of(1, g_ref)
    g_rows.prime()
    normed_columns.prime()
    g_columns.prime()

    def product(t, turn):
        _, chip = order(turn)
        here = at_rows(chip * block, block)
        fresh_at = lax.rem(turn, 2)
        left = ((act_ref, att_ref), (gmix_s, gup_s))[t]
        left = jnp.concatenate([left[0][here, :], left[1][here, :]], axis=1)
        right = pl.ds((0, hidden)[t], hidden + wide)
        if t == 1:
            slot = x_rows.step(turn)

            def load(start):
                return buf[slot, :, pl.ds(start, piece)].astype(F32)

            mean, inv_std = row_stats(load, block, features, piece)
        for start in range(0, features, piece):
            part = pl.ds(start, piece)
            value = mm(left, weights_s[part, right], NT)
            fresh[fresh_at, :, part] = value.astype(BF)
            if t == 1:
                unit = (load(start) - mean) * inv_std
                shift_s[:, part] += jnp.sum(value.reshape(block // 8, 8, piece), axis=0)
                gain_s[:, part] += jnp.sum((unit * value).reshape(block // 8, 8, piece), axis=0)
        if t == 1:
            pl.semaphore_wait(credit, 1)
        else:
            pl.when(turn >= ring)(lambda: pl.semaphore_wait(credit, 1))
        to_core(t, turn).start()

    def stage_core(t, turn):
        _, chip = order(turn)
        to_core(t, turn).wait_recv()
        own[t, chip, :, :] = (
            fresh[lax.rem(turn, 2), both, :].astype(F32)
            + from_core[lax.rem(turn, ring)].astype(F32)
        ).astype(BF)

        def give():
            pl.semaphore_signal(
                credit, inc=1, device_id=place.device[CORE], device_id_type=MESH
            )

        if t == 0:
            give()
        else:
            pl.when(turn < chips - ring)(give)
        pl.when(turn < 2 * shortcuts[0])(lambda: to_other(t, chip).start())
        for nth in shortcuts:
            pl.when(turn == 2 * nth)(lambda nth=nth: to_beyond(t, nth).start())
        to_core(t, turn).wait_send()

    def stage_beyond(t):
        for nth in shortcuts:
            chip = place.far_first(nth) * 2 + b
            to_beyond(t, nth).wait_recv()
            add(t, chip, pl.ds(0, rows), from_beyond[t, nth - shortcuts[0]])
            to_other(t, chip).start()

    def stage_other(t, nth):
        if nth in shortcuts:
            return
        at = place.far_first(nth)
        chip = at * 2 + 1 - b
        to_other(t, chip).wait_recv()
        add(t, chip, mine, from_other[t, chip])
        to_across(t, at).start()

    def stage_line(t, nth):
        at = place.far_first(nth)
        chip = at * 2 + b
        to_other(t, chip).wait_recv()
        if nth in shortcuts:
            add(t, chip, mine, from_other[t, chip])
        else:
            to_across(t, at).wait_recv()
            add(t, chip, mine, from_other[t, chip].astype(F32) + from_across[t, at].astype(F32))

        def down():
            @pl.when(a < line - 1)
            def _():
                to_down(t, at, False).wait_recv()
                add(t, chip, mine, from_line[t, at])

            pl.when(at == a - 1)(lambda: to_down(t, at, True).start())
            pl.when(at < a - 1)(lambda: to_down(t, at, False).start())

        def up():
            @pl.when(a > 0)
            def _():
                to_up(t, at).wait_recv()
                add(t, chip, mine, from_line[t, at])

            to_up(t, at).start()

        if nth < line - 1:
            pl.when(at < a)(down)
            pl.when(at > a)(up)
            return

        @pl.when(a < line - 1)
        def _():
            to_down(t, at, True).wait_recv()
            add(t, chip, mine, from_line[t, line])

        @pl.when(a > 0)
        def _():
            to_up(t, at).wait_recv()
            add(t, chip, mine, from_line[t, at])

        done[t, mine, :] = own[t, chip, mine, :]
        final(t, mine).start()

    def norm_copy(step):
        kind = (CORE, OTHER, ACROSS)[step]
        return remote(
            nsend.at[step], nfrom.at[step], nsend_sem.at[step], nreceive.at[step], place.device[kind]
        )

    def norm_line(other, came):
        return remote(
            nsend.at[3], nline.at[other if came else a], lsend.at[other],
            lreceive.at[other if came else a], (place.index(other, b, c), y),
        )

    for operand in late[:2]:
        operand.wait()
    product(0, 0)

    def turn_over(pieces):
        def one(at, carry):
            here = at_rows(at * 256, 256)
            for n, source in pieces:
                turned_s[n, :, here] = source[here, :].T
            return carry

        lax.fori_loop(0, tokens // 256, one, 0)

    turn_over(((2, att_ref), (3, act_ref)))
    ones = jnp.ones((8, tokens), BF)

    def gradients_down(turn):
        slot = g_columns.step(turn)
        here = at_rows(weights.chip(turn) * pair, pair)
        by_grad = cols[1, slot]
        dsend[2, here, :] = mm(turned_s[3], by_grad).T.astype(BF)
        dsend[0, here, :] = mm(turned_s[2], by_grad).T.astype(BF)
        total_ref[:, here] = mm(ones, by_grad)
        weights.start_chip((2,), turn)

    def first_sum(turn, carry):
        product(0, turn)
        stage_core(0, turn - 1)
        gradients_down(turn - 1)
        return carry

    lax.fori_loop(1, chips, first_sum, 0)
    stage_core(0, chips - 1)
    gradients_down(chips - 1)

    late[2].wait()

    def feed_back(at, carry):
        slot = g_rows.step(at)
        here = at_rows(at * block, block)
        upward = upward_ref[here, :]
        tanh = gelu_parts(upward)
        slope = 0.5 * (1.0 + tanh) + 0.5 * upward * (1.0 - tanh * tanh) * (
            math.sqrt(2.0 / math.pi) * (1.0 + 3 * 0.044715 * upward * upward)
        )
        gup_s[here, :] = (mm(buf[slot], weights_s[:, pl.ds(0, hidden)]) * slope).astype(BF)
        return carry

    lax.fori_loop(0, blocks, feed_back, 0)
    stage_other(0, 0)
    x_rows.prime()

    turn_over(((1, gup_s),))

    def gradients_up(turn, carry):
        slot = normed_columns.step(turn)
        here = at_rows(weights.chip(turn) * pair, pair)
        dsend[1, here, :] = mm(turned_s[1], cols[0, slot]).T.astype(BF)
        weights.start_chip((1,), turn)
        return carry

    lax.fori_loop(0, chips, gradients_up, 0)
    stage_other(0, 1)
    normed_columns.prime()
    for operand in late[3:]:
        operand.wait()

    quarter = tokens // inverse_ref.shape[0]
    quarters = block // quarter
    span = 2 * block
    scale = 1.0 / math.sqrt(HEAD)

    def prepare(at, carry):
        here = at_rows(at * block, block)
        key = qkvs_ref[here, :][:, : 2 * HEAD].astype(F32)
        kt_s[:, here] = key.T[HEAD:].astype(BF)
        dkv_s[here, :] = jnp.zeros((block, 2 * HEAD), F32)
        return carry

    lax.fori_loop(0, blocks, prepare, 0)

    def backward(at, carry):
        here = at_rows(at * span, span)
        query = qkvs_ref[here, :][:, :HEAD]
        grad = jnp.concatenate(
            [gatt_ref[inverse_ref[at * 2 * quarters + n]] for n in range(2 * quarters)], axis=0
        )
        left = lax.broadcasted_iota(jnp.int32, (span, 2 * HEAD), 1) < HEAD
        grad_wide = grad[:, 2 * HEAD :].astype(F32)
        grad_right = jnp.where(left, 0.0, grad_wide).astype(BF)
        query_left = jnp.concatenate([query, jnp.zeros_like(query)], axis=1)
        beside_each = jnp.concatenate([query_left, grad_right], axis=0)
        grad = grad[:, 3 * HEAD :]
        delta = jnp.sum(grad_wide.T[HEAD:] * attt_ref[:, here], axis=0, keepdims=True)
        lse = lse_ref[0:1, here]

        def back(place_at, query_grad, masked):
            there = at_rows(place_at * span, span)
            keyvalue = qkvs_ref[there, :]
            scores = mm(keyvalue[:, HEAD : 2 * HEAD], query, NT)
            if masked:
                scores = jnp.where(seen(0, 0, span, span), scores, NEG)
            prob = jnp.exp(scores - lse)
            dprob = mm(keyvalue[:, 2 * HEAD : 3 * HEAD], grad, NT)
            dscore = (prob * (dprob - delta)).astype(BF)
            dkv_s[there, :] += mm(
                jnp.concatenate([dscore, prob.astype(BF)], axis=1), beside_each
            )
            return query_grad + mm(kt_s[:, there], dscore)

        query_grad = lax.fori_loop(
            0, at, lambda n, total: back(n, total, False), jnp.zeros((HEAD, span), F32)
        )
        query_grad = back(at, query_grad, True)
        query_grad = jnp.concatenate([query_grad, query_grad], axis=0).T[:, :HEAD]
        query_grad = turned(
            query_grad * scale, angle_ref[here, : ROT // 2], -angle_ref[here, ROT // 2 :]
        ).astype(BF)
        gm_s[pl.ds(at * 2 * quarters, 2 * quarters), :, pl.ds(0, HEAD)] = query_grad.reshape(
            2 * quarters, quarter, HEAD
        )
        return carry

    lax.fori_loop(0, blocks // 4, backward, 0)
    stage_beyond(0)
    for nth in range(2, line - 1):
        stage_other(0, nth)
    lax.fori_loop(blocks // 4, blocks // 2, backward, 0)
    if line > 2:
        stage_other(0, line - 1)

    def finish_keys(at, carry):
        here = at_rows(at * block, block)
        keyvalue = jnp.concatenate(
            [
                turned(
                    dkv_s[here, :][:, :HEAD], angle_ref[here, : ROT // 2], -angle_ref[here, ROT // 2 :]
                ).astype(BF),
                dkv_s[here, :][:, HEAD:].astype(BF),
            ],
            axis=1,
        )
        gm_s[pl.ds(at * quarters, quarters), :, pl.ds(HEAD, 2 * HEAD)] = keyvalue.reshape(
            quarters, quarter, 2 * HEAD
        )
        return carry

    lax.fori_loop(0, blocks, finish_keys, 0)

    def unplace(at, carry):
        gmix_s[at_rows(at * quarter, quarter), :] = jnp.concatenate(
            [gm_s[order_ref[at]], jnp.zeros((quarter, HEAD), BF)], axis=1
        )
        return carry

    lax.fori_loop(0, tokens // quarter, unplace, 0)
    turn_over(((0, gmix_s),))
    for n, source in enumerate((gmix_s, gup_s)):
        columns = source.shape[1]

        def tally(at, total, source=source, columns=columns):
            return total + jnp.sum(
                source[at_rows(at * 256, 256), :].astype(F32).reshape(32, 8, columns), axis=0
            )

        total = lax.fori_loop(0, tokens // 256, tally, jnp.zeros((8, columns), F32))
        total = jnp.sum(total, axis=0, keepdims=True)
        for at in range(columns // 128):
            bias_s[pl.ds(n * 2 + at, 1), :] = total[:, at * 128 : (at + 1) * 128]
    bias_s[pl.ds(4, 4), :] = jnp.zeros((4, 128), F32)

    gain_s[...] = jnp.zeros_like(gain_s)
    shift_s[...] = jnp.zeros_like(shift_s)

    def gradients_att(turn, carry):
        slot = normed_columns.step(turn)
        here = at_rows(weights.chip(turn) * pair, pair)
        more = mm(turned_s[0], cols[0, slot]).T
        dsend[0, here, :] = (dsend[0, here, :].astype(F32) + more).astype(BF)
        weights.start_chip((0, 3), turn)
        return carry

    lax.fori_loop(0, chips, gradients_att, 0)
    product(1, 0)

    def second_sum(turn, carry):
        product(1, turn)
        stage_core(1, turn - 1)
        return carry

    lax.fori_loop(1, chips, second_sum, 0)
    stage_core(1, chips - 1)
    for n, source in enumerate((gain_s, shift_s)):
        total = jnp.sum(source[...], axis=0, keepdims=True)
        quarter_of = features // 4
        for at in range(4):
            nsend[0, pl.ds(n * 4 + at, 1), :] = total[:, at * quarter_of : (at + 1) * quarter_of]
    norm_copy(0).start()
    stage_other(1, 0)
    stage_line(0, 0)
    stage_line(0, 1)
    stage_other(1, 1)
    stage_line(0, 2)
    stage_line(1, 0)
    norm_copy(0).wait_recv()
    nsend[1] = nsend[0] + nfrom[0]
    norm_copy(1).start()
    stage_beyond(1)
    stage_other(1, 2)
    norm_copy(1).wait_recv()
    nsend[2] = nsend[1] + nfrom[1]
    norm_copy(2).start()
    stage_line(1, 1)
    stage_line(1, 2)
    norm_copy(2).wait_recv()
    nsend[3] = nsend[2] + nfrom[2]
    nline[a] = nsend[3]
    for other in range(line):
        pl.when(a != other)(lambda other=other: norm_line(other, False).start())
    stage_line(0, 3)
    stage_line(1, 3)
    for other in range(line):
        pl.when(a != other)(lambda other=other: norm_line(other, True).wait_recv())
    total = nline[0]
    for other in range(1, line):
        total += nline[other]
    norms_ref[...] = total

    for step in range(3):
        norm_copy(step).wait_send()
    for other in range(line):
        pl.when(a != other)(lambda other=other: norm_line(other, False).wait_send())
    for t in range(2):
        final(t, theirs).wait_recv()
        final(t, mine).wait_send()
        sums[t][...] = done[t]

        def left(at, carry, t=t):
            to_other(t, at * 2 + b).wait_send()
            pl.when(at != a)(lambda: to_up(t, at).wait_send())

            def also():
                to_other(t, at * 2 + 1 - b).wait_send()
                to_across(t, at).wait_send()

            shorter = at == place.far_first(shortcuts[0])
            for nth in shortcuts[1:]:
                shorter = shorter | (at == place.far_first(nth))
            pl.when(jnp.logical_not(shorter))(also)
            return carry

        lax.fori_loop(0, line, left, 0)
        for nth in shortcuts:
            to_beyond(t, nth).wait_send()
    weights.wait((0, 1, 2, 3))


def spread(
    order, inverse, attended, activated, upward, grad_att, qkvs, lse, attended_t, w_att, w_up, w_down,
    angles, normed, g_all, x_all,
):
    count = lax.axis_size("ctx")
    line = count // 4
    tokens, features = x_all.shape
    rows = tokens // count
    half = rows // 2
    chips = 2 * line
    weight_rows = w_att.shape[0] // count
    wide, hidden = w_att.shape[1], w_up.shape[1]
    hbm, vmem = pl.BlockSpec(memory_space=pl.ANY), pl.BlockSpec(memory_space=pltpu.VMEM)
    smem = pl.BlockSpec(memory_space=pltpu.SMEM)
    dma = pltpu.SemaphoreType.DMA
    own = jax.ShapeDtypeStruct((rows, features), BF)
    back = [
        jax.ShapeDtypeStruct((count, weight_rows, columns), BF) for columns in (wide, hidden, hidden)
    ]
    return pl.pallas_call(
        functools.partial(spread_kernel, line),
        out_shape=[own, own]
        + back
        + [
            jax.ShapeDtypeStruct((count, 8, 128), F32),
            jax.ShapeDtypeStruct((8, features // 4), F32),
            jax.ShapeDtypeStruct((8, features), F32),
        ],
        in_specs=[smem, smem] + [vmem] * 4 + [hbm] * 10,
        out_specs=[vmem, vmem, hbm, hbm, hbm, hbm, vmem, vmem],
        scratch_shapes=[
            pltpu.VMEM((count * weight_rows, wide + 2 * hidden), BF),
            pltpu.VMEM(upward.shape, F32),
            pltpu.VMEM(grad_att.shape, BF),
            pltpu.VMEM(qkvs.shape, BF),
            pltpu.VMEM(attended_t.shape, F32),
            pltpu.VMEM((2, 2 * rows, features), BF),
            pltpu.VMEM((2, chips, rows, features), BF),
            pltpu.VMEM((4, rows, features), BF),
            pltpu.VMEM((2, chips, half, features), BF),
            pltpu.VMEM((2, line, half, features), BF),
            pltpu.VMEM((2, 1, rows, features), BF),
            pltpu.VMEM((2, line + 1, half, features), BF),
            pltpu.VMEM((2, rows, features), BF),
            pltpu.VMEM((4, wide, tokens), BF),
            pltpu.VMEM((3, count * weight_rows, wide), BF),
            pltpu.VMEM((2, 3, tokens, 2 * weight_rows), BF),
            pltpu.VMEM((3, 2 * rows, features), BF),
            pltpu.VMEM((8, features), F32),
            pltpu.VMEM((8, features), F32),
            pltpu.VMEM((4, 8, features // 4), F32),
            pltpu.VMEM((3, 8, features // 4), F32),
            pltpu.VMEM((line, 8, features // 4), F32),
            pltpu.VMEM((8, 128), F32),
            pltpu.VMEM((tokens, wide), BF),
            pltpu.VMEM((tokens, hidden), BF),
            pltpu.VMEM((HEAD, tokens), BF),
            pltpu.VMEM((tokens, 2 * HEAD), F32),
            pltpu.VMEM((order.shape[0], tokens // order.shape[0], 3 * HEAD), BF),
            dma((7,)),
            dma((2, 3)),
            dma((3,)),
            dma((2, chips)),
            dma((4,)),
            pltpu.SemaphoreType.REGULAR,
            dma((2, chips)),
            dma((2, chips)),
            dma((2, line)),
            dma((2, line)),
            dma((2, 1)),
            dma((2, 1)),
            dma((2, line)),
            dma((2, line + 1)),
            dma((2,)),
            dma((2,)),
            dma((4, count)),
            dma((4, count)),
            dma((4,)),
            dma((3,)),
            dma((3,)),
            dma((line,)),
            dma((line,)),
        ],
        compiler_params=pltpu.CompilerParams(
            collective_id=2, has_side_effects=True, vmem_limit_bytes=63 * 1024 * 1024
        ),
    )(
        order, inverse, attended, activated, lse, angles, w_att, w_down, upward, grad_att, qkvs,
        attended_t, w_up, normed, g_all, x_all,
    )


def finish_kernel(
    tok_ref, cot_ref, gain_ref, bias_ref, branch_ref, normed_ref, datt_ref, dup_ref, ddown_ref,
    sums_ref, norms_ref, total_ref,
    out_ref, grad_ref, qkv_ref, wout_ref, up_ref, down_ref, qkvb_ref, upb_ref, gsum_ref, ssum_ref,
    bsum_ref,
):
    inputs = tok_ref[...].astype(F32)
    center = inputs - jnp.mean(inputs, axis=-1, keepdims=True)
    inv_std = lax.rsqrt(jnp.mean(center * center, axis=-1, keepdims=True) + EPS)
    unit = center * inv_std
    out_ref[...] = inputs + branch_ref[...].astype(F32) + bias_ref[...]
    grad_unit = normed_ref[...].astype(F32) * gain_ref[...]
    grad_ref[...] = cot_ref[...].astype(F32) + inv_std * (
        grad_unit
        - jnp.mean(grad_unit, axis=-1, keepdims=True)
        - unit * jnp.mean(grad_unit * unit, axis=-1, keepdims=True)
    )
    count, _, packed = datt_ref.shape
    width, hidden = packed // 4, dup_ref.shape[2]
    pieces = [datt_ref[owner].astype(F32) for owner in range(count)]

    def together(kind):
        return jnp.concatenate(
            [piece[:, kind * width : (kind + 1) * width] for piece in pieces], axis=1
        )

    for kind in range(3):
        qkv_ref[kind, :, :] = together(kind)
        at = kind * width
        qkvb_ref[kind : kind + 1, :] = jnp.concatenate(
            [
                sums_ref[owner, at // 128 : at // 128 + 1, at % 128 : at % 128 + width]
                for owner in range(count)
            ],
            axis=1,
        )
    wout_ref[...] = together(3)
    for owner in range(count):
        columns = pl.ds(owner * hidden, hidden)
        up_ref[:, columns] = dup_ref[owner].astype(F32)
        down_ref[:, columns] = ddown_ref[owner].astype(F32)
        for at in range(hidden // 128):
            upb_ref[:, pl.ds(owner * hidden + at * 128, 128)] = sums_ref[owner, 2 + at : 3 + at, :]
    wide = norms_ref.shape[1]
    for at in range(4):
        gsum_ref[:, pl.ds(at * wide, wide)] = norms_ref[at : at + 1, :]
        ssum_ref[:, pl.ds(at * wide, wide)] = norms_ref[4 + at : 5 + at, :]
    bsum_ref[...] = total_ref[0:1, :]


def finish(tokens, cotangent, gain, bias, branches, own_normed, d_att, d_up, d_down, sums, norms, total):
    count, weight_rows, packed = d_att.shape
    rows, features = tokens.shape
    width, hidden = packed // 4, d_up.shape[2]
    owners = max(128 // width, count // 2)
    steps = count // owners
    by_rows = pl.BlockSpec((rows // steps, features), lambda at: (at, 0))
    line = pl.BlockSpec((1, features), lambda at: (0, 0))

    def whole(array):
        return pl.BlockSpec(array.shape, lambda at: (0,) * array.ndim)

    def by_owner(array):
        return pl.BlockSpec((owners, *array.shape[1:]), lambda at: (at, 0, 0))

    def by_columns(*lead):
        return lambda columns: pl.BlockSpec(
            (*lead, owners * columns), lambda at: (*(0,) * len(lead), at)
        )

    shape = jax.ShapeDtypeStruct
    return pl.pallas_call(
        finish_kernel,
        grid=(steps,),
        out_shape=[
            shape(tokens.shape, F32),
            shape(tokens.shape, F32),
            shape((3, weight_rows, count * width), F32),
            shape((weight_rows, count * width), F32),
            shape((weight_rows, count * hidden), F32),
            shape((weight_rows, count * hidden), F32),
            shape((3, count * width), F32),
            shape((1, count * hidden), F32),
            shape((1, features), F32),
            shape((1, features), F32),
            shape((1, features), F32),
        ],
        in_specs=[by_rows, by_rows, line, line, by_rows, by_rows]
        + [by_owner(array) for array in (d_att, d_up, d_down, sums)]
        + [whole(norms), whole(total)],
        out_specs=[
            by_rows,
            by_rows,
            by_columns(3, weight_rows)(width),
            by_columns(weight_rows)(width),
            by_columns(weight_rows)(hidden),
            by_columns(weight_rows)(hidden),
            by_columns(3)(width),
            by_columns(1)(hidden),
            line,
            line,
            line,
        ],
        compiler_params=pltpu.CompilerParams(vmem_limit_bytes=63 * 1024 * 1024),
    )(
        tokens, cotangent, gain[None], bias[None], branches, own_normed, d_att, d_up, d_down, sums,
        norms, total,
    )


def gelu_tanh(value):
    return jax.nn.gelu(value, approximate=True)


def local(
    tokens, block_order, ln_gain, ln_bias, qkv_weight, qkv_bias, out_weight, fc1_weight, fc1_bias,
    fc2_weight, out_bias, cotangent,
):
    devices = lax.axis_size("ctx")
    myself = lax.axis_index("ctx")
    heads_here = qkv_weight.shape[2] // HEAD
    columns = math.gcd(devices, heads_here)
    mine = myself % columns
    width = qkv_weight.shape[2] // columns
    hidden = fc1_weight.shape[1] // columns
    if devices == columns and columns % 8 == 0 and width == HEAD and lax.axis_size("tp") == 2:
        freqs = 10000.0 ** (-np.arange(0, ROT, 2, dtype=np.float32) / ROT)
        angles = np.arange(devices * tokens.shape[0], dtype=np.float32)[:, None] * freqs[None, :]
        angles = jnp.asarray(np.concatenate([np.cos(angles), np.sin(angles)], axis=1), F32)
        (
            x_all, g_all, w_att, w_up, w_down, normed, qkvs, lse, attended_t, attended, activated,
            upward, grad_att, inverse,
        ) = collect(
            block_order, tokens, cotangent, qkv_weight, out_weight, fc1_weight, fc2_weight,
            ln_gain[None], ln_bias[None], qkv_bias, fc1_bias[None], angles,
        )
        parts = spread(
            block_order, inverse, attended, activated, upward, grad_att, qkvs, lse, attended_t, w_att,
            w_up, w_down, angles, normed, g_all, x_all,
        )
    else:
        bias_att = lax.dynamic_slice_in_dim(qkv_bias, mine * width, width, 1).reshape(-1)
        bias_att = jnp.concatenate([bias_att, jnp.zeros((width,), F32)])[None]
        bias_up = lax.dynamic_slice_in_dim(fc1_bias, mine * hidden, hidden, 0)[None]
        parts = by_groups(
            tokens, block_order, ln_gain, ln_bias, qkv_weight, out_weight, fc1_weight, fc2_weight,
            cotangent, bias_att, bias_up,
        )
    (
        output, input_grad, qkv_grad, out_grad, fc1_grad, fc2_grad, qkv_sums, fc1_sums, gain_sum,
        shift_sum, g_sum,
    ) = finish(tokens, cotangent, ln_gain, out_bias, *parts)
    return (
        output, input_grad, gain_sum[0], shift_sum[0], qkv_grad.transpose(1, 0, 2), qkv_sums, out_grad,
        fc1_grad, fc1_sums[0], fc2_grad, g_sum[0],
    )


def by_groups(
    tokens, block_order, ln_gain, ln_bias, qkv_weight, out_weight, fc1_weight, fc2_weight, cotangent,
    bias_att, bias_up,
):
    devices = lax.axis_size("ctx")
    myself = lax.axis_index("ctx")
    rows_here = tokens.shape[0]
    weight_rows = qkv_weight.shape[0]
    half = devices * rows_here // block_order.shape[0]
    columns = math.gcd(devices, qkv_weight.shape[2] // HEAD)
    groups = devices // columns
    width, hidden = qkv_weight.shape[2] // columns, fc1_weight.shape[1] // columns
    count = columns * rows_here
    side = [[r * columns + c for c in range(columns)] for r in range(groups)]
    across = [[r * columns + c for r in range(groups)] for c in range(columns)]

    def gathered(value, among):
        return lax.all_gather(value, "ctx", axis=0, tiled=True, axis_index_groups=among)

    def scattered(value, among):
        return lax.psum_scatter(
            value, "ctx", scatter_dimension=0, tiled=True, axis_index_groups=among
        )

    def exchanged(value):
        return lax.all_to_all(value, "ctx", split_axis=0, concat_axis=0, tiled=True)

    x_all, g_all = gathered(tokens, side), gathered(cotangent, side)
    kinds = jnp.concatenate([qkv_weight, out_weight[:, None]], axis=1)
    kinds = kinds.reshape(weight_rows, 4, columns, width).transpose(2, 0, 1, 3)
    packed = jnp.concatenate(
        [
            kinds.reshape(columns, weight_rows, 4 * width),
            fc1_weight.reshape(weight_rows, columns, hidden).transpose(1, 0, 2),
            fc2_weight.reshape(weight_rows, columns, hidden).transpose(1, 0, 2),
        ],
        axis=2,
    )
    packed = exchanged(jnp.tile(packed, (groups, 1, 1))).reshape(devices * weight_rows, -1)
    w_att, w_up, w_down = jnp.split(packed, [4 * width, 4 * width + hidden], axis=1)

    inputs = x_all.astype(F32)
    center = inputs - jnp.mean(inputs, axis=-1, keepdims=True)
    inv_std = lax.rsqrt(jnp.mean(center * center, axis=-1, keepdims=True) + EPS)
    unit = center * inv_std
    normed = (unit * ln_gain + ln_bias).astype(BF)
    upward = mm(normed, w_up) + bias_up
    activated, gelu_back = jax.vjp(gelu_tanh, upward)
    activated = activated.astype(BF)
    grad_up = gelu_back(mm(g_all, w_down))[0].astype(BF)
    places = (block_order[:, None] * half + jnp.arange(half, dtype=jnp.int32)[None, :]).reshape(-1)
    attended, grad_mixed = attention_blocks(
        lax.dynamic_slice_in_dim(places, (myself // columns) * count, count),
        places,
        mm(normed, w_att) + bias_att,
        mm(g_all, w_att),
        lambda value: gathered(value, across),
        lambda value: scattered(value, across),
    )
    out_part = (mm(attended, w_att, NT) + mm(activated, w_down, NT)).astype(BF)
    normed_wide = mm(grad_mixed, w_att, NT) + mm(grad_up, w_up, NT)
    branches, own_normed = lax.psum(
        (scattered(out_part, side), scattered(normed_wide.astype(BF), side)), "tp"
    )
    back = jnp.concatenate(
        [
            (mm(normed, grad_mixed, TN) + mm(g_all, attended, TN)).astype(BF),
            mm(normed, grad_up, TN).astype(BF),
            mm(g_all, activated, TN).astype(BF),
        ],
        axis=1,
    )
    back = exchanged(back.reshape(devices, weight_rows, -1))
    back = jnp.sum(back.reshape(groups, columns, weight_rows, -1).astype(F32), axis=0)
    sums = jnp.concatenate(
        [jnp.sum(grad_mixed.astype(F32), axis=0), jnp.sum(grad_up.astype(F32), axis=0)]
    ).reshape(-1, 128)
    sums = jnp.pad(sums, ((0, 8 - sums.shape[0]), (0, 0)))
    sums = gathered(lax.psum(sums, "ctx", axis_index_groups=across)[None], side)
    norms = jnp.stack([jnp.sum(unit * normed_wide, axis=0), jnp.sum(normed_wide, axis=0)])
    norms = lax.psum(norms, ("ctx", "tp")).reshape(8, -1)
    total = lax.psum(jnp.sum(g_all.astype(F32), axis=0), "ctx", axis_index_groups=across)[None]
    return (
        branches, own_normed, *jnp.split(back, [4 * width, 4 * width + hidden], axis=2), sums, norms,
        total,
    )


def solution(mesh):
    rows, tall = P("ctx", None), P("ctx", "tp")
    kinds, bias = P("ctx", None, "tp"), P(None, "tp")
    return jax.shard_map(
        local,
        mesh=mesh,
        in_specs=(rows, P(), P(), P(), kinds, bias, tall, tall, P("tp"), tall, P(), rows),
        out_specs=(rows, rows, P(), P(), kinds, bias, tall, tall, P("tp"), tall, P()),
        check_vma=False,
    )
```
